32 devices in a mesh: kpt: 4 (over y, x), pw: 8 (over z, core).
Axes of the slice: x: 2, y: 2, z: 4, core: 2. Of those that a mesh axis runs over, the one named last changes fastest.
Arguments:
- band_coeffs: float32 [4, 2, 2, 393216], P('kpt', None, None, 'pw'), may hold values from -6 to 6
- miller_third: int32 [4, 393216], P('kpt', 'pw'), may hold values from -64 to 63, as said below
- column_slot: int32 [4, 393216], P('kpt', 'pw'), may hold values from 0 to 383, as said below
- column_map: int32 [3072], P('pw'), may hold values from 0 to 16383, as said below
- kpoint_counts: int32 [4], replicated, may hold values from 1 to 12
Outputs:
- density: float32 [256, 128, 128], P('pw', 'kpt')
- hartree: float32 [256, 128, 128], P('pw', 'kpt')
The draws below stay inside these ranges and needn't reach their ends.
Inputs may be any that keep to these rules, and one draw needn't show every extreme that they name: `miller_third`: on each device of pw and for each k-point, the 49152 entries pair with column_slot so that every pair of a slot and a z index occurs exactly once. `column_slot`: the slot of each coefficient among the 384 columns of the device of pw that holds it. `column_map`: distinct flattened indices x * 128 + y of the 3072 columns with the smallest (s_x / 128)^2 + (s_y / 128)^2 in signed frequencies, ties at the rim taken at random; entries j * 384 to (j + 1) * 384 - 1 are the columns of device j of pw, assigned at random; the same for every k-point.
All inputs are finite; a program needn't handle non-finite values.
Results may differ from the reference program's by a relative error of at most 0.0003.
Values sent between devices are 32-bit elements; how exact they have to be, the bound alone decides.
No kernel may reach another device: no remote copies, remote signals or barrier semaphores. Data moves between devices by JAX's collectives and lax.ppermute only.
A program may use at most 128 MiB of HBM per device.

```python
import math
import jax
import jax.numpy as jnp
from jax import lax

NX = 128
NY = 128
NZ = 256
ZW = 128
NB = 2
KPOOLS = 4
NCOL = 3072
COL_DEV = 384
NG = 393216
NG_DEV = 49152


def shared_pairs(key):
    blocks_all = KPOOLS * (NG // NG_DEV)
    keys_all = jax.random.split(key, blocks_all)
    orders = jax.vmap(lambda single: jax.random.permutation(single, NG_DEV))(keys_all)
    return orders.reshape(KPOOLS, NG).astype(jnp.int32)


def draw_miller_third(key, part):
    orders = shared_pairs(key)
    return (orders % ZW - ZW // 2).astype(jnp.int32)


def draw_column_slot(key, part):
    orders = shared_pairs(key)
    return (orders // ZW).astype(jnp.int32)


def draw_column_map(key, part):
    key = jax.random.fold_in(key, 11)
    first_key, second_key = jax.random.split(key)
    cells = jnp.arange(NX * NY, dtype=jnp.int32)
    freq_x = cells // NY
    freq_y = cells % NY
    freq_x = jnp.where(freq_x >= NX // 2, freq_x - NX, freq_x)
    freq_y = jnp.where(freq_y >= NY // 2, freq_y - NY, freq_y)
    radius = freq_x * freq_x * (NY * NY) + freq_y * freq_y * (NX * NX)
    shuffle = jax.random.permutation(first_key, NX * NY).astype(jnp.int32)
    order_rank = jnp.argsort(radius[shuffle], stable=True)
    chosen = shuffle[order_rank][:NCOL]
    dealt = jax.random.permutation(second_key, NCOL)
    return chosen[dealt].astype(jnp.int32)


def with_ends(array, key, least, largest):
    shape = array.shape
    place = [jax.random.randint(jax.random.fold_in(key, axis), (), 0, shape[axis]) for axis in range(len(shape))]
    array = array.at[tuple(place)].set(least)
    longest = shape.index(max(shape))
    place[longest] = (place[longest] + 1) % shape[longest]
    return array.at[tuple(place)].set(largest)


def shard_levels(rng, dims, shards, low, top_value):
    def one(position, shards_of):
        heights = jax.random.uniform(jax.random.fold_in(jax.random.fold_in(rng, 6), position), (shards_of,), jnp.float32, low / len(shards), top_value / len(shards))
        return jnp.repeat(jnp.exp(heights), dims[position] // shards_of).reshape((-1,) + (1,) * (len(dims) - position - 1))

    gain = one(*shards[0])
    for cut in shards[1:]:
        gain = gain * one(*cut)
    return gain


def gaussian(stream_key, shape, deviation, limit, cuts=(), kind=jnp.bfloat16):
    values = jax.random.normal(stream_key, shape, jnp.float32) * deviation
    if len(cuts) > 0:
        values = shard_levels(stream_key, shape, cuts, -0.22, 0.18) * values
    return jnp.clip(values, min=-limit, max=limit).astype(kind)


def setup_inputs(seed: int = 0) -> dict:
    streams_of = jax.random.split(jax.random.key(seed), 6)
    band_coeffs = gaussian(streams_of[0], (KPOOLS, NB, 2, NG), 1.0, 6.0, ((0, 4), (3, 8)), jnp.float32)
    miller_third = draw_miller_third(jax.random.fold_in(streams_of[5], 71), 0)
    column_slot = draw_column_slot(jax.random.fold_in(streams_of[5], 71), 0)
    column_map = draw_column_map(jax.random.fold_in(streams_of[5], 71), 0)
    kpoint_counts = with_ends(jax.random.randint(streams_of[4], (KPOOLS,), 1, 13), jax.random.fold_in(streams_of[4], 1), 1, 12).astype(jnp.int32)
    return dict(band_coeffs=band_coeffs, miller_third=miller_third, column_slot=column_slot, column_map=column_map, kpoint_counts=kpoint_counts)


SPACING = 0.25


def signed_index(length):
    steps = jnp.arange(length, dtype=jnp.int32)
    return jnp.where(steps >= length // 2, steps - length, steps)


def coulomb(freq_z, freq_x, freq_y):
    wave_z = freq_z.astype(jnp.float32) / (NZ * SPACING)
    wave_x = freq_x.astype(jnp.float32) / (NX * SPACING)
    wave_y = freq_y.astype(jnp.float32) / (NY * SPACING)
    squared = (2.0 * math.pi) ** 2 * (wave_z * wave_z + wave_x * wave_x + wave_y * wave_y)
    anchor = (freq_z == 0) & (freq_x == 0) & (freq_y == 0)
    return jnp.where(anchor, 0.0, 4.0 * math.pi / jnp.where(anchor, 1.0, squared))


def reference(band_coeffs, miller_third, column_slot, column_map, kpoint_counts):
    weights = kpoint_counts.astype(jnp.float32) / jnp.sum(kpoint_counts).astype(jnp.float32)
    owner_device = jnp.arange(NG, dtype=jnp.int32) // NG_DEV

    def add_pool(running, inputs):
        coeff_pool, miller_pool, slot_pool, weight = inputs
        column = column_map[owner_device * COL_DEV + slot_pool]
        row_x = column // NY
        row_y = column % NY
        plane_z = miller_pool % NZ
        values = coeff_pool[:, 0] + 1j * coeff_pool[:, 1]
        spectrum_grid = jnp.zeros((NB, NZ, NX, NY), values.dtype).at[:, plane_z, row_x, row_y].set(values)
        wavefunc = jnp.fft.ifftn(spectrum_grid, axes=(1, 2, 3)) * (NX * NY * NZ)
        summed = jnp.sum(jnp.real(wavefunc) ** 2 + jnp.imag(wavefunc) ** 2, axis=0)
        return running + weight * summed, None

    initial = jnp.zeros((NZ, NX, NY), jnp.float32)
    summed_all, unused = lax.scan(add_pool, initial, (band_coeffs, miller_third, column_slot, weights))
    density = (2.0 / NG) * summed_all
    kernel = coulomb(signed_index(NZ)[:, None, None], signed_index(NX)[None, :, None], signed_index(NY)[None, None, :])
    hartree = jnp.real(jnp.fft.ifftn(jnp.fft.fftn(density) * kernel))
    return density, hartree
```

```python
import functools
import math

import jax
import jax.numpy as jnp
import numpy as np
from jax import lax
from jax.experimental import pallas as pl
from jax.experimental.pallas import tpu as pltpu
from jax.sharding import PartitionSpec as P

NX = 128
NY = 128
NZ = 256


SPACING = 0.25


def contract(pattern, former, latter):
    return jnp.einsum(
        pattern, former, latter, precision=lax.Precision.HIGHEST, preferred_element_type=jnp.float32
    )


def phase_tables(first_index, second_index, length):
    product = first_index[:, None] * second_index[None, :] % length
    angle = product.astype(jnp.float32) * (2.0 * math.pi / length)
    return (jnp.cos(angle), jnp.sin(angle))


def signed_freq(values, length):
    return jnp.where(values >= length // 2, values - length, values)


def coulomb(freq_z, freq_x, freq_y):
    wave_z = freq_z.astype(jnp.float32) / (NZ * SPACING)
    wave_x = freq_x.astype(jnp.float32) / (NX * SPACING)
    wave_y = freq_y.astype(jnp.float32) / (NY * SPACING)
    squared = (2.0 * math.pi) ** 2 * (wave_z * wave_z + wave_x * wave_x + wave_y * wave_y)
    anchor = (freq_z == 0) & (freq_x == 0) & (freq_y == 0)
    return jnp.where(anchor, 0.0, 4.0 * math.pi / jnp.where(anchor, 1.0, squared))


def poisson_columns(real_part, imag_part, freq_x, freq_y):
    length = real_part.shape[0]
    steps_z = jnp.arange(length, dtype=jnp.int32)
    cos_z, sin_z = phase_tables(steps_z, steps_z, length)
    spec_real = contract("zk,km->zm", cos_z, real_part) + contract("zk,km->zm", sin_z, imag_part)
    spec_imag = contract("zk,km->zm", cos_z, imag_part) - contract("zk,km->zm", sin_z, real_part)
    kernel = coulomb(signed_freq(steps_z, length)[:, None], freq_x[None, :], freq_y[None, :]) / (
        NX * NY * NZ
    )
    spec_real = spec_real * kernel
    spec_imag = spec_imag * kernel
    back_real = contract("zk,km->zm", cos_z, spec_real) - contract("zk,km->zm", sin_z, spec_imag)
    back_imag = contract("zk,km->zm", sin_z, spec_real) + contract("zk,km->zm", cos_z, spec_imag)
    return (back_real, back_imag)


def forward_planes(field):
    steps_x = jnp.arange(NX, dtype=jnp.int32)
    steps_y = jnp.arange(NY, dtype=jnp.int32)
    cos_y, sin_y = phase_tables(steps_y, steps_y, NY)
    cos_x, sin_x = phase_tables(steps_x, steps_x, NX)
    half_real = contract("pxy,ky->pxk", field, cos_y)
    half_imag = -contract("pxy,ky->pxk", field, sin_y)
    spec_real = contract("kx,pxy->pky", cos_x, half_real) + contract(
        "kx,pxy->pky", sin_x, half_imag
    )
    spec_imag = contract("kx,pxy->pky", cos_x, half_imag) - contract(
        "kx,pxy->pky", sin_x, half_real
    )
    return (spec_real, spec_imag)


def local_general(band_coeffs, miller_third, column_slot, column_map, kpoint_counts):
    pw_count = lax.axis_size("pw")
    kpt_count = lax.axis_size("kpt")
    pw_index = lax.axis_index("pw")
    kpt_index = lax.axis_index("kpt")
    col_dev = column_map.shape[0]
    ng_dev = column_slot.shape[1]
    band_count = band_coeffs.shape[1]
    z_width = ng_dev // col_dev
    planes = NZ // pw_count
    x_block = NX // kpt_count
    col_total = pw_count * col_dev
    steps_y = jnp.arange(NY, dtype=jnp.int32)
    steps_x = jnp.arange(NX, dtype=jnp.int32)
    cos_y, sin_y = phase_tables(steps_y, steps_y, NY)
    cos_x, sin_x = phase_tables(steps_x, steps_x, NX)
    all_columns = lax.all_gather(column_map, "pw", axis=0, tiled=True)
    position = (miller_third[0] + z_width // 2) * col_dev + column_slot[0]
    source_of = (
        jnp.zeros((ng_dev,), jnp.int32).at[position].set(jnp.arange(ng_dev, dtype=jnp.int32))
    )
    coeff_rows = band_coeffs[0].reshape(band_count * 2, ng_dev).T
    packed = jnp.take(coeff_rows, source_of, axis=0)
    packed = (
        packed.reshape(z_width, col_dev, band_count, 2)
        .transpose(0, 2, 3, 1)
        .reshape(z_width, band_count * 2 * col_dev)
    )
    cos_z, sin_z = phase_tables(
        jnp.arange(NZ, dtype=jnp.int32), jnp.arange(z_width, dtype=jnp.int32) - z_width // 2, NZ
    )
    by_cos = contract("zj,jc->zc", cos_z, packed).reshape(NZ, band_count, 2, col_dev)
    by_sin = contract("zj,jc->zc", sin_z, packed).reshape(NZ, band_count, 2, col_dev)
    pencil = jnp.stack(
        (by_cos[:, :, 0] - by_sin[:, :, 1], by_sin[:, :, 0] + by_cos[:, :, 1]), axis=2
    )
    pencil = pencil.reshape(NZ, band_count * 2 * col_dev)
    arrived = lax.all_to_all(pencil, "pw", split_axis=0, concat_axis=1, tiled=True)
    arrived = arrived.reshape(planes, pw_count, band_count, 2, col_dev).transpose(2, 1, 4, 3, 0)
    arrived = arrived.reshape(band_count, col_total, 2 * planes)
    arrived = jnp.concatenate(
        (arrived, jnp.zeros((band_count, 1, 2 * planes), jnp.float32)), axis=1
    )
    cell_source = (
        jnp.full((NX * NY,), col_total, jnp.int32)
        .at[all_columns]
        .set(jnp.arange(col_total, dtype=jnp.int32))
    )

    def add_band(band, running):
        one_band = lax.dynamic_index_in_dim(arrived, band, 0, keepdims=False)
        placed = jnp.take(one_band, cell_source, axis=0)
        placed = placed.reshape(NX, NY, 2, planes).transpose(2, 3, 0, 1)
        grid_real = placed[0]
        grid_imag = placed[1]
        mixed_real = contract("pxm,ym->pxy", grid_real, cos_y) - contract(
            "pxm,ym->pxy", grid_imag, sin_y
        )
        mixed_imag = contract("pxm,ym->pxy", grid_real, sin_y) + contract(
            "pxm,ym->pxy", grid_imag, cos_y
        )
        wave_real = contract("xm,pmy->pxy", cos_x, mixed_real) - contract(
            "xm,pmy->pxy", sin_x, mixed_imag
        )
        wave_imag = contract("xm,pmy->pxy", sin_x, mixed_real) + contract(
            "xm,pmy->pxy", cos_x, mixed_imag
        )
        return running + wave_real * wave_real + wave_imag * wave_imag

    squares_sum = lax.fori_loop(0, band_count, add_band, jnp.zeros((planes, NX, NY), jnp.float32))
    weight = (
        2.0
        * kpoint_counts[kpt_index].astype(jnp.float32)
        / jnp.sum(kpoint_counts).astype(jnp.float32)
    )
    weight = weight / (ng_dev * pw_count)
    partial_value = weight * squares_sum
    total_density = lax.psum(partial_value, "kpt")
    density = lax.dynamic_slice_in_dim(total_density, kpt_index * x_block, x_block, 1)
    spec_real, spec_imag = forward_planes(total_density)
    rows_pw = NX // pw_count
    pencil_real, pencil_imag = (
        lax.all_to_all(spec_real, "pw", split_axis=1, concat_axis=0, tiled=True),
        lax.all_to_all(spec_imag, "pw", split_axis=1, concat_axis=0, tiled=True),
    )
    local_x = pw_index * rows_pw + jnp.arange(rows_pw, dtype=jnp.int32)
    freq_x = jnp.repeat(signed_freq(local_x, NX), NY)
    freq_y = jnp.tile(signed_freq(steps_y, NY), rows_pw)
    back_real, back_imag = poisson_columns(
        pencil_real.reshape(NZ, rows_pw * NY), pencil_imag.reshape(NZ, rows_pw * NY), freq_x, freq_y
    )
    plane_real, plane_imag = (
        lax.all_to_all(
            back_real.reshape(NZ, rows_pw, NY), "pw", split_axis=0, concat_axis=1, tiled=True
        ),
        lax.all_to_all(
            back_imag.reshape(NZ, rows_pw, NY), "pw", split_axis=0, concat_axis=1, tiled=True
        ),
    )
    own_rows = kpt_index * x_block + jnp.arange(x_block, dtype=jnp.int32)
    cos_rows, sin_rows = phase_tables(own_rows, steps_x, NX)
    rows_real = contract("xk,pky->pxy", cos_rows, plane_real) - contract(
        "xk,pky->pxy", sin_rows, plane_imag
    )
    rows_imag = contract("xk,pky->pxy", sin_rows, plane_real) + contract(
        "xk,pky->pxy", cos_rows, plane_imag
    )
    hartree = contract("pxk,yk->pxy", rows_real, cos_y) - contract("pxk,yk->pxy", rows_imag, sin_y)
    return (density, hartree)


LANES = 128
HALF = 64
VMEM_LIMIT = 56 * 1024 * 1024
NN = (((1,), (0,)), ((), ()))
NT = (((1,), (1,)), ((), ()))
TN = (((0,), (0,)), ((), ()))


def pieces(value):
    high = value.astype(jnp.bfloat16)
    low = (value - high.astype(jnp.float32)).astype(jnp.bfloat16)
    return high, low


def mul(former, latter, dims):
    return lax.dot_general(former, latter, dims, preferred_element_type=jnp.float32)


def mul3(former, latter, dims):
    return (
        mul(former[0], latter[0], dims)
        + mul(former[0], latter[1], dims)
        + mul(former[1], latter[0], dims)
    )


def table(values):
    high = values.astype(np.float32).astype(jnp.bfloat16)
    low = (values - high.astype(np.float64)).astype(np.float32).astype(jnp.bfloat16)
    return jnp.asarray(np.stack((high, low)))


def angles(former, latter, length):
    return np.outer(former, latter) % length * (2.0 * np.pi / length)


def tables(kpts, pws, planes):
    count = kpts * pws
    low_freq = np.arange(HALF) - HALF // 2
    grid_x, grid_y, grid_z = np.arange(NX), np.arange(NY), np.arange(NZ)
    own_y = np.arange(HALF)

    device = np.arange(count)
    plane_of = (
        (device % pws)[:, None] * (NZ // pws)
        + (device // pws)[:, None] * planes
        + np.arange(planes)[None, :]
    )
    return_table = {}

    def pencil(z_width):
        angle = angles(plane_of.ravel(), np.arange(z_width) - z_width // 2, NZ)
        cos, sin = (
            part.reshape(count, 1, planes, z_width) for part in (np.cos(angle), np.sin(angle))
        )
        real = np.concatenate((cos, -sin), axis=3)
        imag = np.concatenate((sin, cos), axis=3)
        return np.concatenate((real, imag), axis=1).reshape(-1, 2 * z_width)

    return_table["pencil"] = pencil

    angle = angles(low_freq, grid_y, NY)
    cos, sin = np.cos(angle), np.sin(angle)
    return_table["wave_y"] = np.block([[cos, sin], [-sin, cos]])

    angle = angles(grid_x, low_freq, NX)
    cos, sin = np.cos(angle), np.sin(angle)
    return_table["wave_x"] = np.block([[cos, -sin], [sin, cos]])

    angle = angles(own_y, grid_y, NY)
    cos, sin = np.cos(angle), np.sin(angle)
    return_table["forth_y"] = np.stack((cos, -sin), axis=1).reshape(2 * HALF, NY)
    twice = np.where(own_y == 0, 1.0, 2.0)[:, None]
    return_table["back_y"] = np.stack((twice * cos, -twice * sin), axis=1).reshape(2 * HALF, NY)

    angle = angles(grid_z, plane_of.ravel(), NZ)
    return_table["forth_z"] = np.concatenate((np.cos(angle), np.sin(angle)), axis=0)
    own = NZ // pws
    merged = own // 8
    order = (
        np.arange(pws)[None, :, None] * own
        + np.arange(8)[None, None, :] * merged
        + np.arange(merged)[:, None, None]
    )
    angle = angles(order.ravel(), grid_z, NZ)
    return_table["back_z"] = np.concatenate((np.cos(angle), np.sin(angle)), axis=0)

    angle = angles(grid_x, grid_x, NX)
    return_table["both_x"] = np.concatenate((np.cos(angle), np.sin(angle)), axis=1)
    return return_table


def pack_kernel(step_width, coeff_ref, miller_ref, slot_ref, pencil_ref, out_ref, total):
    step = pl.program_id(0)
    slots = out_ref.shape[1]
    width = pencil_ref.shape[2] // 2
    chunk = coeff_ref.shape[3]

    @pl.when(step == 0)
    def _():
        total[...] = jnp.zeros_like(total)

    one = jnp.ones((LANES, step_width), jnp.bfloat16)
    zero = jnp.zeros((LANES, step_width), jnp.bfloat16)
    steps = lax.broadcasted_iota(jnp.int32, (LANES, step_width), 0)
    steps = steps.astype(jnp.float32).astype(jnp.bfloat16)
    for start in range(0, chunk, step_width):
        part = pl.ds(start, step_width)
        slot = slot_ref[:, part].astype(jnp.float32)
        depth = (miller_ref[:, part] + width // 2).astype(jnp.float32).astype(jnp.bfloat16)
        chosen = jnp.concatenate(
            [
                jnp.where((slot - first).astype(jnp.bfloat16) == steps, one, zero)
                for first in range(0, slots, LANES)
            ],
            axis=0,
        )
        here = depth == steps
        high, low = pieces(coeff_ref[0, 0, :, part])
        spread = jnp.concatenate(
            [jnp.where(here, piece[c : c + 1], zero) for piece in (high, low) for c in range(2)],
            axis=0,
        )
        total[...] += mul(chosen, spread, NT)

    @pl.when(step == pl.num_programs(0) - 1)
    def _():
        both = (
            total[:, : 2 * width].astype(jnp.bfloat16),
            total[:, 2 * width :].astype(jnp.bfloat16),
        )
        out_ref[...] = mul3((pencil_ref[0], pencil_ref[1]), both, NT)


def pack_band(band, coeffs, miller, slot, pencil, slots):
    total = miller.shape[1]
    width = pencil.shape[2] // 2
    chunk = 4096 if total % 4096 == 0 else total
    return pl.pallas_call(
        functools.partial(pack_kernel, 1024 if chunk % 1024 == 0 else chunk),
        grid=(total // chunk,),
        in_specs=[
            pl.BlockSpec((1, 1, 2, chunk), lambda i: (0, band, 0, i)),
            pl.BlockSpec((1, chunk), lambda i: (0, i)),
            pl.BlockSpec((1, chunk), lambda i: (0, i)),
            pl.BlockSpec(pencil.shape, lambda i: (0, 0, 0)),
        ],
        out_specs=pl.BlockSpec((pencil.shape[1], slots), lambda i: (0, 0)),
        out_shape=jax.ShapeDtypeStruct((pencil.shape[1], slots), jnp.float32),
        scratch_shapes=[pltpu.VMEM((slots, 4 * width), jnp.float32)],
        compiler_params=pltpu.CompilerParams(vmem_limit_bytes=VMEM_LIMIT),
        cost_estimate=pl.CostEstimate(
            flops=2 * total * slots * 4 * width, bytes_accessed=16 * total, transcendentals=0
        ),
        name="pack_band",
    )(coeffs, miller, slot, pencil)


def wave_kernel(kpts, has_former, is_last, *refs):
    weight_ref, came_ref, column_ref, wave_y_ref, wave_x_ref, forth_ref = refs[:6]
    rest = list(refs[6:])
    former_ref = rest.pop(0) if has_former else None
    density_ref = rest.pop(0)
    send_ref = rest.pop(0) if is_last else None
    values, grid = rest
    planes = density_ref.shape[1]
    slots = came_ref.shape[2]
    pws = came_ref.shape[0] // kpts
    rows = kpts * 2 * planes

    for j in range(pws):
        block = jnp.concatenate([came_ref[k * pws + j] for k in range(kpts)], axis=0)
        high, low = pieces(block)
        values[0:rows, pl.ds(j * slots, slots)] = high
        values[rows : 2 * rows, pl.ds(j * slots, slots)] = low

    column = column_ref[...]
    cell = ((column // NY + NX // 2) % NX - HALF // 2) * HALF
    cell = cell + (column % NY + NY // 2) % NY - HALF // 2
    cell = cell.astype(jnp.float32)
    total = cell.shape[1]
    tile = 4 * HALF
    steps = lax.broadcasted_iota(jnp.int32, (tile, total), 0).astype(jnp.float32)
    steps = steps.astype(jnp.bfloat16)
    one = jnp.ones((tile, total), jnp.bfloat16)
    zero = jnp.zeros((tile, total), jnp.bfloat16)
    left = lax.broadcasted_iota(jnp.int32, (kpts * planes, LANES), 1) < HALF

    def place(t, unused):
        near = (cell - (t * tile).astype(jnp.float32)).astype(jnp.bfloat16)
        chosen = jnp.where(near == steps, one, zero)
        found = mul(values[...], chosen, NT)
        found = found[:rows] + found[rows:]
        for h in range(2):
            real, imag = (
                jnp.concatenate(
                    [
                        found[(2 * k + c) * planes : (2 * k + c + 1) * planes, h * LANES : (h + 1) * LANES]
                        for k in range(kpts)
                    ],
                    axis=0,
                )
                for c in range(2)
            )
            even = jnp.where(left, real, pltpu.roll(imag, HALF, 1))
            odd = jnp.where(left, pltpu.roll(real, HALF, 1), imag)
            grid[pl.ds(t * 4 + 2 * h, kpts * planes, stride=HALF), :] = even
            grid[pl.ds(t * 4 + 2 * h + 1, kpts * planes, stride=HALF), :] = odd
        return unused

    lax.fori_loop(0, HALF // 4, place, 0)

    first_row = lax.broadcasted_iota(jnp.int32, (2 * HALF, NX), 0) == 0

    def transform(p, unused):
        lines = jnp.concatenate(
            [
                grid[pl.ds(pl.multiple_of((k * planes + p) * HALF, HALF), HALF), :]
                for k in range(kpts)
            ],
            axis=0,
        )
        mixed = mul3(pieces(lines), (wave_y_ref[0], wave_y_ref[1]), NN)
        mixed = jnp.concatenate(
            [
                jnp.concatenate(
                    [mixed[k * HALF : (k + 1) * HALF, c * NY : (c + 1) * NY] for k in range(kpts)],
                    axis=1,
                )
                for c in range(2)
            ],
            axis=0,
        )
        wave = mul3((wave_x_ref[0], wave_x_ref[1]), pieces(mixed), NN)
        square = wave[:NX] * wave[:NX] + wave[NX:] * wave[NX:]
        density = weight_ref[0] * square[:, :NY]
        for k in range(1, kpts):
            density = density + weight_ref[k] * square[:, k * NY : (k + 1) * NY]
        blocks = density_ref.shape[0]
        block = NX // blocks
        if has_former:
            density = density + jnp.concatenate([former_ref[a, p] for a in range(blocks)], axis=0)
        for a in range(blocks):
            density_ref[a, p] = density[a * block : (a + 1) * block]
        if is_last:
            level = jnp.mean(density[:8], axis=(0, 1), keepdims=True)
            half = mul3((forth_ref[0], forth_ref[1]), pieces(density - level), NT)
            half = half + jnp.where(first_row, level * NY, 0.0)
            send_ref[pl.ds(p, 2 * HALF, stride=planes), :] = half
        return unused

    lax.fori_loop(0, planes, transform, 0)


def wave_band(kpts, weight, came, column, wave_y, wave_x, forth, former, is_last):
    planes = came.shape[1] // 2
    block = NX // kpts
    vmem = pl.BlockSpec(memory_space=pltpu.VMEM)
    operands = [weight, came, column, wave_y, wave_x, forth]
    if former is not None:
        operands.append(former)
    out_shape = [jax.ShapeDtypeStruct((kpts, planes, block, NY), jnp.float32)]
    if is_last:
        out_shape.append(jax.ShapeDtypeStruct((2 * HALF * planes, NX), jnp.float32))
    total = column.shape[1]
    rows = kpts * 2 * planes
    return pl.pallas_call(
        functools.partial(wave_kernel, kpts, former is not None, is_last),
        in_specs=[pl.BlockSpec(memory_space=pltpu.SMEM)] + [vmem] * (len(operands) - 1),
        out_specs=[vmem] * len(out_shape),
        out_shape=out_shape,
        scratch_shapes=[
            pltpu.VMEM((2 * rows, total), jnp.bfloat16),
            pltpu.VMEM((kpts * planes * HALF, LANES), jnp.float32),
        ],
        compiler_params=pltpu.CompilerParams(vmem_limit_bytes=VMEM_LIMIT),
        cost_estimate=pl.CostEstimate(
            flops=4 * rows * total * HALF * HALF, bytes_accessed=4 * came.size, transcendentals=0
        ),
        name="wave_band",
    )(*operands)


def poisson_kernel(pws, first_ref, came_ref, forth_ref, back_ref, both_x_ref, send_ref):
    count, parts, planes, unused = came_ref.shape
    pairs = parts // 2
    forth = (forth_ref[0], forth_ref[1])
    back = (back_ref[0], back_ref[1])
    both_x = (both_x_ref[0], both_x_ref[1])

    fields = [came_ref[:, i].reshape(NZ, NX) for i in range(parts)]
    level = jnp.mean(fields[0], axis=(0, 1), keepdims=True)
    fields[0] = fields[0] - jnp.where(first_ref[0] == 0, level, 0.0)
    field = jnp.concatenate(fields, axis=1)
    turned = mul3(forth, pieces(field), NN)

    def part(array, half, i):
        return array[half * NZ : (half + 1) * NZ, i * NX : (i + 1) * NX]

    lines = []
    for q in range(pairs):
        lines.append(part(turned, 0, 2 * q) + part(turned, 1, 2 * q + 1))
        lines.append(part(turned, 0, 2 * q + 1) - part(turned, 1, 2 * q))
    spectrum = mul3(pieces(jnp.concatenate(lines, axis=0)), both_x, NN)

    step_z = lax.broadcasted_iota(jnp.int32, (NZ, NX), 0)
    step_x = lax.broadcasted_iota(jnp.int32, (NZ, NX), 1)
    lines = []
    for q in range(pairs):
        real = spectrum[2 * q * NZ : (2 * q + 1) * NZ]
        imag = spectrum[(2 * q + 1) * NZ : (2 * q + 2) * NZ]
        freq_y = jnp.full((NZ, NX), first_ref[0] + q, jnp.int32)
        kernel = coulomb(signed_freq(step_z, NZ), signed_freq(step_x, NX), freq_y)
        kernel = kernel * (1.0 / (NX * NY * NZ))
        lines.append((real[:, :NX] + imag[:, NX:]) * kernel)
        lines.append((imag[:, :NX] - real[:, NX:]) * kernel)
    turned = mul3(pieces(jnp.concatenate(lines, axis=0)), both_x, NN)
    lines = []
    for q in range(pairs):
        real = turned[2 * q * NZ : (2 * q + 1) * NZ]
        imag = turned[(2 * q + 1) * NZ : (2 * q + 2) * NZ]
        lines.append(real[:, :NX] - imag[:, NX:])
        lines.append(real[:, NX:] + imag[:, :NX])
    turned = mul3(back, pieces(jnp.concatenate(lines, axis=1)), NN)

    kpts = count // pws
    merged = NZ // pws // 8
    block = NX // kpts
    rows = pws * 8
    lane = lax.broadcasted_iota(jnp.int32, (rows, LANES), 1) // block
    for q in range(pairs):
        real = part(turned, 0, 2 * q) - part(turned, 1, 2 * q + 1)
        imag = part(turned, 0, 2 * q + 1) + part(turned, 1, 2 * q)
        for c, value in enumerate((real, imag)):
            for a in range(kpts):
                packed = None
                for m in range(merged):
                    piece = value[m * rows : (m + 1) * rows]
                    shift = (m - a) * block % LANES
                    if shift:
                        piece = pltpu.roll(piece, shift, 1)
                    packed = piece if m == 0 else jnp.where(lane == m, piece, packed)
                send_ref[a * pws : (a + 1) * pws, 2 * q + c] = packed.reshape(pws, 8, LANES)


def poisson(pws, first, came, forth, back, both_x):
    vmem = pl.BlockSpec(memory_space=pltpu.VMEM)
    count, parts, unused, unused = came.shape
    return pl.pallas_call(
        functools.partial(poisson_kernel, pws),
        in_specs=[pl.BlockSpec(memory_space=pltpu.SMEM)] + [vmem] * 4,
        out_specs=vmem,
        out_shape=jax.ShapeDtypeStruct((count, parts, 8, LANES), jnp.float32),
        compiler_params=pltpu.CompilerParams(vmem_limit_bytes=VMEM_LIMIT),
        name="poisson",
    )(first, came, forth, back, both_x)


def finish_kernel(came_ref, back_ref, out_ref):
    back = (back_ref[0], back_ref[1])
    planes, block, unused = out_ref.shape
    merged = planes // 8
    for h in range(8):
        lines = came_ref[pl.ds(h, 2 * HALF, stride=8), :]
        field = mul3(pieces(lines), back, TN)
        out_ref[h * merged : (h + 1) * merged] = field.reshape(merged, block, NY)


def finish(planes, block, came, back_y):
    vmem = pl.BlockSpec(memory_space=pltpu.VMEM)
    return pl.pallas_call(
        finish_kernel,
        in_specs=[vmem] * 2,
        out_specs=vmem,
        out_shape=jax.ShapeDtypeStruct((planes, block, NY), jnp.float32),
        compiler_params=pltpu.CompilerParams(vmem_limit_bytes=VMEM_LIMIT),
        name="finish",
    )(came, back_y)


def local_planes(band_coeffs, miller_third, column_slot, column_map, kpoint_counts):
    pws = lax.axis_size("pw")
    kpts = lax.axis_size("kpt")
    count = pws * kpts
    everyone = ("kpt", "pw")
    slots = column_map.shape[0]
    band_count = band_coeffs.shape[1]
    z_width = column_slot.shape[1] // slots
    planes = NZ // count
    parts = 2 * HALF // count
    made = tables(kpts, pws, planes)
    pencil = table(made["pencil"](z_width))
    wave_y, wave_x, forth_y, back_y, forth_z, back_z, both_x = (
        table(made[name])
        for name in ("wave_y", "wave_x", "forth_y", "back_y", "forth_z", "back_z", "both_x")
    )

    columns = lax.all_to_all(
        jnp.broadcast_to(column_map[None, None, :], (pws, 1, slots)),
        "pw",
        split_axis=0,
        concat_axis=0,
        tiled=True,
    ).reshape(1, pws * slots)
    weight = (
        2.0 * kpoint_counts.astype(jnp.float32) / jnp.sum(kpoint_counts).astype(jnp.float32)
    ) / (column_slot.shape[1] * pws)

    arrived = []
    for band in range(band_count):
        packed = pack_band(band, band_coeffs, miller_third, column_slot, pencil, slots)
        arrived.append(
            lax.all_to_all(
                packed.reshape(count, 2 * planes, slots),
                everyone,
                split_axis=0,
                concat_axis=0,
                tiled=True,
            )
        )
    former = None
    for band in range(band_count):
        is_last = band == band_count - 1
        made_here = wave_band(
            kpts, weight, arrived[band], columns, wave_y, wave_x, forth_y, former, is_last
        )
        former = made_here[0]
    half = made_here[1].reshape(count, parts, planes, NX)
    half = lax.all_to_all(half, everyone, split_axis=0, concat_axis=0, tiled=True)
    density = lax.all_to_all(former, "kpt", split_axis=0, concat_axis=0, tiled=True)
    density = density.reshape(NZ // pws, NX // kpts, NY)
    device = lax.axis_index("kpt") * pws + lax.axis_index("pw")
    first = (device * (parts // 2)).astype(jnp.int32).reshape(1)
    back = poisson(pws, first, half, forth_z, back_z, both_x)
    back = lax.all_to_all(back, everyone, split_axis=0, concat_axis=0, tiled=True)
    back = back.reshape(count * parts * 8, LANES)
    hartree = finish(NZ // pws, NX // kpts, back, back_y)
    return (density, hartree)


def fits_planes(kpts, pws):
    count = kpts * pws
    own = NZ // pws
    return (
        NZ % count == 0
        and NZ // count == 8
        and 2 * HALF % (2 * count) == 0
        and NX % kpts == 0
        and own % 8 == 0
        and own // 8 * (NX // kpts) == LANES
    )


def solution(mesh):
    chosen = local_planes if fits_planes(mesh.shape["kpt"], mesh.shape["pw"]) else local_general
    return jax.shard_map(
        chosen,
        mesh=mesh,
        in_specs=(P("kpt", None, None, "pw"), P("kpt", "pw"), P("kpt", "pw"), P("pw"), P()),
        out_specs=(P("pw", "kpt", None), P("pw", "kpt", None)),
        check_vma=False,
    )
```

```python
import functools
import math

import jax
import jax.numpy as jnp
import numpy as np
from jax import lax
from jax.experimental import pallas as pl
from jax.experimental.pallas import tpu as pltpu
from jax.sharding import PartitionSpec as P

NX = 128
NY = 128
NZ = 256


SPACING = 0.25


def contract(pattern, former, latter):
    return jnp.einsum(
        pattern, former, latter, precision=lax.Precision.HIGHEST, preferred_element_type=jnp.float32
    )


def phase_tables(first_index, second_index, length):
    product = first_index[:, None] * second_index[None, :] % length
    angle = product.astype(jnp.float32) * (2.0 * math.pi / length)
    return (jnp.cos(angle), jnp.sin(angle))


def signed_freq(values, length):
    return jnp.where(values >= length // 2, values - length, values)


def coulomb(freq_z, freq_x, freq_y):
    wave_z = freq_z.astype(jnp.float32) / (NZ * SPACING)
    wave_x = freq_x.astype(jnp.float32) / (NX * SPACING)
    wave_y = freq_y.astype(jnp.float32) / (NY * SPACING)
    squared = (2.0 * math.pi) ** 2 * (wave_z * wave_z + wave_x * wave_x + wave_y * wave_y)
    anchor = (freq_z == 0) & (freq_x == 0) & (freq_y == 0)
    return jnp.where(anchor, 0.0, 4.0 * math.pi / jnp.where(anchor, 1.0, squared))


def poisson_columns(real_part, imag_part, freq_x, freq_y):
    length = real_part.shape[0]
    steps_z = jnp.arange(length, dtype=jnp.int32)
    cos_z, sin_z = phase_tables(steps_z, steps_z, length)
    spec_real = contract("zk,km->zm", cos_z, real_part) + contract("zk,km->zm", sin_z, imag_part)
    spec_imag = contract("zk,km->zm", cos_z, imag_part) - contract("zk,km->zm", sin_z, real_part)
    kernel = coulomb(signed_freq(steps_z, length)[:, None], freq_x[None, :], freq_y[None, :]) / (
        NX * NY * NZ
    )
    spec_real = spec_real * kernel
    spec_imag = spec_imag * kernel
    back_real = contract("zk,km->zm", cos_z, spec_real) - contract("zk,km->zm", sin_z, spec_imag)
    back_imag = contract("zk,km->zm", sin_z, spec_real) + contract("zk,km->zm", cos_z, spec_imag)
    return (back_real, back_imag)


def forward_planes(field):
    steps_x = jnp.arange(NX, dtype=jnp.int32)
    steps_y = jnp.arange(NY, dtype=jnp.int32)
    cos_y, sin_y = phase_tables(steps_y, steps_y, NY)
    cos_x, sin_x = phase_tables(steps_x, steps_x, NX)
    half_real = contract("pxy,ky->pxk", field, cos_y)
    half_imag = -contract("pxy,ky->pxk", field, sin_y)
    spec_real = contract("kx,pxy->pky", cos_x, half_real) + contract(
        "kx,pxy->pky", sin_x, half_imag
    )
    spec_imag = contract("kx,pxy->pky", cos_x, half_imag) - contract(
        "kx,pxy->pky", sin_x, half_real
    )
    return (spec_real, spec_imag)


def local_general(band_coeffs, miller_third, column_slot, column_map, kpoint_counts):
    pw_count = lax.axis_size("pw")
    kpt_count = lax.axis_size("kpt")
    pw_index = lax.axis_index("pw")
    kpt_index = lax.axis_index("kpt")
    col_dev = column_map.shape[0]
    ng_dev = column_slot.shape[1]
    band_count = band_coeffs.shape[1]
    z_width = ng_dev // col_dev
    planes = NZ // pw_count
    x_block = NX // kpt_count
    col_total = pw_count * col_dev
    steps_y = jnp.arange(NY, dtype=jnp.int32)
    steps_x = jnp.arange(NX, dtype=jnp.int32)
    cos_y, sin_y = phase_tables(steps_y, steps_y, NY)
    cos_x, sin_x = phase_tables(steps_x, steps_x, NX)
    all_columns = lax.all_gather(column_map, "pw", axis=0, tiled=True)
    position = (miller_third[0] + z_width // 2) * col_dev + column_slot[0]
    source_of = (
        jnp.zeros((ng_dev,), jnp.int32).at[position].set(jnp.arange(ng_dev, dtype=jnp.int32))
    )
    coeff_rows = band_coeffs[0].reshape(band_count * 2, ng_dev).T
    packed = jnp.take(coeff_rows, source_of, axis=0)
    packed = (
        packed.reshape(z_width, col_dev, band_count, 2)
        .transpose(0, 2, 3, 1)
        .reshape(z_width, band_count * 2 * col_dev)
    )
    cos_z, sin_z = phase_tables(
        jnp.arange(NZ, dtype=jnp.int32), jnp.arange(z_width, dtype=jnp.int32) - z_width // 2, NZ
    )
    by_cos = contract("zj,jc->zc", cos_z, packed).reshape(NZ, band_count, 2, col_dev)
    by_sin = contract("zj,jc->zc", sin_z, packed).reshape(NZ, band_count, 2, col_dev)
    pencil = jnp.stack(
        (by_cos[:, :, 0] - by_sin[:, :, 1], by_sin[:, :, 0] + by_cos[:, :, 1]), axis=2
    )
    pencil = pencil.reshape(NZ, band_count * 2 * col_dev)
    arrived = lax.all_to_all(pencil, "pw", split_axis=0, concat_axis=1, tiled=True)
    arrived = arrived.reshape(planes, pw_count, band_count, 2, col_dev).transpose(2, 1, 4, 3, 0)
    arrived = arrived.reshape(band_count, col_total, 2 * planes)
    arrived = jnp.concatenate(
        (arrived, jnp.zeros((band_count, 1, 2 * planes), jnp.float32)), axis=1
    )
    cell_source = (
        jnp.full((NX * NY,), col_total, jnp.int32)
        .at[all_columns]
        .set(jnp.arange(col_total, dtype=jnp.int32))
    )

    def add_band(band, running):
        one_band = lax.dynamic_index_in_dim(arrived, band, 0, keepdims=False)
        placed = jnp.take(one_band, cell_source, axis=0)
        placed = placed.reshape(NX, NY, 2, planes).transpose(2, 3, 0, 1)
        grid_real = placed[0]
        grid_imag = placed[1]
        mixed_real = contract("pxm,ym->pxy", grid_real, cos_y) - contract(
            "pxm,ym->pxy", grid_imag, sin_y
        )
        mixed_imag = contract("pxm,ym->pxy", grid_real, sin_y) + contract(
            "pxm,ym->pxy", grid_imag, cos_y
        )
        wave_real = contract("xm,pmy->pxy", cos_x, mixed_real) - contract(
            "xm,pmy->pxy", sin_x, mixed_imag
        )
        wave_imag = contract("xm,pmy->pxy", sin_x, mixed_real) + contract(
            "xm,pmy->pxy", cos_x, mixed_imag
        )
        return running + wave_real * wave_real + wave_imag * wave_imag

    squares_sum = lax.fori_loop(0, band_count, add_band, jnp.zeros((planes, NX, NY), jnp.float32))
    weight = (
        2.0
        * kpoint_counts[kpt_index].astype(jnp.float32)
        / jnp.sum(kpoint_counts).astype(jnp.float32)
    )
    weight = weight / (ng_dev * pw_count)
    partial_value = weight * squares_sum
    total_density = lax.psum(partial_value, "kpt")
    density = lax.dynamic_slice_in_dim(total_density, kpt_index * x_block, x_block, 1)
    spec_real, spec_imag = forward_planes(total_density)
    rows_pw = NX // pw_count
    pencil_real, pencil_imag = (
        lax.all_to_all(spec_real, "pw", split_axis=1, concat_axis=0, tiled=True),
        lax.all_to_all(spec_imag, "pw", split_axis=1, concat_axis=0, tiled=True),
    )
    local_x = pw_index * rows_pw + jnp.arange(rows_pw, dtype=jnp.int32)
    freq_x = jnp.repeat(signed_freq(local_x, NX), NY)
    freq_y = jnp.tile(signed_freq(steps_y, NY), rows_pw)
    back_real, back_imag = poisson_columns(
        pencil_real.reshape(NZ, rows_pw * NY), pencil_imag.reshape(NZ, rows_pw * NY), freq_x, freq_y
    )
    plane_real, plane_imag = (
        lax.all_to_all(
            back_real.reshape(NZ, rows_pw, NY), "pw", split_axis=0, concat_axis=1, tiled=True
        ),
        lax.all_to_all(
            back_imag.reshape(NZ, rows_pw, NY), "pw", split_axis=0, concat_axis=1, tiled=True
        ),
    )
    own_rows = kpt_index * x_block + jnp.arange(x_block, dtype=jnp.int32)
    cos_rows, sin_rows = phase_tables(own_rows, steps_x, NX)
    rows_real = contract("xk,pky->pxy", cos_rows, plane_real) - contract(
        "xk,pky->pxy", sin_rows, plane_imag
    )
    rows_imag = contract("xk,pky->pxy", sin_rows, plane_real) + contract(
        "xk,pky->pxy", cos_rows, plane_imag
    )
    hartree = contract("pxk,yk->pxy", rows_real, cos_y) - contract("pxk,yk->pxy", rows_imag, sin_y)
    return (density, hartree)


LANES = 128
HALF = 64
VMEM_LIMIT = 56 * 1024 * 1024
NN = (((1,), (0,)), ((), ()))
NT = (((1,), (1,)), ((), ()))
TN = (((0,), (0,)), ((), ()))


def pieces(value):
    high = value.astype(jnp.bfloat16)
    low = (value - high.astype(jnp.float32)).astype(jnp.bfloat16)
    return high, low


def mul(former, latter, dims):
    return lax.dot_general(former, latter, dims, preferred_element_type=jnp.float32)


def mul3(former, latter, dims):
    (of_former,), (of_latter,) = dims[0]
    return mul(
        jnp.concatenate((former[0], former[0], former[1]), axis=of_former),
        jnp.concatenate((latter[0], latter[1], latter[0]), axis=of_latter),
        dims,
    )


def table(values):
    high = values.astype(np.float32).astype(jnp.bfloat16)
    low = (values - high.astype(np.float64)).astype(np.float32).astype(jnp.bfloat16)
    return jnp.asarray(np.stack((high, low)))


def angles(former, latter, length):
    return np.outer(former, latter) % length * (2.0 * np.pi / length)


def tables(kpts, pws, planes):
    count = kpts * pws
    low_freq = np.arange(HALF) - HALF // 2
    grid_x, grid_y, grid_z = np.arange(NX), np.arange(NY), np.arange(NZ)
    own_y = np.arange(HALF)

    device = np.arange(count)
    plane_of = (
        (device % pws)[:, None] * (NZ // pws)
        + (device // pws)[:, None] * planes
        + np.arange(planes)[None, :]
    )
    return_table = {}

    def pencil(z_width):
        angle = angles(plane_of.ravel(), np.arange(z_width) - z_width // 2, NZ)
        cos, sin = (
            part.reshape(count, 1, planes, z_width) for part in (np.cos(angle), np.sin(angle))
        )
        real = np.concatenate((cos, -sin), axis=3)
        imag = np.concatenate((sin, cos), axis=3)
        return np.concatenate((real, imag), axis=1).reshape(-1, 2 * z_width)

    return_table["pencil"] = pencil

    angle = angles(low_freq, grid_y, NY)
    cos, sin = np.cos(angle), np.sin(angle)
    return_table["wave_y"] = np.block([[cos, sin], [-sin, cos]])

    angle = angles(grid_x, low_freq, NX)
    cos, sin = np.cos(angle), np.sin(angle)
    return_table["wave_x"] = np.block([[cos, -sin], [sin, cos]])

    angle = angles(own_y, grid_y, NY)
    cos, sin = np.cos(angle), np.sin(angle)
    return_table["forth_y"] = np.stack((cos, -sin), axis=1).reshape(2 * HALF, NY)
    twice = np.where(own_y == 0, 1.0, 2.0)[:, None]
    return_table["back_y"] = np.stack((twice * cos, -twice * sin), axis=1).reshape(2 * HALF, NY)

    angle = angles(grid_z, plane_of.ravel(), NZ)
    return_table["forth_z"] = np.concatenate((np.cos(angle), np.sin(angle)), axis=0)
    own = NZ // pws
    merged = own // 8
    order = (
        np.arange(pws)[None, :, None] * own
        + np.arange(8)[None, None, :] * merged
        + np.arange(merged)[:, None, None]
    )
    angle = angles(order.ravel(), grid_z, NZ)
    return_table["back_z"] = np.concatenate((np.cos(angle), np.sin(angle)), axis=0)

    angle = angles(grid_x, grid_x, NX)
    return_table["both_x"] = np.concatenate((np.cos(angle), np.sin(angle)), axis=1)
    return return_table


def pack_kernel(width, has_column, *refs):
    coeff_ref, miller_ref, slot_ref, pencil_ref = refs[:4]
    rest = list(refs[4:])
    column_ref = rest.pop(0) if has_column else None
    out_ref, total, chosen_a, spread_a, chosen_b, spread_b = rest
    slots, step_width = chosen_a.shape
    count = out_ref.shape[0]
    rows = pencil_ref.shape[1] // count
    step_count = miller_ref.shape[1] // step_width

    one = jnp.ones((LANES, step_width), jnp.bfloat16)
    zero = jnp.zeros((LANES, step_width), jnp.bfloat16)
    steps = lax.broadcasted_iota(jnp.int32, (LANES, step_width), 0)
    steps = steps.astype(jnp.float32).astype(jnp.bfloat16)

    def build(step, chosen_ref, spread_ref):
        part = pl.ds(pl.multiple_of(step * step_width, step_width), step_width)
        slot = slot_ref[:, part].astype(jnp.float32)
        depth = (miller_ref[:, part] + width // 2).astype(jnp.float32).astype(jnp.bfloat16)
        for first in range(0, slots, LANES):
            found = (slot - first).astype(jnp.bfloat16) == steps
            chosen_ref[first : first + LANES] = jnp.where(found, one, zero)
        here = depth == steps
        for at, piece in enumerate(pieces(coeff_ref[0, 0, :, part])):
            for c in range(2):
                first = (2 * at + c) * LANES
                spread_ref[first : first + LANES] = jnp.where(here, piece[c : c + 1], zero)

    def use(chosen_ref, spread_ref):
        total[...] += mul(chosen_ref[...], spread_ref[...], NT)

    total[...] = jnp.zeros_like(total)
    build(0, chosen_a, spread_a)

    def two_steps(i, unused):
        build(2 * i + 1, chosen_b, spread_b)
        use(chosen_a, spread_a)
        build(jnp.minimum(2 * i + 2, step_count - 1), chosen_a, spread_a)
        use(chosen_b, spread_b)
        return unused

    lax.fori_loop(0, step_count // 2, two_steps, 0)
    if step_count % 2:
        use(chosen_a, spread_a)

    both = (
        total[:, : 2 * width].astype(jnp.bfloat16),
        total[:, 2 * width :].astype(jnp.bfloat16),
    )
    pencils = mul3((pencil_ref[0], pencil_ref[1]), both, NT)
    tiles = slots // LANES
    for t in range(tiles):
        tile = pencils[:, t * LANES : (t + 1) * LANES].reshape(count, rows, LANES)
        out_ref[:, t * rows : (t + 1) * rows] = tile
    if has_column:
        column = column_ref[...].astype(jnp.float32)
        column = [column[:, t * LANES : (t + 1) * LANES] for t in range(tiles)]
        blank = [jnp.zeros((8 - tiles, LANES), jnp.float32)]
        column = jnp.concatenate(column + blank, axis=0)
        out_ref[:, tiles * rows :] = jnp.broadcast_to(column[None], (count, 8, LANES))


def pack_band(band, count, coeffs, miller, slot, pencil, slots, column):
    total = miller.shape[1]
    width = pencil.shape[2] // 2
    rows = pencil.shape[1] // count * (slots // LANES)
    step_width = 1024 if total % 1024 == 0 else total
    operands = [coeffs, miller, slot, pencil]
    if column is not None:
        operands.append(column)
        rows += 8
    one_band = pl.BlockSpec((1, 1, 2, total), lambda i: (0, band, 0, 0))
    buffers = [
        pltpu.VMEM((slots, step_width), jnp.bfloat16),
        pltpu.VMEM((4 * width, step_width), jnp.bfloat16),
    ]
    return pl.pallas_call(
        functools.partial(pack_kernel, width, column is not None),
        grid=(1,),
        in_specs=[one_band]
        + [pl.BlockSpec(x.shape, lambda i, n=x.ndim: (0,) * n) for x in operands[1:]],
        out_specs=pl.BlockSpec((count, rows, LANES), lambda i: (0, 0, 0)),
        out_shape=jax.ShapeDtypeStruct((count, rows, LANES), jnp.float32),
        scratch_shapes=[pltpu.VMEM((slots, 4 * width), jnp.float32)] + buffers + buffers,
        compiler_params=pltpu.CompilerParams(vmem_limit_bytes=VMEM_LIMIT),
        cost_estimate=pl.CostEstimate(
            flops=2 * total * slots * 4 * width, bytes_accessed=16 * total, transcendentals=0
        ),
        name="pack_band",
    )(*operands)


def wave_kernel(kpts, tiles, scale, is_first, is_last, *refs):
    count_ref, came_ref, wave_y_ref, wave_x_ref = refs[:4]
    rest = list(refs[4:])
    forth_ref = rest.pop(0) if is_last else None
    former_ref, cell_ref = (None, None) if is_first else (rest.pop(0), rest.pop(0))
    density_ref = rest.pop(0)
    cell_out = rest.pop(0) if is_first and not is_last else None
    send_ref = rest.pop(0) if is_last else None
    values, grid, chosen_a, chosen_b = rest
    blocks, planes, block, unused = density_ref.shape
    part_rows = 2 * planes
    pws = came_ref.shape[0] // kpts
    rows = kpts * part_rows
    total = values.shape[1]

    for j in range(pws):
        for t in range(tiles):
            taken = jnp.concatenate(
                [came_ref[k * pws + j, t * part_rows : (t + 1) * part_rows] for k in range(kpts)],
                axis=0,
            )
            high, low = pieces(taken)
            first = (j * tiles + t) * LANES
            values[0:rows, first : first + LANES] = high
            values[rows : 2 * rows, first : first + LANES] = low

    if is_first:
        column = jnp.concatenate(
            [
                came_ref[j, tiles * part_rows + t : tiles * part_rows + t + 1]
                for j in range(pws)
                for t in range(tiles)
            ],
            axis=1,
        ).astype(jnp.int32)
        cell = ((column // NY + NX // 2) % NX - HALF // 2) * HALF
        cell = cell + (column % NY + NY // 2) % NY - HALF // 2
        cell = cell.astype(jnp.float32)
        if cell_out is not None:
            cell_out[...] = cell
    else:
        cell = cell_ref[...]
    tile = 4 * HALF
    steps = lax.broadcasted_iota(jnp.int32, (tile, total), 0).astype(jnp.float32)
    steps = steps.astype(jnp.bfloat16)
    one = jnp.ones((tile, total), jnp.bfloat16)
    zero = jnp.zeros((tile, total), jnp.bfloat16)
    left = lax.broadcasted_iota(jnp.int32, (kpts * planes, LANES), 1) < HALF

    def build(t, chosen_ref):
        near = (cell - (t * tile).astype(jnp.float32)).astype(jnp.bfloat16)
        chosen_ref[...] = jnp.where(near == steps, one, zero)

    def place(t, chosen_ref):
        found = mul(values[...], chosen_ref[...], NT)
        found = found[:rows] + found[rows:]
        for h in range(2):
            real, imag = (
                jnp.concatenate(
                    [
                        found[(2 * k + c) * planes : (2 * k + c + 1) * planes, h * LANES : (h + 1) * LANES]
                        for k in range(kpts)
                    ],
                    axis=0,
                )
                for c in range(2)
            )
            even = jnp.where(left, real, pltpu.roll(imag, HALF, 1))
            odd = jnp.where(left, pltpu.roll(real, HALF, 1), imag)
            grid[pl.ds(t * 4 + 2 * h, kpts * planes, stride=HALF), :] = even
            grid[pl.ds(t * 4 + 2 * h + 1, kpts * planes, stride=HALF), :] = odd

    build(jnp.int32(0), chosen_a)

    def two_tiles(i, unused):
        build(2 * i + 1, chosen_b)
        place(2 * i, chosen_a)
        build(2 * i + 2, chosen_a)
        place(2 * i + 1, chosen_b)
        return unused

    lax.fori_loop(0, HALF // 8, two_tiles, 0)

    sum_of = count_ref[0]
    for k in range(1, kpts):
        sum_of = sum_of + count_ref[k]

    def spread(number):
        return jnp.full((8, NY), number, jnp.int32).astype(jnp.float32)

    weights = [
        jnp.concatenate([spread(count_ref[k]) / spread(sum_of) * scale] * (NX // 8), axis=0)
        for k in range(kpts)
    ]
    first_row = lax.broadcasted_iota(jnp.int32, (2 * HALF, NX), 0) == 0

    def transform(p):
        lines = jnp.concatenate(
            [
                grid[pl.ds(pl.multiple_of((k * planes + p) * HALF, HALF), HALF), :]
                for k in range(kpts)
            ],
            axis=0,
        )
        mixed = mul3(pieces(lines), (wave_y_ref[0], wave_y_ref[1]), NN)
        mixed = jnp.concatenate(
            [
                jnp.concatenate(
                    [mixed[k * HALF : (k + 1) * HALF, c * NY : (c + 1) * NY] for k in range(kpts)],
                    axis=1,
                )
                for c in range(2)
            ],
            axis=0,
        )
        wave = mul3((wave_x_ref[0], wave_x_ref[1]), pieces(mixed), NN)
        square = wave[:NX] * wave[:NX] + wave[NX:] * wave[NX:]
        density = weights[0] * square[:, :NY]
        for k in range(1, kpts):
            density = density + weights[k] * square[:, k * NY : (k + 1) * NY]
        if former_ref is not None:
            density = density + jnp.concatenate([former_ref[a, p] for a in range(blocks)], axis=0)
        for a in range(blocks):
            density_ref[a, p] = density[a * block : (a + 1) * block]
        if is_last:
            level = jnp.mean(density[:8], axis=(0, 1), keepdims=True)
            half = mul3((forth_ref[0], forth_ref[1]), pieces(density - level), NT)
            half = half + jnp.where(first_row, level * NY, 0.0)
            send_ref[pl.ds(p, 2 * HALF, stride=planes), :] = half

    together = 4

    def some_planes(i, unused):
        for s in range(together):
            transform(together * i + s)
        return unused

    lax.fori_loop(0, planes // together, some_planes, 0)


def wave_band(kpts, tiles, total, scale, counts, came, wave_y, wave_x, forth, former, cell):
    planes = NZ // came.shape[0]
    block = NX // kpts
    is_first, is_last = former is None, forth is not None
    vmem = pl.BlockSpec(memory_space=pltpu.VMEM)
    operands = [counts, came, wave_y, wave_x]
    if is_last:
        operands.append(forth)
    if not is_first:
        operands += [former, cell]
    out_shape = [jax.ShapeDtypeStruct((kpts, planes, block, NY), jnp.float32)]
    if is_first and not is_last:
        out_shape.append(jax.ShapeDtypeStruct((1, total), jnp.float32))
    if is_last:
        out_shape.append(jax.ShapeDtypeStruct((2 * HALF * planes, NX), jnp.float32))
    rows = kpts * 2 * planes
    return pl.pallas_call(
        functools.partial(wave_kernel, kpts, tiles, scale, is_first, is_last),
        in_specs=[pl.BlockSpec(memory_space=pltpu.SMEM)] + [vmem] * (len(operands) - 1),
        out_specs=[vmem] * len(out_shape),
        out_shape=out_shape,
        scratch_shapes=[
            pltpu.VMEM((2 * rows, total), jnp.bfloat16),
            pltpu.VMEM((kpts * planes * HALF, LANES), jnp.float32),
            pltpu.VMEM((4 * HALF, total), jnp.bfloat16),
            pltpu.VMEM((4 * HALF, total), jnp.bfloat16),
        ],
        compiler_params=pltpu.CompilerParams(vmem_limit_bytes=VMEM_LIMIT),
        cost_estimate=pl.CostEstimate(
            flops=4 * rows * total * HALF * HALF, bytes_accessed=4 * came.size, transcendentals=0
        ),
        name="wave_band",
    )(*operands)


def poisson_kernel(pws, first_ref, came_ref, forth_ref, back_ref, both_x_ref, send_ref):
    count, parts, planes, unused = came_ref.shape
    pairs = parts // 2
    forth = (forth_ref[0], forth_ref[1])
    back = (back_ref[0], back_ref[1])
    both_x = (both_x_ref[0], both_x_ref[1])

    fields = [came_ref[:, i].reshape(NZ, NX) for i in range(parts)]
    level = jnp.mean(fields[0], axis=(0, 1), keepdims=True)
    fields[0] = fields[0] - jnp.where(first_ref[0] == 0, level, 0.0)
    field = jnp.concatenate(fields, axis=1)
    turned = mul3(forth, pieces(field), NN)

    def part(array, half, i):
        return array[half * NZ : (half + 1) * NZ, i * NX : (i + 1) * NX]

    lines = []
    for q in range(pairs):
        lines.append(part(turned, 0, 2 * q) + part(turned, 1, 2 * q + 1))
        lines.append(part(turned, 0, 2 * q + 1) - part(turned, 1, 2 * q))
    spectrum = mul3(pieces(jnp.concatenate(lines, axis=0)), both_x, NN)

    step_z = lax.broadcasted_iota(jnp.int32, (NZ, NX), 0)
    step_x = lax.broadcasted_iota(jnp.int32, (NZ, NX), 1)
    lines = []
    for q in range(pairs):
        real = spectrum[2 * q * NZ : (2 * q + 1) * NZ]
        imag = spectrum[(2 * q + 1) * NZ : (2 * q + 2) * NZ]
        freq_y = jnp.full((NZ, NX), first_ref[0] + q, jnp.int32)
        kernel = coulomb(signed_freq(step_z, NZ), signed_freq(step_x, NX), freq_y)
        kernel = kernel * (1.0 / (NX * NY * NZ))
        lines.append((real[:, :NX] + imag[:, NX:]) * kernel)
        lines.append((imag[:, :NX] - real[:, NX:]) * kernel)
    turned = mul3(pieces(jnp.concatenate(lines, axis=0)), both_x, NN)
    lines = []
    for q in range(pairs):
        real = turned[2 * q * NZ : (2 * q + 1) * NZ]
        imag = turned[(2 * q + 1) * NZ : (2 * q + 2) * NZ]
        lines.append(real[:, :NX] - imag[:, NX:])
        lines.append(real[:, NX:] + imag[:, :NX])
    turned = mul3(back, pieces(jnp.concatenate(lines, axis=1)), NN)

    kpts = count // pws
    merged = NZ // pws // 8
    block = NX // kpts
    rows = pws * 8
    lane = lax.broadcasted_iota(jnp.int32, (rows, LANES), 1) // block
    for q in range(pairs):
        real = part(turned, 0, 2 * q) - part(turned, 1, 2 * q + 1)
        imag = part(turned, 0, 2 * q + 1) + part(turned, 1, 2 * q)
        for c, value in enumerate((real, imag)):
            for a in range(kpts):
                packed = None
                for m in range(merged):
                    piece = value[m * rows : (m + 1) * rows]
                    shift = (m - a) * block % LANES
                    if shift:
                        piece = pltpu.roll(piece, shift, 1)
                    packed = piece if m == 0 else jnp.where(lane == m, piece, packed)
                send_ref[a * pws : (a + 1) * pws, 2 * q + c] = packed.reshape(pws, 8, LANES)


def poisson(pws, first, came, forth, back, both_x):
    vmem = pl.BlockSpec(memory_space=pltpu.VMEM)
    count, parts, unused, unused = came.shape
    return pl.pallas_call(
        functools.partial(poisson_kernel, pws),
        in_specs=[pl.BlockSpec(memory_space=pltpu.SMEM)] + [vmem] * 4,
        out_specs=vmem,
        out_shape=jax.ShapeDtypeStruct((count, parts, 8, LANES), jnp.float32),
        compiler_params=pltpu.CompilerParams(vmem_limit_bytes=VMEM_LIMIT),
        name="poisson",
    )(first, came, forth, back, both_x)


def finish_kernel(came_ref, back_ref, out_ref):
    back = (back_ref[0], back_ref[1])
    planes, block, unused = out_ref.shape
    merged = planes // 8
    for h in range(8):
        lines = came_ref[pl.ds(h, 2 * HALF, stride=8), :]
        field = mul3(pieces(lines), back, TN)
        out_ref[h * merged : (h + 1) * merged] = field.reshape(merged, block, NY)


def finish(planes, block, came, back_y):
    vmem = pl.BlockSpec(memory_space=pltpu.VMEM)
    return pl.pallas_call(
        finish_kernel,
        in_specs=[vmem] * 2,
        out_specs=vmem,
        out_shape=jax.ShapeDtypeStruct((planes, block, NY), jnp.float32),
        compiler_params=pltpu.CompilerParams(vmem_limit_bytes=VMEM_LIMIT),
        name="finish",
    )(came, back_y)


def exchange(array, axes):
    return lax.all_to_all(array, axes, split_axis=0, concat_axis=0, tiled=True)


def local_planes(band_coeffs, miller_third, column_slot, column_map, kpoint_counts):
    pws = lax.axis_size("pw")
    kpts = lax.axis_size("kpt")
    count = pws * kpts
    everyone = ("kpt", "pw")
    slots = column_map.shape[0]
    band_count = band_coeffs.shape[1]
    z_width = column_slot.shape[1] // slots
    planes = NZ // count
    parts = 2 * HALF // count
    made = tables(kpts, pws, planes)
    pencil = table(made["pencil"](z_width))
    wave_y, wave_x, forth_y, back_y, forth_z, back_z, both_x = (
        table(made[name])
        for name in ("wave_y", "wave_x", "forth_y", "back_y", "forth_z", "back_z", "both_x")
    )

    tiles = slots // LANES
    scale = 2.0 / (column_slot.shape[1] * pws)
    arrived = []
    for band in range(band_count):
        column = column_map.reshape(1, slots) if band == 0 else None
        packed = pack_band(
            band, count, band_coeffs, miller_third, column_slot, pencil, slots, column
        )
        arrived.append(exchange(packed, everyone))
    former = cell = None
    for band in range(band_count):
        forth = forth_y if band == band_count - 1 else None
        former, other = wave_band(
            kpts,
            tiles,
            pws * slots,
            scale,
            kpoint_counts,
            arrived[band],
            wave_y,
            wave_x,
            forth,
            former,
            cell,
        )
        cell = other if band == 0 else cell
    half = exchange(other.reshape(count, parts, planes, NX), everyone)
    device = lax.axis_index("kpt") * pws + lax.axis_index("pw")
    first = (device * (parts // 2)).astype(jnp.int32).reshape(1)
    back = poisson(pws, first, half, forth_z, back_z, both_x)
    back, former = lax.optimization_barrier((back, former))
    back = exchange(back, everyone)
    density = exchange(former, "kpt").reshape(NZ // pws, NX // kpts, NY)
    back = back.reshape(count * parts * 8, LANES)
    hartree = finish(NZ // pws, NX // kpts, back, back_y)
    return (density, hartree)


def fits_planes(kpts, pws):
    count = kpts * pws
    own = NZ // pws
    return (
        NZ % count == 0
        and NZ // count == 8
        and 2 * HALF % (2 * count) == 0
        and NX % kpts == 0
        and own % 8 == 0
        and own // 8 * (NX // kpts) == LANES
    )


def solution(mesh):
    chosen = local_planes if fits_planes(mesh.shape["kpt"], mesh.shape["pw"]) else local_general
    return jax.shard_map(
        chosen,
        mesh=mesh,
        in_specs=(P("kpt", None, None, "pw"), P("kpt", "pw"), P("kpt", "pw"), P("pw"), P()),
        out_specs=(P("pw", "kpt", None), P("pw", "kpt", None)),
        check_vma=False,
    )
```

```python
import functools
import math

import jax
import jax.numpy as jnp
import numpy as np
from jax import lax
from jax.experimental import pallas as pl
from jax.experimental.pallas import tpu as pltpu
from jax.sharding import PartitionSpec as P

NX = 128
NY = 128
NZ = 256


SPACING = 0.25


def contract(pattern, former, latter):
    return jnp.einsum(
        pattern, former, latter, precision=lax.Precision.HIGHEST, preferred_element_type=jnp.float32
    )


def phase_tables(first_index, second_index, length):
    product = first_index[:, None] * second_index[None, :] % length
    angle = product.astype(jnp.float32) * (2.0 * math.pi / length)
    return (jnp.cos(angle), jnp.sin(angle))


def signed_freq(values, length):
    return jnp.where(values >= length // 2, values - length, values)


def coulomb(freq_z, freq_x, freq_y):
    wave_z = freq_z.astype(jnp.float32) / (NZ * SPACING)
    wave_x = freq_x.astype(jnp.float32) / (NX * SPACING)
    wave_y = freq_y.astype(jnp.float32) / (NY * SPACING)
    squared = (2.0 * math.pi) ** 2 * (wave_z * wave_z + wave_x * wave_x + wave_y * wave_y)
    anchor = (freq_z == 0) & (freq_x == 0) & (freq_y == 0)
    return jnp.where(anchor, 0.0, 4.0 * math.pi / jnp.where(anchor, 1.0, squared))


def poisson_columns(real_part, imag_part, freq_x, freq_y):
    length = real_part.shape[0]
    steps_z = jnp.arange(length, dtype=jnp.int32)
    cos_z, sin_z = phase_tables(steps_z, steps_z, length)
    spec_real = contract("zk,km->zm", cos_z, real_part) + contract("zk,km->zm", sin_z, imag_part)
    spec_imag = contract("zk,km->zm", cos_z, imag_part) - contract("zk,km->zm", sin_z, real_part)
    kernel = coulomb(signed_freq(steps_z, length)[:, None], freq_x[None, :], freq_y[None, :]) / (
        NX * NY * NZ
    )
    spec_real = spec_real * kernel
    spec_imag = spec_imag * kernel
    back_real = contract("zk,km->zm", cos_z, spec_real) - contract("zk,km->zm", sin_z, spec_imag)
    back_imag = contract("zk,km->zm", sin_z, spec_real) + contract("zk,km->zm", cos_z, spec_imag)
    return (back_real, back_imag)


def forward_planes(field):
    steps_x = jnp.arange(NX, dtype=jnp.int32)
    steps_y = jnp.arange(NY, dtype=jnp.int32)
    cos_y, sin_y = phase_tables(steps_y, steps_y, NY)
    cos_x, sin_x = phase_tables(steps_x, steps_x, NX)
    half_real = contract("pxy,ky->pxk", field, cos_y)
    half_imag = -contract("pxy,ky->pxk", field, sin_y)
    spec_real = contract("kx,pxy->pky", cos_x, half_real) + contract(
        "kx,pxy->pky", sin_x, half_imag
    )
    spec_imag = contract("kx,pxy->pky", cos_x, half_imag) - contract(
        "kx,pxy->pky", sin_x, half_real
    )
    return (spec_real, spec_imag)


def local_general(band_coeffs, miller_third, column_slot, column_map, kpoint_counts):
    pw_count = lax.axis_size("pw")
    kpt_count = lax.axis_size("kpt")
    pw_index = lax.axis_index("pw")
    kpt_index = lax.axis_index("kpt")
    col_dev = column_map.shape[0]
    ng_dev = column_slot.shape[1]
    band_count = band_coeffs.shape[1]
    z_width = ng_dev // col_dev
    planes = NZ // pw_count
    x_block = NX // kpt_count
    col_total = pw_count * col_dev
    steps_y = jnp.arange(NY, dtype=jnp.int32)
    steps_x = jnp.arange(NX, dtype=jnp.int32)
    cos_y, sin_y = phase_tables(steps_y, steps_y, NY)
    cos_x, sin_x = phase_tables(steps_x, steps_x, NX)
    all_columns = lax.all_gather(column_map, "pw", axis=0, tiled=True)
    position = (miller_third[0] + z_width // 2) * col_dev + column_slot[0]
    source_of = (
        jnp.zeros((ng_dev,), jnp.int32).at[position].set(jnp.arange(ng_dev, dtype=jnp.int32))
    )
    coeff_rows = band_coeffs[0].reshape(band_count * 2, ng_dev).T
    packed = jnp.take(coeff_rows, source_of, axis=0)
    packed = (
        packed.reshape(z_width, col_dev, band_count, 2)
        .transpose(0, 2, 3, 1)
        .reshape(z_width, band_count * 2 * col_dev)
    )
    cos_z, sin_z = phase_tables(
        jnp.arange(NZ, dtype=jnp.int32), jnp.arange(z_width, dtype=jnp.int32) - z_width // 2, NZ
    )
    by_cos = contract("zj,jc->zc", cos_z, packed).reshape(NZ, band_count, 2, col_dev)
    by_sin = contract("zj,jc->zc", sin_z, packed).reshape(NZ, band_count, 2, col_dev)
    pencil = jnp.stack(
        (by_cos[:, :, 0] - by_sin[:, :, 1], by_sin[:, :, 0] + by_cos[:, :, 1]), axis=2
    )
    pencil = pencil.reshape(NZ, band_count * 2 * col_dev)
    arrived = lax.all_to_all(pencil, "pw", split_axis=0, concat_axis=1, tiled=True)
    arrived = arrived.reshape(planes, pw_count, band_count, 2, col_dev).transpose(2, 1, 4, 3, 0)
    arrived = arrived.reshape(band_count, col_total, 2 * planes)
    arrived = jnp.concatenate(
        (arrived, jnp.zeros((band_count, 1, 2 * planes), jnp.float32)), axis=1
    )
    cell_source = (
        jnp.full((NX * NY,), col_total, jnp.int32)
        .at[all_columns]
        .set(jnp.arange(col_total, dtype=jnp.int32))
    )

    def add_band(band, running):
        one_band = lax.dynamic_index_in_dim(arrived, band, 0, keepdims=False)
        placed = jnp.take(one_band, cell_source, axis=0)
        placed = placed.reshape(NX, NY, 2, planes).transpose(2, 3, 0, 1)
        grid_real = placed[0]
        grid_imag = placed[1]
        mixed_real = contract("pxm,ym->pxy", grid_real, cos_y) - contract(
            "pxm,ym->pxy", grid_imag, sin_y
        )
        mixed_imag = contract("pxm,ym->pxy", grid_real, sin_y) + contract(
            "pxm,ym->pxy", grid_imag, cos_y
        )
        wave_real = contract("xm,pmy->pxy", cos_x, mixed_real) - contract(
            "xm,pmy->pxy", sin_x, mixed_imag
        )
        wave_imag = contract("xm,pmy->pxy", sin_x, mixed_real) + contract(
            "xm,pmy->pxy", cos_x, mixed_imag
        )
        return running + wave_real * wave_real + wave_imag * wave_imag

    squares_sum = lax.fori_loop(0, band_count, add_band, jnp.zeros((planes, NX, NY), jnp.float32))
    weight = (
        2.0
        * kpoint_counts[kpt_index].astype(jnp.float32)
        / jnp.sum(kpoint_counts).astype(jnp.float32)
    )
    weight = weight / (ng_dev * pw_count)
    partial_value = weight * squares_sum
    total_density = lax.psum(partial_value, "kpt")
    density = lax.dynamic_slice_in_dim(total_density, kpt_index * x_block, x_block, 1)
    spec_real, spec_imag = forward_planes(total_density)
    rows_pw = NX // pw_count
    pencil_real, pencil_imag = (
        lax.all_to_all(spec_real, "pw", split_axis=1, concat_axis=0, tiled=True),
        lax.all_to_all(spec_imag, "pw", split_axis=1, concat_axis=0, tiled=True),
    )
    local_x = pw_index * rows_pw + jnp.arange(rows_pw, dtype=jnp.int32)
    freq_x = jnp.repeat(signed_freq(local_x, NX), NY)
    freq_y = jnp.tile(signed_freq(steps_y, NY), rows_pw)
    back_real, back_imag = poisson_columns(
        pencil_real.reshape(NZ, rows_pw * NY), pencil_imag.reshape(NZ, rows_pw * NY), freq_x, freq_y
    )
    plane_real, plane_imag = (
        lax.all_to_all(
            back_real.reshape(NZ, rows_pw, NY), "pw", split_axis=0, concat_axis=1, tiled=True
        ),
        lax.all_to_all(
            back_imag.reshape(NZ, rows_pw, NY), "pw", split_axis=0, concat_axis=1, tiled=True
        ),
    )
    own_rows = kpt_index * x_block + jnp.arange(x_block, dtype=jnp.int32)
    cos_rows, sin_rows = phase_tables(own_rows, steps_x, NX)
    rows_real = contract("xk,pky->pxy", cos_rows, plane_real) - contract(
        "xk,pky->pxy", sin_rows, plane_imag
    )
    rows_imag = contract("xk,pky->pxy", sin_rows, plane_real) + contract(
        "xk,pky->pxy", cos_rows, plane_imag
    )
    hartree = contract("pxk,yk->pxy", rows_real, cos_y) - contract("pxk,yk->pxy", rows_imag, sin_y)
    return (density, hartree)


LANES = 128
HALF = 64
VMEM_LIMIT = 56 * 1024 * 1024
NN = (((1,), (0,)), ((), ()))
NT = (((1,), (1,)), ((), ()))
TN = (((0,), (0,)), ((), ()))


def pieces(value):
    high = value.astype(jnp.bfloat16)
    low = (value - high.astype(jnp.float32)).astype(jnp.bfloat16)
    return high, low


def mul(former, latter, dims):
    return lax.dot_general(former, latter, dims, preferred_element_type=jnp.float32)


def mul3(former, latter, dims):
    (of_former,), (of_latter,) = dims[0]
    return mul(
        jnp.concatenate((former[0], former[0], former[1]), axis=of_former),
        jnp.concatenate((latter[0], latter[1], latter[0]), axis=of_latter),
        dims,
    )


def table(values):
    high = values.astype(np.float32).astype(jnp.bfloat16)
    low = (values - high.astype(np.float64)).astype(np.float32).astype(jnp.bfloat16)
    return jnp.asarray(np.stack((high, low)))


def angles(former, latter, length):
    return np.outer(former, latter) % length * (2.0 * np.pi / length)


def tables(kpts, pws, planes):
    count = kpts * pws
    low_freq = np.arange(HALF) - HALF // 2
    grid_x, grid_y, grid_z = np.arange(NX), np.arange(NY), np.arange(NZ)
    own_y = np.arange(HALF)

    device = np.arange(count)
    plane_of = (
        (device % pws)[:, None] * (NZ // pws)
        + (device // pws)[:, None] * planes
        + np.arange(planes)[None, :]
    )
    return_table = {}

    def pencil(z_width):
        angle = angles(plane_of.ravel(), np.arange(z_width) - z_width // 2, NZ)
        cos, sin = (
            part.reshape(count, 1, planes, z_width) for part in (np.cos(angle), np.sin(angle))
        )
        real = np.concatenate((cos, -sin), axis=3)
        imag = np.concatenate((sin, cos), axis=3)
        return np.concatenate((real, imag), axis=1).reshape(-1, 2 * z_width)

    return_table["pencil"] = pencil

    angle = angles(low_freq, grid_y, NY)
    cos, sin = np.cos(angle), np.sin(angle)
    return_table["wave_y"] = np.block([[cos, sin], [-sin, cos]])

    angle = angles(grid_x, low_freq, NX)
    cos, sin = np.cos(angle), np.sin(angle)
    return_table["wave_x"] = np.block([[cos, -sin], [sin, cos]])

    angle = angles(own_y, grid_y, NY)
    cos, sin = np.cos(angle), np.sin(angle)
    return_table["forth_y"] = np.stack((cos, -sin), axis=1).reshape(2 * HALF, NY)
    twice = np.where(own_y == 0, 1.0, 2.0)[:, None]
    return_table["back_y"] = np.stack((twice * cos, -twice * sin), axis=1).reshape(2 * HALF, NY)

    angle = angles(grid_z, plane_of.ravel(), NZ)
    return_table["forth_z"] = np.concatenate((np.cos(angle), np.sin(angle)), axis=0)
    own = NZ // pws
    merged = own // 8
    order = (
        np.arange(pws)[None, :, None] * own
        + np.arange(8)[None, None, :] * merged
        + np.arange(merged)[:, None, None]
    )
    angle = angles(order.ravel(), grid_z, NZ)
    return_table["back_z"] = np.concatenate((np.cos(angle), np.sin(angle)), axis=0)

    angle = angles(grid_x, grid_x, NX)
    return_table["both_x"] = np.concatenate((np.cos(angle), np.sin(angle)), axis=1)
    return return_table


def spread_lanes(row):
    return jnp.transpose(jnp.broadcast_to(row, (LANES, row.shape[1])))


def one_hot_lanes(row, lanes):
    column = spread_lanes(row.astype(jnp.float32)).astype(jnp.bfloat16)
    step = lax.broadcasted_iota(jnp.int32, column.shape, 1)
    one = jnp.ones(column.shape, jnp.bfloat16)
    zero = jnp.zeros(column.shape, jnp.bfloat16)
    return jnp.concatenate(
        [
            jnp.where(column == (step + first).astype(jnp.float32).astype(jnp.bfloat16), one, zero)
            for first in range(0, lanes, LANES)
        ],
        axis=1,
    )


def pack_kernel(width, has_column, *refs):
    coeff_ref, miller_ref, slot_ref, pencil_ref = refs[:4]
    rest = list(refs[4:])
    column_ref = rest.pop(0) if has_column else None
    out_ref, total = rest
    half = total.shape[0] // 4
    slots = 2 * half
    count = out_ref.shape[0]
    rows = pencil_ref.shape[1] // count
    size = miller_ref.shape[1]
    step_width = 1024 if size % 1024 == 0 else size
    together = 4 if size % (4 * step_width) == 0 else 1

    zero = jnp.zeros((half, step_width), jnp.bfloat16)
    steps = lax.broadcasted_iota(jnp.int32, (half, step_width), 0)
    steps = steps.astype(jnp.float32).astype(jnp.bfloat16)

    def add(step):
        part = pl.ds(pl.multiple_of(step * step_width, step_width), step_width)
        slot = slot_ref[:, part]
        second = slot >= half
        row = jnp.where(second, slot - half, slot).astype(jnp.float32).astype(jnp.bfloat16)
        lane = miller_ref[:, part] + width // 2
        lane = jnp.where(second, lane + width, lane)
        here = row == steps
        spread = jnp.concatenate(
            [
                jnp.where(here, piece[c : c + 1], zero)
                for piece in pieces(coeff_ref[0, 0, :, part])
                for c in range(2)
            ],
            axis=0,
        )
        total[...] += mul(spread, one_hot_lanes(lane, 2 * width), NN)

    total[...] = jnp.zeros_like(total)

    def some_steps(i, unused):
        for s in range(together):
            add(together * i + s)
        return unused

    lax.fori_loop(0, size // (together * step_width), some_steps, 0)

    both = []
    for at in range(2):
        parts = [
            total[(2 * at + c) * half : (2 * at + c + 1) * half].astype(jnp.bfloat16)
            for c in range(2)
        ]
        both.append(
            jnp.concatenate(
                [
                    jnp.concatenate([part[:, h * width : (h + 1) * width] for part in parts], axis=1)
                    for h in range(2)
                ],
                axis=0,
            )
        )
    pencils = mul3((pencil_ref[0], pencil_ref[1]), both, NT)
    tiles = slots // LANES
    for t in range(tiles):
        tile = pencils[:, t * LANES : (t + 1) * LANES].reshape(count, rows, LANES)
        out_ref[:, t * rows : (t + 1) * rows] = tile
    if has_column:
        column = column_ref[...].astype(jnp.float32)
        column = [column[:, t * LANES : (t + 1) * LANES] for t in range(tiles)]
        blank = [jnp.zeros((8 - tiles, LANES), jnp.float32)]
        column = jnp.concatenate(column + blank, axis=0)
        out_ref[:, tiles * rows :] = jnp.broadcast_to(column[None], (count, 8, LANES))


def pack_band(band, count, coeffs, miller, slot, pencil, slots, column):
    total = miller.shape[1]
    width = pencil.shape[2] // 2
    rows = pencil.shape[1] // count * (slots // LANES)
    operands = [coeffs, miller, slot, pencil]
    if column is not None:
        operands.append(column)
        rows += 8
    one_band = pl.BlockSpec((1, 1, 2, total), lambda i: (0, band, 0, 0))
    return pl.pallas_call(
        functools.partial(pack_kernel, width, column is not None),
        grid=(1,),
        in_specs=[one_band]
        + [pl.BlockSpec(x.shape, lambda i, n=x.ndim: (0,) * n) for x in operands[1:]],
        out_specs=pl.BlockSpec((count, rows, LANES), lambda i: (0, 0, 0)),
        out_shape=jax.ShapeDtypeStruct((count, rows, LANES), jnp.float32),
        scratch_shapes=[pltpu.VMEM((2 * slots, 2 * width), jnp.float32)],
        compiler_params=pltpu.CompilerParams(vmem_limit_bytes=VMEM_LIMIT),
        cost_estimate=pl.CostEstimate(
            flops=2 * total * slots * 4 * width, bytes_accessed=16 * total, transcendentals=0
        ),
        name="pack_band",
    )(*operands)


def wave_kernel(kpts, tiles, scale, is_first, is_last, *refs):
    own_ref, count_ref, came_ref, wave_y_ref, wave_x_ref = refs[:5]
    rest = list(refs[5:])
    forth_ref = rest.pop(0) if is_last else None
    former_ref, cell_ref = (None, None) if is_first else (rest.pop(0), rest.pop(0))
    density_refs = [rest.pop(0) for _ in range(kpts if is_last else 1)]
    cell_out = rest.pop(0) if is_first and not is_last else None
    send_ref = rest.pop(0) if is_last else None
    values, grid, chosen, whole = rest
    planes = density_refs[0].shape[0]
    block = NX // kpts
    part_rows = 2 * planes
    pws = came_ref.shape[0] // kpts
    rows = kpts * part_rows
    total = values.shape[1]

    for j in range(pws):
        for t in range(tiles):
            taken = jnp.concatenate(
                [came_ref[k * pws + j, t * part_rows : (t + 1) * part_rows] for k in range(kpts)],
                axis=0,
            )
            high, low = pieces(taken)
            first = (j * tiles + t) * LANES
            values[0:rows, first : first + LANES] = high
            values[rows : 2 * rows, first : first + LANES] = low

    if is_first:
        column = jnp.concatenate(
            [
                came_ref[j, tiles * part_rows + t : tiles * part_rows + t + 1]
                for j in range(pws)
                for t in range(tiles)
            ],
            axis=1,
        ).astype(jnp.int32)
        cell = ((column // NY + NX // 2) % NX - HALF // 2) * HALF
        cell = cell + (column % NY + NY // 2) % NY - HALF // 2
        cell = cell.astype(jnp.float32)
        if cell_out is not None:
            cell_out[...] = cell
    else:
        cell = cell_ref[...]
    tile = 4 * HALF
    high = jnp.floor(cell * (1.0 / tile))
    chosen[...] = one_hot_lanes(cell - high * tile, tile)
    high = high.astype(jnp.bfloat16)
    left = lax.broadcasted_iota(jnp.int32, (kpts * planes, LANES), 1) < HALF
    together = 4

    def place(t, found):
        found = found[:rows] + found[rows:]
        for h in range(2):
            real, imag = (
                jnp.concatenate(
                    [
                        found[(2 * k + c) * planes : (2 * k + c + 1) * planes, h * LANES : (h + 1) * LANES]
                        for k in range(kpts)
                    ],
                    axis=0,
                )
                for c in range(2)
            )
            even = jnp.where(left, real, pltpu.roll(imag, HALF, 1))
            odd = jnp.where(left, pltpu.roll(real, HALF, 1), imag)
            grid[pl.ds(t * 4 + 2 * h, kpts * planes, stride=HALF), :] = even
            grid[pl.ds(t * 4 + 2 * h + 1, kpts * planes, stride=HALF), :] = odd

    def some_tiles(i, unused):
        held = values[...]
        kept = []
        for s in range(together):
            here = high == (together * i + s).astype(jnp.float32).astype(jnp.bfloat16)
            kept.append(jnp.where(here, held, jnp.zeros_like(held)))
        found = mul(jnp.concatenate(kept, axis=0), chosen[...], NN)
        for s in range(together):
            place(together * i + s, found[2 * rows * s : 2 * rows * (s + 1)])
        return unused

    lax.fori_loop(0, HALF // 4 // together, some_tiles, 0)

    sum_of = count_ref[0]
    for k in range(1, kpts):
        sum_of = sum_of + count_ref[k]

    def spread(number):
        return jnp.full((8, NY), number, jnp.int32).astype(jnp.float32)

    weights = [
        jnp.concatenate([spread(count_ref[k]) / spread(sum_of) * scale] * (NX // 8), axis=0)
        for k in range(kpts)
    ]
    first_row = lax.broadcasted_iota(jnp.int32, (2 * HALF, NX), 0) == 0

    def transform(p):
        lines = jnp.concatenate(
            [
                grid[pl.ds(pl.multiple_of((k * planes + p) * HALF, HALF), HALF), :]
                for k in range(kpts)
            ],
            axis=0,
        )
        mixed = mul3(pieces(lines), (wave_y_ref[0], wave_y_ref[1]), NN)
        mixed = jnp.concatenate(
            [
                jnp.concatenate(
                    [mixed[k * HALF : (k + 1) * HALF, c * NY : (c + 1) * NY] for k in range(kpts)],
                    axis=1,
                )
                for c in range(2)
            ],
            axis=0,
        )
        wave = mul3((wave_x_ref[0], wave_x_ref[1]), pieces(mixed), NN)
        square = wave[:NX] * wave[:NX] + wave[NX:] * wave[NX:]
        density = weights[0] * square[:, :NY]
        for k in range(1, kpts):
            density = density + weights[k] * square[:, k * NY : (k + 1) * NY]
        if former_ref is not None:
            density = density + former_ref[p]
        if is_last:
            whole[...] = density
            for s, density_ref in enumerate(density_refs):
                first = pl.multiple_of(lax.rem(own_ref[0] + s, kpts) * block, block)
                density_ref[p] = whole[pl.ds(first, block), :]
        else:
            density_refs[0][p] = density
        if is_last:
            level = jnp.mean(density[:8], axis=(0, 1), keepdims=True)
            half = mul3((forth_ref[0], forth_ref[1]), pieces(density - level), NT)
            half = half + jnp.where(first_row, level * NY, 0.0)
            send_ref[pl.ds(p, 2 * HALF, stride=planes), :] = half

    def some_planes(i, unused):
        for s in range(together):
            transform(together * i + s)
        return unused

    lax.fori_loop(0, planes // together, some_planes, 0)


def wave_band(kpts, tiles, total, scale, own, counts, came, wave_y, wave_x, forth, former, cell):
    planes = NZ // came.shape[0]
    block = NX // kpts
    is_first, is_last = former is None, forth is not None
    vmem = pl.BlockSpec(memory_space=pltpu.VMEM)
    operands = [own, counts, came, wave_y, wave_x]
    if is_last:
        operands.append(forth)
    if not is_first:
        operands += [former, cell]
    if is_last:
        out_shape = [jax.ShapeDtypeStruct((planes, block, NY), jnp.float32)] * kpts
    else:
        out_shape = [jax.ShapeDtypeStruct((planes, NX, NY), jnp.float32)]
    if is_first and not is_last:
        out_shape.append(jax.ShapeDtypeStruct((1, total), jnp.float32))
    if is_last:
        out_shape.append(jax.ShapeDtypeStruct((2 * HALF * planes, NX), jnp.float32))
    rows = kpts * 2 * planes
    return pl.pallas_call(
        functools.partial(wave_kernel, kpts, tiles, scale, is_first, is_last),
        in_specs=[pl.BlockSpec(memory_space=pltpu.SMEM)] * 2 + [vmem] * (len(operands) - 2),
        out_specs=[vmem] * len(out_shape),
        out_shape=out_shape,
        scratch_shapes=[
            pltpu.VMEM((2 * rows, total), jnp.bfloat16),
            pltpu.VMEM((kpts * planes * HALF, LANES), jnp.float32),
            pltpu.VMEM((total, 4 * HALF), jnp.bfloat16),
            pltpu.VMEM((NX, NY), jnp.float32),
        ],
        compiler_params=pltpu.CompilerParams(vmem_limit_bytes=VMEM_LIMIT),
        cost_estimate=pl.CostEstimate(
            flops=4 * rows * total * HALF * HALF, bytes_accessed=4 * came.size, transcendentals=0
        ),
        name="wave_band",
    )(*operands)


def poisson_kernel(pws, first_ref, came_ref, forth_ref, back_ref, both_x_ref, send_ref):
    count, parts, planes, unused = came_ref.shape
    pairs = parts // 2
    forth = (forth_ref[0], forth_ref[1])
    back = (back_ref[0], back_ref[1])
    both_x = (both_x_ref[0], both_x_ref[1])

    fields = [came_ref[:, i].reshape(NZ, NX) for i in range(parts)]
    level = jnp.mean(fields[0], axis=(0, 1), keepdims=True)
    fields[0] = fields[0] - jnp.where(first_ref[0] == 0, level, 0.0)
    field = jnp.concatenate(fields, axis=1)
    turned = mul3(forth, pieces(field), NN)

    def part(array, half, i):
        return array[half * NZ : (half + 1) * NZ, i * NX : (i + 1) * NX]

    lines = []
    for q in range(pairs):
        lines.append(part(turned, 0, 2 * q) + part(turned, 1, 2 * q + 1))
        lines.append(part(turned, 0, 2 * q + 1) - part(turned, 1, 2 * q))
    spectrum = mul3(pieces(jnp.concatenate(lines, axis=0)), both_x, NN)

    step_z = lax.broadcasted_iota(jnp.int32, (NZ, NX), 0)
    step_x = lax.broadcasted_iota(jnp.int32, (NZ, NX), 1)
    lines = []
    for q in range(pairs):
        real = spectrum[2 * q * NZ : (2 * q + 1) * NZ]
        imag = spectrum[(2 * q + 1) * NZ : (2 * q + 2) * NZ]
        freq_y = jnp.full((NZ, NX), first_ref[0] + q, jnp.int32)
        kernel = coulomb(signed_freq(step_z, NZ), signed_freq(step_x, NX), freq_y)
        kernel = kernel * (1.0 / (NX * NY * NZ))
        lines.append((real[:, :NX] + imag[:, NX:]) * kernel)
        lines.append((imag[:, :NX] - real[:, NX:]) * kernel)
    turned = mul3(pieces(jnp.concatenate(lines, axis=0)), both_x, NN)
    lines = []
    for q in range(pairs):
        real = turned[2 * q * NZ : (2 * q + 1) * NZ]
        imag = turned[(2 * q + 1) * NZ : (2 * q + 2) * NZ]
        lines.append(real[:, :NX] - imag[:, NX:])
        lines.append(real[:, NX:] + imag[:, :NX])
    turned = mul3(back, pieces(jnp.concatenate(lines, axis=1)), NN)

    kpts = count // pws
    merged = NZ // pws // 8
    block = NX // kpts
    rows = pws * 8
    lane = lax.broadcasted_iota(jnp.int32, (rows, LANES), 1) // block
    for q in range(pairs):
        real = part(turned, 0, 2 * q) - part(turned, 1, 2 * q + 1)
        imag = part(turned, 0, 2 * q + 1) + part(turned, 1, 2 * q)
        for c, value in enumerate((real, imag)):
            for a in range(kpts):
                packed = None
                for m in range(merged):
                    piece = value[m * rows : (m + 1) * rows]
                    shift = (m - a) * block % LANES
                    if shift:
                        piece = pltpu.roll(piece, shift, 1)
                    packed = piece if m == 0 else jnp.where(lane == m, piece, packed)
                send_ref[a * pws : (a + 1) * pws, 2 * q + c] = packed.reshape(pws, 8, LANES)


def poisson(pws, first, came, forth, back, both_x):
    vmem = pl.BlockSpec(memory_space=pltpu.VMEM)
    count, parts, unused, unused = came.shape
    return pl.pallas_call(
        functools.partial(poisson_kernel, pws),
        in_specs=[pl.BlockSpec(memory_space=pltpu.SMEM)] + [vmem] * 4,
        out_specs=vmem,
        out_shape=jax.ShapeDtypeStruct((count, parts, 8, LANES), jnp.float32),
        compiler_params=pltpu.CompilerParams(vmem_limit_bytes=VMEM_LIMIT),
        name="poisson",
    )(first, came, forth, back, both_x)


def finish_kernel(own_ref, came_ref, back_ref, *refs):
    block_refs, density_ref, out_ref = refs[:-2], refs[-2], refs[-1]
    kpts = len(block_refs)
    back = (back_ref[0], back_ref[1])
    planes, block, unused = out_ref.shape
    merged = planes // 8
    for s, block_ref in enumerate(block_refs):
        sender = lax.rem(own_ref[0] + kpts - s, kpts)
        density_ref[pl.ds(sender * (planes // kpts), planes // kpts)] = block_ref[...]
    for h in range(8):
        lines = came_ref[pl.ds(h, 2 * HALF, stride=8), :]
        field = mul3(pieces(lines), back, TN)
        out_ref[h * merged : (h + 1) * merged] = field.reshape(merged, block, NY)


def finish(planes, block, own, came, back_y, blocks):
    vmem = pl.BlockSpec(memory_space=pltpu.VMEM)
    return pl.pallas_call(
        finish_kernel,
        in_specs=[pl.BlockSpec(memory_space=pltpu.SMEM)] + [vmem] * (2 + len(blocks)),
        out_specs=[vmem] * 2,
        out_shape=[jax.ShapeDtypeStruct((planes, block, NY), jnp.float32)] * 2,
        compiler_params=pltpu.CompilerParams(vmem_limit_bytes=VMEM_LIMIT),
        name="finish",
    )(own, came, back_y, *blocks)


def exchange(array, axes):
    return lax.all_to_all(array, axes, split_axis=0, concat_axis=0, tiled=True)


def local_planes(band_coeffs, miller_third, column_slot, column_map, kpoint_counts):
    pws = lax.axis_size("pw")
    kpts = lax.axis_size("kpt")
    count = pws * kpts
    everyone = ("kpt", "pw")
    slots = column_map.shape[0]
    band_count = band_coeffs.shape[1]
    z_width = column_slot.shape[1] // slots
    planes = NZ // count
    parts = 2 * HALF // count
    made = tables(kpts, pws, planes)
    pencil = table(made["pencil"](z_width))
    wave_y, wave_x, forth_y, back_y, forth_z, back_z, both_x = (
        table(made[name])
        for name in ("wave_y", "wave_x", "forth_y", "back_y", "forth_z", "back_z", "both_x")
    )

    tiles = slots // LANES
    scale = 2.0 / (column_slot.shape[1] * pws)
    arrived = []
    for band in range(band_count):
        column = column_map.reshape(1, slots) if band == 0 else None
        packed = pack_band(
            band, count, band_coeffs, miller_third, column_slot, pencil, slots, column
        )
        arrived.append(exchange(packed, everyone))
    own = lax.axis_index("kpt").astype(jnp.int32).reshape(1)
    former = cell = None
    for band in range(band_count):
        forth = forth_y if band == band_count - 1 else None
        *made_here, other = wave_band(
            kpts,
            tiles,
            pws * slots,
            scale,
            own,
            kpoint_counts,
            arrived[band],
            wave_y,
            wave_x,
            forth,
            former,
            cell,
        )
        former = made_here[0]
        cell = other if band == 0 else cell
    half = exchange(other.reshape(count, parts, planes, NX), everyone)
    blocks = [made_here[0]] + [
        lax.ppermute(made_here[s], "kpt", [(a, (a + s) % kpts) for a in range(kpts)])
        for s in range(1, kpts)
    ]
    device = lax.axis_index("kpt") * pws + lax.axis_index("pw")
    first = (device * (parts // 2)).astype(jnp.int32).reshape(1)
    back = poisson(pws, first, half, forth_z, back_z, both_x)
    back = exchange(back, everyone).reshape(count * parts * 8, LANES)
    return tuple(finish(NZ // pws, NX // kpts, own, back, back_y, blocks))


def fits_planes(kpts, pws):
    count = kpts * pws
    own = NZ // pws
    return (
        NZ % count == 0
        and NZ // count == 8
        and 2 * HALF % (2 * count) == 0
        and NX % kpts == 0
        and own % 8 == 0
        and own // 8 * (NX // kpts) == LANES
    )


def local(band_coeffs, miller_third, column_slot, column_map, kpoint_counts):
    slots = column_map.shape[0]
    plain = slots % LANES == 0 and slots // LANES <= 8 and slots // 2 <= 256
    plain = plain and column_slot.shape[1] == slots * LANES
    fits = plain and fits_planes(lax.axis_size("kpt"), lax.axis_size("pw"))
    chosen = local_planes if fits else local_general
    return chosen(band_coeffs, miller_third, column_slot, column_map, kpoint_counts)


def solution(mesh):
    return jax.shard_map(
        local,
        mesh=mesh,
        in_specs=(P("kpt", None, None, "pw"), P("kpt", "pw"), P("kpt", "pw"), P("pw"), P()),
        out_specs=(P("pw", "kpt", None), P("pw", "kpt", None)),
        check_vma=False,
    )
```

```python
import functools
import math

import jax
import jax.numpy as jnp
import numpy as np
from jax import lax
from jax.experimental import pallas as pl
from jax.experimental.pallas import tpu as pltpu
from jax.sharding import PartitionSpec as P

NX = 128
NY = 128
NZ = 256


SPACING = 0.25


def contract(pattern, former, latter):
    return jnp.einsum(
        pattern, former, latter, precision=lax.Precision.HIGHEST, preferred_element_type=jnp.float32
    )


def phase_tables(first_index, second_index, length):
    product = first_index[:, None] * second_index[None, :] % length
    angle = product.astype(jnp.float32) * (2.0 * math.pi / length)
    return (jnp.cos(angle), jnp.sin(angle))


def signed_freq(values, length):
    return jnp.where(values >= length // 2, values - length, values)


def coulomb(freq_z, freq_x, freq_y):
    wave_z = freq_z.astype(jnp.float32) / (NZ * SPACING)
    wave_x = freq_x.astype(jnp.float32) / (NX * SPACING)
    wave_y = freq_y.astype(jnp.float32) / (NY * SPACING)
    squared = (2.0 * math.pi) ** 2 * (wave_z * wave_z + wave_x * wave_x + wave_y * wave_y)
    anchor = (freq_z == 0) & (freq_x == 0) & (freq_y == 0)
    return jnp.where(anchor, 0.0, 4.0 * math.pi / jnp.where(anchor, 1.0, squared))


def poisson_columns(real_part, imag_part, freq_x, freq_y):
    length = real_part.shape[0]
    steps_z = jnp.arange(length, dtype=jnp.int32)
    cos_z, sin_z = phase_tables(steps_z, steps_z, length)
    spec_real = contract("zk,km->zm", cos_z, real_part) + contract("zk,km->zm", sin_z, imag_part)
    spec_imag = contract("zk,km->zm", cos_z, imag_part) - contract("zk,km->zm", sin_z, real_part)
    kernel = coulomb(signed_freq(steps_z, length)[:, None], freq_x[None, :], freq_y[None, :]) / (
        NX * NY * NZ
    )
    spec_real = spec_real * kernel
    spec_imag = spec_imag * kernel
    back_real = contract("zk,km->zm", cos_z, spec_real) - contract("zk,km->zm", sin_z, spec_imag)
    back_imag = contract("zk,km->zm", sin_z, spec_real) + contract("zk,km->zm", cos_z, spec_imag)
    return (back_real, back_imag)


def forward_planes(field):
    steps_x = jnp.arange(NX, dtype=jnp.int32)
    steps_y = jnp.arange(NY, dtype=jnp.int32)
    cos_y, sin_y = phase_tables(steps_y, steps_y, NY)
    cos_x, sin_x = phase_tables(steps_x, steps_x, NX)
    half_real = contract("pxy,ky->pxk", field, cos_y)
    half_imag = -contract("pxy,ky->pxk", field, sin_y)
    spec_real = contract("kx,pxy->pky", cos_x, half_real) + contract(
        "kx,pxy->pky", sin_x, half_imag
    )
    spec_imag = contract("kx,pxy->pky", cos_x, half_imag) - contract(
        "kx,pxy->pky", sin_x, half_real
    )
    return (spec_real, spec_imag)


def local_general(band_coeffs, miller_third, column_slot, column_map, kpoint_counts):
    pw_count = lax.axis_size("pw")
    kpt_count = lax.axis_size("kpt")
    pw_index = lax.axis_index("pw")
    kpt_index = lax.axis_index("kpt")
    col_dev = column_map.shape[0]
    ng_dev = column_slot.shape[1]
    band_count = band_coeffs.shape[1]
    z_width = ng_dev // col_dev
    planes = NZ // pw_count
    x_block = NX // kpt_count
    col_total = pw_count * col_dev
    steps_y = jnp.arange(NY, dtype=jnp.int32)
    steps_x = jnp.arange(NX, dtype=jnp.int32)
    cos_y, sin_y = phase_tables(steps_y, steps_y, NY)
    cos_x, sin_x = phase_tables(steps_x, steps_x, NX)
    all_columns = lax.all_gather(column_map, "pw", axis=0, tiled=True)
    position = (miller_third[0] + z_width // 2) * col_dev + column_slot[0]
    source_of = (
        jnp.zeros((ng_dev,), jnp.int32).at[position].set(jnp.arange(ng_dev, dtype=jnp.int32))
    )
    coeff_rows = band_coeffs[0].reshape(band_count * 2, ng_dev).T
    packed = jnp.take(coeff_rows, source_of, axis=0)
    packed = (
        packed.reshape(z_width, col_dev, band_count, 2)
        .transpose(0, 2, 3, 1)
        .reshape(z_width, band_count * 2 * col_dev)
    )
    cos_z, sin_z = phase_tables(
        jnp.arange(NZ, dtype=jnp.int32), jnp.arange(z_width, dtype=jnp.int32) - z_width // 2, NZ
    )
    by_cos = contract("zj,jc->zc", cos_z, packed).reshape(NZ, band_count, 2, col_dev)
    by_sin = contract("zj,jc->zc", sin_z, packed).reshape(NZ, band_count, 2, col_dev)
    pencil = jnp.stack(
        (by_cos[:, :, 0] - by_sin[:, :, 1], by_sin[:, :, 0] + by_cos[:, :, 1]), axis=2
    )
    pencil = pencil.reshape(NZ, band_count * 2 * col_dev)
    arrived = lax.all_to_all(pencil, "pw", split_axis=0, concat_axis=1, tiled=True)
    arrived = arrived.reshape(planes, pw_count, band_count, 2, col_dev).transpose(2, 1, 4, 3, 0)
    arrived = arrived.reshape(band_count, col_total, 2 * planes)
    arrived = jnp.concatenate(
        (arrived, jnp.zeros((band_count, 1, 2 * planes), jnp.float32)), axis=1
    )
    cell_source = (
        jnp.full((NX * NY,), col_total, jnp.int32)
        .at[all_columns]
        .set(jnp.arange(col_total, dtype=jnp.int32))
    )

    def add_band(band, running):
        one_band = lax.dynamic_index_in_dim(arrived, band, 0, keepdims=False)
        placed = jnp.take(one_band, cell_source, axis=0)
        placed = placed.reshape(NX, NY, 2, planes).transpose(2, 3, 0, 1)
        grid_real = placed[0]
        grid_imag = placed[1]
        mixed_real = contract("pxm,ym->pxy", grid_real, cos_y) - contract(
            "pxm,ym->pxy", grid_imag, sin_y
        )
        mixed_imag = contract("pxm,ym->pxy", grid_real, sin_y) + contract(
            "pxm,ym->pxy", grid_imag, cos_y
        )
        wave_real = contract("xm,pmy->pxy", cos_x, mixed_real) - contract(
            "xm,pmy->pxy", sin_x, mixed_imag
        )
        wave_imag = contract("xm,pmy->pxy", sin_x, mixed_real) + contract(
            "xm,pmy->pxy", cos_x, mixed_imag
        )
        return running + wave_real * wave_real + wave_imag * wave_imag

    squares_sum = lax.fori_loop(0, band_count, add_band, jnp.zeros((planes, NX, NY), jnp.float32))
    weight = (
        2.0
        * kpoint_counts[kpt_index].astype(jnp.float32)
        / jnp.sum(kpoint_counts).astype(jnp.float32)
    )
    weight = weight / (ng_dev * pw_count)
    partial_value = weight * squares_sum
    total_density = lax.psum(partial_value, "kpt")
    density = lax.dynamic_slice_in_dim(total_density, kpt_index * x_block, x_block, 1)
    spec_real, spec_imag = forward_planes(total_density)
    rows_pw = NX // pw_count
    pencil_real, pencil_imag = (
        lax.all_to_all(spec_real, "pw", split_axis=1, concat_axis=0, tiled=True),
        lax.all_to_all(spec_imag, "pw", split_axis=1, concat_axis=0, tiled=True),
    )
    local_x = pw_index * rows_pw + jnp.arange(rows_pw, dtype=jnp.int32)
    freq_x = jnp.repeat(signed_freq(local_x, NX), NY)
    freq_y = jnp.tile(signed_freq(steps_y, NY), rows_pw)
    back_real, back_imag = poisson_columns(
        pencil_real.reshape(NZ, rows_pw * NY), pencil_imag.reshape(NZ, rows_pw * NY), freq_x, freq_y
    )
    plane_real, plane_imag = (
        lax.all_to_all(
            back_real.reshape(NZ, rows_pw, NY), "pw", split_axis=0, concat_axis=1, tiled=True
        ),
        lax.all_to_all(
            back_imag.reshape(NZ, rows_pw, NY), "pw", split_axis=0, concat_axis=1, tiled=True
        ),
    )
    own_rows = kpt_index * x_block + jnp.arange(x_block, dtype=jnp.int32)
    cos_rows, sin_rows = phase_tables(own_rows, steps_x, NX)
    rows_real = contract("xk,pky->pxy", cos_rows, plane_real) - contract(
        "xk,pky->pxy", sin_rows, plane_imag
    )
    rows_imag = contract("xk,pky->pxy", sin_rows, plane_real) + contract(
        "xk,pky->pxy", cos_rows, plane_imag
    )
    hartree = contract("pxk,yk->pxy", rows_real, cos_y) - contract("pxk,yk->pxy", rows_imag, sin_y)
    return (density, hartree)


LANES = 128
HALF = 64
VMEM_LIMIT = 56 * 1024 * 1024
NN = (((1,), (0,)), ((), ()))
NT = (((1,), (1,)), ((), ()))
TN = (((0,), (0,)), ((), ()))


def pieces(value):
    high = value.astype(jnp.bfloat16)
    low = (value - high.astype(jnp.float32)).astype(jnp.bfloat16)
    return high, low


def mul(former, latter, dims):
    return lax.dot_general(former, latter, dims, preferred_element_type=jnp.float32)


def mul3(former, latter, dims):
    (of_former,), (of_latter,) = dims[0]
    return mul(
        jnp.concatenate((former[0], former[0], former[1]), axis=of_former),
        jnp.concatenate((latter[0], latter[1], latter[0]), axis=of_latter),
        dims,
    )


def table(values):
    high = values.astype(np.float32).astype(jnp.bfloat16)
    low = (values - high.astype(np.float64)).astype(np.float32).astype(jnp.bfloat16)
    return jnp.asarray(np.stack((high, low)))


def angles(former, latter, length):
    return np.outer(former, latter) % length * (2.0 * np.pi / length)


def tables(kpts, pws, planes):
    count = kpts * pws
    low_freq = np.arange(HALF) - HALF // 2
    grid_x, grid_y, grid_z = np.arange(NX), np.arange(NY), np.arange(NZ)
    own_y = np.arange(HALF)

    device = np.arange(count)
    plane_of = (
        (device % pws)[:, None] * (NZ // pws)
        + (device // pws)[:, None] * planes
        + np.arange(planes)[None, :]
    )
    return_table = {}

    def pencil(z_width):
        angle = angles(plane_of.ravel(), np.arange(z_width) - z_width // 2, NZ)
        cos, sin = (
            part.reshape(count, 1, planes, z_width) for part in (np.cos(angle), np.sin(angle))
        )
        real = np.concatenate((cos, -sin), axis=3)
        imag = np.concatenate((sin, cos), axis=3)
        return np.concatenate((real, imag), axis=1).reshape(-1, 2 * z_width)

    return_table["pencil"] = pencil

    angle = angles(low_freq, grid_y, NY)
    cos, sin = np.cos(angle), np.sin(angle)
    return_table["wave_y"] = np.block([[cos, sin], [-sin, cos]])

    angle = angles(grid_x, low_freq, NX)
    cos, sin = np.cos(angle), np.sin(angle)
    return_table["wave_x"] = np.block([[cos, -sin], [sin, cos]])

    angle = angles(own_y, grid_y, NY)
    cos, sin = np.cos(angle), np.sin(angle)
    return_table["forth_y"] = np.stack((cos, -sin), axis=1).reshape(2 * HALF, NY)
    twice = np.where(own_y == 0, 1.0, 2.0)[:, None]
    return_table["back_y"] = np.stack((twice * cos, -twice * sin), axis=1).reshape(2 * HALF, NY)

    angle = angles(grid_z, plane_of.ravel(), NZ)
    return_table["forth_z"] = np.concatenate((np.cos(angle), np.sin(angle)), axis=0)
    own = NZ // pws
    merged = own // 8
    order = (
        np.arange(pws)[None, :, None] * own
        + np.arange(8)[None, None, :] * merged
        + np.arange(merged)[:, None, None]
    )
    angle = angles(order.ravel(), grid_z, NZ)
    return_table["back_z"] = np.concatenate((np.cos(angle), np.sin(angle)), axis=0)

    angle = angles(grid_x, grid_x, NX)
    return_table["both_x"] = np.concatenate((np.cos(angle), np.sin(angle)), axis=1)
    return return_table


def spread_lanes(row):
    return jnp.transpose(jnp.broadcast_to(row, (LANES, row.shape[1])))


def one_hot_lanes(row, lanes):
    column = spread_lanes(row.astype(jnp.float32).astype(jnp.bfloat16))
    step = lax.broadcasted_iota(jnp.int32, column.shape, 1)
    one = jnp.ones(column.shape, jnp.bfloat16)
    zero = jnp.zeros(column.shape, jnp.bfloat16)
    return jnp.concatenate(
        [
            jnp.where(column == (step + first).astype(jnp.float32).astype(jnp.bfloat16), one, zero)
            for first in range(0, lanes, LANES)
        ],
        axis=1,
    )


def pack_kernel(width, has_column, *refs):
    coeff_ref, miller_ref, slot_ref, pencil_ref = refs[:4]
    rest = list(refs[4:])
    column_ref = rest.pop(0) if has_column else None
    out_ref, total = rest
    half = total.shape[0] // 4
    slots = 2 * half
    count = out_ref.shape[0]
    rows = pencil_ref.shape[1] // count
    size = miller_ref.shape[1]
    step_width = 1024 if size % 1024 == 0 else size
    together = 4 if size % (4 * step_width) == 0 else 1

    zero = jnp.zeros((half, step_width), jnp.bfloat16)
    steps = lax.broadcasted_iota(jnp.int32, (half, step_width), 0)
    steps = steps.astype(jnp.float32).astype(jnp.bfloat16)

    def add(step):
        part = pl.ds(pl.multiple_of(step * step_width, step_width), step_width)
        slot = slot_ref[:, part]
        second = slot >= half
        row = jnp.where(second, slot - half, slot).astype(jnp.float32).astype(jnp.bfloat16)
        lane = miller_ref[:, part] + width // 2
        lane = jnp.where(second, lane + width, lane)
        here = row == steps
        spread = jnp.concatenate(
            [
                jnp.where(here, piece[c : c + 1], zero)
                for piece in pieces(coeff_ref[0, 0, :, part])
                for c in range(2)
            ],
            axis=0,
        )
        total[...] += mul(spread, one_hot_lanes(lane, 2 * width), NN)

    total[...] = jnp.zeros_like(total)

    def some_steps(i, unused):
        for s in range(together):
            add(together * i + s)
        return unused

    lax.fori_loop(0, size // (together * step_width), some_steps, 0)

    both = []
    for at in range(2):
        parts = [
            total[(2 * at + c) * half : (2 * at + c + 1) * half].astype(jnp.bfloat16)
            for c in range(2)
        ]
        both.append(
            jnp.concatenate(
                [
                    jnp.concatenate([part[:, h * width : (h + 1) * width] for part in parts], axis=1)
                    for h in range(2)
                ],
                axis=0,
            )
        )
    pencils = mul3((pencil_ref[0], pencil_ref[1]), both, NT)
    tiles = slots // LANES
    for t in range(tiles):
        tile = pencils[:, t * LANES : (t + 1) * LANES].reshape(count, rows, LANES)
        out_ref[:, t * rows : (t + 1) * rows] = tile
    if has_column:
        column = [
            column_ref[t * LANES : (t + 1) * LANES].astype(jnp.float32).reshape(1, LANES)
            for t in range(tiles)
        ]
        blank = [jnp.zeros((8 - tiles, LANES), jnp.float32)]
        column = jnp.concatenate(column + blank, axis=0)
        out_ref[:, tiles * rows :] = jnp.broadcast_to(column[None], (count, 8, LANES))


def pack_band(band, count, coeffs, miller, slot, pencil, slots, column):
    total = miller.shape[1]
    width = pencil.shape[2] // 2
    rows = pencil.shape[1] // count * (slots // LANES)
    operands = [coeffs, miller, slot, pencil]
    if column is not None:
        operands.append(column)
        rows += 8
    one_band = pl.BlockSpec((1, 1, 2, total), lambda i: (0, band, 0, 0))
    return pl.pallas_call(
        functools.partial(pack_kernel, width, column is not None),
        grid=(1,),
        in_specs=[one_band]
        + [pl.BlockSpec(x.shape, lambda i, n=x.ndim: (0,) * n) for x in operands[1:]],
        out_specs=pl.BlockSpec((count, rows, LANES), lambda i: (0, 0, 0)),
        out_shape=jax.ShapeDtypeStruct((count, rows, LANES), jnp.float32),
        scratch_shapes=[pltpu.VMEM((2 * slots, 2 * width), jnp.float32)],
        compiler_params=pltpu.CompilerParams(vmem_limit_bytes=VMEM_LIMIT),
        cost_estimate=pl.CostEstimate(
            flops=2 * total * slots * 4 * width, bytes_accessed=16 * total, transcendentals=0
        ),
        name="pack_band",
    )(*operands)


def wave_kernel(kpts, tiles, scale, is_first, is_last, *refs):
    own_ref, count_ref, came_ref, wave_y_ref, wave_x_ref = refs[:5]
    rest = list(refs[5:])
    forth_ref = rest.pop(0) if is_last else None
    former_ref, cell_ref = (None, None) if is_first else (rest.pop(0), rest.pop(0))
    density_refs = [rest.pop(0) for _ in range(kpts if is_last else 1)]
    cell_out = rest.pop(0) if is_first and not is_last else None
    send_ref = rest.pop(0) if is_last else None
    values, grid, chosen, whole = rest
    planes = density_refs[0].shape[0]
    block = NX // kpts
    part_rows = 2 * planes
    pws = came_ref.shape[0] // kpts
    rows = kpts * part_rows
    total = values.shape[1]

    for j in range(pws):
        for t in range(tiles):
            taken = jnp.concatenate(
                [came_ref[k * pws + j, t * part_rows : (t + 1) * part_rows] for k in range(kpts)],
                axis=0,
            )
            high, low = pieces(taken)
            first = (j * tiles + t) * LANES
            values[0:rows, first : first + LANES] = high
            values[rows : 2 * rows, first : first + LANES] = low

    if is_first:
        column = jnp.concatenate(
            [
                came_ref[j, tiles * part_rows + t : tiles * part_rows + t + 1]
                for j in range(pws)
                for t in range(tiles)
            ],
            axis=1,
        ).astype(jnp.int32)
        cell = ((column // NY + NX // 2) % NX - HALF // 2) * HALF
        cell = cell + (column % NY + NY // 2) % NY - HALF // 2
        cell = cell.astype(jnp.float32)
        if cell_out is not None:
            cell_out[...] = cell
    else:
        cell = cell_ref[...]
    tile = 4 * HALF
    high = jnp.floor(cell * (1.0 / tile))
    chosen[...] = one_hot_lanes(cell - high * tile, tile)
    high = high.astype(jnp.bfloat16)
    left = lax.broadcasted_iota(jnp.int32, (kpts * planes, LANES), 1) < HALF
    together = 4

    def place(t, found):
        found = found[:rows] + found[rows:]
        for h in range(2):
            real, imag = (
                jnp.concatenate(
                    [
                        found[(2 * k + c) * planes : (2 * k + c + 1) * planes, h * LANES : (h + 1) * LANES]
                        for k in range(kpts)
                    ],
                    axis=0,
                )
                for c in range(2)
            )
            even = jnp.where(left, real, pltpu.roll(imag, HALF, 1))
            odd = jnp.where(left, pltpu.roll(real, HALF, 1), imag)
            grid[pl.ds(t * 4 + 2 * h, kpts * planes, stride=HALF), :] = even
            grid[pl.ds(t * 4 + 2 * h + 1, kpts * planes, stride=HALF), :] = odd

    def some_tiles(i, unused):
        held = values[...]
        kept = []
        for s in range(together):
            here = high == (together * i + s).astype(jnp.float32).astype(jnp.bfloat16)
            kept.append(jnp.where(here, held, jnp.zeros_like(held)))
        found = mul(jnp.concatenate(kept, axis=0), chosen[...], NN)
        for s in range(together):
            place(together * i + s, found[2 * rows * s : 2 * rows * (s + 1)])
        return unused

    lax.fori_loop(0, HALF // 4 // together, some_tiles, 0)

    sum_of = count_ref[0]
    for k in range(1, kpts):
        sum_of = sum_of + count_ref[k]

    def spread(number):
        return jnp.full((8, NY), number, jnp.int32).astype(jnp.float32)

    weights = [
        jnp.concatenate([spread(count_ref[k]) / spread(sum_of) * scale] * (NX // 8), axis=0)
        for k in range(kpts)
    ]
    first_row = lax.broadcasted_iota(jnp.int32, (2 * HALF, NX), 0) == 0

    def transform(p):
        lines = jnp.concatenate(
            [
                grid[pl.ds(pl.multiple_of((k * planes + p) * HALF, HALF), HALF), :]
                for k in range(kpts)
            ],
            axis=0,
        )
        mixed = mul3(pieces(lines), (wave_y_ref[0], wave_y_ref[1]), NN)
        mixed = jnp.concatenate(
            [
                jnp.concatenate(
                    [mixed[k * HALF : (k + 1) * HALF, c * NY : (c + 1) * NY] for k in range(kpts)],
                    axis=1,
                )
                for c in range(2)
            ],
            axis=0,
        )
        wave = mul3((wave_x_ref[0], wave_x_ref[1]), pieces(mixed), NN)
        square = wave[:NX] * wave[:NX] + wave[NX:] * wave[NX:]
        density = weights[0] * square[:, :NY]
        for k in range(1, kpts):
            density = density + weights[k] * square[:, k * NY : (k + 1) * NY]
        if former_ref is not None:
            density = density + former_ref[p]
        if is_last:
            whole[...] = density
            for s, density_ref in enumerate(density_refs):
                first = pl.multiple_of(lax.rem(own_ref[0] + s, kpts) * block, block)
                density_ref[p] = whole[pl.ds(first, block), :]
        else:
            density_refs[0][p] = density
        if is_last:
            level = jnp.mean(density[:8], axis=(0, 1), keepdims=True)
            half = mul3((forth_ref[0], forth_ref[1]), pieces(density - level), NT)
            half = half + jnp.where(first_row, level * NY, 0.0)
            send_ref[pl.ds(p, 2 * HALF, stride=planes), :] = half

    def some_planes(i, unused):
        for s in range(together):
            transform(together * i + s)
        return unused

    lax.fori_loop(0, planes // together, some_planes, 0)


def wave_band(kpts, tiles, total, scale, own, counts, came, wave_y, wave_x, forth, former, cell):
    planes = NZ // came.shape[0]
    block = NX // kpts
    is_first, is_last = former is None, forth is not None
    vmem = pl.BlockSpec(memory_space=pltpu.VMEM)
    operands = [own, counts, came, wave_y, wave_x]
    if is_last:
        operands.append(forth)
    if not is_first:
        operands += [former, cell]
    if is_last:
        out_shape = [jax.ShapeDtypeStruct((planes, block, NY), jnp.float32)] * kpts
    else:
        out_shape = [jax.ShapeDtypeStruct((planes, NX, NY), jnp.float32)]
    if is_first and not is_last:
        out_shape.append(jax.ShapeDtypeStruct((1, total), jnp.float32))
    if is_last:
        out_shape.append(jax.ShapeDtypeStruct((2 * HALF * planes, NX), jnp.float32))
    rows = kpts * 2 * planes
    return pl.pallas_call(
        functools.partial(wave_kernel, kpts, tiles, scale, is_first, is_last),
        in_specs=[pl.BlockSpec(memory_space=pltpu.SMEM)] * 2 + [vmem] * (len(operands) - 2),
        out_specs=[vmem] * len(out_shape),
        out_shape=out_shape,
        scratch_shapes=[
            pltpu.VMEM((2 * rows, total), jnp.bfloat16),
            pltpu.VMEM((kpts * planes * HALF, LANES), jnp.float32),
            pltpu.VMEM((total, 4 * HALF), jnp.bfloat16),
            pltpu.VMEM((NX, NY), jnp.float32),
        ],
        compiler_params=pltpu.CompilerParams(vmem_limit_bytes=VMEM_LIMIT),
        cost_estimate=pl.CostEstimate(
            flops=4 * rows * total * HALF * HALF, bytes_accessed=4 * came.size, transcendentals=0
        ),
        name="wave_band",
    )(*operands)


def poisson_kernel(pws, first_ref, came_ref, forth_ref, back_ref, both_x_ref, send_ref):
    count, parts, planes, unused = came_ref.shape
    pairs = parts // 2
    forth = (forth_ref[0], forth_ref[1])
    back = (back_ref[0], back_ref[1])
    both_x = (both_x_ref[0], both_x_ref[1])

    fields = [came_ref[:, i].reshape(NZ, NX) for i in range(parts)]
    level = jnp.mean(fields[0], axis=(0, 1), keepdims=True)
    fields[0] = fields[0] - jnp.where(first_ref[0] == 0, level, 0.0)
    field = jnp.concatenate(fields, axis=1)
    turned = mul3(forth, pieces(field), NN)

    def part(array, half, i):
        return array[half * NZ : (half + 1) * NZ, i * NX : (i + 1) * NX]

    lines = []
    for q in range(pairs):
        lines.append(part(turned, 0, 2 * q) + part(turned, 1, 2 * q + 1))
        lines.append(part(turned, 0, 2 * q + 1) - part(turned, 1, 2 * q))
    spectrum = mul3(pieces(jnp.concatenate(lines, axis=0)), both_x, NN)

    step_z = lax.broadcasted_iota(jnp.int32, (NZ, NX), 0)
    step_x = lax.broadcasted_iota(jnp.int32, (NZ, NX), 1)
    lines = []
    for q in range(pairs):
        real = spectrum[2 * q * NZ : (2 * q + 1) * NZ]
        imag = spectrum[(2 * q + 1) * NZ : (2 * q + 2) * NZ]
        freq_y = jnp.full((NZ, NX), first_ref[0] + q, jnp.int32)
        kernel = coulomb(signed_freq(step_z, NZ), signed_freq(step_x, NX), freq_y)
        kernel = kernel * (1.0 / (NX * NY * NZ))
        lines.append((real[:, :NX] + imag[:, NX:]) * kernel)
        lines.append((imag[:, :NX] - real[:, NX:]) * kernel)
    turned = mul3(pieces(jnp.concatenate(lines, axis=0)), both_x, NN)
    lines = []
    for q in range(pairs):
        real = turned[2 * q * NZ : (2 * q + 1) * NZ]
        imag = turned[(2 * q + 1) * NZ : (2 * q + 2) * NZ]
        lines.append(real[:, :NX] - imag[:, NX:])
        lines.append(real[:, NX:] + imag[:, :NX])
    turned = mul3(back, pieces(jnp.concatenate(lines, axis=1)), NN)

    kpts = count // pws
    merged = NZ // pws // 8
    block = NX // kpts
    rows = pws * 8
    lane = lax.broadcasted_iota(jnp.int32, (rows, LANES), 1) // block
    for q in range(pairs):
        real = part(turned, 0, 2 * q) - part(turned, 1, 2 * q + 1)
        imag = part(turned, 0, 2 * q + 1) + part(turned, 1, 2 * q)
        for c, value in enumerate((real, imag)):
            for a in range(kpts):
                packed = None
                for m in range(merged):
                    piece = value[m * rows : (m + 1) * rows]
                    shift = (m - a) * block % LANES
                    if shift:
                        piece = pltpu.roll(piece, shift, 1)
                    packed = piece if m == 0 else jnp.where(lane == m, piece, packed)
                send_ref[a * pws : (a + 1) * pws, 2 * q + c] = packed.reshape(pws, 8, LANES)


def poisson(pws, first, came, forth, back, both_x):
    vmem = pl.BlockSpec(memory_space=pltpu.VMEM)
    count, parts, unused, unused = came.shape
    return pl.pallas_call(
        functools.partial(poisson_kernel, pws),
        in_specs=[pl.BlockSpec(memory_space=pltpu.SMEM)] + [vmem] * 4,
        out_specs=vmem,
        out_shape=jax.ShapeDtypeStruct((count, parts, 8, LANES), jnp.float32),
        compiler_params=pltpu.CompilerParams(vmem_limit_bytes=VMEM_LIMIT),
        name="poisson",
    )(first, came, forth, back, both_x)


def finish_kernel(own_ref, came_ref, back_ref, *refs):
    block_refs, density_ref, out_ref = refs[:-2], refs[-2], refs[-1]
    kpts = len(block_refs)
    back = (back_ref[0], back_ref[1])
    planes, block, unused = out_ref.shape
    merged = planes // 8
    for s, block_ref in enumerate(block_refs):
        sender = lax.rem(own_ref[0] + kpts - s, kpts)
        density_ref[pl.ds(sender * (planes // kpts), planes // kpts)] = block_ref[...]
    for h in range(8):
        lines = came_ref[pl.ds(h, 2 * HALF, stride=8), :]
        field = mul3(pieces(lines), back, TN)
        out_ref[h * merged : (h + 1) * merged] = field.reshape(merged, block, NY)


def finish(planes, block, own, came, back_y, blocks):
    vmem = pl.BlockSpec(memory_space=pltpu.VMEM)
    return pl.pallas_call(
        finish_kernel,
        in_specs=[pl.BlockSpec(memory_space=pltpu.SMEM)] + [vmem] * (2 + len(blocks)),
        out_specs=[vmem] * 2,
        out_shape=[jax.ShapeDtypeStruct((planes, block, NY), jnp.float32)] * 2,
        compiler_params=pltpu.CompilerParams(vmem_limit_bytes=VMEM_LIMIT),
        name="finish",
    )(own, came, back_y, *blocks)


def exchange(array, axes):
    return lax.all_to_all(array, axes, split_axis=0, concat_axis=0, tiled=True)


def local_planes(band_coeffs, miller_third, column_slot, column_map, kpoint_counts):
    pws = lax.axis_size("pw")
    kpts = lax.axis_size("kpt")
    count = pws * kpts
    everyone = ("kpt", "pw")
    slots = column_map.shape[0]
    band_count = band_coeffs.shape[1]
    z_width = column_slot.shape[1] // slots
    planes = NZ // count
    parts = 2 * HALF // count
    made = tables(kpts, pws, planes)
    pencil = table(made["pencil"](z_width))
    wave_y, wave_x, forth_y, back_y, forth_z, back_z, both_x = (
        table(made[name])
        for name in ("wave_y", "wave_x", "forth_y", "back_y", "forth_z", "back_z", "both_x")
    )

    tiles = slots // LANES
    scale = 2.0 / (column_slot.shape[1] * pws)
    arrived = []
    for band in range(band_count):
        column = column_map if band == 0 else None
        packed = pack_band(
            band, count, band_coeffs, miller_third, column_slot, pencil, slots, column
        )
        arrived.append(exchange(packed, everyone))
    own = lax.axis_index("kpt").astype(jnp.int32).reshape(1)
    former = cell = None
    for band in range(band_count):
        forth = forth_y if band == band_count - 1 else None
        *made_here, other = wave_band(
            kpts,
            tiles,
            pws * slots,
            scale,
            own,
            kpoint_counts,
            arrived[band],
            wave_y,
            wave_x,
            forth,
            former,
            cell,
        )
        former = made_here[0]
        cell = other if band == 0 else cell
    half = exchange(other.reshape(count, parts, planes, NX), everyone)
    blocks = [made_here[0]] + [
        lax.ppermute(made_here[s], "kpt", [(a, (a + s) % kpts) for a in range(kpts)])
        for s in range(1, kpts)
    ]
    device = lax.axis_index("kpt") * pws + lax.axis_index("pw")
    first = (device * (parts // 2)).astype(jnp.int32).reshape(1)
    back = poisson(pws, first, half, forth_z, back_z, both_x)
    back = exchange(back, everyone).reshape(count * parts * 8, LANES)
    return tuple(finish(NZ // pws, NX // kpts, own, back, back_y, blocks))


def fits_planes(kpts, pws):
    count = kpts * pws
    own = NZ // pws
    return (
        NZ % count == 0
        and NZ // count == 8
        and 2 * HALF % (2 * count) == 0
        and NX % kpts == 0
        and own % 8 == 0
        and own // 8 * (NX // kpts) == LANES
    )


def local(band_coeffs, miller_third, column_slot, column_map, kpoint_counts):
    slots = column_map.shape[0]
    plain = slots % LANES == 0 and slots // LANES <= 8 and slots // 2 <= 256
    plain = plain and column_slot.shape[1] == slots * LANES
    fits = plain and fits_planes(lax.axis_size("kpt"), lax.axis_size("pw"))
    chosen = local_planes if fits else local_general
    return chosen(band_coeffs, miller_third, column_slot, column_map, kpoint_counts)


def solution(mesh):
    return jax.shard_map(
        local,
        mesh=mesh,
        in_specs=(P("kpt", None, None, "pw"), P("kpt", "pw"), P("kpt", "pw"), P("pw"), P()),
        out_specs=(P("pw", "kpt", None), P("pw", "kpt", None)),
        check_vma=False,
    )
```

```python
import functools
import math

import jax
import jax.numpy as jnp
import numpy as np
from jax import lax
from jax.experimental import pallas as pl
from jax.experimental.pallas import tpu as pltpu
from jax.sharding import PartitionSpec as P

NX = 128
NY = 128
NZ = 256


SPACING = 0.25


def contract(pattern, former, latter):
    return jnp.einsum(
        pattern, former, latter, precision=lax.Precision.HIGHEST, preferred_element_type=jnp.float32
    )


def phase_tables(first_index, second_index, length):
    product = first_index[:, None] * second_index[None, :] % length
    angle = product.astype(jnp.float32) * (2.0 * math.pi / length)
    return (jnp.cos(angle), jnp.sin(angle))


def signed_freq(values, length):
    return jnp.where(values >= length // 2, values - length, values)


def coulomb(freq_z, freq_x, freq_y):
    wave_z = freq_z.astype(jnp.float32) / (NZ * SPACING)
    wave_x = freq_x.astype(jnp.float32) / (NX * SPACING)
    wave_y = freq_y.astype(jnp.float32) / (NY * SPACING)
    squared = (2.0 * math.pi) ** 2 * (wave_z * wave_z + wave_x * wave_x + wave_y * wave_y)
    anchor = (freq_z == 0) & (freq_x == 0) & (freq_y == 0)
    return jnp.where(anchor, 0.0, 4.0 * math.pi / jnp.where(anchor, 1.0, squared))


def poisson_columns(real_part, imag_part, freq_x, freq_y):
    length = real_part.shape[0]
    steps_z = jnp.arange(length, dtype=jnp.int32)
    cos_z, sin_z = phase_tables(steps_z, steps_z, length)
    spec_real = contract("zk,km->zm", cos_z, real_part) + contract("zk,km->zm", sin_z, imag_part)
    spec_imag = contract("zk,km->zm", cos_z, imag_part) - contract("zk,km->zm", sin_z, real_part)
    kernel = coulomb(signed_freq(steps_z, length)[:, None], freq_x[None, :], freq_y[None, :]) / (
        NX * NY * NZ
    )
    spec_real = spec_real * kernel
    spec_imag = spec_imag * kernel
    back_real = contract("zk,km->zm", cos_z, spec_real) - contract("zk,km->zm", sin_z, spec_imag)
    back_imag = contract("zk,km->zm", sin_z, spec_real) + contract("zk,km->zm", cos_z, spec_imag)
    return (back_real, back_imag)


def forward_planes(field):
    steps_x = jnp.arange(NX, dtype=jnp.int32)
    steps_y = jnp.arange(NY, dtype=jnp.int32)
    cos_y, sin_y = phase_tables(steps_y, steps_y, NY)
    cos_x, sin_x = phase_tables(steps_x, steps_x, NX)
    half_real = contract("pxy,ky->pxk", field, cos_y)
    half_imag = -contract("pxy,ky->pxk", field, sin_y)
    spec_real = contract("kx,pxy->pky", cos_x, half_real) + contract(
        "kx,pxy->pky", sin_x, half_imag
    )
    spec_imag = contract("kx,pxy->pky", cos_x, half_imag) - contract(
        "kx,pxy->pky", sin_x, half_real
    )
    return (spec_real, spec_imag)


def local_general(band_coeffs, miller_third, column_slot, column_map, kpoint_counts):
    pw_count = lax.axis_size("pw")
    kpt_count = lax.axis_size("kpt")
    pw_index = lax.axis_index("pw")
    kpt_index = lax.axis_index("kpt")
    col_dev = column_map.shape[0]
    ng_dev = column_slot.shape[1]
    band_count = band_coeffs.shape[1]
    z_width = ng_dev // col_dev
    planes = NZ // pw_count
    x_block = NX // kpt_count
    col_total = pw_count * col_dev
    steps_y = jnp.arange(NY, dtype=jnp.int32)
    steps_x = jnp.arange(NX, dtype=jnp.int32)
    cos_y, sin_y = phase_tables(steps_y, steps_y, NY)
    cos_x, sin_x = phase_tables(steps_x, steps_x, NX)
    all_columns = lax.all_gather(column_map, "pw", axis=0, tiled=True)
    position = (miller_third[0] + z_width // 2) * col_dev + column_slot[0]
    source_of = (
        jnp.zeros((ng_dev,), jnp.int32).at[position].set(jnp.arange(ng_dev, dtype=jnp.int32))
    )
    coeff_rows = band_coeffs[0].reshape(band_count * 2, ng_dev).T
    packed = jnp.take(coeff_rows, source_of, axis=0)
    packed = (
        packed.reshape(z_width, col_dev, band_count, 2)
        .transpose(0, 2, 3, 1)
        .reshape(z_width, band_count * 2 * col_dev)
    )
    cos_z, sin_z = phase_tables(
        jnp.arange(NZ, dtype=jnp.int32), jnp.arange(z_width, dtype=jnp.int32) - z_width // 2, NZ
    )
    by_cos = contract("zj,jc->zc", cos_z, packed).reshape(NZ, band_count, 2, col_dev)
    by_sin = contract("zj,jc->zc", sin_z, packed).reshape(NZ, band_count, 2, col_dev)
    pencil = jnp.stack(
        (by_cos[:, :, 0] - by_sin[:, :, 1], by_sin[:, :, 0] + by_cos[:, :, 1]), axis=2
    )
    pencil = pencil.reshape(NZ, band_count * 2 * col_dev)
    arrived = lax.all_to_all(pencil, "pw", split_axis=0, concat_axis=1, tiled=True)
    arrived = arrived.reshape(planes, pw_count, band_count, 2, col_dev).transpose(2, 1, 4, 3, 0)
    arrived = arrived.reshape(band_count, col_total, 2 * planes)
    arrived = jnp.concatenate(
        (arrived, jnp.zeros((band_count, 1, 2 * planes), jnp.float32)), axis=1
    )
    cell_source = (
        jnp.full((NX * NY,), col_total, jnp.int32)
        .at[all_columns]
        .set(jnp.arange(col_total, dtype=jnp.int32))
    )

    def add_band(band, running):
        one_band = lax.dynamic_index_in_dim(arrived, band, 0, keepdims=False)
        placed = jnp.take(one_band, cell_source, axis=0)
        placed = placed.reshape(NX, NY, 2, planes).transpose(2, 3, 0, 1)
        grid_real = placed[0]
        grid_imag = placed[1]
        mixed_real = contract("pxm,ym->pxy", grid_real, cos_y) - contract(
            "pxm,ym->pxy", grid_imag, sin_y
        )
        mixed_imag = contract("pxm,ym->pxy", grid_real, sin_y) + contract(
            "pxm,ym->pxy", grid_imag, cos_y
        )
        wave_real = contract("xm,pmy->pxy", cos_x, mixed_real) - contract(
            "xm,pmy->pxy", sin_x, mixed_imag
        )
        wave_imag = contract("xm,pmy->pxy", sin_x, mixed_real) + contract(
            "xm,pmy->pxy", cos_x, mixed_imag
        )
        return running + wave_real * wave_real + wave_imag * wave_imag

    squares_sum = lax.fori_loop(0, band_count, add_band, jnp.zeros((planes, NX, NY), jnp.float32))
    weight = (
        2.0
        * kpoint_counts[kpt_index].astype(jnp.float32)
        / jnp.sum(kpoint_counts).astype(jnp.float32)
    )
    weight = weight / (ng_dev * pw_count)
    partial_value = weight * squares_sum
    total_density = lax.psum(partial_value, "kpt")
    density = lax.dynamic_slice_in_dim(total_density, kpt_index * x_block, x_block, 1)
    spec_real, spec_imag = forward_planes(total_density)
    rows_pw = NX // pw_count
    pencil_real, pencil_imag = (
        lax.all_to_all(spec_real, "pw", split_axis=1, concat_axis=0, tiled=True),
        lax.all_to_all(spec_imag, "pw", split_axis=1, concat_axis=0, tiled=True),
    )
    local_x = pw_index * rows_pw + jnp.arange(rows_pw, dtype=jnp.int32)
    freq_x = jnp.repeat(signed_freq(local_x, NX), NY)
    freq_y = jnp.tile(signed_freq(steps_y, NY), rows_pw)
    back_real, back_imag = poisson_columns(
        pencil_real.reshape(NZ, rows_pw * NY), pencil_imag.reshape(NZ, rows_pw * NY), freq_x, freq_y
    )
    plane_real, plane_imag = (
        lax.all_to_all(
            back_real.reshape(NZ, rows_pw, NY), "pw", split_axis=0, concat_axis=1, tiled=True
        ),
        lax.all_to_all(
            back_imag.reshape(NZ, rows_pw, NY), "pw", split_axis=0, concat_axis=1, tiled=True
        ),
    )
    own_rows = kpt_index * x_block + jnp.arange(x_block, dtype=jnp.int32)
    cos_rows, sin_rows = phase_tables(own_rows, steps_x, NX)
    rows_real = contract("xk,pky->pxy", cos_rows, plane_real) - contract(
        "xk,pky->pxy", sin_rows, plane_imag
    )
    rows_imag = contract("xk,pky->pxy", sin_rows, plane_real) + contract(
        "xk,pky->pxy", cos_rows, plane_imag
    )
    hartree = contract("pxk,yk->pxy", rows_real, cos_y) - contract("pxk,yk->pxy", rows_imag, sin_y)
    return (density, hartree)


LANES = 128
HALF = 64
VMEM_LIMIT = 56 * 1024 * 1024
NN = (((1,), (0,)), ((), ()))
NT = (((1,), (1,)), ((), ()))
TN = (((0,), (0,)), ((), ()))


def pieces(value):
    high = value.astype(jnp.bfloat16)
    low = (value - high.astype(jnp.float32)).astype(jnp.bfloat16)
    return high, low


def mul(former, latter, dims):
    return lax.dot_general(former, latter, dims, preferred_element_type=jnp.float32)


def mul3(former, latter, dims):
    (of_former,), (of_latter,) = dims[0]
    return mul(
        jnp.concatenate((former[0], former[0], former[1]), axis=of_former),
        jnp.concatenate((latter[0], latter[1], latter[0]), axis=of_latter),
        dims,
    )


def table(values):
    high = values.astype(np.float32).astype(jnp.bfloat16)
    low = (values - high.astype(np.float64)).astype(np.float32).astype(jnp.bfloat16)
    return jnp.asarray(np.stack((high, low)))


def angles(former, latter, length):
    return np.outer(former, latter) % length * (2.0 * np.pi / length)


def tables(kpts, pws, planes):
    count = kpts * pws
    low_freq = np.arange(HALF) - HALF // 2
    grid_x, grid_y, grid_z = np.arange(NX), np.arange(NY), np.arange(NZ)
    own_y = np.arange(HALF)

    device = np.arange(count)
    plane_of = (
        (device % pws)[:, None] * (NZ // pws)
        + (device // pws)[:, None] * planes
        + np.arange(planes)[None, :]
    )
    return_table = {}

    def pencil(z_width):
        angle = angles(plane_of.ravel(), np.arange(z_width) - z_width // 2, NZ)
        cos, sin = (
            part.reshape(count, 1, planes, z_width) for part in (np.cos(angle), np.sin(angle))
        )
        real = np.concatenate((cos, -sin), axis=3)
        imag = np.concatenate((sin, cos), axis=3)
        return np.concatenate((real, imag), axis=1).reshape(-1, 2 * z_width)

    return_table["pencil"] = pencil

    angle = angles(low_freq, grid_y, NY)
    cos, sin = np.cos(angle), np.sin(angle)
    return_table["wave_y"] = np.block([[cos, sin], [-sin, cos]])

    angle = angles(grid_x, low_freq, NX)
    cos, sin = np.cos(angle), np.sin(angle)
    return_table["wave_x"] = np.block([[cos, -sin], [sin, cos]])

    angle = angles(own_y, grid_y, NY)
    cos, sin = np.cos(angle), np.sin(angle)
    return_table["forth_y"] = np.stack((cos, -sin), axis=1).reshape(2 * HALF, NY)
    twice = np.where(own_y == 0, 1.0, 2.0)[:, None]
    return_table["back_y"] = np.stack((twice * cos, -twice * sin), axis=1).reshape(2 * HALF, NY)

    angle = angles(grid_z, plane_of.ravel(), NZ)
    return_table["forth_z"] = np.concatenate((np.cos(angle), np.sin(angle)), axis=0)
    own = NZ // pws
    merged = own // 8
    order = (
        np.arange(pws)[None, :, None] * own
        + np.arange(8)[None, None, :] * merged
        + np.arange(merged)[:, None, None]
    )
    angle = angles(order.ravel(), grid_z, NZ)
    return_table["back_z"] = np.concatenate((np.cos(angle), np.sin(angle)), axis=0)

    angle = angles(grid_x, grid_x, NX)
    return_table["both_x"] = np.concatenate((np.cos(angle), np.sin(angle)), axis=1)
    return return_table


def spread_lanes(row):
    return jnp.transpose(jnp.broadcast_to(row, (LANES, row.shape[1])))


def one_hot_lanes(row, lanes):
    column = spread_lanes(row.astype(jnp.float32).astype(jnp.bfloat16))
    step = lax.broadcasted_iota(jnp.int32, column.shape, 1)
    one = jnp.ones(column.shape, jnp.bfloat16)
    zero = jnp.zeros(column.shape, jnp.bfloat16)
    return jnp.concatenate(
        [
            jnp.where(column == (step + first).astype(jnp.float32).astype(jnp.bfloat16), one, zero)
            for first in range(0, lanes, LANES)
        ],
        axis=1,
    )


RANK_LOW = 64
WINDOW = 64


def exchange_rows(refs, low_bits, size_bits, descending):
    for outer in range(RANK_LOW):
        if any(outer >> bit & 1 for bit in low_bits[0]):
            continue
        touched = sorted(
            outer + sum(1 << bit for i, bit in enumerate(low_bits[0]) if pattern >> i & 1)
            for pattern in range(1 << len(low_bits[0]))
        )
        held = {v: [ref[v * 8 : v * 8 + 8, :] for ref in refs] for v in touched}
        for size, bits in zip(size_bits, low_bits[1:]):
            for bit in bits:
                for v in touched:
                    if v >> bit & 1:
                        continue
                    former, latter = held[v], held[v | 1 << bit]
                    if size < 6:
                        down = bool(v >> size & 1)
                        swap = former[0] < latter[0] if down else former[0] > latter[0]
                    else:
                        swap = former[0] > latter[0]
                        if descending is not None:
                            swap = jnp.logical_xor(swap, descending)
                    held[v] = [jnp.where(swap, y, x) for x, y in zip(former, latter)]
                    held[v | 1 << bit] = [jnp.where(swap, x, y) for x, y in zip(former, latter)]
        for v in touched:
            for ref, value in zip(refs, held[v]):
                ref[v * 8 : v * 8 + 8, :] = value


def exchange_sublanes(refs, stride, descending):
    sublane = lax.broadcasted_iota(jnp.int32, (8, LANES), 0)
    upper = sublane // stride % 2 == 1
    want_least = upper if descending is not None else jnp.logical_not(upper)
    if descending is not None:
        want_least = jnp.logical_not(jnp.logical_xor(upper, descending))

    def partner(value):
        if stride == 4:
            return pltpu.roll(value, 4, 0)
        return jnp.where(upper, pltpu.roll(value, stride, 0), pltpu.roll(value, 8 - stride, 0))

    for v in range(RANK_LOW):
        here = [ref[v * 8 : v * 8 + 8, :] for ref in refs]
        there = [partner(value) for value in here]
        take = jnp.where(
            want_least, (here[0] > there[0]).astype(jnp.int32), (here[0] < there[0]).astype(jnp.int32)
        )
        take = take == 1
        for ref, x, y in zip(refs, here, there):
            ref[v * 8 : v * 8 + 8, :] = jnp.where(take, y, x)


def sort_columns(refs):
    sublane = lax.broadcasted_iota(jnp.int32, (8, LANES), 0)
    exchange_rows(refs, [(0, 1, 2), (0,), (1, 0), (2, 1, 0)], [1, 2, 3], None)
    exchange_rows(refs, [(3,), (3,)], [4], None)
    exchange_rows(refs, [(0, 1, 2), (2, 1, 0)], [4], None)
    exchange_rows(refs, [(3, 4), (4, 3)], [5], None)
    exchange_rows(refs, [(0, 1, 2), (2, 1, 0)], [5], None)
    for size in range(6, 10):
        descending = None if size == 9 else sublane // (1 << (size - 6)) % 2 == 1
        for bit in range(size - 1, 5, -1):
            exchange_sublanes(refs, 1 << (bit - 6), descending)
        exchange_rows(refs, [(3, 4, 5), (5, 4, 3)], [size], descending)
        exchange_rows(refs, [(0, 1, 2), (2, 1, 0)], [size], descending)


def pack_kernel(width, has_column, *refs):
    coeff_ref, miller_ref, slot_ref, pencil_ref = refs[:4]
    rest = list(refs[4:])
    column_ref = rest.pop(0) if has_column else None
    out_ref, total, key_ref, real_ref, imag_ref = rest
    half = total.shape[0] // 4
    slots = 2 * half
    count = out_ref.shape[0]
    rows = pencil_ref.shape[1] // count
    length = miller_ref.shape[0]
    ranks = key_ref.shape[0]

    slot = slot_ref[...]
    second = slot >= half
    lane = miller_ref[...] + width // 2
    key = jnp.where(second, slot - half, slot) * (2 * width) + jnp.where(second, lane + width, lane)
    key_ref[0:length] = key.astype(jnp.float32)
    real_ref[0:length] = coeff_ref[0, pl.ds(0, length, stride=2), :]
    imag_ref[0:length] = coeff_ref[0, pl.ds(1, length, stride=2), :]
    blank = jnp.zeros((ranks - length, LANES), jnp.float32)
    key_ref[length:] = blank + 2.0 * slots * width
    real_ref[length:] = blank
    imag_ref[length:] = blank
    sort_columns((key_ref, real_ref, imag_ref))

    def base_of(block):
        base = 8 * (block // 2) + 8 * (block % 2) - WINDOW // 2
        return jnp.minimum(jnp.maximum(base, 0), half - WINDOW)

    sublane = lax.broadcasted_iota(jnp.int32, (8, LANES), 0)
    astray = jnp.zeros((8, LANES), jnp.float32)
    for v in range(RANK_LOW):
        base = base_of(sublane * (RANK_LOW // 8) + v // 8) * (2 * width)
        offset = key_ref[v * 8 : v * 8 + 8, :] - base.astype(jnp.float32)
        outside = jnp.logical_or(offset < 0.0, offset >= 2.0 * width * WINDOW)
        astray = jnp.where(outside, 1.0, astray)
    astray = jnp.max(jnp.where(sublane * RANK_LOW < length, astray, 0.0))

    def add(block, base, window):
        first = block % (RANK_LOW // 8) * 64 + block // (RANK_LOW // 8)
        where = pl.ds(first, 8, stride=8)
        keys = key_ref[where, :]
        high = jnp.floor(keys * (1.0 / (2 * width)))
        lane = keys - high * (2.0 * width)
        high = (high - base).astype(jnp.bfloat16)
        values = [piece for ref in (real_ref, imag_ref) for piece in pieces(ref[where, :])]
        values = [values[0], values[2], values[1], values[3]]
        steps = lax.broadcasted_iota(jnp.int32, (window, LANES), 0)
        steps = steps.astype(jnp.float32).astype(jnp.bfloat16)
        zero = jnp.zeros((window, LANES), jnp.bfloat16)
        spread, chosen = [], []
        for t in range(8):
            here = high[t : t + 1] == steps
            spread.append(
                jnp.concatenate([jnp.where(here, value[t : t + 1], zero) for value in values], axis=0)
            )
            chosen.append(one_hot_lanes(lane[t : t + 1], 2 * width))
        found = mul(jnp.concatenate(spread, axis=1), jnp.concatenate(chosen, axis=0), NN)
        for i in range(4):
            if window == half:
                into = pl.ds(i * half, half)
            else:
                into = pl.ds(pl.multiple_of(i * half + base, 8), window)
            total[into, :] += found[i * window : (i + 1) * window]

    total[...] = jnp.zeros_like(total)
    blocks = length // 8
    together = 4 if blocks % 4 == 0 else 1

    @pl.when(astray == 0.0)
    def _():
        def some_blocks(i, unused):
            for s in range(together):
                block = together * i + s
                add(block, base_of(block), WINDOW)
            return unused

        lax.fori_loop(0, blocks // together, some_blocks, 0)

    @pl.when(astray > 0.0)
    def _():
        def one_block(block, unused):
            add(block, 0, half)
            return unused

        lax.fori_loop(0, blocks, one_block, 0)

    both = []
    for at in range(2):
        parts = [
            total[(2 * at + c) * half : (2 * at + c + 1) * half].astype(jnp.bfloat16)
            for c in range(2)
        ]
        both.append(
            jnp.concatenate(
                [
                    jnp.concatenate([part[:, h * width : (h + 1) * width] for part in parts], axis=1)
                    for h in range(2)
                ],
                axis=0,
            )
        )
    pencils = mul3((pencil_ref[0], pencil_ref[1]), both, NT)
    tiles = slots // LANES
    for t in range(tiles):
        tile = pencils[:, t * LANES : (t + 1) * LANES].reshape(count, rows, LANES)
        out_ref[:, t * rows : (t + 1) * rows] = tile
    if has_column:
        column = [
            column_ref[t * LANES : (t + 1) * LANES].astype(jnp.float32).reshape(1, LANES)
            for t in range(tiles)
        ]
        blank = [jnp.zeros((8 - tiles, LANES), jnp.float32)]
        column = jnp.concatenate(column + blank, axis=0)
        out_ref[:, tiles * rows :] = jnp.broadcast_to(column[None], (count, 8, LANES))


def pack_band(band, count, coeffs, miller, slot, pencil, slots, column):
    length = miller.shape[0]
    width = pencil.shape[2] // 2
    rows = pencil.shape[1] // count * (slots // LANES)
    operands = [coeffs, miller, slot, pencil]
    if column is not None:
        operands.append(column)
        rows += 8
    one_band = pl.BlockSpec((1, 2 * length, LANES), lambda i: (band, 0, 0))
    return pl.pallas_call(
        functools.partial(pack_kernel, width, column is not None),
        grid=(1,),
        in_specs=[one_band]
        + [pl.BlockSpec(x.shape, lambda i, n=x.ndim: (0,) * n) for x in operands[1:]],
        out_specs=pl.BlockSpec((count, rows, LANES), lambda i: (0, 0, 0)),
        out_shape=jax.ShapeDtypeStruct((count, rows, LANES), jnp.float32),
        scratch_shapes=[pltpu.VMEM((2 * slots, 2 * width), jnp.float32)]
        + [pltpu.VMEM((8 * RANK_LOW, LANES), jnp.float32)] * 3,
        compiler_params=pltpu.CompilerParams(vmem_limit_bytes=VMEM_LIMIT),
        cost_estimate=pl.CostEstimate(
            flops=2 * length * LANES * slots * 4 * width,
            bytes_accessed=16 * length * LANES,
            transcendentals=0,
        ),
        name="pack_band",
    )(*operands)


def wave_kernel(kpts, tiles, scale, is_first, is_last, *refs):
    own_ref, count_ref, came_ref, wave_y_ref, wave_x_ref = refs[:5]
    rest = list(refs[5:])
    forth_ref = rest.pop(0) if is_last else None
    former_ref, cell_ref = (None, None) if is_first else (rest.pop(0), rest.pop(0))
    density_refs = [rest.pop(0) for _ in range(kpts if is_last else 1)]
    cell_out = rest.pop(0) if is_first and not is_last else None
    send_ref = rest.pop(0) if is_last else None
    values, grid, chosen, whole = rest
    planes = density_refs[0].shape[0]
    block = NX // kpts
    part_rows = 2 * planes
    pws = came_ref.shape[0] // kpts
    rows = kpts * part_rows
    total = values.shape[1]

    for j in range(pws):
        for t in range(tiles):
            taken = jnp.concatenate(
                [came_ref[k * pws + j, t * part_rows : (t + 1) * part_rows] for k in range(kpts)],
                axis=0,
            )
            high, low = pieces(taken)
            first = (j * tiles + t) * LANES
            values[0:rows, first : first + LANES] = high
            values[rows : 2 * rows, first : first + LANES] = low

    if is_first:
        column = jnp.concatenate(
            [
                came_ref[j, tiles * part_rows + t : tiles * part_rows + t + 1]
                for j in range(pws)
                for t in range(tiles)
            ],
            axis=1,
        ).astype(jnp.int32)
        cell = ((column // NY + NX // 2) % NX - HALF // 2) * HALF
        cell = cell + (column % NY + NY // 2) % NY - HALF // 2
        cell = cell.astype(jnp.float32)
        if cell_out is not None:
            cell_out[...] = cell
    else:
        cell = cell_ref[...]
    tile = 4 * HALF
    high = jnp.floor(cell * (1.0 / tile))
    chosen[...] = one_hot_lanes(cell - high * tile, tile)
    high = high.astype(jnp.bfloat16)
    left = lax.broadcasted_iota(jnp.int32, (kpts * planes, LANES), 1) < HALF
    together = 4

    def place(t, found):
        found = found[:rows] + found[rows:]
        for h in range(2):
            real, imag = (
                jnp.concatenate(
                    [
                        found[(2 * k + c) * planes : (2 * k + c + 1) * planes, h * LANES : (h + 1) * LANES]
                        for k in range(kpts)
                    ],
                    axis=0,
                )
                for c in range(2)
            )
            even = jnp.where(left, real, pltpu.roll(imag, HALF, 1))
            odd = jnp.where(left, pltpu.roll(real, HALF, 1), imag)
            grid[pl.ds(t * 4 + 2 * h, kpts * planes, stride=HALF), :] = even
            grid[pl.ds(t * 4 + 2 * h + 1, kpts * planes, stride=HALF), :] = odd

    def some_tiles(i, unused):
        held = values[...]
        kept = []
        for s in range(together):
            here = high == (together * i + s).astype(jnp.float32).astype(jnp.bfloat16)
            kept.append(jnp.where(here, held, jnp.zeros_like(held)))
        found = mul(jnp.concatenate(kept, axis=0), chosen[...], NN)
        for s in range(together):
            place(together * i + s, found[2 * rows * s : 2 * rows * (s + 1)])
        return unused

    lax.fori_loop(0, HALF // 4 // together, some_tiles, 0)

    sum_of = count_ref[0]
    for k in range(1, kpts):
        sum_of = sum_of + count_ref[k]

    def spread(number):
        return jnp.full((8, NY), number, jnp.int32).astype(jnp.float32)

    weights = [
        jnp.concatenate([spread(count_ref[k]) / spread(sum_of) * scale] * (NX // 8), axis=0)
        for k in range(kpts)
    ]
    first_row = lax.broadcasted_iota(jnp.int32, (2 * HALF, NX), 0) == 0

    def transform(p):
        lines = jnp.concatenate(
            [
                grid[pl.ds(pl.multiple_of((k * planes + p) * HALF, HALF), HALF), :]
                for k in range(kpts)
            ],
            axis=0,
        )
        mixed = mul3(pieces(lines), (wave_y_ref[0], wave_y_ref[1]), NN)
        mixed = jnp.concatenate(
            [
                jnp.concatenate(
                    [mixed[k * HALF : (k + 1) * HALF, c * NY : (c + 1) * NY] for k in range(kpts)],
                    axis=1,
                )
                for c in range(2)
            ],
            axis=0,
        )
        wave = mul3((wave_x_ref[0], wave_x_ref[1]), pieces(mixed), NN)
        square = wave[:NX] * wave[:NX] + wave[NX:] * wave[NX:]
        density = weights[0] * square[:, :NY]
        for k in range(1, kpts):
            density = density + weights[k] * square[:, k * NY : (k + 1) * NY]
        if former_ref is not None:
            density = density + former_ref[p]
        if is_last:
            whole[...] = density
            for s, density_ref in enumerate(density_refs):
                first = pl.multiple_of(lax.rem(own_ref[0] + s, kpts) * block, block)
                density_ref[p] = whole[pl.ds(first, block), :]
        else:
            density_refs[0][p] = density
        if is_last:
            level = jnp.mean(density[:8], axis=(0, 1), keepdims=True)
            half = mul3((forth_ref[0], forth_ref[1]), pieces(density - level), NT)
            half = half + jnp.where(first_row, level * NY, 0.0)
            send_ref[pl.ds(p, 2 * HALF, stride=planes), :] = half

    def some_planes(i, unused):
        for s in range(together):
            transform(together * i + s)
        return unused

    lax.fori_loop(0, planes // together, some_planes, 0)


def wave_band(kpts, tiles, total, scale, own, counts, came, wave_y, wave_x, forth, former, cell):
    planes = NZ // came.shape[0]
    block = NX // kpts
    is_first, is_last = former is None, forth is not None
    vmem = pl.BlockSpec(memory_space=pltpu.VMEM)
    operands = [own, counts, came, wave_y, wave_x]
    if is_last:
        operands.append(forth)
    if not is_first:
        operands += [former, cell]
    if is_last:
        out_shape = [jax.ShapeDtypeStruct((planes, block, NY), jnp.float32)] * kpts
    else:
        out_shape = [jax.ShapeDtypeStruct((planes, NX, NY), jnp.float32)]
    if is_first and not is_last:
        out_shape.append(jax.ShapeDtypeStruct((1, total), jnp.float32))
    if is_last:
        out_shape.append(jax.ShapeDtypeStruct((2 * HALF * planes, NX), jnp.float32))
    rows = kpts * 2 * planes
    return pl.pallas_call(
        functools.partial(wave_kernel, kpts, tiles, scale, is_first, is_last),
        in_specs=[pl.BlockSpec(memory_space=pltpu.SMEM)] * 2 + [vmem] * (len(operands) - 2),
        out_specs=[vmem] * len(out_shape),
        out_shape=out_shape,
        scratch_shapes=[
            pltpu.VMEM((2 * rows, total), jnp.bfloat16),
            pltpu.VMEM((kpts * planes * HALF, LANES), jnp.float32),
            pltpu.VMEM((total, 4 * HALF), jnp.bfloat16),
            pltpu.VMEM((NX, NY), jnp.float32),
        ],
        compiler_params=pltpu.CompilerParams(vmem_limit_bytes=VMEM_LIMIT),
        cost_estimate=pl.CostEstimate(
            flops=4 * rows * total * HALF * HALF, bytes_accessed=4 * came.size, transcendentals=0
        ),
        name="wave_band",
    )(*operands)


def poisson_kernel(pws, first_ref, came_ref, forth_ref, back_ref, both_x_ref, send_ref):
    count, parts, planes, unused = came_ref.shape
    pairs = parts // 2
    forth = (forth_ref[0], forth_ref[1])
    back = (back_ref[0], back_ref[1])
    both_x = (both_x_ref[0], both_x_ref[1])

    fields = [came_ref[:, i].reshape(NZ, NX) for i in range(parts)]
    level = jnp.mean(fields[0], axis=(0, 1), keepdims=True)
    fields[0] = fields[0] - jnp.where(first_ref[0] == 0, level, 0.0)
    field = jnp.concatenate(fields, axis=1)
    turned = mul3(forth, pieces(field), NN)

    def part(array, half, i):
        return array[half * NZ : (half + 1) * NZ, i * NX : (i + 1) * NX]

    lines = []
    for q in range(pairs):
        lines.append(part(turned, 0, 2 * q) + part(turned, 1, 2 * q + 1))
        lines.append(part(turned, 0, 2 * q + 1) - part(turned, 1, 2 * q))
    spectrum = mul3(pieces(jnp.concatenate(lines, axis=0)), both_x, NN)

    step_z = lax.broadcasted_iota(jnp.int32, (NZ, NX), 0)
    step_x = lax.broadcasted_iota(jnp.int32, (NZ, NX), 1)
    lines = []
    for q in range(pairs):
        real = spectrum[2 * q * NZ : (2 * q + 1) * NZ]
        imag = spectrum[(2 * q + 1) * NZ : (2 * q + 2) * NZ]
        freq_y = jnp.full((NZ, NX), first_ref[0] + q, jnp.int32)
        kernel = coulomb(signed_freq(step_z, NZ), signed_freq(step_x, NX), freq_y)
        kernel = kernel * (1.0 / (NX * NY * NZ))
        lines.append((real[:, :NX] + imag[:, NX:]) * kernel)
        lines.append((imag[:, :NX] - real[:, NX:]) * kernel)
    turned = mul3(pieces(jnp.concatenate(lines, axis=0)), both_x, NN)
    lines = []
    for q in range(pairs):
        real = turned[2 * q * NZ : (2 * q + 1) * NZ]
        imag = turned[(2 * q + 1) * NZ : (2 * q + 2) * NZ]
        lines.append(real[:, :NX] - imag[:, NX:])
        lines.append(real[:, NX:] + imag[:, :NX])
    turned = mul3(back, pieces(jnp.concatenate(lines, axis=1)), NN)

    kpts = count // pws
    merged = NZ // pws // 8
    block = NX // kpts
    rows = pws * 8
    lane = lax.broadcasted_iota(jnp.int32, (rows, LANES), 1) // block
    for q in range(pairs):
        real = part(turned, 0, 2 * q) - part(turned, 1, 2 * q + 1)
        imag = part(turned, 0, 2 * q + 1) + part(turned, 1, 2 * q)
        for c, value in enumerate((real, imag)):
            for a in range(kpts):
                packed = None
                for m in range(merged):
                    piece = value[m * rows : (m + 1) * rows]
                    shift = (m - a) * block % LANES
                    if shift:
                        piece = pltpu.roll(piece, shift, 1)
                    packed = piece if m == 0 else jnp.where(lane == m, piece, packed)
                send_ref[a * pws : (a + 1) * pws, 2 * q + c] = packed.reshape(pws, 8, LANES)


def poisson(pws, first, came, forth, back, both_x):
    vmem = pl.BlockSpec(memory_space=pltpu.VMEM)
    count, parts, unused, unused = came.shape
    return pl.pallas_call(
        functools.partial(poisson_kernel, pws),
        in_specs=[pl.BlockSpec(memory_space=pltpu.SMEM)] + [vmem] * 4,
        out_specs=vmem,
        out_shape=jax.ShapeDtypeStruct((count, parts, 8, LANES), jnp.float32),
        compiler_params=pltpu.CompilerParams(vmem_limit_bytes=VMEM_LIMIT),
        name="poisson",
    )(first, came, forth, back, both_x)


def finish_kernel(own_ref, came_ref, back_ref, *refs):
    block_refs, density_ref, out_ref = refs[:-2], refs[-2], refs[-1]
    kpts = len(block_refs)
    back = (back_ref[0], back_ref[1])
    planes, block, unused = out_ref.shape
    merged = planes // 8
    for s, block_ref in enumerate(block_refs):
        sender = lax.rem(own_ref[0] + kpts - s, kpts)
        density_ref[pl.ds(sender * (planes // kpts), planes // kpts)] = block_ref[...]
    for h in range(8):
        lines = came_ref[pl.ds(h, 2 * HALF, stride=8), :]
        field = mul3(pieces(lines), back, TN)
        out_ref[h * merged : (h + 1) * merged] = field.reshape(merged, block, NY)


def finish(planes, block, own, came, back_y, blocks):
    vmem = pl.BlockSpec(memory_space=pltpu.VMEM)
    return pl.pallas_call(
        finish_kernel,
        in_specs=[pl.BlockSpec(memory_space=pltpu.SMEM)] + [vmem] * (2 + len(blocks)),
        out_specs=[vmem] * 2,
        out_shape=[jax.ShapeDtypeStruct((planes, block, NY), jnp.float32)] * 2,
        compiler_params=pltpu.CompilerParams(vmem_limit_bytes=VMEM_LIMIT),
        name="finish",
    )(own, came, back_y, *blocks)


def exchange(array, axes):
    return lax.all_to_all(array, axes, split_axis=0, concat_axis=0, tiled=True)


def local_planes(band_coeffs, miller_third, column_slot, column_map, kpoint_counts):
    pws = lax.axis_size("pw")
    kpts = lax.axis_size("kpt")
    count = pws * kpts
    everyone = ("kpt", "pw")
    slots = column_map.shape[0]
    band_count = band_coeffs.shape[1]
    z_width = column_slot.shape[1] // slots
    planes = NZ // count
    parts = 2 * HALF // count
    made = tables(kpts, pws, planes)
    pencil = table(made["pencil"](z_width))
    wave_y, wave_x, forth_y, back_y, forth_z, back_z, both_x = (
        table(made[name])
        for name in ("wave_y", "wave_x", "forth_y", "back_y", "forth_z", "back_z", "both_x")
    )

    tiles = slots // LANES
    length = column_slot.shape[1] // LANES
    coeffs = band_coeffs.reshape(band_count, 2, length, LANES).transpose(0, 2, 1, 3)
    coeffs = coeffs.reshape(band_count, 2 * length, LANES)
    miller = miller_third.reshape(length, LANES)
    slot = column_slot.reshape(length, LANES)
    scale = 2.0 / (column_slot.shape[1] * pws)
    arrived = []
    for band in range(band_count):
        column = column_map if band == 0 else None
        packed = pack_band(
            band, count, coeffs, miller, slot, pencil, slots, column
        )
        arrived.append(exchange(packed, everyone))
    own = lax.axis_index("kpt").astype(jnp.int32).reshape(1)
    former = cell = None
    for band in range(band_count):
        forth = forth_y if band == band_count - 1 else None
        *made_here, other = wave_band(
            kpts,
            tiles,
            pws * slots,
            scale,
            own,
            kpoint_counts,
            arrived[band],
            wave_y,
            wave_x,
            forth,
            former,
            cell,
        )
        former = made_here[0]
        cell = other if band == 0 else cell
    half = exchange(other.reshape(count, parts, planes, NX), everyone)
    blocks = [made_here[0]] + [
        lax.ppermute(made_here[s], "kpt", [(a, (a + s) % kpts) for a in range(kpts)])
        for s in range(1, kpts)
    ]
    device = lax.axis_index("kpt") * pws + lax.axis_index("pw")
    first = (device * (parts // 2)).astype(jnp.int32).reshape(1)
    back = poisson(pws, first, half, forth_z, back_z, both_x)
    back = exchange(back, everyone).reshape(count * parts * 8, LANES)
    return tuple(finish(NZ // pws, NX // kpts, own, back, back_y, blocks))


def fits_planes(kpts, pws):
    count = kpts * pws
    own = NZ // pws
    return (
        NZ % count == 0
        and NZ // count == 8
        and 2 * HALF % (2 * count) == 0
        and NX % kpts == 0
        and own % 8 == 0
        and own // 8 * (NX // kpts) == LANES
    )


def local(band_coeffs, miller_third, column_slot, column_map, kpoint_counts):
    slots = column_map.shape[0]
    plain = slots % LANES == 0 and LANES <= slots <= 8 * RANK_LOW
    plain = plain and column_slot.shape[1] == slots * LANES
    fits = plain and fits_planes(lax.axis_size("kpt"), lax.axis_size("pw"))
    chosen = local_planes if fits else local_general
    return chosen(band_coeffs, miller_third, column_slot, column_map, kpoint_counts)


def solution(mesh):
    return jax.shard_map(
        local,
        mesh=mesh,
        in_specs=(P("kpt", None, None, "pw"), P("kpt", "pw"), P("kpt", "pw"), P("pw"), P()),
        out_specs=(P("pw", "kpt", None), P("pw", "kpt", None)),
        check_vma=False,
    )
```

```python
import functools
import math

import jax
import jax.numpy as jnp
import numpy as np
from jax import lax
from jax.experimental import pallas as pl
from jax.experimental.pallas import tpu as pltpu
from jax.sharding import PartitionSpec as P

NX = 128
NY = 128
NZ = 256


SPACING = 0.25


def contract(pattern, former, latter):
    return jnp.einsum(
        pattern, former, latter, precision=lax.Precision.HIGHEST, preferred_element_type=jnp.float32
    )


def phase_tables(first_index, second_index, length):
    product = first_index[:, None] * second_index[None, :] % length
    angle = product.astype(jnp.float32) * (2.0 * math.pi / length)
    return (jnp.cos(angle), jnp.sin(angle))


def signed_freq(values, length):
    return jnp.where(values >= length // 2, values - length, values)


def coulomb(freq_z, freq_x, freq_y):
    wave_z = freq_z.astype(jnp.float32) / (NZ * SPACING)
    wave_x = freq_x.astype(jnp.float32) / (NX * SPACING)
    wave_y = freq_y.astype(jnp.float32) / (NY * SPACING)
    squared = (2.0 * math.pi) ** 2 * (wave_z * wave_z + wave_x * wave_x + wave_y * wave_y)
    anchor = (freq_z == 0) & (freq_x == 0) & (freq_y == 0)
    return jnp.where(anchor, 0.0, 4.0 * math.pi / jnp.where(anchor, 1.0, squared))


def poisson_columns(real_part, imag_part, freq_x, freq_y):
    length = real_part.shape[0]
    steps_z = jnp.arange(length, dtype=jnp.int32)
    cos_z, sin_z = phase_tables(steps_z, steps_z, length)
    spec_real = contract("zk,km->zm", cos_z, real_part) + contract("zk,km->zm", sin_z, imag_part)
    spec_imag = contract("zk,km->zm", cos_z, imag_part) - contract("zk,km->zm", sin_z, real_part)
    kernel = coulomb(signed_freq(steps_z, length)[:, None], freq_x[None, :], freq_y[None, :]) / (
        NX * NY * NZ
    )
    spec_real = spec_real * kernel
    spec_imag = spec_imag * kernel
    back_real = contract("zk,km->zm", cos_z, spec_real) - contract("zk,km->zm", sin_z, spec_imag)
    back_imag = contract("zk,km->zm", sin_z, spec_real) + contract("zk,km->zm", cos_z, spec_imag)
    return (back_real, back_imag)


def forward_planes(field):
    steps_x = jnp.arange(NX, dtype=jnp.int32)
    steps_y = jnp.arange(NY, dtype=jnp.int32)
    cos_y, sin_y = phase_tables(steps_y, steps_y, NY)
    cos_x, sin_x = phase_tables(steps_x, steps_x, NX)
    half_real = contract("pxy,ky->pxk", field, cos_y)
    half_imag = -contract("pxy,ky->pxk", field, sin_y)
    spec_real = contract("kx,pxy->pky", cos_x, half_real) + contract(
        "kx,pxy->pky", sin_x, half_imag
    )
    spec_imag = contract("kx,pxy->pky", cos_x, half_imag) - contract(
        "kx,pxy->pky", sin_x, half_real
    )
    return (spec_real, spec_imag)


def local_general(band_coeffs, miller_third, column_slot, column_map, kpoint_counts):
    pw_count = lax.axis_size("pw")
    kpt_count = lax.axis_size("kpt")
    pw_index = lax.axis_index("pw")
    kpt_index = lax.axis_index("kpt")
    col_dev = column_map.shape[0]
    ng_dev = column_slot.shape[1]
    band_count = band_coeffs.shape[1]
    z_width = ng_dev // col_dev
    planes = NZ // pw_count
    x_block = NX // kpt_count
    col_total = pw_count * col_dev
    steps_y = jnp.arange(NY, dtype=jnp.int32)
    steps_x = jnp.arange(NX, dtype=jnp.int32)
    cos_y, sin_y = phase_tables(steps_y, steps_y, NY)
    cos_x, sin_x = phase_tables(steps_x, steps_x, NX)
    all_columns = lax.all_gather(column_map, "pw", axis=0, tiled=True)
    position = (miller_third[0] + z_width // 2) * col_dev + column_slot[0]
    source_of = (
        jnp.zeros((ng_dev,), jnp.int32).at[position].set(jnp.arange(ng_dev, dtype=jnp.int32))
    )
    coeff_rows = band_coeffs[0].reshape(band_count * 2, ng_dev).T
    packed = jnp.take(coeff_rows, source_of, axis=0)
    packed = (
        packed.reshape(z_width, col_dev, band_count, 2)
        .transpose(0, 2, 3, 1)
        .reshape(z_width, band_count * 2 * col_dev)
    )
    cos_z, sin_z = phase_tables(
        jnp.arange(NZ, dtype=jnp.int32), jnp.arange(z_width, dtype=jnp.int32) - z_width // 2, NZ
    )
    by_cos = contract("zj,jc->zc", cos_z, packed).reshape(NZ, band_count, 2, col_dev)
    by_sin = contract("zj,jc->zc", sin_z, packed).reshape(NZ, band_count, 2, col_dev)
    pencil = jnp.stack(
        (by_cos[:, :, 0] - by_sin[:, :, 1], by_sin[:, :, 0] + by_cos[:, :, 1]), axis=2
    )
    pencil = pencil.reshape(NZ, band_count * 2 * col_dev)
    arrived = lax.all_to_all(pencil, "pw", split_axis=0, concat_axis=1, tiled=True)
    arrived = arrived.reshape(planes, pw_count, band_count, 2, col_dev).transpose(2, 1, 4, 3, 0)
    arrived = arrived.reshape(band_count, col_total, 2 * planes)
    arrived = jnp.concatenate(
        (arrived, jnp.zeros((band_count, 1, 2 * planes), jnp.float32)), axis=1
    )
    cell_source = (
        jnp.full((NX * NY,), col_total, jnp.int32)
        .at[all_columns]
        .set(jnp.arange(col_total, dtype=jnp.int32))
    )

    def add_band(band, running):
        one_band = lax.dynamic_index_in_dim(arrived, band, 0, keepdims=False)
        placed = jnp.take(one_band, cell_source, axis=0)
        placed = placed.reshape(NX, NY, 2, planes).transpose(2, 3, 0, 1)
        grid_real = placed[0]
        grid_imag = placed[1]
        mixed_real = contract("pxm,ym->pxy", grid_real, cos_y) - contract(
            "pxm,ym->pxy", grid_imag, sin_y
        )
        mixed_imag = contract("pxm,ym->pxy", grid_real, sin_y) + contract(
            "pxm,ym->pxy", grid_imag, cos_y
        )
        wave_real = contract("xm,pmy->pxy", cos_x, mixed_real) - contract(
            "xm,pmy->pxy", sin_x, mixed_imag
        )
        wave_imag = contract("xm,pmy->pxy", sin_x, mixed_real) + contract(
            "xm,pmy->pxy", cos_x, mixed_imag
        )
        return running + wave_real * wave_real + wave_imag * wave_imag

    squares_sum = lax.fori_loop(0, band_count, add_band, jnp.zeros((planes, NX, NY), jnp.float32))
    weight = (
        2.0
        * kpoint_counts[kpt_index].astype(jnp.float32)
        / jnp.sum(kpoint_counts).astype(jnp.float32)
    )
    weight = weight / (ng_dev * pw_count)
    partial_value = weight * squares_sum
    total_density = lax.psum(partial_value, "kpt")
    density = lax.dynamic_slice_in_dim(total_density, kpt_index * x_block, x_block, 1)
    spec_real, spec_imag = forward_planes(total_density)
    rows_pw = NX // pw_count
    pencil_real, pencil_imag = (
        lax.all_to_all(spec_real, "pw", split_axis=1, concat_axis=0, tiled=True),
        lax.all_to_all(spec_imag, "pw", split_axis=1, concat_axis=0, tiled=True),
    )
    local_x = pw_index * rows_pw + jnp.arange(rows_pw, dtype=jnp.int32)
    freq_x = jnp.repeat(signed_freq(local_x, NX), NY)
    freq_y = jnp.tile(signed_freq(steps_y, NY), rows_pw)
    back_real, back_imag = poisson_columns(
        pencil_real.reshape(NZ, rows_pw * NY), pencil_imag.reshape(NZ, rows_pw * NY), freq_x, freq_y
    )
    plane_real, plane_imag = (
        lax.all_to_all(
            back_real.reshape(NZ, rows_pw, NY), "pw", split_axis=0, concat_axis=1, tiled=True
        ),
        lax.all_to_all(
            back_imag.reshape(NZ, rows_pw, NY), "pw", split_axis=0, concat_axis=1, tiled=True
        ),
    )
    own_rows = kpt_index * x_block + jnp.arange(x_block, dtype=jnp.int32)
    cos_rows, sin_rows = phase_tables(own_rows, steps_x, NX)
    rows_real = contract("xk,pky->pxy", cos_rows, plane_real) - contract(
        "xk,pky->pxy", sin_rows, plane_imag
    )
    rows_imag = contract("xk,pky->pxy", sin_rows, plane_real) + contract(
        "xk,pky->pxy", cos_rows, plane_imag
    )
    hartree = contract("pxk,yk->pxy", rows_real, cos_y) - contract("pxk,yk->pxy", rows_imag, sin_y)
    return (density, hartree)


LANES = 128
HALF = 64
VMEM_LIMIT = 56 * 1024 * 1024
NN = (((1,), (0,)), ((), ()))
NT = (((1,), (1,)), ((), ()))
TN = (((0,), (0,)), ((), ()))


def pieces(value):
    high = value.astype(jnp.bfloat16)
    low = (value - high.astype(jnp.float32)).astype(jnp.bfloat16)
    return high, low


def mul(former, latter, dims):
    return lax.dot_general(former, latter, dims, preferred_element_type=jnp.float32)


def mul3_left(former, latter, dims):
    high, low = pieces(latter)
    (unused,), (axis,) = dims[0]
    return mul(former, jnp.concatenate((high, high, low), axis=axis), dims)


def mul3_right(former, latter, dims):
    high, low = pieces(former)
    (axis,), (unused,) = dims[0]
    return mul(jnp.concatenate((high, high, low), axis=axis), latter, dims)


def stack_table(values, axis):
    high = values.astype(np.float32).astype(jnp.bfloat16)
    low = (values - high.astype(np.float64)).astype(np.float32).astype(jnp.bfloat16)
    return jnp.asarray(np.concatenate((high, low, high), axis=axis))


def angles(former, latter, length):
    return np.outer(former, latter) % length * (2.0 * np.pi / length)


def tables(kpts, pws, planes):
    count = kpts * pws
    low_freq = np.arange(HALF) - HALF // 2
    grid_x, grid_y, grid_z = np.arange(NX), np.arange(NY), np.arange(NZ)
    own_y = np.arange(HALF)

    device = np.arange(count)
    plane_of = (
        (device % pws)[:, None] * (NZ // pws)
        + (device // pws)[:, None] * planes
        + np.arange(planes)[None, :]
    )
    return_table = {}

    def pencil(z_width):
        angle = angles(plane_of.ravel(), np.arange(z_width) - z_width // 2, NZ)
        cos, sin = (
            part.reshape(count, 1, planes, z_width) for part in (np.cos(angle), np.sin(angle))
        )
        real = np.concatenate((cos, -sin), axis=3)
        imag = np.concatenate((sin, cos), axis=3)
        return np.concatenate((real, imag), axis=1).reshape(-1, 2 * z_width)

    return_table["pencil"] = pencil

    angle = angles(low_freq, grid_y, NY)
    cos, sin = np.cos(angle), np.sin(angle)
    return_table["wave_y"] = np.block([[cos, sin], [-sin, cos]])

    angle = angles(grid_x, low_freq, NX)
    cos, sin = np.cos(angle), np.sin(angle)
    return_table["wave_x"] = np.block([[cos, -sin], [sin, cos]])

    angle = angles(own_y, grid_y, NY)
    cos, sin = np.cos(angle), np.sin(angle)
    return_table["forth_y"] = np.stack((cos, -sin), axis=1).reshape(2 * HALF, NY)
    twice = np.where(own_y == 0, 1.0, 2.0)[:, None]
    return_table["back_y"] = np.stack((twice * cos, -twice * sin), axis=1).reshape(2 * HALF, NY)

    angle = angles(grid_z, plane_of.ravel(), NZ)
    return_table["forth_z"] = np.concatenate((np.cos(angle), np.sin(angle)), axis=0)
    own = NZ // pws
    merged = own // 8
    order = (
        np.arange(pws)[None, :, None] * own
        + np.arange(8)[None, None, :] * merged
        + np.arange(merged)[:, None, None]
    )
    angle = angles(order.ravel(), grid_z, NZ)
    return_table["back_z"] = np.concatenate((np.cos(angle), np.sin(angle)), axis=0)

    angle = angles(grid_x, grid_x, NX)
    return_table["both_x"] = np.concatenate((np.cos(angle), np.sin(angle)), axis=1)
    return return_table


def ramp(shape, axis, first=0):
    steps = lax.broadcasted_iota(jnp.int32, shape, axis) + first
    return steps.astype(jnp.float32).astype(jnp.bfloat16)


def sixteen(row):
    return jnp.broadcast_to(row, (16, row.shape[1])).astype(jnp.bfloat16)


def one_hot_lanes(row, ramps):
    column = jnp.transpose(jnp.concatenate([sixteen(row)] * (LANES // 16), axis=0))
    one = jnp.ones(column.shape, jnp.bfloat16)
    zero = jnp.zeros(column.shape, jnp.bfloat16)
    return jnp.concatenate(
        [
            jnp.where(column == ramps[:, first : first + LANES], one, zero)
            for first in range(0, ramps.shape[1], LANES)
        ],
        axis=1,
    )


RANK_LOW = 64
WINDOW = 64


def exchange_rows(refs, low_bits, size_bits, descending):
    for outer in range(RANK_LOW):
        if any(outer >> bit & 1 for bit in low_bits[0]):
            continue
        touched = sorted(
            outer + sum(1 << bit for i, bit in enumerate(low_bits[0]) if pattern >> i & 1)
            for pattern in range(1 << len(low_bits[0]))
        )
        held = {v: [ref[v * 8 : v * 8 + 8, :] for ref in refs] for v in touched}
        for size, bits in zip(size_bits, low_bits[1:]):
            for bit in bits:
                for v in touched:
                    if v >> bit & 1:
                        continue
                    former, latter = held[v], held[v | 1 << bit]
                    if size < 6:
                        down = bool(v >> size & 1)
                        swap = former[0] < latter[0] if down else former[0] > latter[0]
                    else:
                        swap = former[0] > latter[0]
                        if descending is not None:
                            swap = jnp.logical_xor(swap, descending)
                    held[v] = [jnp.where(swap, y, x) for x, y in zip(former, latter)]
                    held[v | 1 << bit] = [jnp.where(swap, x, y) for x, y in zip(former, latter)]
        for v in touched:
            for ref, value in zip(refs, held[v]):
                ref[v * 8 : v * 8 + 8, :] = value


def exchange_sublanes(refs, stride, descending):
    sublane = lax.broadcasted_iota(jnp.int32, (8, LANES), 0)
    upper = sublane // stride % 2 == 1
    want_least = upper if descending is not None else jnp.logical_not(upper)
    if descending is not None:
        want_least = jnp.logical_not(jnp.logical_xor(upper, descending))

    def partner(value):
        if stride == 4:
            return pltpu.roll(value, 4, 0)
        return jnp.where(upper, pltpu.roll(value, stride, 0), pltpu.roll(value, 8 - stride, 0))

    for v in range(RANK_LOW):
        here = [ref[v * 8 : v * 8 + 8, :] for ref in refs]
        there = [partner(value) for value in here]
        take = jnp.where(
            want_least, (here[0] > there[0]).astype(jnp.int32), (here[0] < there[0]).astype(jnp.int32)
        )
        take = take == 1
        for ref, x, y in zip(refs, here, there):
            ref[v * 8 : v * 8 + 8, :] = jnp.where(take, y, x)


def sort_columns(refs):
    sublane = lax.broadcasted_iota(jnp.int32, (8, LANES), 0)
    exchange_rows(refs, [(0, 1, 2), (0,), (1, 0), (2, 1, 0)], [1, 2, 3], None)
    exchange_rows(refs, [(3,), (3,)], [4], None)
    exchange_rows(refs, [(0, 1, 2), (2, 1, 0)], [4], None)
    exchange_rows(refs, [(3, 4), (4, 3)], [5], None)
    exchange_rows(refs, [(0, 1, 2), (2, 1, 0)], [5], None)
    for size in range(6, 10):
        descending = None if size == 9 else sublane // (1 << (size - 6)) % 2 == 1
        for bit in range(size - 1, 5, -1):
            exchange_sublanes(refs, 1 << (bit - 6), descending)
        exchange_rows(refs, [(3, 4, 5), (5, 4, 3)], [size], descending)
        exchange_rows(refs, [(0, 1, 2), (2, 1, 0)], [size], descending)


def pack_kernel(width, has_column, *refs):
    coeff_ref, miller_ref, slot_ref, pencil_ref = refs[:4]
    rest = list(refs[4:])
    column_ref = rest.pop(0) if has_column else None
    out_ref, total, key_ref, real_ref, imag_ref, lane_ref, real_low, imag_low, ramp_ref, step_ref = rest
    half = total.shape[0] // 4
    slots = 2 * half
    count = out_ref.shape[0]
    rows = pencil_ref.shape[0] // count
    length = miller_ref.shape[0]
    ranks = key_ref.shape[0]

    slot = slot_ref[...]
    second = slot >= half
    lane = miller_ref[...] + width // 2
    key = jnp.where(second, slot - half, slot) * (2 * width) + jnp.where(second, lane + width, lane)
    key_ref[0:length] = key.astype(jnp.float32)
    real_ref[0:length] = coeff_ref[0, pl.ds(0, length, stride=2), :]
    imag_ref[0:length] = coeff_ref[0, pl.ds(1, length, stride=2), :]
    blank = jnp.zeros((ranks - length, LANES), jnp.float32)
    key_ref[length:] = blank + 2.0 * slots * width
    real_ref[length:] = blank
    imag_ref[length:] = blank
    sort_columns((key_ref, real_ref, imag_ref))

    def base_of(block):
        base = 8 * (block // 2) + 8 * (block % 2) - WINDOW // 2
        return jnp.minimum(jnp.maximum(base, 0), half - WINDOW)

    ramp_ref[...] = ramp(ramp_ref.shape, 1)
    step_ref[...] = ramp(step_ref.shape, 0)
    sublane = lax.broadcasted_iota(jnp.int32, (8, LANES), 0)
    astray = jnp.zeros((8, LANES), jnp.float32)
    for v in range(RANK_LOW):
        at = slice(v * 8, v * 8 + 8)
        keys = key_ref[at, :]
        high = jnp.floor(keys * (1.0 / (2 * width)))
        lane_ref[at, :] = keys - high * (2.0 * width)
        key_ref[at, :] = high
        for ref, low_ref in ((real_ref, real_low), (imag_ref, imag_low)):
            value = ref[at, :]
            rounded = value.astype(jnp.bfloat16).astype(jnp.float32)
            ref[at, :] = rounded
            low_ref[at, :] = value - rounded
        offset = high - base_of(sublane * (RANK_LOW // 8) + v // 8).astype(jnp.float32)
        outside = jnp.logical_or(offset < 0.0, offset >= 1.0 * WINDOW)
        astray = jnp.where(outside, 1.0, astray)
    astray = jnp.max(jnp.where(sublane * RANK_LOW < length, astray, 0.0))

    def add(block, base, window):
        first = block % (RANK_LOW // 8) * 64 + block // (RANK_LOW // 8)
        base_row = jnp.full((1, LANES), base, jnp.int32).astype(jnp.float32)
        zero = jnp.zeros((16, LANES), jnp.bfloat16)
        spread, chosen = [], []
        for t in range(8):
            row = pl.ds(first + 8 * t, 1)
            high = sixteen(key_ref[row, :] - base_row)
            masks = [high == step_ref[r : r + 16, :] for r in range(0, window, 16)]
            spread.append(
                jnp.concatenate(
                    [
                        jnp.where(mask, value, zero)
                        for value in [
                            sixteen(ref[row, :]) for ref in (real_ref, imag_ref, real_low, imag_low)
                        ]
                        for mask in masks
                    ],
                    axis=0,
                )
            )
            chosen.append(one_hot_lanes(lane_ref[row, :], ramp_ref[...]))
        found = mul(jnp.concatenate(spread, axis=1), jnp.concatenate(chosen, axis=0), NN)
        for i in range(4):
            if window == half:
                into = pl.ds(i * half, half)
            else:
                into = pl.ds(pl.multiple_of(i * half + base, 8), window)
            total[into, :] += found[i * window : (i + 1) * window]

    total[...] = jnp.zeros_like(total)
    blocks = length // 8
    together = 4 if blocks % 4 == 0 else 1

    @pl.when(astray == 0.0)
    def _():
        def some_blocks(i, unused):
            for s in range(together):
                block = together * i + s
                add(block, base_of(block), WINDOW)
            return unused

        lax.fori_loop(0, blocks // together, some_blocks, 0)

    @pl.when(astray > 0.0)
    def _():
        def one_block(block, unused):
            add(block, 0, half)
            return unused

        lax.fori_loop(0, blocks, one_block, 0)

    both = []
    for at in range(2):
        parts = [
            total[(2 * at + c) * half : (2 * at + c + 1) * half].astype(jnp.bfloat16)
            for c in range(2)
        ]
        both.append(
            jnp.concatenate(
                [
                    jnp.concatenate([part[:, h * width : (h + 1) * width] for part in parts], axis=1)
                    for h in range(2)
                ],
                axis=0,
            )
        )
    pencils = mul(pencil_ref[...], jnp.concatenate((both[0], both[0], both[1]), axis=1), NT)
    tiles = slots // LANES
    for t in range(tiles):
        tile = pencils[:, t * LANES : (t + 1) * LANES].reshape(count, rows, LANES)
        out_ref[:, t * rows : (t + 1) * rows] = tile
    if has_column:
        column = [
            column_ref[t * LANES : (t + 1) * LANES].astype(jnp.float32).reshape(1, LANES)
            for t in range(tiles)
        ]
        blank = [jnp.zeros((8 - tiles, LANES), jnp.float32)]
        column = jnp.concatenate(column + blank, axis=0)
        out_ref[:, tiles * rows :] = jnp.broadcast_to(column[None], (count, 8, LANES))


def pack_band(band, count, coeffs, miller, slot, pencil, slots, column):
    length = miller.shape[0]
    width = pencil.shape[1] // 6
    rows = pencil.shape[0] // count * (slots // LANES)
    operands = [coeffs, miller, slot, pencil]
    if column is not None:
        operands.append(column)
        rows += 8
    one_band = pl.BlockSpec((1, 2 * length, LANES), lambda i: (band, 0, 0))
    return pl.pallas_call(
        functools.partial(pack_kernel, width, column is not None),
        grid=(1,),
        in_specs=[one_band]
        + [pl.BlockSpec(x.shape, lambda i, n=x.ndim: (0,) * n) for x in operands[1:]],
        out_specs=pl.BlockSpec((count, rows, LANES), lambda i: (0, 0, 0)),
        out_shape=jax.ShapeDtypeStruct((count, rows, LANES), jnp.float32),
        scratch_shapes=[pltpu.VMEM((2 * slots, 2 * width), jnp.float32)]
        + [pltpu.VMEM((8 * RANK_LOW, LANES), jnp.float32)] * 6
        + [
            pltpu.VMEM((LANES, 2 * width), jnp.bfloat16),
            pltpu.VMEM((slots // 2, LANES), jnp.bfloat16),
        ],
        compiler_params=pltpu.CompilerParams(vmem_limit_bytes=VMEM_LIMIT),
        cost_estimate=pl.CostEstimate(
            flops=2 * length * LANES * slots * 4 * width,
            bytes_accessed=16 * length * LANES,
            transcendentals=0,
        ),
        name="pack_band",
    )(*operands)


def wave_kernel(kpts, tiles, scale, is_first, is_last, *refs):
    own_ref, count_ref, came_ref, wave_y_ref, wave_x_ref = refs[:5]
    rest = list(refs[5:])
    forth_ref = rest.pop(0) if is_last else None
    former_ref, chosen_ref, high_ref = (None,) * 3 if is_first else [rest.pop(0) for _ in range(3)]
    density_refs = [rest.pop(0) for _ in range(kpts if is_last else 1)]
    if is_first:
        chosen_ref, high_ref = rest.pop(0), rest.pop(0)
    send_ref = rest.pop(0) if is_last else None
    values, grid, whole = rest
    planes = density_refs[0].shape[0]
    block = NX // kpts
    part_rows = 2 * planes
    pws = came_ref.shape[0] // kpts
    rows = kpts * part_rows
    total = values.shape[1]

    for j in range(pws):
        for t in range(tiles):
            taken = jnp.concatenate(
                [came_ref[k * pws + j, t * part_rows : (t + 1) * part_rows] for k in range(kpts)],
                axis=0,
            )
            high, low = pieces(taken)
            first = (j * tiles + t) * LANES
            values[0:rows, first : first + LANES] = high
            values[rows : 2 * rows, first : first + LANES] = low

    tile = 4 * HALF
    if is_first:
        ramps = ramp((LANES, tile), 1)
        for j in range(pws):
            for t in range(tiles):
                column = came_ref[j, tiles * part_rows + t : tiles * part_rows + t + 1]
                column = column.astype(jnp.int32)
                cell = ((column // NY + NX // 2) % NX - HALF // 2) * HALF
                cell = cell + (column % NY + NY // 2) % NY - HALF // 2
                first = (j * tiles + t) * LANES
                lane = (cell % tile).astype(jnp.float32)
                chosen_ref[first : first + LANES, :] = one_hot_lanes(lane, ramps)
                high_ref[:, first : first + LANES] = sixteen((cell // tile).astype(jnp.float32))
    left = lax.broadcasted_iota(jnp.int32, (kpts * planes, LANES), 1) < HALF
    together = 4

    def place(t, found):
        found = found[:rows] + found[rows:]
        for h in range(2):
            real, imag = (
                jnp.concatenate(
                    [
                        found[(2 * k + c) * planes : (2 * k + c + 1) * planes, h * LANES : (h + 1) * LANES]
                        for k in range(kpts)
                    ],
                    axis=0,
                )
                for c in range(2)
            )
            even = jnp.where(left, real, pltpu.roll(imag, HALF, 1))
            odd = jnp.where(left, pltpu.roll(real, HALF, 1), imag)
            grid[pl.ds(t * 4 + 2 * h, kpts * planes, stride=HALF), :] = even
            grid[pl.ds(t * 4 + 2 * h + 1, kpts * planes, stride=HALF), :] = odd

    def some_tiles(i, unused):
        high = high_ref[...]
        zero = jnp.zeros_like(high)
        kept = []
        for s in range(together):
            here = high == (together * i + s).astype(jnp.float32).astype(jnp.bfloat16)
            kept += [
                jnp.where(here, values[r : r + 16, :], zero) for r in range(0, 2 * rows, 16)
            ]
        found = mul(jnp.concatenate(kept, axis=0), chosen_ref[...], NN)
        for s in range(together):
            place(together * i + s, found[2 * rows * s : 2 * rows * (s + 1)])
        return unused

    lax.fori_loop(0, HALF // 4 // together, some_tiles, 0)

    sum_of = count_ref[0]
    for k in range(1, kpts):
        sum_of = sum_of + count_ref[k]

    def spread(number):
        return jnp.full((8, NY), number, jnp.int32).astype(jnp.float32)

    weights = [
        jnp.concatenate([spread(count_ref[k]) / spread(sum_of) * scale] * (NX // 8), axis=0)
        for k in range(kpts)
    ]
    first_row = lax.broadcasted_iota(jnp.int32, (2 * HALF, NX), 0) == 0

    def transform(p):
        lines = jnp.concatenate(
            [
                grid[(k * planes + p) * HALF : (k * planes + p + 1) * HALF, :]
                for k in range(kpts)
            ],
            axis=0,
        )
        mixed = mul3_right(lines, wave_y_ref[...], NN)
        mixed = jnp.concatenate(
            [
                jnp.concatenate(
                    [mixed[k * HALF : (k + 1) * HALF, c * NY : (c + 1) * NY] for k in range(kpts)],
                    axis=1,
                )
                for c in range(2)
            ],
            axis=0,
        )
        wave = mul3_left(wave_x_ref[...], mixed, NN)
        square = wave[:NX] * wave[:NX] + wave[NX:] * wave[NX:]
        density = weights[0] * square[:, :NY]
        for k in range(1, kpts):
            density = density + weights[k] * square[:, k * NY : (k + 1) * NY]
        if former_ref is not None:
            density = density + former_ref[p]
        if is_last:
            whole[...] = density
            for s, density_ref in enumerate(density_refs):
                first = pl.multiple_of(lax.rem(own_ref[0] + s, kpts) * block, block)
                density_ref[p] = whole[pl.ds(first, block), :]
        else:
            density_refs[0][p] = density
        if is_last:
            level = jnp.mean(density[:8], axis=(0, 1), keepdims=True)
            half = mul3_left(forth_ref[...], density - level, NT)
            half = half + jnp.where(first_row, level * NY, 0.0)
            send_ref[pl.ds(p, 2 * HALF, stride=planes), :] = half

    for p in range(planes):
        transform(p)


def wave_band(kpts, tiles, total, scale, own, counts, came, wave_y, wave_x, forth, former, chosen):
    planes = NZ // came.shape[0]
    block = NX // kpts
    is_first, is_last = former is None, forth is not None
    vmem = pl.BlockSpec(memory_space=pltpu.VMEM)
    operands = [own, counts, came, wave_y, wave_x]
    if is_last:
        operands.append(forth)
    if not is_first:
        operands += [former, *chosen]
    if is_last:
        out_shape = [jax.ShapeDtypeStruct((planes, block, NY), jnp.float32)] * kpts
    else:
        out_shape = [jax.ShapeDtypeStruct((planes, NX, NY), jnp.float32)]
    if is_first:
        out_shape.append(jax.ShapeDtypeStruct((total, 4 * HALF), jnp.bfloat16))
        out_shape.append(jax.ShapeDtypeStruct((16, total), jnp.bfloat16))
    if is_last:
        out_shape.append(jax.ShapeDtypeStruct((2 * HALF * planes, NX), jnp.float32))
    rows = kpts * 2 * planes
    return pl.pallas_call(
        functools.partial(wave_kernel, kpts, tiles, scale, is_first, is_last),
        in_specs=[pl.BlockSpec(memory_space=pltpu.SMEM)] * 2 + [vmem] * (len(operands) - 2),
        out_specs=[vmem] * len(out_shape),
        out_shape=out_shape,
        scratch_shapes=[
            pltpu.VMEM((2 * rows, total), jnp.bfloat16),
            pltpu.VMEM((kpts * planes * HALF, LANES), jnp.float32),
            pltpu.VMEM((NX, NY), jnp.float32),
        ],
        compiler_params=pltpu.CompilerParams(vmem_limit_bytes=VMEM_LIMIT),
        cost_estimate=pl.CostEstimate(
            flops=4 * rows * total * HALF * HALF, bytes_accessed=4 * came.size, transcendentals=0
        ),
        name="wave_band",
    )(*operands)


def poisson_kernel(pws, first_ref, came_ref, forth_ref, back_ref, both_x_ref, send_ref):
    count, parts, planes, unused = came_ref.shape
    pairs = parts // 2
    fields = [came_ref[:, i].reshape(NZ, NX) for i in range(parts)]
    level = jnp.mean(fields[0], axis=(0, 1), keepdims=True)
    fields[0] = fields[0] - jnp.where(first_ref[0] == 0, level, 0.0)
    field = jnp.concatenate(fields, axis=1)
    turned = mul3_left(forth_ref[...], field, NN)

    def part(array, half, i):
        return array[half * NZ : (half + 1) * NZ, i * NX : (i + 1) * NX]

    lines = []
    for q in range(pairs):
        lines.append(part(turned, 0, 2 * q) + part(turned, 1, 2 * q + 1))
        lines.append(part(turned, 0, 2 * q + 1) - part(turned, 1, 2 * q))
    spectrum = mul3_right(jnp.concatenate(lines, axis=0), both_x_ref[...], NN)

    step_z = lax.broadcasted_iota(jnp.int32, (NZ, NX), 0)
    step_x = lax.broadcasted_iota(jnp.int32, (NZ, NX), 1)
    lines = []
    for q in range(pairs):
        real = spectrum[2 * q * NZ : (2 * q + 1) * NZ]
        imag = spectrum[(2 * q + 1) * NZ : (2 * q + 2) * NZ]
        freq_y = jnp.full((NZ, NX), first_ref[0] + q, jnp.int32)
        kernel = coulomb(signed_freq(step_z, NZ), signed_freq(step_x, NX), freq_y)
        kernel = kernel * (1.0 / (NX * NY * NZ))
        lines.append((real[:, :NX] + imag[:, NX:]) * kernel)
        lines.append((imag[:, :NX] - real[:, NX:]) * kernel)
    turned = mul3_right(jnp.concatenate(lines, axis=0), both_x_ref[...], NN)
    lines = []
    for q in range(pairs):
        real = turned[2 * q * NZ : (2 * q + 1) * NZ]
        imag = turned[(2 * q + 1) * NZ : (2 * q + 2) * NZ]
        lines.append(real[:, :NX] - imag[:, NX:])
        lines.append(real[:, NX:] + imag[:, :NX])
    turned = mul3_left(back_ref[...], jnp.concatenate(lines, axis=1), NN)

    kpts = count // pws
    merged = NZ // pws // 8
    block = NX // kpts
    rows = pws * 8
    lane = lax.broadcasted_iota(jnp.int32, (rows, LANES), 1) // block
    for q in range(pairs):
        real = part(turned, 0, 2 * q) - part(turned, 1, 2 * q + 1)
        imag = part(turned, 0, 2 * q + 1) + part(turned, 1, 2 * q)
        for c, value in enumerate((real, imag)):
            for a in range(kpts):
                packed = None
                for m in range(merged):
                    piece = value[m * rows : (m + 1) * rows]
                    shift = (m - a) * block % LANES
                    if shift:
                        piece = pltpu.roll(piece, shift, 1)
                    packed = piece if m == 0 else jnp.where(lane == m, piece, packed)
                send_ref[a * pws : (a + 1) * pws, 2 * q + c] = packed.reshape(pws, 8, LANES)


def poisson(pws, first, came, forth, back, both_x):
    vmem = pl.BlockSpec(memory_space=pltpu.VMEM)
    count, parts, unused, unused = came.shape
    return pl.pallas_call(
        functools.partial(poisson_kernel, pws),
        in_specs=[pl.BlockSpec(memory_space=pltpu.SMEM)] + [vmem] * 4,
        out_specs=vmem,
        out_shape=jax.ShapeDtypeStruct((count, parts, 8, LANES), jnp.float32),
        compiler_params=pltpu.CompilerParams(vmem_limit_bytes=VMEM_LIMIT),
        name="poisson",
    )(first, came, forth, back, both_x)


def assemble_kernel(own_ref, *refs):
    block_refs, density_ref = refs[:-1], refs[-1]
    kpts = len(block_refs)
    part = density_ref.shape[0] // kpts
    for s, block_ref in enumerate(block_refs):
        sender = lax.rem(own_ref[0] + kpts - s, kpts)
        density_ref[pl.ds(sender * part, part)] = block_ref[...]


def assemble(own, blocks):
    vmem = pl.BlockSpec(memory_space=pltpu.VMEM)
    part, block, length = blocks[0].shape
    return pl.pallas_call(
        assemble_kernel,
        in_specs=[pl.BlockSpec(memory_space=pltpu.SMEM)] + [vmem] * len(blocks),
        out_specs=vmem,
        out_shape=jax.ShapeDtypeStruct((part * len(blocks), block, length), jnp.float32),
        name="assemble",
    )(own, *blocks)


def finish_kernel(came_ref, back_ref, out_ref):
    planes, block, unused = out_ref.shape
    merged = planes // 8
    for h in range(8):
        lines = came_ref[pl.ds(h, 2 * HALF, stride=8), :]
        field = mul3_right(lines, back_ref[...], TN)
        out_ref[h * merged : (h + 1) * merged] = field.reshape(merged, block, NY)


def finish(planes, block, came, back_y):
    vmem = pl.BlockSpec(memory_space=pltpu.VMEM)
    return pl.pallas_call(
        finish_kernel,
        in_specs=[vmem] * 2,
        out_specs=vmem,
        out_shape=jax.ShapeDtypeStruct((planes, block, NY), jnp.float32),
        compiler_params=pltpu.CompilerParams(vmem_limit_bytes=VMEM_LIMIT),
        name="finish",
    )(came, back_y)


def exchange(array, axes):
    return lax.all_to_all(array, axes, split_axis=0, concat_axis=0, tiled=True)


def local_planes(band_coeffs, miller_third, column_slot, column_map, kpoint_counts):
    pws = lax.axis_size("pw")
    kpts = lax.axis_size("kpt")
    count = pws * kpts
    everyone = ("kpt", "pw")
    slots = column_map.shape[0]
    band_count = band_coeffs.shape[1]
    z_width = column_slot.shape[1] // slots
    planes = NZ // count
    parts = 2 * HALF // count
    made = tables(kpts, pws, planes)
    pencil = stack_table(made["pencil"](z_width), 1)
    wave_x, forth_y, forth_z, back_z = (
        stack_table(made[name], 1) for name in ("wave_x", "forth_y", "forth_z", "back_z")
    )
    wave_y, back_y, both_x = (stack_table(made[name], 0) for name in ("wave_y", "back_y", "both_x"))

    tiles = slots // LANES
    length = column_slot.shape[1] // LANES
    coeffs = band_coeffs.reshape(band_count, 2, length, LANES).transpose(0, 2, 1, 3)
    coeffs = coeffs.reshape(band_count, 2 * length, LANES)
    miller = miller_third.reshape(length, LANES)
    slot = column_slot.reshape(length, LANES)
    scale = 2.0 / (column_slot.shape[1] * pws)
    arrived = []
    for band in range(band_count):
        column = column_map if band == 0 else None
        packed = pack_band(
            band, count, coeffs, miller, slot, pencil, slots, column
        )
        arrived.append(exchange(packed, everyone))
    own = lax.axis_index("kpt").astype(jnp.int32).reshape(1)
    former = chosen = None
    for band in range(band_count):
        forth = forth_y if band == band_count - 1 else None
        made_here = wave_band(
            kpts,
            tiles,
            pws * slots,
            scale,
            own,
            kpoint_counts,
            arrived[band],
            wave_y,
            wave_x,
            forth,
            former,
            chosen,
        )
        former = made_here[0]
        chosen = made_here[-2:] if band == 0 else chosen
    half = exchange(made_here[-1].reshape(count, parts, planes, NX), everyone)
    blocks = [made_here[0]] + [
        lax.ppermute(made_here[s], "kpt", [(a, (a + s) % kpts) for a in range(kpts)])
        for s in range(1, kpts)
    ]
    device = lax.axis_index("kpt") * pws + lax.axis_index("pw")
    first = (device * (parts // 2)).astype(jnp.int32).reshape(1)
    back = poisson(pws, first, half, forth_z, back_z, both_x)
    back = exchange(back, everyone).reshape(count * parts * 8, LANES)
    return assemble(own, blocks), finish(NZ // pws, NX // kpts, back, back_y)


def fits_planes(kpts, pws):
    count = kpts * pws
    own = NZ // pws
    return (
        NZ % count == 0
        and NZ // count == 8
        and 2 * HALF % (2 * count) == 0
        and NX % kpts == 0
        and own % 8 == 0
        and own // 8 * (NX // kpts) == LANES
    )


def local(band_coeffs, miller_third, column_slot, column_map, kpoint_counts):
    slots = column_map.shape[0]
    plain = slots % LANES == 0 and LANES <= slots <= 8 * RANK_LOW
    plain = plain and column_slot.shape[1] == slots * LANES
    fits = plain and fits_planes(lax.axis_size("kpt"), lax.axis_size("pw"))
    chosen = local_planes if fits else local_general
    return chosen(band_coeffs, miller_third, column_slot, column_map, kpoint_counts)


def solution(mesh):
    return jax.shard_map(
        local,
        mesh=mesh,
        in_specs=(P("kpt", None, None, "pw"), P("kpt", "pw"), P("kpt", "pw"), P("pw"), P()),
        out_specs=(P("pw", "kpt", None), P("pw", "kpt", None)),
        check_vma=False,
    )
```

```python
import functools
import math

import jax
import jax.numpy as jnp
import numpy as np
from jax import lax
from jax.experimental import pallas as pl
from jax.experimental.pallas import tpu as pltpu
from jax.sharding import PartitionSpec as P

NX = 128
NY = 128
NZ = 256


SPACING = 0.25


def contract(pattern, former, latter):
    return jnp.einsum(
        pattern, former, latter, precision=lax.Precision.HIGHEST, preferred_element_type=jnp.float32
    )


def phase_tables(first_index, second_index, length):
    product = first_index[:, None] * second_index[None, :] % length
    angle = product.astype(jnp.float32) * (2.0 * math.pi / length)
    return (jnp.cos(angle), jnp.sin(angle))


def signed_freq(values, length):
    return jnp.where(values >= length // 2, values - length, values)


def coulomb(freq_z, freq_x, freq_y):
    wave_z = freq_z.astype(jnp.float32) / (NZ * SPACING)
    wave_x = freq_x.astype(jnp.float32) / (NX * SPACING)
    wave_y = freq_y.astype(jnp.float32) / (NY * SPACING)
    squared = (2.0 * math.pi) ** 2 * (wave_z * wave_z + wave_x * wave_x + wave_y * wave_y)
    anchor = (freq_z == 0) & (freq_x == 0) & (freq_y == 0)
    return jnp.where(anchor, 0.0, 4.0 * math.pi / jnp.where(anchor, 1.0, squared))


def poisson_columns(real_part, imag_part, freq_x, freq_y):
    length = real_part.shape[0]
    steps_z = jnp.arange(length, dtype=jnp.int32)
    cos_z, sin_z = phase_tables(steps_z, steps_z, length)
    spec_real = contract("zk,km->zm", cos_z, real_part) + contract("zk,km->zm", sin_z, imag_part)
    spec_imag = contract("zk,km->zm", cos_z, imag_part) - contract("zk,km->zm", sin_z, real_part)
    kernel = coulomb(signed_freq(steps_z, length)[:, None], freq_x[None, :], freq_y[None, :]) / (
        NX * NY * NZ
    )
    spec_real = spec_real * kernel
    spec_imag = spec_imag * kernel
    back_real = contract("zk,km->zm", cos_z, spec_real) - contract("zk,km->zm", sin_z, spec_imag)
    back_imag = contract("zk,km->zm", sin_z, spec_real) + contract("zk,km->zm", cos_z, spec_imag)
    return (back_real, back_imag)


def forward_planes(field):
    steps_x = jnp.arange(NX, dtype=jnp.int32)
    steps_y = jnp.arange(NY, dtype=jnp.int32)
    cos_y, sin_y = phase_tables(steps_y, steps_y, NY)
    cos_x, sin_x = phase_tables(steps_x, steps_x, NX)
    half_real = contract("pxy,ky->pxk", field, cos_y)
    half_imag = -contract("pxy,ky->pxk", field, sin_y)
    spec_real = contract("kx,pxy->pky", cos_x, half_real) + contract(
        "kx,pxy->pky", sin_x, half_imag
    )
    spec_imag = contract("kx,pxy->pky", cos_x, half_imag) - contract(
        "kx,pxy->pky", sin_x, half_real
    )
    return (spec_real, spec_imag)


def local_general(band_coeffs, miller_third, column_slot, column_map, kpoint_counts):
    pw_count = lax.axis_size("pw")
    kpt_count = lax.axis_size("kpt")
    pw_index = lax.axis_index("pw")
    kpt_index = lax.axis_index("kpt")
    col_dev = column_map.shape[0]
    ng_dev = column_slot.shape[1]
    band_count = band_coeffs.shape[1]
    z_width = ng_dev // col_dev
    planes = NZ // pw_count
    x_block = NX // kpt_count
    col_total = pw_count * col_dev
    steps_y = jnp.arange(NY, dtype=jnp.int32)
    steps_x = jnp.arange(NX, dtype=jnp.int32)
    cos_y, sin_y = phase_tables(steps_y, steps_y, NY)
    cos_x, sin_x = phase_tables(steps_x, steps_x, NX)
    all_columns = lax.all_gather(column_map, "pw", axis=0, tiled=True)
    position = (miller_third[0] + z_width // 2) * col_dev + column_slot[0]
    source_of = (
        jnp.zeros((ng_dev,), jnp.int32).at[position].set(jnp.arange(ng_dev, dtype=jnp.int32))
    )
    coeff_rows = band_coeffs[0].reshape(band_count * 2, ng_dev).T
    packed = jnp.take(coeff_rows, source_of, axis=0)
    packed = (
        packed.reshape(z_width, col_dev, band_count, 2)
        .transpose(0, 2, 3, 1)
        .reshape(z_width, band_count * 2 * col_dev)
    )
    cos_z, sin_z = phase_tables(
        jnp.arange(NZ, dtype=jnp.int32), jnp.arange(z_width, dtype=jnp.int32) - z_width // 2, NZ
    )
    by_cos = contract("zj,jc->zc", cos_z, packed).reshape(NZ, band_count, 2, col_dev)
    by_sin = contract("zj,jc->zc", sin_z, packed).reshape(NZ, band_count, 2, col_dev)
    pencil = jnp.stack(
        (by_cos[:, :, 0] - by_sin[:, :, 1], by_sin[:, :, 0] + by_cos[:, :, 1]), axis=2
    )
    pencil = pencil.reshape(NZ, band_count * 2 * col_dev)
    arrived = lax.all_to_all(pencil, "pw", split_axis=0, concat_axis=1, tiled=True)
    arrived = arrived.reshape(planes, pw_count, band_count, 2, col_dev).transpose(2, 1, 4, 3, 0)
    arrived = arrived.reshape(band_count, col_total, 2 * planes)
    arrived = jnp.concatenate(
        (arrived, jnp.zeros((band_count, 1, 2 * planes), jnp.float32)), axis=1
    )
    cell_source = (
        jnp.full((NX * NY,), col_total, jnp.int32)
        .at[all_columns]
        .set(jnp.arange(col_total, dtype=jnp.int32))
    )

    def add_band(band, running):
        one_band = lax.dynamic_index_in_dim(arrived, band, 0, keepdims=False)
        placed = jnp.take(one_band, cell_source, axis=0)
        placed = placed.reshape(NX, NY, 2, planes).transpose(2, 3, 0, 1)
        grid_real = placed[0]
        grid_imag = placed[1]
        mixed_real = contract("pxm,ym->pxy", grid_real, cos_y) - contract(
            "pxm,ym->pxy", grid_imag, sin_y
        )
        mixed_imag = contract("pxm,ym->pxy", grid_real, sin_y) + contract(
            "pxm,ym->pxy", grid_imag, cos_y
        )
        wave_real = contract("xm,pmy->pxy", cos_x, mixed_real) - contract(
            "xm,pmy->pxy", sin_x, mixed_imag
        )
        wave_imag = contract("xm,pmy->pxy", sin_x, mixed_real) + contract(
            "xm,pmy->pxy", cos_x, mixed_imag
        )
        return running + wave_real * wave_real + wave_imag * wave_imag

    squares_sum = lax.fori_loop(0, band_count, add_band, jnp.zeros((planes, NX, NY), jnp.float32))
    weight = (
        2.0
        * kpoint_counts[kpt_index].astype(jnp.float32)
        / jnp.sum(kpoint_counts).astype(jnp.float32)
    )
    weight = weight / (ng_dev * pw_count)
    partial_value = weight * squares_sum
    total_density = lax.psum(partial_value, "kpt")
    density = lax.dynamic_slice_in_dim(total_density, kpt_index * x_block, x_block, 1)
    spec_real, spec_imag = forward_planes(total_density)
    rows_pw = NX // pw_count
    pencil_real, pencil_imag = (
        lax.all_to_all(spec_real, "pw", split_axis=1, concat_axis=0, tiled=True),
        lax.all_to_all(spec_imag, "pw", split_axis=1, concat_axis=0, tiled=True),
    )
    local_x = pw_index * rows_pw + jnp.arange(rows_pw, dtype=jnp.int32)
    freq_x = jnp.repeat(signed_freq(local_x, NX), NY)
    freq_y = jnp.tile(signed_freq(steps_y, NY), rows_pw)
    back_real, back_imag = poisson_columns(
        pencil_real.reshape(NZ, rows_pw * NY), pencil_imag.reshape(NZ, rows_pw * NY), freq_x, freq_y
    )
    plane_real, plane_imag = (
        lax.all_to_all(
            back_real.reshape(NZ, rows_pw, NY), "pw", split_axis=0, concat_axis=1, tiled=True
        ),
        lax.all_to_all(
            back_imag.reshape(NZ, rows_pw, NY), "pw", split_axis=0, concat_axis=1, tiled=True
        ),
    )
    own_rows = kpt_index * x_block + jnp.arange(x_block, dtype=jnp.int32)
    cos_rows, sin_rows = phase_tables(own_rows, steps_x, NX)
    rows_real = contract("xk,pky->pxy", cos_rows, plane_real) - contract(
        "xk,pky->pxy", sin_rows, plane_imag
    )
    rows_imag = contract("xk,pky->pxy", sin_rows, plane_real) + contract(
        "xk,pky->pxy", cos_rows, plane_imag
    )
    hartree = contract("pxk,yk->pxy", rows_real, cos_y) - contract("pxk,yk->pxy", rows_imag, sin_y)
    return (density, hartree)


LANES = 128
HALF = 64
VMEM_LIMIT = 56 * 1024 * 1024
NN = (((1,), (0,)), ((), ()))
NT = (((1,), (1,)), ((), ()))
TN = (((0,), (0,)), ((), ()))


def pieces(value):
    high = value.astype(jnp.bfloat16)
    low = (value - high.astype(jnp.float32)).astype(jnp.bfloat16)
    return high, low


def mul(former, latter, dims):
    return lax.dot_general(former, latter, dims, preferred_element_type=jnp.float32)


def mul3_left(former, latter, dims):
    high, low = pieces(latter)
    (unused,), (axis,) = dims[0]
    return mul(former, jnp.concatenate((high, high, low), axis=axis), dims)


def mul3_right(former, latter, dims):
    high, low = pieces(former)
    (axis,), (unused,) = dims[0]
    return mul(jnp.concatenate((high, high, low), axis=axis), latter, dims)


def stack_table(values, axis):
    high = values.astype(np.float32).astype(jnp.bfloat16)
    low = (values - high.astype(np.float64)).astype(np.float32).astype(jnp.bfloat16)
    return jnp.asarray(np.concatenate((high, low, high), axis=axis))


def angles(former, latter, length):
    return np.outer(former, latter) % length * (2.0 * np.pi / length)


def tables(kpts, pws, planes):
    count = kpts * pws
    low_freq = np.arange(HALF) - HALF // 2
    grid_x, grid_y, grid_z = np.arange(NX), np.arange(NY), np.arange(NZ)
    own_y = np.arange(HALF)

    device = np.arange(count)
    plane_of = (
        (device % pws)[:, None] * (NZ // pws)
        + (device // pws)[:, None] * planes
        + np.arange(planes)[None, :]
    )
    return_table = {}

    def pencil(z_width):
        angle = angles(plane_of.ravel(), np.arange(z_width) - z_width // 2, NZ)
        cos, sin = (
            part.reshape(count, 1, planes, z_width) for part in (np.cos(angle), np.sin(angle))
        )
        real = np.concatenate((cos, -sin), axis=3)
        imag = np.concatenate((sin, cos), axis=3)
        return np.concatenate((real, imag), axis=1).reshape(-1, 2 * z_width)

    return_table["pencil"] = pencil

    angle = angles(low_freq, grid_y, NY)
    cos, sin = np.cos(angle), np.sin(angle)
    return_table["wave_y"] = np.block([[cos, sin], [-sin, cos]])

    angle = angles(grid_x, low_freq, NX)
    cos, sin = np.cos(angle), np.sin(angle)
    return_table["wave_x"] = np.block([[cos, -sin], [sin, cos]])

    angle = angles(own_y, grid_y, NY)
    cos, sin = np.cos(angle), np.sin(angle)
    return_table["forth_y"] = np.stack((cos, -sin), axis=1).reshape(2 * HALF, NY)
    twice = np.where(own_y == 0, 1.0, 2.0)[:, None]
    return_table["back_y"] = np.stack((twice * cos, -twice * sin), axis=1).reshape(2 * HALF, NY)

    angle = angles(grid_z, plane_of.ravel(), NZ)
    return_table["forth_z"] = np.concatenate((np.cos(angle), np.sin(angle)), axis=0)
    own = NZ // pws
    merged = own // 8
    order = (
        np.arange(pws)[None, :, None] * own
        + np.arange(8)[None, None, :] * merged
        + np.arange(merged)[:, None, None]
    )
    angle = angles(order.ravel(), grid_z, NZ)
    return_table["back_z"] = np.concatenate((np.cos(angle), np.sin(angle)), axis=0)

    angle = angles(grid_x, grid_x, NX)
    return_table["both_x"] = np.concatenate((np.cos(angle), np.sin(angle)), axis=1)
    return return_table


def ramp(shape, axis, first=0):
    steps = lax.broadcasted_iota(jnp.int32, shape, axis) + first
    return steps.astype(jnp.float32).astype(jnp.bfloat16)


def sixteen(row):
    return jnp.broadcast_to(row, (16, row.shape[1])).astype(jnp.bfloat16)


def one_hot_lanes(row, ramps):
    column = jnp.transpose(jnp.concatenate([sixteen(row)] * (LANES // 16), axis=0))
    one = jnp.ones(column.shape, jnp.bfloat16)
    zero = jnp.zeros(column.shape, jnp.bfloat16)
    return jnp.concatenate(
        [
            jnp.where(column == ramps[:, first : first + LANES], one, zero)
            for first in range(0, ramps.shape[1], LANES)
        ],
        axis=1,
    )


RANK_LOW = 64
WINDOW = 64


def exchange_rows(refs, low_bits, size_bits, descending):
    for outer in range(RANK_LOW):
        if any(outer >> bit & 1 for bit in low_bits[0]):
            continue
        touched = sorted(
            outer + sum(1 << bit for i, bit in enumerate(low_bits[0]) if pattern >> i & 1)
            for pattern in range(1 << len(low_bits[0]))
        )
        held = {v: [ref[v * 8 : v * 8 + 8, :] for ref in refs] for v in touched}
        for size, bits in zip(size_bits, low_bits[1:]):
            for bit in bits:
                for v in touched:
                    if v >> bit & 1:
                        continue
                    former, latter = held[v], held[v | 1 << bit]
                    if size < 6:
                        down = bool(v >> size & 1)
                        swap = former[0] < latter[0] if down else former[0] > latter[0]
                    else:
                        swap = former[0] > latter[0]
                        if descending is not None:
                            swap = jnp.logical_xor(swap, descending)
                    held[v] = [jnp.where(swap, y, x) for x, y in zip(former, latter)]
                    held[v | 1 << bit] = [jnp.where(swap, x, y) for x, y in zip(former, latter)]
        for v in touched:
            for ref, value in zip(refs, held[v]):
                ref[v * 8 : v * 8 + 8, :] = value


def exchange_sublanes(refs, stride, descending):
    sublane = lax.broadcasted_iota(jnp.int32, (8, LANES), 0)
    upper = sublane // stride % 2 == 1
    want_least = upper if descending is not None else jnp.logical_not(upper)
    if descending is not None:
        want_least = jnp.logical_not(jnp.logical_xor(upper, descending))

    def partner(value):
        if stride == 4:
            return pltpu.roll(value, 4, 0)
        return jnp.where(upper, pltpu.roll(value, stride, 0), pltpu.roll(value, 8 - stride, 0))

    for v in range(RANK_LOW):
        here = [ref[v * 8 : v * 8 + 8, :] for ref in refs]
        there = [partner(value) for value in here]
        take = jnp.where(
            want_least, (here[0] > there[0]).astype(jnp.int32), (here[0] < there[0]).astype(jnp.int32)
        )
        take = take == 1
        for ref, x, y in zip(refs, here, there):
            ref[v * 8 : v * 8 + 8, :] = jnp.where(take, y, x)


def sort_columns(refs):
    sublane = lax.broadcasted_iota(jnp.int32, (8, LANES), 0)
    exchange_rows(refs, [(0, 1, 2), (0,), (1, 0), (2, 1, 0)], [1, 2, 3], None)
    exchange_rows(refs, [(3,), (3,)], [4], None)
    exchange_rows(refs, [(0, 1, 2), (2, 1, 0)], [4], None)
    exchange_rows(refs, [(3, 4), (4, 3)], [5], None)
    exchange_rows(refs, [(0, 1, 2), (2, 1, 0)], [5], None)
    for size in range(6, 10):
        descending = None if size == 9 else sublane // (1 << (size - 6)) % 2 == 1
        for bit in range(size - 1, 5, -1):
            exchange_sublanes(refs, 1 << (bit - 6), descending)
        exchange_rows(refs, [(3, 4, 5), (5, 4, 3)], [size], descending)
        exchange_rows(refs, [(0, 1, 2), (2, 1, 0)], [size], descending)


def pack_kernel(width, has_column, *refs):
    coeff_ref, miller_ref, slot_ref, pencil_ref = refs[:4]
    rest = list(refs[4:])
    column_ref = rest.pop(0) if has_column else None
    out_ref, total, key_ref, real_ref, imag_ref, lane_ref, real_low, imag_low, ramp_ref, step_ref = rest
    half = total.shape[0] // 4
    slots = 2 * half
    count = out_ref.shape[0]
    rows = pencil_ref.shape[0] // count
    length = miller_ref.shape[0]
    ranks = key_ref.shape[0]

    slot = slot_ref[...]
    second = slot >= half
    lane = miller_ref[...] + width // 2
    key = jnp.where(second, slot - half, slot) * (2 * width) + jnp.where(second, lane + width, lane)
    key_ref[0:length] = key.astype(jnp.float32)
    real_ref[0:length] = coeff_ref[0, pl.ds(0, length, stride=2), :]
    imag_ref[0:length] = coeff_ref[0, pl.ds(1, length, stride=2), :]
    blank = jnp.zeros((ranks - length, LANES), jnp.float32)
    key_ref[length:] = blank + 2.0 * slots * width
    real_ref[length:] = blank
    imag_ref[length:] = blank
    sort_columns((key_ref, real_ref, imag_ref))

    def base_of(block):
        base = 8 * (block // 2) + 8 * (block % 2) - WINDOW // 2
        return jnp.minimum(jnp.maximum(base, 0), half - WINDOW)

    ramp_ref[...] = ramp(ramp_ref.shape, 1)
    step_ref[...] = ramp(step_ref.shape, 0)
    sublane = lax.broadcasted_iota(jnp.int32, (8, LANES), 0)
    astray = jnp.zeros((8, LANES), jnp.float32)
    for v in range(RANK_LOW):
        at = slice(v * 8, v * 8 + 8)
        keys = key_ref[at, :]
        high = jnp.floor(keys * (1.0 / (2 * width)))
        lane_ref[at, :] = keys - high * (2.0 * width)
        key_ref[at, :] = high
        for ref, low_ref in ((real_ref, real_low), (imag_ref, imag_low)):
            value = ref[at, :]
            rounded = value.astype(jnp.bfloat16).astype(jnp.float32)
            ref[at, :] = rounded
            low_ref[at, :] = value - rounded
        offset = high - base_of(sublane * (RANK_LOW // 8) + v // 8).astype(jnp.float32)
        outside = jnp.logical_or(offset < 0.0, offset >= 1.0 * WINDOW)
        astray = jnp.where(outside, 1.0, astray)
    astray = jnp.max(jnp.where(sublane * RANK_LOW < length, astray, 0.0))

    def add(block, base, window):
        first = block % (RANK_LOW // 8) * 64 + block // (RANK_LOW // 8)
        base_row = jnp.full((1, LANES), base, jnp.int32).astype(jnp.float32)
        zero = jnp.zeros((16, LANES), jnp.bfloat16)
        spread, chosen = [], []
        for t in range(8):
            row = pl.ds(first + 8 * t, 1)
            high = sixteen(key_ref[row, :] - base_row)
            masks = [high == step_ref[r : r + 16, :] for r in range(0, window, 16)]
            spread.append(
                jnp.concatenate(
                    [
                        jnp.where(mask, value, zero)
                        for value in [
                            sixteen(ref[row, :]) for ref in (real_ref, imag_ref, real_low, imag_low)
                        ]
                        for mask in masks
                    ],
                    axis=0,
                )
            )
            chosen.append(one_hot_lanes(lane_ref[row, :], ramp_ref[...]))
        found = mul(jnp.concatenate(spread, axis=1), jnp.concatenate(chosen, axis=0), NN)
        for i in range(4):
            if window == half:
                into = pl.ds(i * half, half)
            else:
                into = pl.ds(pl.multiple_of(i * half + base, 8), window)
            total[into, :] += found[i * window : (i + 1) * window]

    total[...] = jnp.zeros_like(total)
    blocks = length // 8
    together = 4 if blocks % 4 == 0 else 1

    @pl.when(astray == 0.0)
    def _():
        def some_blocks(i, unused):
            for s in range(together):
                block = together * i + s
                add(block, base_of(block), WINDOW)
            return unused

        lax.fori_loop(0, blocks // together, some_blocks, 0)

    @pl.when(astray > 0.0)
    def _():
        def one_block(block, unused):
            add(block, 0, half)
            return unused

        lax.fori_loop(0, blocks, one_block, 0)

    both = []
    for at in range(2):
        parts = [
            total[(2 * at + c) * half : (2 * at + c + 1) * half].astype(jnp.bfloat16)
            for c in range(2)
        ]
        both.append(
            jnp.concatenate(
                [
                    jnp.concatenate([part[:, h * width : (h + 1) * width] for part in parts], axis=1)
                    for h in range(2)
                ],
                axis=0,
            )
        )
    pencils = mul(pencil_ref[...], jnp.concatenate((both[0], both[0], both[1]), axis=1), NT)
    tiles = slots // LANES
    for t in range(tiles):
        tile = pencils[:, t * LANES : (t + 1) * LANES].reshape(count, rows, LANES)
        if not has_column:
            out_ref[:, t * rows : (t + 1) * rows] = tile
            continue
        for g in range(rows // 4):
            out_ref[:, t * (rows // 4) + g] = tile[:, 4 * g : 4 * g + 4]
    if has_column:
        column = [
            column_ref[t * LANES : (t + 1) * LANES].astype(jnp.float32).reshape(1, LANES)
            for t in range(tiles)
        ]
        column = jnp.concatenate(column + [jnp.zeros((4 - tiles, LANES), jnp.float32)], axis=0)
        out_ref[:, tiles * rows // 4] = jnp.broadcast_to(column[None], (count, 4, LANES))


def pack_band(band, count, coeffs, miller, slot, pencil, slots, column):
    length = miller.shape[0]
    width = pencil.shape[1] // 6
    rows = pencil.shape[0] // count * (slots // LANES)
    operands = [coeffs, miller, slot, pencil]
    out_shape = (count, rows, LANES)
    if column is not None:
        operands.append(column)
        out_shape = (count, rows // 4 + 1, 4, LANES)
    one_band = pl.BlockSpec((1, 2 * length, LANES), lambda i: (band, 0, 0))
    return pl.pallas_call(
        functools.partial(pack_kernel, width, column is not None),
        grid=(1,),
        in_specs=[one_band]
        + [pl.BlockSpec(x.shape, lambda i, n=x.ndim: (0,) * n) for x in operands[1:]],
        out_specs=pl.BlockSpec(out_shape, lambda i: (0,) * len(out_shape)),
        out_shape=jax.ShapeDtypeStruct(out_shape, jnp.float32),
        scratch_shapes=[pltpu.VMEM((2 * slots, 2 * width), jnp.float32)]
        + [pltpu.VMEM((8 * RANK_LOW, LANES), jnp.float32)] * 6
        + [
            pltpu.VMEM((LANES, 2 * width), jnp.bfloat16),
            pltpu.VMEM((slots // 2, LANES), jnp.bfloat16),
        ],
        compiler_params=pltpu.CompilerParams(vmem_limit_bytes=VMEM_LIMIT),
        cost_estimate=pl.CostEstimate(
            flops=2 * length * LANES * slots * 4 * width,
            bytes_accessed=16 * length * LANES,
            transcendentals=0,
        ),
        name="pack_band",
    )(*operands)


def wave_kernel(kpts, tiles, scale, is_first, is_last, *refs):
    own_ref, count_ref, came_ref, wave_y_ref, wave_x_ref = refs[:5]
    rest = list(refs[5:])
    forth_ref = rest.pop(0) if is_last else None
    former_ref, chosen_ref, high_ref = (None,) * 3 if is_first else [rest.pop(0) for _ in range(3)]
    density_refs = [rest.pop(0) for _ in range(kpts if is_last else 1)]
    if is_first:
        coulomb_ref, chosen_ref, high_ref = rest.pop(0), rest.pop(0), rest.pop(0)
    send_ref = rest.pop(0) if is_last else None
    values, grid, whole = rest
    planes = density_refs[0].shape[0]
    block = NX // kpts
    part_rows = 2 * planes
    pws = came_ref.shape[0] // kpts
    rows = kpts * part_rows
    total = values.shape[1]

    for j in range(pws):
        for t in range(tiles):
            if is_first:
                groups = [
                    came_ref[k * pws + j, t * (part_rows // 4) + g]
                    for k in range(kpts)
                    for g in range(part_rows // 4)
                ]
            else:
                groups = [
                    came_ref[k * pws + j, t * part_rows : (t + 1) * part_rows] for k in range(kpts)
                ]
            taken = jnp.concatenate(groups, axis=0)
            high, low = pieces(taken)
            first = (j * tiles + t) * LANES
            values[0:rows, first : first + LANES] = high
            values[rows : 2 * rows, first : first + LANES] = low

    tile = 4 * HALF
    if is_first:
        ramps = ramp((LANES, tile), 1)
        for j in range(pws):
            for t in range(tiles):
                column = came_ref[j, tiles * part_rows // 4, t : t + 1]
                column = column.astype(jnp.int32)
                cell = ((column // NY + NX // 2) % NX - HALF // 2) * HALF
                cell = cell + (column % NY + NY // 2) % NY - HALF // 2
                first = (j * tiles + t) * LANES
                lane = (cell % tile).astype(jnp.float32)
                chosen_ref[first : first + LANES, :] = one_hot_lanes(lane, ramps)
                high_ref[:, first : first + LANES] = sixteen((cell // tile).astype(jnp.float32))
        step_z = lax.broadcasted_iota(jnp.int32, (NZ, NX), 0)
        step_x = lax.broadcasted_iota(jnp.int32, (NZ, NX), 1)
        for q in range(coulomb_ref.shape[0]):
            freq_y = jnp.full((NZ, NX), own_ref[1] + q, jnp.int32)
            kernel = coulomb(signed_freq(step_z, NZ), signed_freq(step_x, NX), freq_y)
            coulomb_ref[q] = kernel * (1.0 / (NX * NY * NZ))
    left = lax.broadcasted_iota(jnp.int32, (planes, LANES), 1) < HALF
    together = 4

    def place(t, found):
        found = found[:rows] + found[rows:]
        for h in range(2):
            for k in range(kpts):
                real, imag = (
                    found[(2 * k + c) * planes : (2 * k + c + 1) * planes, h * LANES : (h + 1) * LANES]
                    for c in range(2)
                )
                first = (k * HALF + 4 * t + 2 * h) * planes
                grid[first : first + planes, :] = jnp.where(left, real, pltpu.roll(imag, HALF, 1))
                grid[first + planes : first + 2 * planes, :] = jnp.where(
                    left, pltpu.roll(real, HALF, 1), imag
                )

    high = high_ref[...]
    zero = jnp.zeros_like(high)
    for start in range(0, HALF // 4, together):
        kept = []
        for t in range(start, start + together):
            here = high == jnp.full_like(high, t)
            kept += [jnp.where(here, values[r : r + 16, :], zero) for r in range(0, 2 * rows, 16)]
        found = mul(jnp.concatenate(kept, axis=0), chosen_ref[...], NN)
        for s in range(together):
            place(start + s, found[2 * rows * s : 2 * rows * (s + 1)])

    sum_of = count_ref[0]
    for k in range(1, kpts):
        sum_of = sum_of + count_ref[k]

    def spread(number):
        return jnp.full((8, NY), number, jnp.int32).astype(jnp.float32)

    weights = [
        jnp.concatenate([spread(count_ref[k]) / spread(sum_of) * scale] * (NX // 8), axis=0)
        for k in range(kpts)
    ]
    first_row = lax.broadcasted_iota(jnp.int32, (2 * HALF, NX), 0) == 0

    def transform(p):
        lines = grid[pl.ds(p, kpts * HALF, stride=planes), :]
        mixed = mul3_right(lines, wave_y_ref[...], NN)
        mixed = jnp.concatenate(
            [
                jnp.concatenate(
                    [mixed[k * HALF : (k + 1) * HALF, c * NY : (c + 1) * NY] for k in range(kpts)],
                    axis=1,
                )
                for c in range(2)
            ],
            axis=0,
        )
        wave = mul3_left(wave_x_ref[...], mixed, NN)
        square = wave[:NX] * wave[:NX] + wave[NX:] * wave[NX:]
        density = weights[0] * square[:, :NY]
        for k in range(1, kpts):
            density = density + weights[k] * square[:, k * NY : (k + 1) * NY]
        if former_ref is not None:
            density = density + former_ref[p]
        if is_last:
            whole[p] = density
            for s, density_ref in enumerate(density_refs):
                first = pl.multiple_of(lax.rem(own_ref[0] + s, kpts) * block, block)
                density_ref[p] = whole[p, pl.ds(first, block), :]
        else:
            density_refs[0][p] = density
        if is_last:
            level = jnp.mean(density[:8], axis=(0, 1), keepdims=True)
            half = mul3_left(forth_ref[...], density - level, NT)
            half = half + jnp.where(first_row, level * NY, 0.0)
            send_ref[pl.ds(p, 2 * HALF, stride=planes), :] = half

    for p in range(planes):
        transform(p)


def wave_band(kpts, tiles, total, scale, own, counts, came, wave_y, wave_x, forth, former, chosen):
    planes = NZ // came.shape[0]
    block = NX // kpts
    is_first, is_last = former is None, forth is not None
    vmem = pl.BlockSpec(memory_space=pltpu.VMEM)
    operands = [own, counts, came, wave_y, wave_x]
    if is_last:
        operands.append(forth)
    if not is_first:
        operands += [former, *chosen]
    if is_last:
        out_shape = [jax.ShapeDtypeStruct((planes, block, NY), jnp.float32)] * kpts
    else:
        out_shape = [jax.ShapeDtypeStruct((planes, NX, NY), jnp.float32)]
    if is_first:
        out_shape.append(jax.ShapeDtypeStruct((HALF // came.shape[0], NZ, NX), jnp.float32))
        out_shape.append(jax.ShapeDtypeStruct((total, 4 * HALF), jnp.bfloat16))
        out_shape.append(jax.ShapeDtypeStruct((16, total), jnp.bfloat16))
    if is_last:
        out_shape.append(jax.ShapeDtypeStruct((2 * HALF * planes, NX), jnp.float32))
    rows = kpts * 2 * planes
    return pl.pallas_call(
        functools.partial(wave_kernel, kpts, tiles, scale, is_first, is_last),
        in_specs=[pl.BlockSpec(memory_space=pltpu.SMEM)] * 2 + [vmem] * (len(operands) - 2),
        out_specs=[vmem] * len(out_shape),
        out_shape=out_shape,
        scratch_shapes=[
            pltpu.VMEM((2 * rows, total), jnp.bfloat16),
            pltpu.VMEM((kpts * planes * HALF, LANES), jnp.float32),
            pltpu.VMEM((planes, NX, NY), jnp.float32),
        ],
        compiler_params=pltpu.CompilerParams(vmem_limit_bytes=VMEM_LIMIT),
        cost_estimate=pl.CostEstimate(
            flops=4 * rows * total * HALF * HALF, bytes_accessed=4 * came.size, transcendentals=0
        ),
        name="wave_band",
    )(*operands)


def poisson_kernel(pws, own_ref, kernel_ref, came_ref, forth_ref, back_ref, both_x_ref, send_ref):
    count, parts, planes, unused = came_ref.shape
    kpts = count // pws
    merged = NZ // pws // 8
    block = NX // kpts
    rows = pws * 8
    lane = lax.broadcasted_iota(jnp.int32, (rows, LANES), 1) // block

    def quarter(array, half, c):
        return array[half * NZ : (half + 1) * NZ, c * NX : (c + 1) * NX]

    for q in range(parts // 2):
        real, imag = (came_ref[:, 2 * q + c].reshape(NZ, NX) for c in range(2))
        if q == 0:
            level = jnp.mean(real, axis=(0, 1), keepdims=True)
            real = real - jnp.where(own_ref[1] == 0, level, 0.0)
        turned = mul3_left(forth_ref[...], jnp.concatenate((real, imag), axis=1), NN)
        lines = (
            quarter(turned, 0, 0) + quarter(turned, 1, 1),
            quarter(turned, 0, 1) - quarter(turned, 1, 0),
        )
        turned = mul3_right(jnp.concatenate(lines, axis=0), both_x_ref[...], NN)
        kernel = kernel_ref[q]
        lines = (
            (quarter(turned, 0, 0) + quarter(turned, 1, 1)) * kernel,
            (quarter(turned, 1, 0) - quarter(turned, 0, 1)) * kernel,
        )
        turned = mul3_right(jnp.concatenate(lines, axis=0), both_x_ref[...], NN)
        lines = (
            quarter(turned, 0, 0) - quarter(turned, 1, 1),
            quarter(turned, 0, 1) + quarter(turned, 1, 0),
        )
        turned = mul3_left(back_ref[...], jnp.concatenate(lines, axis=1), NN)
        real = quarter(turned, 0, 0) - quarter(turned, 1, 1)
        imag = quarter(turned, 0, 1) + quarter(turned, 1, 0)
        for c, value in enumerate((real, imag)):
            for a in range(kpts):
                packed = None
                for m in range(merged):
                    piece = value[m * rows : (m + 1) * rows]
                    shift = (m - a) * block % LANES
                    if shift:
                        piece = pltpu.roll(piece, shift, 1)
                    packed = piece if m == 0 else jnp.where(lane == m, piece, packed)
                send_ref[a * pws : (a + 1) * pws, 2 * q + c] = packed.reshape(pws, 8, LANES)


def poisson(pws, own, kernel, came, forth, back, both_x):
    vmem = pl.BlockSpec(memory_space=pltpu.VMEM)
    count, parts, unused, unused = came.shape
    return pl.pallas_call(
        functools.partial(poisson_kernel, pws),
        in_specs=[pl.BlockSpec(memory_space=pltpu.SMEM)] + [vmem] * 5,
        out_specs=vmem,
        out_shape=jax.ShapeDtypeStruct((count, parts, 8, LANES), jnp.float32),
        compiler_params=pltpu.CompilerParams(vmem_limit_bytes=VMEM_LIMIT),
        name="poisson",
    )(own, kernel, came, forth, back, both_x)


def assemble_kernel(own_ref, *refs):
    *block_refs, density_ref, sems = refs
    kpts = len(block_refs)
    part = density_ref.shape[0] // kpts
    copies = []
    for s, block_ref in enumerate(block_refs):
        sender = lax.rem(own_ref[0] + kpts - s, kpts)
        copies.append(
            pltpu.make_async_copy(block_ref, density_ref.at[pl.ds(sender * part, part)], sems.at[s])
        )
    for copy in copies:
        copy.start()
    for copy in copies:
        copy.wait()


def assemble(own, blocks):
    part, block, length = blocks[0].shape
    return pl.pallas_call(
        assemble_kernel,
        in_specs=[pl.BlockSpec(memory_space=pltpu.SMEM)]
        + [pl.BlockSpec(memory_space=pl.ANY)] * len(blocks),
        out_specs=pl.BlockSpec(memory_space=pl.ANY),
        out_shape=jax.ShapeDtypeStruct((part * len(blocks), block, length), jnp.float32),
        scratch_shapes=[pltpu.SemaphoreType.DMA((len(blocks),))],
        name="assemble",
    )(own, *blocks)


def finish_kernel(came_ref, back_ref, out_ref):
    planes, block, unused = out_ref.shape
    merged = planes // 8
    for h in range(8):
        lines = came_ref[pl.ds(h, 2 * HALF, stride=8), :]
        field = mul3_right(lines, back_ref[...], TN)
        out_ref[h * merged : (h + 1) * merged] = field.reshape(merged, block, NY)


def finish(planes, block, came, back_y):
    vmem = pl.BlockSpec(memory_space=pltpu.VMEM)
    return pl.pallas_call(
        finish_kernel,
        in_specs=[vmem] * 2,
        out_specs=vmem,
        out_shape=jax.ShapeDtypeStruct((planes, block, NY), jnp.float32),
        compiler_params=pltpu.CompilerParams(vmem_limit_bytes=VMEM_LIMIT),
        name="finish",
    )(came, back_y)


def exchange(array, axes):
    return lax.all_to_all(array, axes, split_axis=0, concat_axis=0, tiled=True)


def local_planes(band_coeffs, miller_third, column_slot, column_map, kpoint_counts):
    pws = lax.axis_size("pw")
    kpts = lax.axis_size("kpt")
    count = pws * kpts
    everyone = ("kpt", "pw")
    slots = column_map.shape[0]
    band_count = band_coeffs.shape[1]
    z_width = column_slot.shape[1] // slots
    planes = NZ // count
    parts = 2 * HALF // count
    made = tables(kpts, pws, planes)
    pencil = stack_table(made["pencil"](z_width), 1)
    wave_x, forth_y, forth_z, back_z = (
        stack_table(made[name], 1) for name in ("wave_x", "forth_y", "forth_z", "back_z")
    )
    wave_y, back_y, both_x = (stack_table(made[name], 0) for name in ("wave_y", "back_y", "both_x"))

    tiles = slots // LANES
    length = column_slot.shape[1] // LANES
    coeffs = band_coeffs.reshape(band_count, 2, length, LANES).transpose(0, 2, 1, 3)
    coeffs = coeffs.reshape(band_count, 2 * length, LANES)
    miller = miller_third.reshape(length, LANES)
    slot = column_slot.reshape(length, LANES)
    scale = 2.0 / (column_slot.shape[1] * pws)
    arrived = []
    for band in range(band_count):
        column = column_map if band == 0 else None
        packed = pack_band(
            band, count, coeffs, miller, slot, pencil, slots, column
        )
        arrived.append(exchange(packed, everyone))
    device = lax.axis_index("kpt") * pws + lax.axis_index("pw")
    own = jnp.stack((lax.axis_index("kpt"), device * (parts // 2))).astype(jnp.int32)
    former = chosen = None
    for band in range(band_count):
        forth = forth_y if band == band_count - 1 else None
        made_here = wave_band(
            kpts,
            tiles,
            pws * slots,
            scale,
            own,
            kpoint_counts,
            arrived[band],
            wave_y,
            wave_x,
            forth,
            former,
            chosen,
        )
        former = made_here[0]
        if band == 0:
            kernel, *chosen = made_here[kpts if forth is not None else 1 :][:3]
    half = exchange(made_here[-1].reshape(count, parts, planes, NX), everyone)
    blocks = [made_here[0]] + [
        lax.ppermute(made_here[s], "kpt", [(a, (a + s) % kpts) for a in range(kpts)])
        for s in range(1, kpts)
    ]
    back = poisson(pws, own, kernel, half, forth_z, back_z, both_x)
    back = exchange(back, everyone).reshape(count * parts * 8, LANES)
    return assemble(own, blocks), finish(NZ // pws, NX // kpts, back, back_y)


def fits_planes(kpts, pws):
    count = kpts * pws
    own = NZ // pws
    return (
        NZ % count == 0
        and NZ // count == 8
        and 2 * HALF % (2 * count) == 0
        and NX % kpts == 0
        and own % 8 == 0
        and own // 8 * (NX // kpts) == LANES
    )


def local(band_coeffs, miller_third, column_slot, column_map, kpoint_counts):
    slots = column_map.shape[0]
    plain = slots % LANES == 0 and LANES <= slots <= 8 * RANK_LOW
    plain = plain and column_slot.shape[1] == slots * LANES
    fits = plain and fits_planes(lax.axis_size("kpt"), lax.axis_size("pw"))
    chosen = local_planes if fits else local_general
    return chosen(band_coeffs, miller_third, column_slot, column_map, kpoint_counts)


def solution(mesh):
    return jax.shard_map(
        local,
        mesh=mesh,
        in_specs=(P("kpt", None, None, "pw"), P("kpt", "pw"), P("kpt", "pw"), P("pw"), P()),
        out_specs=(P("pw", "kpt", None), P("pw", "kpt", None)),
        check_vma=False,
    )
```

```python
import functools
import math

import jax
import jax.numpy as jnp
import numpy as np
from jax import lax
from jax.experimental import pallas as pl
from jax.experimental.pallas import tpu as pltpu
from jax.sharding import PartitionSpec as P

NX = 128
NY = 128
NZ = 256


SPACING = 0.25


def contract(pattern, former, latter):
    return jnp.einsum(
        pattern, former, latter, precision=lax.Precision.HIGHEST, preferred_element_type=jnp.float32
    )


def phase_tables(first_index, second_index, length):
    product = first_index[:, None] * second_index[None, :] % length
    angle = product.astype(jnp.float32) * (2.0 * math.pi / length)
    return (jnp.cos(angle), jnp.sin(angle))


def signed_freq(values, length):
    return jnp.where(values >= length // 2, values - length, values)


def coulomb(freq_z, freq_x, freq_y):
    wave_z = freq_z.astype(jnp.float32) / (NZ * SPACING)
    wave_x = freq_x.astype(jnp.float32) / (NX * SPACING)
    wave_y = freq_y.astype(jnp.float32) / (NY * SPACING)
    squared = (2.0 * math.pi) ** 2 * (wave_z * wave_z + wave_x * wave_x + wave_y * wave_y)
    anchor = (freq_z == 0) & (freq_x == 0) & (freq_y == 0)
    return jnp.where(anchor, 0.0, 4.0 * math.pi / jnp.where(anchor, 1.0, squared))


def poisson_columns(real_part, imag_part, freq_x, freq_y):
    length = real_part.shape[0]
    steps_z = jnp.arange(length, dtype=jnp.int32)
    cos_z, sin_z = phase_tables(steps_z, steps_z, length)
    spec_real = contract("zk,km->zm", cos_z, real_part) + contract("zk,km->zm", sin_z, imag_part)
    spec_imag = contract("zk,km->zm", cos_z, imag_part) - contract("zk,km->zm", sin_z, real_part)
    kernel = coulomb(signed_freq(steps_z, length)[:, None], freq_x[None, :], freq_y[None, :]) / (
        NX * NY * NZ
    )
    spec_real = spec_real * kernel
    spec_imag = spec_imag * kernel
    back_real = contract("zk,km->zm", cos_z, spec_real) - contract("zk,km->zm", sin_z, spec_imag)
    back_imag = contract("zk,km->zm", sin_z, spec_real) + contract("zk,km->zm", cos_z, spec_imag)
    return (back_real, back_imag)


def forward_planes(field):
    steps_x = jnp.arange(NX, dtype=jnp.int32)
    steps_y = jnp.arange(NY, dtype=jnp.int32)
    cos_y, sin_y = phase_tables(steps_y, steps_y, NY)
    cos_x, sin_x = phase_tables(steps_x, steps_x, NX)
    half_real = contract("pxy,ky->pxk", field, cos_y)
    half_imag = -contract("pxy,ky->pxk", field, sin_y)
    spec_real = contract("kx,pxy->pky", cos_x, half_real) + contract(
        "kx,pxy->pky", sin_x, half_imag
    )
    spec_imag = contract("kx,pxy->pky", cos_x, half_imag) - contract(
        "kx,pxy->pky", sin_x, half_real
    )
    return (spec_real, spec_imag)


def local_general(band_coeffs, miller_third, column_slot, column_map, kpoint_counts):
    pw_count = lax.axis_size("pw")
    kpt_count = lax.axis_size("kpt")
    pw_index = lax.axis_index("pw")
    kpt_index = lax.axis_index("kpt")
    col_dev = column_map.shape[0]
    ng_dev = column_slot.shape[1]
    band_count = band_coeffs.shape[1]
    z_width = ng_dev // col_dev
    planes = NZ // pw_count
    x_block = NX // kpt_count
    col_total = pw_count * col_dev
    steps_y = jnp.arange(NY, dtype=jnp.int32)
    steps_x = jnp.arange(NX, dtype=jnp.int32)
    cos_y, sin_y = phase_tables(steps_y, steps_y, NY)
    cos_x, sin_x = phase_tables(steps_x, steps_x, NX)
    all_columns = lax.all_gather(column_map, "pw", axis=0, tiled=True)
    position = (miller_third[0] + z_width // 2) * col_dev + column_slot[0]
    source_of = (
        jnp.zeros((ng_dev,), jnp.int32).at[position].set(jnp.arange(ng_dev, dtype=jnp.int32))
    )
    coeff_rows = band_coeffs[0].reshape(band_count * 2, ng_dev).T
    packed = jnp.take(coeff_rows, source_of, axis=0)
    packed = (
        packed.reshape(z_width, col_dev, band_count, 2)
        .transpose(0, 2, 3, 1)
        .reshape(z_width, band_count * 2 * col_dev)
    )
    cos_z, sin_z = phase_tables(
        jnp.arange(NZ, dtype=jnp.int32), jnp.arange(z_width, dtype=jnp.int32) - z_width // 2, NZ
    )
    by_cos = contract("zj,jc->zc", cos_z, packed).reshape(NZ, band_count, 2, col_dev)
    by_sin = contract("zj,jc->zc", sin_z, packed).reshape(NZ, band_count, 2, col_dev)
    pencil = jnp.stack(
        (by_cos[:, :, 0] - by_sin[:, :, 1], by_sin[:, :, 0] + by_cos[:, :, 1]), axis=2
    )
    pencil = pencil.reshape(NZ, band_count * 2 * col_dev)
    arrived = lax.all_to_all(pencil, "pw", split_axis=0, concat_axis=1, tiled=True)
    arrived = arrived.reshape(planes, pw_count, band_count, 2, col_dev).transpose(2, 1, 4, 3, 0)
    arrived = arrived.reshape(band_count, col_total, 2 * planes)
    arrived = jnp.concatenate(
        (arrived, jnp.zeros((band_count, 1, 2 * planes), jnp.float32)), axis=1
    )
    cell_source = (
        jnp.full((NX * NY,), col_total, jnp.int32)
        .at[all_columns]
        .set(jnp.arange(col_total, dtype=jnp.int32))
    )

    def add_band(band, running):
        one_band = lax.dynamic_index_in_dim(arrived, band, 0, keepdims=False)
        placed = jnp.take(one_band, cell_source, axis=0)
        placed = placed.reshape(NX, NY, 2, planes).transpose(2, 3, 0, 1)
        grid_real = placed[0]
        grid_imag = placed[1]
        mixed_real = contract("pxm,ym->pxy", grid_real, cos_y) - contract(
            "pxm,ym->pxy", grid_imag, sin_y
        )
        mixed_imag = contract("pxm,ym->pxy", grid_real, sin_y) + contract(
            "pxm,ym->pxy", grid_imag, cos_y
        )
        wave_real = contract("xm,pmy->pxy", cos_x, mixed_real) - contract(
            "xm,pmy->pxy", sin_x, mixed_imag
        )
        wave_imag = contract("xm,pmy->pxy", sin_x, mixed_real) + contract(
            "xm,pmy->pxy", cos_x, mixed_imag
        )
        return running + wave_real * wave_real + wave_imag * wave_imag

    squares_sum = lax.fori_loop(0, band_count, add_band, jnp.zeros((planes, NX, NY), jnp.float32))
    weight = (
        2.0
        * kpoint_counts[kpt_index].astype(jnp.float32)
        / jnp.sum(kpoint_counts).astype(jnp.float32)
    )
    weight = weight / (ng_dev * pw_count)
    partial_value = weight * squares_sum
    total_density = lax.psum(partial_value, "kpt")
    density = lax.dynamic_slice_in_dim(total_density, kpt_index * x_block, x_block, 1)
    spec_real, spec_imag = forward_planes(total_density)
    rows_pw = NX // pw_count
    pencil_real, pencil_imag = (
        lax.all_to_all(spec_real, "pw", split_axis=1, concat_axis=0, tiled=True),
        lax.all_to_all(spec_imag, "pw", split_axis=1, concat_axis=0, tiled=True),
    )
    local_x = pw_index * rows_pw + jnp.arange(rows_pw, dtype=jnp.int32)
    freq_x = jnp.repeat(signed_freq(local_x, NX), NY)
    freq_y = jnp.tile(signed_freq(steps_y, NY), rows_pw)
    back_real, back_imag = poisson_columns(
        pencil_real.reshape(NZ, rows_pw * NY), pencil_imag.reshape(NZ, rows_pw * NY), freq_x, freq_y
    )
    plane_real, plane_imag = (
        lax.all_to_all(
            back_real.reshape(NZ, rows_pw, NY), "pw", split_axis=0, concat_axis=1, tiled=True
        ),
        lax.all_to_all(
            back_imag.reshape(NZ, rows_pw, NY), "pw", split_axis=0, concat_axis=1, tiled=True
        ),
    )
    own_rows = kpt_index * x_block + jnp.arange(x_block, dtype=jnp.int32)
    cos_rows, sin_rows = phase_tables(own_rows, steps_x, NX)
    rows_real = contract("xk,pky->pxy", cos_rows, plane_real) - contract(
        "xk,pky->pxy", sin_rows, plane_imag
    )
    rows_imag = contract("xk,pky->pxy", sin_rows, plane_real) + contract(
        "xk,pky->pxy", cos_rows, plane_imag
    )
    hartree = contract("pxk,yk->pxy", rows_real, cos_y) - contract("pxk,yk->pxy", rows_imag, sin_y)
    return (density, hartree)


LANES = 128
HALF = 64
VMEM_LIMIT = 56 * 1024 * 1024
NN = (((1,), (0,)), ((), ()))
NT = (((1,), (1,)), ((), ()))
TN = (((0,), (0,)), ((), ()))


def pieces(value):
    high = value.astype(jnp.bfloat16)
    low = (value - high.astype(jnp.float32)).astype(jnp.bfloat16)
    return high, low


def mul(former, latter, dims):
    return lax.dot_general(former, latter, dims, preferred_element_type=jnp.float32)


def mul3_left(former, latter, dims):
    high, low = pieces(latter)
    (unused,), (axis,) = dims[0]
    return mul(former, jnp.concatenate((high, high, low), axis=axis), dims)


def mul3_right(former, latter, dims):
    high, low = pieces(former)
    (axis,), (unused,) = dims[0]
    return mul(jnp.concatenate((high, high, low), axis=axis), latter, dims)


def stack_table(values, axis):
    high = values.astype(np.float32).astype(jnp.bfloat16)
    low = (values - high.astype(np.float64)).astype(np.float32).astype(jnp.bfloat16)
    return jnp.asarray(np.concatenate((high, low, high), axis=axis))


def angles(former, latter, length):
    return np.outer(former, latter) % length * (2.0 * np.pi / length)


def tables(kpts, pws, planes):
    count = kpts * pws
    low_freq = np.arange(HALF) - HALF // 2
    grid_x, grid_y, grid_z = np.arange(NX), np.arange(NY), np.arange(NZ)
    own_y = np.arange(HALF)

    device = np.arange(count)
    plane_of = (
        (device % pws)[:, None] * (NZ // pws)
        + (device // pws)[:, None] * planes
        + np.arange(planes)[None, :]
    )
    return_table = {}

    def pencil(z_width):
        angle = angles(plane_of.ravel(), np.arange(z_width) - z_width // 2, NZ)
        cos, sin = (
            part.reshape(count, 1, planes, z_width) for part in (np.cos(angle), np.sin(angle))
        )
        real = np.concatenate((cos, -sin), axis=3)
        imag = np.concatenate((sin, cos), axis=3)
        return np.concatenate((real, imag), axis=1).reshape(-1, 2 * z_width)

    return_table["pencil"] = pencil

    angle = angles(low_freq, grid_y, NY)
    cos, sin = np.cos(angle), np.sin(angle)
    return_table["wave_y"] = np.block([[cos, sin], [-sin, cos]])

    angle = angles(grid_x, low_freq, NX)
    cos, sin = np.cos(angle), np.sin(angle)
    return_table["wave_x"] = np.block([[cos, -sin], [sin, cos]])

    angle = angles(own_y, grid_y, NY)
    cos, sin = np.cos(angle), np.sin(angle)
    return_table["forth_y"] = np.stack((cos, -sin), axis=1).reshape(2 * HALF, NY).T
    twice = np.where(own_y == 0, 1.0, 2.0)[:, None]
    return_table["back_y"] = np.stack((twice * cos, -twice * sin), axis=1).reshape(2 * HALF, NY)

    angle = angles(grid_z, plane_of.ravel(), NZ)
    return_table["forth_z"] = np.concatenate((np.cos(angle), np.sin(angle)), axis=0)
    own = NZ // pws
    merged = own // 8
    order = (
        np.arange(pws)[None, :, None] * own
        + np.arange(8)[None, None, :] * merged
        + np.arange(merged)[:, None, None]
    )
    angle = angles(order.ravel(), grid_z, NZ)
    return_table["back_z"] = np.concatenate((np.cos(angle), np.sin(angle)), axis=0)

    angle = angles(grid_x, grid_x, NX)
    return_table["both_x"] = np.concatenate((np.cos(angle), np.sin(angle)), axis=1)
    return return_table


def ramp(shape, axis, first=0):
    steps = lax.broadcasted_iota(jnp.int32, shape, axis) + first
    return steps.astype(jnp.float32).astype(jnp.bfloat16)


def sixteen(row):
    return jnp.broadcast_to(row, (16, row.shape[1])).astype(jnp.bfloat16)


def one_hot_lanes(row, ramps):
    column = jnp.transpose(jnp.concatenate([sixteen(row)] * (LANES // 16), axis=0))
    one = jnp.ones(column.shape, jnp.bfloat16)
    zero = jnp.zeros(column.shape, jnp.bfloat16)
    return jnp.concatenate(
        [
            jnp.where(column == ramps[:, first : first + LANES], one, zero)
            for first in range(0, ramps.shape[1], LANES)
        ],
        axis=1,
    )


RANK_LOW = 64
WINDOW = 64


def exchange_rows(refs, low_bits, size_bits, descending):
    for outer in range(RANK_LOW):
        if any(outer >> bit & 1 for bit in low_bits[0]):
            continue
        touched = sorted(
            outer + sum(1 << bit for i, bit in enumerate(low_bits[0]) if pattern >> i & 1)
            for pattern in range(1 << len(low_bits[0]))
        )
        held = {v: [ref[v * 8 : v * 8 + 8, :] for ref in refs] for v in touched}
        for size, bits in zip(size_bits, low_bits[1:]):
            for bit in bits:
                for v in touched:
                    if v >> bit & 1:
                        continue
                    former, latter = held[v], held[v | 1 << bit]
                    if size < 6:
                        down = bool(v >> size & 1)
                        swap = former[0] < latter[0] if down else former[0] > latter[0]
                    else:
                        swap = former[0] > latter[0]
                        if descending is not None:
                            swap = jnp.logical_xor(swap, descending)
                    held[v] = [jnp.where(swap, y, x) for x, y in zip(former, latter)]
                    held[v | 1 << bit] = [jnp.where(swap, x, y) for x, y in zip(former, latter)]
        for v in touched:
            for ref, value in zip(refs, held[v]):
                ref[v * 8 : v * 8 + 8, :] = value


def exchange_sublanes(refs, stride, descending):
    sublane = lax.broadcasted_iota(jnp.int32, (8, LANES), 0)
    upper = sublane // stride % 2 == 1
    want_least = upper if descending is not None else jnp.logical_not(upper)
    if descending is not None:
        want_least = jnp.logical_not(jnp.logical_xor(upper, descending))

    def partner(value):
        if stride == 4:
            return pltpu.roll(value, 4, 0)
        return jnp.where(upper, pltpu.roll(value, stride, 0), pltpu.roll(value, 8 - stride, 0))

    for v in range(RANK_LOW):
        here = [ref[v * 8 : v * 8 + 8, :] for ref in refs]
        there = [partner(value) for value in here]
        take = jnp.where(
            want_least, (here[0] > there[0]).astype(jnp.int32), (here[0] < there[0]).astype(jnp.int32)
        )
        take = take == 1
        for ref, x, y in zip(refs, here, there):
            ref[v * 8 : v * 8 + 8, :] = jnp.where(take, y, x)


def sort_columns(refs):
    sublane = lax.broadcasted_iota(jnp.int32, (8, LANES), 0)
    exchange_rows(refs, [(0, 1, 2), (0,), (1, 0), (2, 1, 0)], [1, 2, 3], None)
    exchange_rows(refs, [(3,), (3,)], [4], None)
    exchange_rows(refs, [(0, 1, 2), (2, 1, 0)], [4], None)
    exchange_rows(refs, [(3, 4), (4, 3)], [5], None)
    exchange_rows(refs, [(0, 1, 2), (2, 1, 0)], [5], None)
    for size in range(6, 10):
        descending = None if size == 9 else sublane // (1 << (size - 6)) % 2 == 1
        for bit in range(size - 1, 5, -1):
            exchange_sublanes(refs, 1 << (bit - 6), descending)
        exchange_rows(refs, [(3, 4, 5), (5, 4, 3)], [size], descending)
        exchange_rows(refs, [(0, 1, 2), (2, 1, 0)], [size], descending)


def pack_kernel(width, has_column, *refs):
    coeff_ref, miller_ref, slot_ref, pencil_ref = refs[:4]
    rest = list(refs[4:])
    column_ref = rest.pop(0) if has_column else None
    out_ref, total, key_ref, real_ref, imag_ref, lane_ref, real_low, imag_low, ramp_ref, step_ref, held, sem = rest
    fetch = pltpu.make_async_copy(pencil_ref, held, sem)
    fetch.start()
    half = total.shape[0] // 4
    slots = 2 * half
    count = out_ref.shape[0]
    rows = pencil_ref.shape[0] // count
    length = miller_ref.shape[0]
    ranks = key_ref.shape[0]

    slot = slot_ref[...]
    second = slot >= half
    lane = miller_ref[...] + width // 2
    key = jnp.where(second, slot - half, slot) * (2 * width) + jnp.where(second, lane + width, lane)
    key_ref[0:length] = key.astype(jnp.float32)
    real_ref[0:length] = coeff_ref[0, pl.ds(0, length, stride=2), :]
    imag_ref[0:length] = coeff_ref[0, pl.ds(1, length, stride=2), :]
    blank = jnp.zeros((ranks - length, LANES), jnp.float32)
    key_ref[length:] = blank + 2.0 * slots * width
    real_ref[length:] = blank
    imag_ref[length:] = blank
    sort_columns((key_ref, real_ref, imag_ref))

    def base_of(block):
        base = 8 * (block // 2) + 8 * (block % 2) - WINDOW // 2
        return jnp.minimum(jnp.maximum(base, 0), half - WINDOW)

    ramp_ref[...] = ramp(ramp_ref.shape, 1)
    step_ref[...] = ramp(step_ref.shape, 0)
    sublane = lax.broadcasted_iota(jnp.int32, (8, LANES), 0)
    astray = jnp.zeros((8, LANES), jnp.float32)
    for v in range(RANK_LOW):
        at = slice(v * 8, v * 8 + 8)
        keys = key_ref[at, :]
        high = jnp.floor(keys * (1.0 / (2 * width)))
        lane_ref[at, :] = keys - high * (2.0 * width)
        key_ref[at, :] = high
        for ref, low_ref in ((real_ref, real_low), (imag_ref, imag_low)):
            value = ref[at, :]
            rounded = value.astype(jnp.bfloat16).astype(jnp.float32)
            ref[at, :] = rounded
            low_ref[at, :] = value - rounded
        offset = high - base_of(sublane * (RANK_LOW // 8) + v // 8).astype(jnp.float32)
        outside = jnp.logical_or(offset < 0.0, offset >= 1.0 * WINDOW)
        astray = jnp.where(outside, 1.0, astray)
    astray = jnp.max(jnp.where(sublane * RANK_LOW < length, astray, 0.0))

    def add(block, base, window):
        first = block % (RANK_LOW // 8) * 64 + block // (RANK_LOW // 8)
        base_row = jnp.full((1, LANES), base, jnp.int32).astype(jnp.float32)
        zero = jnp.zeros((16, LANES), jnp.bfloat16)
        spread, chosen = [], []
        for t in range(8):
            row = pl.ds(first + 8 * t, 1)
            high = sixteen(key_ref[row, :] - base_row)
            masks = [high == step_ref[r : r + 16, :] for r in range(0, window, 16)]
            spread.append(
                jnp.concatenate(
                    [
                        jnp.where(mask, value, zero)
                        for value in [
                            sixteen(ref[row, :]) for ref in (real_ref, imag_ref, real_low, imag_low)
                        ]
                        for mask in masks
                    ],
                    axis=0,
                )
            )
            chosen.append(one_hot_lanes(lane_ref[row, :], ramp_ref[...]))
        found = mul(jnp.concatenate(spread, axis=1), jnp.concatenate(chosen, axis=0), NN)
        for i in range(4):
            if window == half:
                into = pl.ds(i * half, half)
            else:
                into = pl.ds(pl.multiple_of(i * half + base, 8), window)
            total[into, :] += found[i * window : (i + 1) * window]

    total[...] = jnp.zeros_like(total)
    blocks = length // 8
    together = 4 if blocks % 4 == 0 else 1

    @pl.when(astray == 0.0)
    def _():
        def some_blocks(i, unused):
            for s in range(together):
                block = together * i + s
                add(block, base_of(block), WINDOW)
            return unused

        lax.fori_loop(0, blocks // together, some_blocks, 0)

    @pl.when(astray > 0.0)
    def _():
        def one_block(block, unused):
            add(block, 0, half)
            return unused

        lax.fori_loop(0, blocks, one_block, 0)

    both = []
    for at in range(2):
        parts = [
            total[(2 * at + c) * half : (2 * at + c + 1) * half].astype(jnp.bfloat16)
            for c in range(2)
        ]
        both.append(
            jnp.concatenate(
                [
                    jnp.concatenate([part[:, h * width : (h + 1) * width] for part in parts], axis=1)
                    for h in range(2)
                ],
                axis=0,
            )
        )
    fetch.wait()
    pencils = mul(held[...], jnp.concatenate((both[0], both[0], both[1]), axis=1), NT)
    tiles = slots // LANES
    for t in range(tiles):
        tile = pencils[:, t * LANES : (t + 1) * LANES].reshape(count, rows, LANES)
        if not has_column:
            out_ref[:, t * rows : (t + 1) * rows] = tile
            continue
        for g in range(rows // 4):
            out_ref[:, t * (rows // 4) + g] = tile[:, 4 * g : 4 * g + 4]
    if has_column:
        column = [
            column_ref[t * LANES : (t + 1) * LANES].astype(jnp.float32).reshape(1, LANES)
            for t in range(tiles)
        ]
        column = jnp.concatenate(column + [jnp.zeros((4 - tiles, LANES), jnp.float32)], axis=0)
        out_ref[:, tiles * rows // 4] = jnp.broadcast_to(column[None], (count, 4, LANES))


def pack_band(band, count, coeffs, miller, slot, pencil, slots, column):
    length = miller.shape[0]
    width = pencil.shape[1] // 6
    rows = pencil.shape[0] // count * (slots // LANES)
    operands = [coeffs, miller, slot, pencil]
    out_shape = (count, rows, LANES)
    if column is not None:
        operands.append(column)
        out_shape = (count, rows // 4 + 1, 4, LANES)
    one_band = pl.BlockSpec((1, 2 * length, LANES), lambda i: (band, 0, 0))
    return pl.pallas_call(
        functools.partial(pack_kernel, width, column is not None),
        grid=(1,),
        in_specs=[one_band]
        + [
            pl.BlockSpec(memory_space=pl.ANY)
            if x is pencil
            else pl.BlockSpec(x.shape, lambda i, n=x.ndim: (0,) * n)
            for x in operands[1:]
        ],
        out_specs=pl.BlockSpec(out_shape, lambda i: (0,) * len(out_shape)),
        out_shape=jax.ShapeDtypeStruct(out_shape, jnp.float32),
        scratch_shapes=[pltpu.VMEM((2 * slots, 2 * width), jnp.float32)]
        + [pltpu.VMEM((8 * RANK_LOW, LANES), jnp.float32)] * 6
        + [
            pltpu.VMEM((LANES, 2 * width), jnp.bfloat16),
            pltpu.VMEM((slots // 2, LANES), jnp.bfloat16),
            pltpu.VMEM(pencil.shape, jnp.bfloat16),
            pltpu.SemaphoreType.DMA,
        ],
        compiler_params=pltpu.CompilerParams(vmem_limit_bytes=VMEM_LIMIT),
        cost_estimate=pl.CostEstimate(
            flops=2 * length * LANES * slots * 4 * width,
            bytes_accessed=16 * length * LANES,
            transcendentals=0,
        ),
        name="pack_band",
    )(*operands)


def wave_kernel(kpts, tiles, scale, is_first, is_last, *refs):
    own_ref, count_ref, came_ref, wave_y_ref, wave_x_ref = refs[:5]
    rest = list(refs[5:])
    forth_ref = rest.pop(0) if is_last else None
    former_ref, chosen_ref, high_ref = (None,) * 3 if is_first else [rest.pop(0) for _ in range(3)]
    density_refs = [rest.pop(0) for _ in range(kpts if is_last else 1)]
    if is_first:
        coulomb_ref, chosen_ref, high_ref = rest.pop(0), rest.pop(0), rest.pop(0)
    send_ref = rest.pop(0) if is_last else None
    values, grid, whole = rest
    planes = density_refs[0].shape[0]
    block = NX // kpts
    part_rows = 2 * planes
    pws = came_ref.shape[0] // kpts
    rows = kpts * part_rows
    total = values.shape[1]

    for j in range(pws):
        for t in range(tiles):
            if is_first:
                groups = [
                    came_ref[k * pws + j, t * (part_rows // 4) + g]
                    for k in range(kpts)
                    for g in range(part_rows // 4)
                ]
            else:
                groups = [
                    came_ref[k * pws + j, t * part_rows : (t + 1) * part_rows] for k in range(kpts)
                ]
            taken = jnp.concatenate(groups, axis=0)
            high, low = pieces(taken)
            first = (j * tiles + t) * LANES
            values[0:rows, first : first + LANES] = high
            values[rows : 2 * rows, first : first + LANES] = low

    tile = 4 * HALF
    if is_first:
        ramps = ramp((LANES, tile), 1)
        for j in range(pws):
            for t in range(tiles):
                column = came_ref[j, tiles * part_rows // 4, t : t + 1]
                column = column.astype(jnp.int32)
                cell = ((column // NY + NX // 2) % NX - HALF // 2) * HALF
                cell = cell + (column % NY + NY // 2) % NY - HALF // 2
                first = (j * tiles + t) * LANES
                lane = (cell % tile).astype(jnp.float32)
                chosen_ref[first : first + LANES, :] = one_hot_lanes(lane, ramps)
                high_ref[:, first : first + LANES] = sixteen((cell // tile).astype(jnp.float32))
        step_z = lax.broadcasted_iota(jnp.int32, (NZ, NX), 0)
        step_x = lax.broadcasted_iota(jnp.int32, (NZ, NX), 1)
        for q in range(coulomb_ref.shape[0]):
            freq_y = jnp.full((NZ, NX), own_ref[1] + q, jnp.int32)
            kernel = coulomb(signed_freq(step_z, NZ), signed_freq(step_x, NX), freq_y)
            coulomb_ref[q] = kernel * (1.0 / (NX * NY * NZ))
    left = lax.broadcasted_iota(jnp.int32, (planes, LANES), 1) < HALF
    together = 4

    def place(t, found):
        found = found[:rows] + found[rows:]
        for h in range(2):
            for k in range(kpts):
                real, imag = (
                    found[(2 * k + c) * planes : (2 * k + c + 1) * planes, h * LANES : (h + 1) * LANES]
                    for c in range(2)
                )
                first = (k * HALF + 4 * t + 2 * h) * planes
                grid[first : first + planes, :] = jnp.where(left, real, pltpu.roll(imag, HALF, 1))
                grid[first + planes : first + 2 * planes, :] = jnp.where(
                    left, pltpu.roll(real, HALF, 1), imag
                )

    high = high_ref[...]
    zero = jnp.zeros_like(high)
    for start in range(0, HALF // 4, together):
        kept = []
        for t in range(start, start + together):
            here = high == jnp.full_like(high, t)
            kept += [jnp.where(here, values[r : r + 16, :], zero) for r in range(0, 2 * rows, 16)]
        found = mul(jnp.concatenate(kept, axis=0), chosen_ref[...], NN)
        for s in range(together):
            place(start + s, found[2 * rows * s : 2 * rows * (s + 1)])

    sum_of = count_ref[0]
    for k in range(1, kpts):
        sum_of = sum_of + count_ref[k]

    def spread(number):
        return jnp.full((8, NY), number, jnp.int32).astype(jnp.float32)

    weights = [
        jnp.concatenate([spread(count_ref[k]) / spread(sum_of) * scale] * (NX // 8), axis=0)
        for k in range(kpts)
    ]
    lines = [grid[pl.ds(p, kpts * HALF, stride=planes), :] for p in range(planes)]
    lines = mul3_right(jnp.concatenate(lines, axis=0), wave_y_ref[...], NN)

    for p in range(planes):
        mixed = lines[p * kpts * HALF : (p + 1) * kpts * HALF]
        mixed = jnp.concatenate(
            [
                jnp.concatenate(
                    [mixed[k * HALF : (k + 1) * HALF, c * NY : (c + 1) * NY] for k in range(kpts)],
                    axis=1,
                )
                for c in range(2)
            ],
            axis=0,
        )
        wave = mul3_left(wave_x_ref[...], mixed, NN)
        square = wave[:NX] * wave[:NX] + wave[NX:] * wave[NX:]
        density = weights[0] * square[:, :NY]
        for k in range(1, kpts):
            density = density + weights[k] * square[:, k * NY : (k + 1) * NY]
        if former_ref is not None:
            density = density + former_ref[p]
        if is_last:
            whole[p] = density
        else:
            density_refs[0][p] = density

    if is_last:
        for s, density_ref in enumerate(density_refs):
            first = pl.multiple_of(lax.rem(own_ref[0] + s, kpts) * block, block)
            density_ref[...] = whole[:, pl.ds(first, block), :]
        level = jnp.mean(whole[0, :8, :], axis=(0, 1), keepdims=True)
        field = whole[...].reshape(planes * NX, NY) - level
        half = mul3_right(field, forth_ref[...], NN)
        first_row = lax.broadcasted_iota(jnp.int32, (2 * HALF, NX), 0) == 0
        for p in range(planes):
            turned = jnp.transpose(half[p * NX : (p + 1) * NX])
            turned = turned + jnp.where(first_row, level * NY, 0.0)
            send_ref[pl.ds(p, 2 * HALF, stride=planes), :] = turned


def wave_band(kpts, tiles, total, scale, own, counts, came, wave_y, wave_x, forth, former, chosen):
    planes = NZ // came.shape[0]
    block = NX // kpts
    is_first, is_last = former is None, forth is not None
    vmem = pl.BlockSpec(memory_space=pltpu.VMEM)
    operands = [own, counts, came, wave_y, wave_x]
    if is_last:
        operands.append(forth)
    if not is_first:
        operands += [former, *chosen]
    if is_last:
        out_shape = [jax.ShapeDtypeStruct((planes, block, NY), jnp.float32)] * kpts
    else:
        out_shape = [jax.ShapeDtypeStruct((planes, NX, NY), jnp.float32)]
    if is_first:
        out_shape.append(jax.ShapeDtypeStruct((HALF // came.shape[0], NZ, NX), jnp.float32))
        out_shape.append(jax.ShapeDtypeStruct((total, 4 * HALF), jnp.bfloat16))
        out_shape.append(jax.ShapeDtypeStruct((16, total), jnp.bfloat16))
    if is_last:
        out_shape.append(jax.ShapeDtypeStruct((2 * HALF * planes, NX), jnp.float32))
    rows = kpts * 2 * planes
    return pl.pallas_call(
        functools.partial(wave_kernel, kpts, tiles, scale, is_first, is_last),
        in_specs=[pl.BlockSpec(memory_space=pltpu.SMEM)] * 2 + [vmem] * (len(operands) - 2),
        out_specs=[vmem] * len(out_shape),
        out_shape=out_shape,
        scratch_shapes=[
            pltpu.VMEM((2 * rows, total), jnp.bfloat16),
            pltpu.VMEM((kpts * planes * HALF, LANES), jnp.float32),
            pltpu.VMEM((planes, NX, NY), jnp.float32),
        ],
        compiler_params=pltpu.CompilerParams(vmem_limit_bytes=VMEM_LIMIT),
        cost_estimate=pl.CostEstimate(
            flops=4 * rows * total * HALF * HALF, bytes_accessed=4 * came.size, transcendentals=0
        ),
        name="wave_band",
    )(*operands)


def poisson_kernel(pws, own_ref, kernel_ref, came_ref, forth_ref, back_ref, both_x_ref, send_ref):
    count, parts, planes, unused = came_ref.shape
    pairs = parts // 2
    fields = [came_ref[:, i].reshape(NZ, NX) for i in range(parts)]
    level = jnp.mean(fields[0], axis=(0, 1), keepdims=True)
    fields[0] = fields[0] - jnp.where(own_ref[1] == 0, level, 0.0)
    field = jnp.concatenate(fields, axis=1)
    turned = mul3_left(forth_ref[...], field, NN)

    def part(array, half, i):
        return array[half * NZ : (half + 1) * NZ, i * NX : (i + 1) * NX]

    lines = []
    for q in range(pairs):
        lines.append(part(turned, 0, 2 * q) + part(turned, 1, 2 * q + 1))
        lines.append(part(turned, 0, 2 * q + 1) - part(turned, 1, 2 * q))
    spectrum = mul3_right(jnp.concatenate(lines, axis=0), both_x_ref[...], NN)

    lines = []
    for q in range(pairs):
        real = spectrum[2 * q * NZ : (2 * q + 1) * NZ]
        imag = spectrum[(2 * q + 1) * NZ : (2 * q + 2) * NZ]
        kernel = kernel_ref[q]
        lines.append((real[:, :NX] + imag[:, NX:]) * kernel)
        lines.append((imag[:, :NX] - real[:, NX:]) * kernel)
    turned = mul3_right(jnp.concatenate(lines, axis=0), both_x_ref[...], NN)
    lines = []
    for q in range(pairs):
        real = turned[2 * q * NZ : (2 * q + 1) * NZ]
        imag = turned[(2 * q + 1) * NZ : (2 * q + 2) * NZ]
        lines.append(real[:, :NX] - imag[:, NX:])
        lines.append(real[:, NX:] + imag[:, :NX])
    turned = mul3_left(back_ref[...], jnp.concatenate(lines, axis=1), NN)

    kpts = count // pws
    merged = NZ // pws // 8
    block = NX // kpts
    rows = pws * 8
    lane = lax.broadcasted_iota(jnp.int32, (rows, LANES), 1) // block
    for q in range(pairs):
        real = part(turned, 0, 2 * q) - part(turned, 1, 2 * q + 1)
        imag = part(turned, 0, 2 * q + 1) + part(turned, 1, 2 * q)
        for c, value in enumerate((real, imag)):
            for a in range(kpts):
                packed = None
                for m in range(merged):
                    piece = value[m * rows : (m + 1) * rows]
                    shift = (m - a) * block % LANES
                    if shift:
                        piece = pltpu.roll(piece, shift, 1)
                    packed = piece if m == 0 else jnp.where(lane == m, piece, packed)
                send_ref[a * pws : (a + 1) * pws, 2 * q + c] = packed.reshape(pws, 8, LANES)


def poisson(pws, own, kernel, came, forth, back, both_x):
    vmem = pl.BlockSpec(memory_space=pltpu.VMEM)
    count, parts, unused, unused = came.shape
    return pl.pallas_call(
        functools.partial(poisson_kernel, pws),
        in_specs=[pl.BlockSpec(memory_space=pltpu.SMEM)] + [vmem] * 5,
        out_specs=vmem,
        out_shape=jax.ShapeDtypeStruct((count, parts, 8, LANES), jnp.float32),
        compiler_params=pltpu.CompilerParams(vmem_limit_bytes=VMEM_LIMIT),
        name="poisson",
    )(own, kernel, came, forth, back, both_x)


def finish_kernel(own_ref, came_ref, back_ref, *refs):
    block_refs, density_ref, out_ref = refs[:-2], refs[-2], refs[-1]
    kpts = len(block_refs)
    planes, block, unused = out_ref.shape
    merged = planes // 8
    for s, block_ref in enumerate(block_refs):
        sender = lax.rem(own_ref[0] + kpts - s, kpts)
        density_ref[pl.ds(sender * (planes // kpts), planes // kpts)] = block_ref[...]
    for h in range(8):
        lines = came_ref[pl.ds(h, 2 * HALF, stride=8), :]
        field = mul3_right(lines, back_ref[...], TN)
        out_ref[h * merged : (h + 1) * merged] = field.reshape(merged, block, NY)


def finish(planes, block, own, came, back_y, blocks):
    vmem = pl.BlockSpec(memory_space=pltpu.VMEM)
    return pl.pallas_call(
        finish_kernel,
        in_specs=[pl.BlockSpec(memory_space=pltpu.SMEM)] + [vmem] * (2 + len(blocks)),
        out_specs=[vmem] * 2,
        out_shape=[jax.ShapeDtypeStruct((planes, block, NY), jnp.float32)] * 2,
        compiler_params=pltpu.CompilerParams(vmem_limit_bytes=VMEM_LIMIT),
        name="finish",
    )(own, came, back_y, *blocks)


def exchange(array, axes):
    return lax.all_to_all(array, axes, split_axis=0, concat_axis=0, tiled=True)


def local_planes(band_coeffs, miller_third, column_slot, column_map, kpoint_counts):
    pws = lax.axis_size("pw")
    kpts = lax.axis_size("kpt")
    count = pws * kpts
    everyone = ("kpt", "pw")
    slots = column_map.shape[0]
    band_count = band_coeffs.shape[1]
    z_width = column_slot.shape[1] // slots
    planes = NZ // count
    parts = 2 * HALF // count
    made = tables(kpts, pws, planes)
    pencil = stack_table(made["pencil"](z_width), 1)
    wave_x, forth_z, back_z = (
        stack_table(made[name], 1) for name in ("wave_x", "forth_z", "back_z")
    )
    wave_y, forth_y, back_y, both_x = (
        stack_table(made[name], 0) for name in ("wave_y", "forth_y", "back_y", "both_x")
    )

    tiles = slots // LANES
    length = column_slot.shape[1] // LANES
    coeffs = band_coeffs.reshape(band_count, 2, length, LANES).transpose(0, 2, 1, 3)
    coeffs = coeffs.reshape(band_count, 2 * length, LANES)
    miller = miller_third.reshape(length, LANES)
    slot = column_slot.reshape(length, LANES)
    scale = 2.0 / (column_slot.shape[1] * pws)
    arrived = []
    for band in range(band_count):
        column = column_map if band == 0 else None
        packed = pack_band(
            band, count, coeffs, miller, slot, pencil, slots, column
        )
        arrived.append(exchange(packed, everyone))
    device = lax.axis_index("kpt") * pws + lax.axis_index("pw")
    own = jnp.stack((lax.axis_index("kpt"), device * (parts // 2))).astype(jnp.int32)
    former = chosen = None
    for band in range(band_count):
        forth = forth_y if band == band_count - 1 else None
        made_here = wave_band(
            kpts,
            tiles,
            pws * slots,
            scale,
            own,
            kpoint_counts,
            arrived[band],
            wave_y,
            wave_x,
            forth,
            former,
            chosen,
        )
        former = made_here[0]
        if band == 0:
            kernel, *chosen = made_here[kpts if forth is not None else 1 :][:3]
    half = exchange(made_here[-1].reshape(count, parts, planes, NX), everyone)
    blocks = [made_here[0]] + [
        lax.ppermute(made_here[s], "kpt", [(a, (a + s) % kpts) for a in range(kpts)])
        for s in range(1, kpts)
    ]
    back = poisson(pws, own, kernel, half, forth_z, back_z, both_x)
    back = exchange(back, everyone).reshape(count * parts * 8, LANES)
    return tuple(finish(NZ // pws, NX // kpts, own, back, back_y, blocks))


def fits_planes(kpts, pws):
    count = kpts * pws
    own = NZ // pws
    return (
        NZ % count == 0
        and NZ // count == 8
        and 2 * HALF % (2 * count) == 0
        and NX % kpts == 0
        and own % 8 == 0
        and own // 8 * (NX // kpts) == LANES
    )


def local(band_coeffs, miller_third, column_slot, column_map, kpoint_counts):
    slots = column_map.shape[0]
    plain = slots % LANES == 0 and LANES <= slots <= 8 * RANK_LOW
    plain = plain and column_slot.shape[1] == slots * LANES
    fits = plain and fits_planes(lax.axis_size("kpt"), lax.axis_size("pw"))
    chosen = local_planes if fits else local_general
    return chosen(band_coeffs, miller_third, column_slot, column_map, kpoint_counts)


def solution(mesh):
    return jax.shard_map(
        local,
        mesh=mesh,
        in_specs=(P("kpt", None, None, "pw"), P("kpt", "pw"), P("kpt", "pw"), P("pw"), P()),
        out_specs=(P("pw", "kpt", None), P("pw", "kpt", None)),
        check_vma=False,
    )
```

```python
import functools
import math

import jax
import jax.numpy as jnp
import numpy as np
from jax import lax
from jax.experimental import pallas as pl
from jax.experimental.pallas import tpu as pltpu
from jax.sharding import PartitionSpec as P

NX = 128
NY = 128
NZ = 256


SPACING = 0.25


def contract(pattern, former, latter):
    return jnp.einsum(
        pattern, former, latter, precision=lax.Precision.HIGHEST, preferred_element_type=jnp.float32
    )


def phase_tables(first_index, second_index, length):
    product = first_index[:, None] * second_index[None, :] % length
    angle = product.astype(jnp.float32) * (2.0 * math.pi / length)
    return (jnp.cos(angle), jnp.sin(angle))


def signed_freq(values, length):
    return jnp.where(values >= length // 2, values - length, values)


def coulomb(freq_z, freq_x, freq_y):
    wave_z = freq_z.astype(jnp.float32) / (NZ * SPACING)
    wave_x = freq_x.astype(jnp.float32) / (NX * SPACING)
    wave_y = freq_y.astype(jnp.float32) / (NY * SPACING)
    squared = (2.0 * math.pi) ** 2 * (wave_z * wave_z + wave_x * wave_x + wave_y * wave_y)
    anchor = (freq_z == 0) & (freq_x == 0) & (freq_y == 0)
    return jnp.where(anchor, 0.0, 4.0 * math.pi / jnp.where(anchor, 1.0, squared))


def poisson_columns(real_part, imag_part, freq_x, freq_y):
    length = real_part.shape[0]
    steps_z = jnp.arange(length, dtype=jnp.int32)
    cos_z, sin_z = phase_tables(steps_z, steps_z, length)
    spec_real = contract("zk,km->zm", cos_z, real_part) + contract("zk,km->zm", sin_z, imag_part)
    spec_imag = contract("zk,km->zm", cos_z, imag_part) - contract("zk,km->zm", sin_z, real_part)
    kernel = coulomb(signed_freq(steps_z, length)[:, None], freq_x[None, :], freq_y[None, :]) / (
        NX * NY * NZ
    )
    spec_real = spec_real * kernel
    spec_imag = spec_imag * kernel
    back_real = contract("zk,km->zm", cos_z, spec_real) - contract("zk,km->zm", sin_z, spec_imag)
    back_imag = contract("zk,km->zm", sin_z, spec_real) + contract("zk,km->zm", cos_z, spec_imag)
    return (back_real, back_imag)


def forward_planes(field):
    steps_x = jnp.arange(NX, dtype=jnp.int32)
    steps_y = jnp.arange(NY, dtype=jnp.int32)
    cos_y, sin_y = phase_tables(steps_y, steps_y, NY)
    cos_x, sin_x = phase_tables(steps_x, steps_x, NX)
    half_real = contract("pxy,ky->pxk", field, cos_y)
    half_imag = -contract("pxy,ky->pxk", field, sin_y)
    spec_real = contract("kx,pxy->pky", cos_x, half_real) + contract(
        "kx,pxy->pky", sin_x, half_imag
    )
    spec_imag = contract("kx,pxy->pky", cos_x, half_imag) - contract(
        "kx,pxy->pky", sin_x, half_real
    )
    return (spec_real, spec_imag)


def local_general(band_coeffs, miller_third, column_slot, column_map, kpoint_counts):
    pw_count = lax.axis_size("pw")
    kpt_count = lax.axis_size("kpt")
    pw_index = lax.axis_index("pw")
    kpt_index = lax.axis_index("kpt")
    col_dev = column_map.shape[0]
    ng_dev = column_slot.shape[1]
    band_count = band_coeffs.shape[1]
    z_width = ng_dev // col_dev
    planes = NZ // pw_count
    x_block = NX // kpt_count
    col_total = pw_count * col_dev
    steps_y = jnp.arange(NY, dtype=jnp.int32)
    steps_x = jnp.arange(NX, dtype=jnp.int32)
    cos_y, sin_y = phase_tables(steps_y, steps_y, NY)
    cos_x, sin_x = phase_tables(steps_x, steps_x, NX)
    all_columns = lax.all_gather(column_map, "pw", axis=0, tiled=True)
    position = (miller_third[0] + z_width // 2) * col_dev + column_slot[0]
    source_of = (
        jnp.zeros((ng_dev,), jnp.int32).at[position].set(jnp.arange(ng_dev, dtype=jnp.int32))
    )
    coeff_rows = band_coeffs[0].reshape(band_count * 2, ng_dev).T
    packed = jnp.take(coeff_rows, source_of, axis=0)
    packed = (
        packed.reshape(z_width, col_dev, band_count, 2)
        .transpose(0, 2, 3, 1)
        .reshape(z_width, band_count * 2 * col_dev)
    )
    cos_z, sin_z = phase_tables(
        jnp.arange(NZ, dtype=jnp.int32), jnp.arange(z_width, dtype=jnp.int32) - z_width // 2, NZ
    )
    by_cos = contract("zj,jc->zc", cos_z, packed).reshape(NZ, band_count, 2, col_dev)
    by_sin = contract("zj,jc->zc", sin_z, packed).reshape(NZ, band_count, 2, col_dev)
    pencil = jnp.stack(
        (by_cos[:, :, 0] - by_sin[:, :, 1], by_sin[:, :, 0] + by_cos[:, :, 1]), axis=2
    )
    pencil = pencil.reshape(NZ, band_count * 2 * col_dev)
    arrived = lax.all_to_all(pencil, "pw", split_axis=0, concat_axis=1, tiled=True)
    arrived = arrived.reshape(planes, pw_count, band_count, 2, col_dev).transpose(2, 1, 4, 3, 0)
    arrived = arrived.reshape(band_count, col_total, 2 * planes)
    arrived = jnp.concatenate(
        (arrived, jnp.zeros((band_count, 1, 2 * planes), jnp.float32)), axis=1
    )
    cell_source = (
        jnp.full((NX * NY,), col_total, jnp.int32)
        .at[all_columns]
        .set(jnp.arange(col_total, dtype=jnp.int32))
    )

    def add_band(band, running):
        one_band = lax.dynamic_index_in_dim(arrived, band, 0, keepdims=False)
        placed = jnp.take(one_band, cell_source, axis=0)
        placed = placed.reshape(NX, NY, 2, planes).transpose(2, 3, 0, 1)
        grid_real = placed[0]
        grid_imag = placed[1]
        mixed_real = contract("pxm,ym->pxy", grid_real, cos_y) - contract(
            "pxm,ym->pxy", grid_imag, sin_y
        )
        mixed_imag = contract("pxm,ym->pxy", grid_real, sin_y) + contract(
            "pxm,ym->pxy", grid_imag, cos_y
        )
        wave_real = contract("xm,pmy->pxy", cos_x, mixed_real) - contract(
            "xm,pmy->pxy", sin_x, mixed_imag
        )
        wave_imag = contract("xm,pmy->pxy", sin_x, mixed_real) + contract(
            "xm,pmy->pxy", cos_x, mixed_imag
        )
        return running + wave_real * wave_real + wave_imag * wave_imag

    squares_sum = lax.fori_loop(0, band_count, add_band, jnp.zeros((planes, NX, NY), jnp.float32))
    weight = (
        2.0
        * kpoint_counts[kpt_index].astype(jnp.float32)
        / jnp.sum(kpoint_counts).astype(jnp.float32)
    )
    weight = weight / (ng_dev * pw_count)
    partial_value = weight * squares_sum
    total_density = lax.psum(partial_value, "kpt")
    density = lax.dynamic_slice_in_dim(total_density, kpt_index * x_block, x_block, 1)
    spec_real, spec_imag = forward_planes(total_density)
    rows_pw = NX // pw_count
    pencil_real, pencil_imag = (
        lax.all_to_all(spec_real, "pw", split_axis=1, concat_axis=0, tiled=True),
        lax.all_to_all(spec_imag, "pw", split_axis=1, concat_axis=0, tiled=True),
    )
    local_x = pw_index * rows_pw + jnp.arange(rows_pw, dtype=jnp.int32)
    freq_x = jnp.repeat(signed_freq(local_x, NX), NY)
    freq_y = jnp.tile(signed_freq(steps_y, NY), rows_pw)
    back_real, back_imag = poisson_columns(
        pencil_real.reshape(NZ, rows_pw * NY), pencil_imag.reshape(NZ, rows_pw * NY), freq_x, freq_y
    )
    plane_real, plane_imag = (
        lax.all_to_all(
            back_real.reshape(NZ, rows_pw, NY), "pw", split_axis=0, concat_axis=1, tiled=True
        ),
        lax.all_to_all(
            back_imag.reshape(NZ, rows_pw, NY), "pw", split_axis=0, concat_axis=1, tiled=True
        ),
    )
    own_rows = kpt_index * x_block + jnp.arange(x_block, dtype=jnp.int32)
    cos_rows, sin_rows = phase_tables(own_rows, steps_x, NX)
    rows_real = contract("xk,pky->pxy", cos_rows, plane_real) - contract(
        "xk,pky->pxy", sin_rows, plane_imag
    )
    rows_imag = contract("xk,pky->pxy", sin_rows, plane_real) + contract(
        "xk,pky->pxy", cos_rows, plane_imag
    )
    hartree = contract("pxk,yk->pxy", rows_real, cos_y) - contract("pxk,yk->pxy", rows_imag, sin_y)
    return (density, hartree)


LANES = 128
HALF = 64
VMEM_LIMIT = 16 * 1024 * 1024
NN = (((1,), (0,)), ((), ()))
NT = (((1,), (1,)), ((), ()))
TN = (((0,), (0,)), ((), ()))


def pieces(value):
    high = value.astype(jnp.bfloat16)
    low = (value - high.astype(jnp.float32)).astype(jnp.bfloat16)
    return high, low


def mul(former, latter, dims):
    return lax.dot_general(former, latter, dims, preferred_element_type=jnp.float32)


def mul3_left(former, latter, dims):
    high, low = pieces(latter)
    (unused,), (axis,) = dims[0]
    return mul(former, jnp.concatenate((high, high, low), axis=axis), dims)


def mul3_right(former, latter, dims):
    high, low = pieces(former)
    (axis,), (unused,) = dims[0]
    return mul(jnp.concatenate((high, high, low), axis=axis), latter, dims)


def stack_table(values, axis):
    high = values.astype(np.float32).astype(jnp.bfloat16)
    low = (values - high.astype(np.float64)).astype(np.float32).astype(jnp.bfloat16)
    return jnp.asarray(np.concatenate((high, low, high), axis=axis))


def angles(former, latter, length):
    return np.outer(former, latter) % length * (2.0 * np.pi / length)


def tables(kpts, pws, planes):
    count = kpts * pws
    low_freq = np.arange(HALF) - HALF // 2
    grid_x, grid_y, grid_z = np.arange(NX), np.arange(NY), np.arange(NZ)
    own_y = np.arange(HALF)

    device = np.arange(count)
    plane_of = (
        (device % pws)[:, None] * (NZ // pws)
        + (device // pws)[:, None] * planes
        + np.arange(planes)[None, :]
    )
    return_table = {}

    def pencil(z_width):
        angle = angles(plane_of.ravel(), np.arange(z_width) - z_width // 2, NZ)
        cos, sin = (
            part.reshape(count, 1, planes, z_width) for part in (np.cos(angle), np.sin(angle))
        )
        real = np.concatenate((cos, -sin), axis=3)
        imag = np.concatenate((sin, cos), axis=3)
        return np.concatenate((real, imag), axis=1).reshape(-1, 2 * z_width)

    return_table["pencil"] = pencil

    angle = angles(low_freq, grid_y, NY)
    cos, sin = np.cos(angle), np.sin(angle)
    return_table["wave_y"] = np.block([[cos, sin], [-sin, cos]])

    angle = angles(grid_x, low_freq, NX)
    cos, sin = np.cos(angle), np.sin(angle)
    return_table["wave_x"] = np.block([[cos, -sin], [sin, cos]])

    angle = angles(own_y, grid_y, NY)
    cos, sin = np.cos(angle), np.sin(angle)
    return_table["forth_y"] = np.stack((cos, -sin), axis=1).reshape(2 * HALF, NY).T
    twice = np.where(own_y == 0, 1.0, 2.0)[:, None]
    return_table["back_y"] = np.stack((twice * cos, -twice * sin), axis=1).reshape(2 * HALF, NY)

    angle = angles(grid_z, plane_of.ravel(), NZ)
    return_table["forth_z"] = np.concatenate((np.cos(angle), np.sin(angle)), axis=0)
    own = NZ // pws
    merged = own // 8
    order = (
        np.arange(pws)[None, :, None] * own
        + np.arange(8)[None, None, :] * merged
        + np.arange(merged)[:, None, None]
    )
    angle = angles(order.ravel(), grid_z, NZ)
    return_table["back_z"] = np.concatenate((np.cos(angle), np.sin(angle)), axis=0)

    angle = angles(grid_x, grid_x, NX)
    return_table["both_x"] = np.concatenate((np.cos(angle), np.sin(angle)), axis=1)
    return return_table


def ramp(shape, axis, first=0):
    steps = lax.broadcasted_iota(jnp.int32, shape, axis) + first
    return steps.astype(jnp.float32).astype(jnp.bfloat16)


def sixteen(row):
    return jnp.broadcast_to(row, (16, row.shape[1])).astype(jnp.bfloat16)


def one_hot_lanes(row, ramps):
    column = jnp.transpose(jnp.concatenate([sixteen(row)] * (LANES // 16), axis=0))
    one = jnp.ones(column.shape, jnp.bfloat16)
    zero = jnp.zeros(column.shape, jnp.bfloat16)
    return jnp.concatenate(
        [
            jnp.where(column == ramps[:, first : first + LANES], one, zero)
            for first in range(0, ramps.shape[1], LANES)
        ],
        axis=1,
    )


RANK_LOW = 64
WINDOW = 64


def exchange_rows(refs, low_bits, size_bits, descending):
    for outer in range(RANK_LOW):
        if any(outer >> bit & 1 for bit in low_bits[0]):
            continue
        touched = sorted(
            outer + sum(1 << bit for i, bit in enumerate(low_bits[0]) if pattern >> i & 1)
            for pattern in range(1 << len(low_bits[0]))
        )
        held = {v: [ref[v * 8 : v * 8 + 8, :] for ref in refs] for v in touched}
        for size, bits in zip(size_bits, low_bits[1:]):
            for bit in bits:
                for v in touched:
                    if v >> bit & 1:
                        continue
                    former, latter = held[v], held[v | 1 << bit]
                    if size < 6:
                        down = bool(v >> size & 1)
                        swap = former[0] < latter[0] if down else former[0] > latter[0]
                    else:
                        swap = former[0] > latter[0]
                        if descending is not None:
                            swap = jnp.logical_xor(swap, descending)
                    held[v] = [jnp.where(swap, y, x) for x, y in zip(former, latter)]
                    held[v | 1 << bit] = [jnp.where(swap, x, y) for x, y in zip(former, latter)]
        for v in touched:
            for ref, value in zip(refs, held[v]):
                ref[v * 8 : v * 8 + 8, :] = value


def exchange_sublanes(refs, stride, descending):
    sublane = lax.broadcasted_iota(jnp.int32, (8, LANES), 0)
    upper = sublane // stride % 2 == 1
    want_most = upper if descending is None else jnp.logical_xor(upper, descending)
    other = jnp.where(upper, sublane - stride, sublane + stride)

    for v in range(RANK_LOW):
        here = [ref[v * 8 : v * 8 + 8, :] for ref in refs]
        there = [jnp.take_along_axis(value, other, axis=0) for value in here]
        take = jnp.logical_xor(here[0] > there[0], want_most)
        for ref, x, y in zip(refs, here, there):
            ref[v * 8 : v * 8 + 8, :] = jnp.where(take, y, x)


def sort_columns(refs):
    sublane = lax.broadcasted_iota(jnp.int32, (8, LANES), 0)
    exchange_rows(refs, [(0, 1, 2), (0,), (1, 0), (2, 1, 0)], [1, 2, 3], None)
    exchange_rows(refs, [(3,), (3,)], [4], None)
    exchange_rows(refs, [(0, 1, 2), (2, 1, 0)], [4], None)
    exchange_rows(refs, [(3, 4), (4, 3)], [5], None)
    exchange_rows(refs, [(0, 1, 2), (2, 1, 0)], [5], None)
    for size in range(6, 10):
        descending = None if size == 9 else sublane // (1 << (size - 6)) % 2 == 1
        for bit in range(size - 1, 5, -1):
            exchange_sublanes(refs, 1 << (bit - 6), descending)
        exchange_rows(refs, [(3, 4, 5), (5, 4, 3)], [size], descending)
        exchange_rows(refs, [(0, 1, 2), (2, 1, 0)], [size], descending)


def pack_kernel(width, has_column, *refs):
    coeff_ref, miller_ref, slot_ref, pencil_ref = refs[:4]
    rest = list(refs[4:])
    column_ref = rest.pop(0) if has_column else None
    out_ref, total, key_ref, real_ref, imag_ref, lane_ref, real_low, imag_low, ramp_ref, step_ref, held, sem = rest
    fetch = pltpu.make_async_copy(pencil_ref, held, sem)
    fetch.start()
    half = total.shape[0] // 4
    slots = 2 * half
    count = out_ref.shape[0]
    rows = pencil_ref.shape[0] // count
    length = miller_ref.shape[0]
    ranks = key_ref.shape[0]

    slot = slot_ref[...]
    second = slot >= half
    lane = miller_ref[...] + width // 2
    key = jnp.where(second, slot - half, slot) * (2 * width) + jnp.where(second, lane + width, lane)
    key_ref[0:length] = key.astype(jnp.float32)
    real_ref[0:length] = coeff_ref[0, pl.ds(0, length, stride=2), :]
    imag_ref[0:length] = coeff_ref[0, pl.ds(1, length, stride=2), :]
    blank = jnp.zeros((ranks - length, LANES), jnp.float32)
    key_ref[length:] = blank + 2.0 * slots * width
    real_ref[length:] = blank
    imag_ref[length:] = blank
    sort_columns((key_ref, real_ref, imag_ref))

    def base_of(block):
        base = 8 * (block // 2) + 8 * (block % 2) - WINDOW // 2
        return jnp.minimum(jnp.maximum(base, 0), half - WINDOW)

    ramp_ref[...] = ramp(ramp_ref.shape, 1)
    step_ref[...] = ramp(step_ref.shape, 0)
    sublane = lax.broadcasted_iota(jnp.int32, (8, LANES), 0)
    astray = jnp.zeros((8, LANES), jnp.float32)
    for v in range(RANK_LOW):
        at = slice(v * 8, v * 8 + 8)
        keys = key_ref[at, :]
        high = jnp.floor(keys * (1.0 / (2 * width)))
        lane_ref[at, :] = keys - high * (2.0 * width)
        key_ref[at, :] = high
        for ref, low_ref in ((real_ref, real_low), (imag_ref, imag_low)):
            value = ref[at, :]
            rounded = value.astype(jnp.bfloat16).astype(jnp.float32)
            ref[at, :] = rounded
            low_ref[at, :] = value - rounded
        offset = high - base_of(sublane * (RANK_LOW // 8) + v // 8).astype(jnp.float32)
        outside = jnp.logical_or(offset < 0.0, offset >= 1.0 * WINDOW)
        astray = jnp.where(outside, 1.0, astray)
    astray = jnp.max(jnp.where(sublane * RANK_LOW < length, astray, 0.0))

    def add(block, base, window):
        first = block % (RANK_LOW // 8) * 64 + block // (RANK_LOW // 8)
        base_row = jnp.full((1, LANES), base, jnp.int32).astype(jnp.float32)
        zero = jnp.zeros((16, LANES), jnp.bfloat16)
        spread, chosen = [], []
        for t in range(8):
            row = pl.ds(first + 8 * t, 1)
            high = sixteen(key_ref[row, :] - base_row)
            masks = [high == step_ref[r : r + 16, :] for r in range(0, window, 16)]
            spread.append(
                jnp.concatenate(
                    [
                        jnp.where(mask, value, zero)
                        for value in [
                            sixteen(ref[row, :]) for ref in (real_ref, imag_ref, real_low, imag_low)
                        ]
                        for mask in masks
                    ],
                    axis=0,
                )
            )
            chosen.append(one_hot_lanes(lane_ref[row, :], ramp_ref[...]))
        found = mul(jnp.concatenate(spread, axis=1), jnp.concatenate(chosen, axis=0), NN)
        for i in range(4):
            if window == half:
                into = pl.ds(i * half, half)
            else:
                into = pl.ds(pl.multiple_of(i * half + base, 8), window)
            total[into, :] += found[i * window : (i + 1) * window]

    total[...] = jnp.zeros_like(total)
    blocks = length // 8
    together = 4 if blocks % 4 == 0 else 1

    @pl.when(astray == 0.0)
    def _():
        def some_blocks(i, unused):
            for s in range(together):
                block = together * i + s
                add(block, base_of(block), WINDOW)
            return unused

        lax.fori_loop(0, blocks // together, some_blocks, 0)

    @pl.when(astray > 0.0)
    def _():
        def one_block(block, unused):
            add(block, 0, half)
            return unused

        lax.fori_loop(0, blocks, one_block, 0)

    both = []
    for at in range(2):
        parts = [
            total[(2 * at + c) * half : (2 * at + c + 1) * half].astype(jnp.bfloat16)
            for c in range(2)
        ]
        both.append(
            jnp.concatenate(
                [
                    jnp.concatenate([part[:, h * width : (h + 1) * width] for part in parts], axis=1)
                    for h in range(2)
                ],
                axis=0,
            )
        )
    fetch.wait()
    pencils = mul(held[...], jnp.concatenate((both[0], both[0], both[1]), axis=1), NT)
    tiles = slots // LANES
    for t in range(tiles):
        tile = pencils[:, t * LANES : (t + 1) * LANES].reshape(count, rows, LANES)
        if not has_column:
            out_ref[:, t * rows : (t + 1) * rows] = tile
            continue
        for g in range(rows // 4):
            out_ref[:, t * (rows // 4) + g] = tile[:, 4 * g : 4 * g + 4]
    if has_column:
        column = [
            column_ref[t * LANES : (t + 1) * LANES].astype(jnp.float32).reshape(1, LANES)
            for t in range(tiles)
        ]
        column = jnp.concatenate(column + [jnp.zeros((4 - tiles, LANES), jnp.float32)], axis=0)
        out_ref[:, tiles * rows // 4] = jnp.broadcast_to(column[None], (count, 4, LANES))


def pack_band(band, count, coeffs, miller, slot, pencil, slots, column):
    length = miller.shape[0]
    width = pencil.shape[1] // 6
    rows = pencil.shape[0] // count * (slots // LANES)
    operands = [coeffs, miller, slot, pencil]
    out_shape = (count, rows, LANES)
    if column is not None:
        operands.append(column)
        out_shape = (count, rows // 4 + 1, 4, LANES)
    one_band = pl.BlockSpec((1, 2 * length, LANES), lambda i: (band, 0, 0))
    return pl.pallas_call(
        functools.partial(pack_kernel, width, column is not None),
        grid=(1,),
        in_specs=[one_band]
        + [
            pl.BlockSpec(memory_space=pl.ANY)
            if x is pencil
            else pl.BlockSpec(x.shape, lambda i, n=x.ndim: (0,) * n)
            for x in operands[1:]
        ],
        out_specs=pl.BlockSpec(out_shape, lambda i: (0,) * len(out_shape)),
        out_shape=jax.ShapeDtypeStruct(out_shape, jnp.float32),
        scratch_shapes=[pltpu.VMEM((2 * slots, 2 * width), jnp.float32)]
        + [pltpu.VMEM((8 * RANK_LOW, LANES), jnp.float32)] * 6
        + [
            pltpu.VMEM((LANES, 2 * width), jnp.bfloat16),
            pltpu.VMEM((slots // 2, LANES), jnp.bfloat16),
            pltpu.VMEM(pencil.shape, jnp.bfloat16),
            pltpu.SemaphoreType.DMA,
        ],
        compiler_params=pltpu.CompilerParams(vmem_limit_bytes=VMEM_LIMIT),
        cost_estimate=pl.CostEstimate(
            flops=2 * length * LANES * slots * 4 * width,
            bytes_accessed=16 * length * LANES,
            transcendentals=0,
        ),
        name="pack_band",
    )(*operands)


def wave_kernel(kpts, tiles, scale, is_first, is_last, *refs):
    own_ref, count_ref, came_ref, wave_y_ref, wave_x_ref = refs[:5]
    rest = list(refs[5:])
    forth_ref = rest.pop(0) if is_last else None
    former_ref, chosen_ref, high_ref = (None,) * 3 if is_first else [rest.pop(0) for _ in range(3)]
    density_refs = [rest.pop(0) for _ in range(kpts if is_last else 1)]
    if is_first:
        coulomb_ref, chosen_ref, high_ref = rest.pop(0), rest.pop(0), rest.pop(0)
    send_ref = rest.pop(0) if is_last else None
    values, grid, whole = rest
    planes = density_refs[0].shape[0]
    block = NX // kpts
    part_rows = 2 * planes
    pws = came_ref.shape[0] // kpts
    rows = kpts * part_rows
    total = values.shape[1]

    for j in range(pws):
        for t in range(tiles):
            if is_first:
                groups = [
                    came_ref[k * pws + j, t * (part_rows // 4) + g]
                    for k in range(kpts)
                    for g in range(part_rows // 4)
                ]
            else:
                groups = [
                    came_ref[k * pws + j, t * part_rows : (t + 1) * part_rows] for k in range(kpts)
                ]
            taken = jnp.concatenate(groups, axis=0)
            high, low = pieces(taken)
            first = (j * tiles + t) * LANES
            values[0:rows, first : first + LANES] = high
            values[rows : 2 * rows, first : first + LANES] = low

    tile = 4 * HALF
    if is_first:
        ramps = ramp((LANES, tile), 1)
        for j in range(pws):
            for t in range(tiles):
                column = came_ref[j, tiles * part_rows // 4, t : t + 1]
                column = column.astype(jnp.int32)
                cell = ((column // NY + NX // 2) % NX - HALF // 2) * HALF
                cell = cell + (column % NY + NY // 2) % NY - HALF // 2
                first = (j * tiles + t) * LANES
                lane = (cell % tile).astype(jnp.float32)
                chosen_ref[first : first + LANES, :] = one_hot_lanes(lane, ramps)
                high_ref[:, first : first + LANES] = sixteen((cell // tile).astype(jnp.float32))
        step_z = lax.broadcasted_iota(jnp.int32, (NZ, NX), 0)
        step_x = lax.broadcasted_iota(jnp.int32, (NZ, NX), 1)
        for q in range(coulomb_ref.shape[0]):
            freq_y = jnp.full((NZ, NX), own_ref[1] + q, jnp.int32)
            kernel = coulomb(signed_freq(step_z, NZ), signed_freq(step_x, NX), freq_y)
            coulomb_ref[q] = kernel * (1.0 / (NX * NY * NZ))
    left = lax.broadcasted_iota(jnp.int32, (planes, LANES), 1) < HALF
    together = 4

    def place(t, found):
        found = found[:rows] + found[rows:]
        for h in range(2):
            for k in range(kpts):
                real, imag = (
                    found[(2 * k + c) * planes : (2 * k + c + 1) * planes, h * LANES : (h + 1) * LANES]
                    for c in range(2)
                )
                first = (k * HALF + 4 * t + 2 * h) * planes
                grid[first : first + planes, :] = jnp.where(left, real, pltpu.roll(imag, HALF, 1))
                grid[first + planes : first + 2 * planes, :] = jnp.where(
                    left, pltpu.roll(real, HALF, 1), imag
                )

    high = high_ref[...]
    zero = jnp.zeros_like(high)
    for start in range(0, HALF // 4, together):
        kept = []
        for t in range(start, start + together):
            here = high == jnp.full_like(high, t)
            kept += [jnp.where(here, values[r : r + 16, :], zero) for r in range(0, 2 * rows, 16)]
        found = mul(jnp.concatenate(kept, axis=0), chosen_ref[...], NN)
        for s in range(together):
            place(start + s, found[2 * rows * s : 2 * rows * (s + 1)])

    sum_of = count_ref[0]
    for k in range(1, kpts):
        sum_of = sum_of + count_ref[k]

    def spread(number):
        return jnp.full((8, NY), number, jnp.int32).astype(jnp.float32)

    weights = [
        jnp.concatenate([spread(count_ref[k]) / spread(sum_of) * scale] * (NX // 8), axis=0)
        for k in range(kpts)
    ]
    lines = [grid[pl.ds(p, kpts * HALF, stride=planes), :] for p in range(planes)]
    lines = mul3_right(jnp.concatenate(lines, axis=0), wave_y_ref[...], NN)

    for p in range(planes):
        mixed = lines[p * kpts * HALF : (p + 1) * kpts * HALF]
        mixed = jnp.concatenate(
            [
                jnp.concatenate(
                    [mixed[k * HALF : (k + 1) * HALF, c * NY : (c + 1) * NY] for k in range(kpts)],
                    axis=1,
                )
                for c in range(2)
            ],
            axis=0,
        )
        wave = mul3_left(wave_x_ref[...], mixed, NN)
        square = wave[:NX] * wave[:NX] + wave[NX:] * wave[NX:]
        density = weights[0] * square[:, :NY]
        for k in range(1, kpts):
            density = density + weights[k] * square[:, k * NY : (k + 1) * NY]
        if former_ref is not None:
            density = density + former_ref[p]
        if is_last:
            whole[p] = density
        else:
            density_refs[0][p] = density

    if is_last:
        for s, density_ref in enumerate(density_refs):
            first = pl.multiple_of(lax.rem(own_ref[0] + s, kpts) * block, block)
            density_ref[...] = whole[:, pl.ds(first, block), :]
        level = jnp.mean(whole[0, :8, :], axis=(0, 1), keepdims=True)
        field = whole[...].reshape(planes * NX, NY) - level
        half = mul3_right(field, forth_ref[...], NN)
        first_row = lax.broadcasted_iota(jnp.int32, (2 * HALF, NX), 0) == 0
        for p in range(planes):
            turned = jnp.transpose(half[p * NX : (p + 1) * NX])
            turned = turned + jnp.where(first_row, level * NY, 0.0)
            send_ref[pl.ds(p, 2 * HALF, stride=planes), :] = turned


def wave_band(kpts, tiles, total, scale, own, counts, came, wave_y, wave_x, forth, former, chosen):
    planes = NZ // came.shape[0]
    block = NX // kpts
    is_first, is_last = former is None, forth is not None
    vmem = pl.BlockSpec(memory_space=pltpu.VMEM)
    operands = [own, counts, came, wave_y, wave_x]
    if is_last:
        operands.append(forth)
    if not is_first:
        operands += [former, *chosen]
    if is_last:
        out_shape = [jax.ShapeDtypeStruct((planes, block, NY), jnp.float32)] * kpts
    else:
        out_shape = [jax.ShapeDtypeStruct((planes, NX, NY), jnp.float32)]
    if is_first:
        out_shape.append(jax.ShapeDtypeStruct((HALF // came.shape[0], NZ, NX), jnp.float32))
        out_shape.append(jax.ShapeDtypeStruct((total, 4 * HALF), jnp.bfloat16))
        out_shape.append(jax.ShapeDtypeStruct((16, total), jnp.bfloat16))
    if is_last:
        out_shape.append(jax.ShapeDtypeStruct((2 * HALF * planes, NX), jnp.float32))
    rows = kpts * 2 * planes
    return pl.pallas_call(
        functools.partial(wave_kernel, kpts, tiles, scale, is_first, is_last),
        in_specs=[pl.BlockSpec(memory_space=pltpu.SMEM)] * 2 + [vmem] * (len(operands) - 2),
        out_specs=[vmem] * len(out_shape),
        out_shape=out_shape,
        scratch_shapes=[
            pltpu.VMEM((2 * rows, total), jnp.bfloat16),
            pltpu.VMEM((kpts * planes * HALF, LANES), jnp.float32),
            pltpu.VMEM((planes, NX, NY), jnp.float32),
        ],
        compiler_params=pltpu.CompilerParams(vmem_limit_bytes=VMEM_LIMIT),
        cost_estimate=pl.CostEstimate(
            flops=4 * rows * total * HALF * HALF, bytes_accessed=4 * came.size, transcendentals=0
        ),
        name="wave_band",
    )(*operands)


def poisson_kernel(pws, own_ref, kernel_ref, came_ref, forth_ref, back_ref, both_x_ref, send_ref):
    count, parts, planes, unused = came_ref.shape
    pairs = parts // 2
    fields = [came_ref[:, i].reshape(NZ, NX) for i in range(parts)]
    level = jnp.mean(fields[0], axis=(0, 1), keepdims=True)
    fields[0] = fields[0] - jnp.where(own_ref[1] == 0, level, 0.0)
    field = jnp.concatenate(fields, axis=1)
    turned = mul3_left(forth_ref[...], field, NN)

    def part(array, half, i):
        return array[half * NZ : (half + 1) * NZ, i * NX : (i + 1) * NX]

    lines = []
    for q in range(pairs):
        lines.append(part(turned, 0, 2 * q) + part(turned, 1, 2 * q + 1))
        lines.append(part(turned, 0, 2 * q + 1) - part(turned, 1, 2 * q))
    spectrum = mul3_right(jnp.concatenate(lines, axis=0), both_x_ref[...], NN)

    lines = []
    for q in range(pairs):
        real = spectrum[2 * q * NZ : (2 * q + 1) * NZ]
        imag = spectrum[(2 * q + 1) * NZ : (2 * q + 2) * NZ]
        kernel = kernel_ref[q]
        lines.append((real[:, :NX] + imag[:, NX:]) * kernel)
        lines.append((imag[:, :NX] - real[:, NX:]) * kernel)
    turned = mul3_right(jnp.concatenate(lines, axis=0), both_x_ref[...], NN)
    lines = []
    for q in range(pairs):
        real = turned[2 * q * NZ : (2 * q + 1) * NZ]
        imag = turned[(2 * q + 1) * NZ : (2 * q + 2) * NZ]
        lines.append(real[:, :NX] - imag[:, NX:])
        lines.append(real[:, NX:] + imag[:, :NX])
    turned = mul3_left(back_ref[...], jnp.concatenate(lines, axis=1), NN)

    kpts = count // pws
    merged = NZ // pws // 8
    block = NX // kpts
    rows = pws * 8
    lane = lax.broadcasted_iota(jnp.int32, (rows, LANES), 1) // block
    for q in range(pairs):
        real = part(turned, 0, 2 * q) - part(turned, 1, 2 * q + 1)
        imag = part(turned, 0, 2 * q + 1) + part(turned, 1, 2 * q)
        for c, value in enumerate((real, imag)):
            for a in range(kpts):
                packed = None
                for m in range(merged):
                    piece = value[m * rows : (m + 1) * rows]
                    shift = (m - a) * block % LANES
                    if shift:
                        piece = pltpu.roll(piece, shift, 1)
                    packed = piece if m == 0 else jnp.where(lane == m, piece, packed)
                send_ref[a * pws : (a + 1) * pws, 2 * q + c] = packed.reshape(pws, 8, LANES)


def poisson(pws, own, kernel, came, forth, back, both_x):
    vmem = pl.BlockSpec(memory_space=pltpu.VMEM)
    count, parts, unused, unused = came.shape
    return pl.pallas_call(
        functools.partial(poisson_kernel, pws),
        in_specs=[pl.BlockSpec(memory_space=pltpu.SMEM)] + [vmem] * 5,
        out_specs=vmem,
        out_shape=jax.ShapeDtypeStruct((count, parts, 8, LANES), jnp.float32),
        compiler_params=pltpu.CompilerParams(vmem_limit_bytes=VMEM_LIMIT),
        name="poisson",
    )(own, kernel, came, forth, back, both_x)


def finish_kernel(own_ref, came_ref, back_ref, *refs):
    block_refs, density_ref, out_ref = refs[:-2], refs[-2], refs[-1]
    kpts = len(block_refs)
    planes, block, unused = out_ref.shape
    merged = planes // 8
    for s, block_ref in enumerate(block_refs):
        sender = lax.rem(own_ref[0] + kpts - s, kpts)
        density_ref[pl.ds(sender * (planes // kpts), planes // kpts)] = block_ref[...]
    for h in range(8):
        lines = came_ref[pl.ds(h, 2 * HALF, stride=8), :]
        field = mul3_right(lines, back_ref[...], TN)
        out_ref[h * merged : (h + 1) * merged] = field.reshape(merged, block, NY)


def finish(planes, block, own, came, back_y, blocks):
    vmem = pl.BlockSpec(memory_space=pltpu.VMEM)
    return pl.pallas_call(
        finish_kernel,
        in_specs=[pl.BlockSpec(memory_space=pltpu.SMEM)] + [vmem] * (2 + len(blocks)),
        out_specs=[vmem] * 2,
        out_shape=[jax.ShapeDtypeStruct((planes, block, NY), jnp.float32)] * 2,
        compiler_params=pltpu.CompilerParams(vmem_limit_bytes=VMEM_LIMIT),
        name="finish",
    )(own, came, back_y, *blocks)


def exchange(array, axes):
    return lax.all_to_all(array, axes, split_axis=0, concat_axis=0, tiled=True)


def local_planes(band_coeffs, miller_third, column_slot, column_map, kpoint_counts):
    pws = lax.axis_size("pw")
    kpts = lax.axis_size("kpt")
    count = pws * kpts
    everyone = ("kpt", "pw")
    slots = column_map.shape[0]
    band_count = band_coeffs.shape[1]
    z_width = column_slot.shape[1] // slots
    planes = NZ // count
    parts = 2 * HALF // count
    made = tables(kpts, pws, planes)
    pencil = stack_table(made["pencil"](z_width), 1)
    wave_x, forth_z, back_z = (
        stack_table(made[name], 1) for name in ("wave_x", "forth_z", "back_z")
    )
    wave_y, forth_y, back_y, both_x = (
        stack_table(made[name], 0) for name in ("wave_y", "forth_y", "back_y", "both_x")
    )

    tiles = slots // LANES
    length = column_slot.shape[1] // LANES
    coeffs = band_coeffs.reshape(band_count, 2, length, LANES).transpose(0, 2, 1, 3)
    coeffs = coeffs.reshape(band_count, 2 * length, LANES)
    miller = miller_third.reshape(length, LANES)
    slot = column_slot.reshape(length, LANES)
    scale = 2.0 / (column_slot.shape[1] * pws)
    arrived = []
    for band in range(band_count):
        column = column_map if band == 0 else None
        packed = pack_band(
            band, count, coeffs, miller, slot, pencil, slots, column
        )
        arrived.append(exchange(packed, everyone))
    device = lax.axis_index("kpt") * pws + lax.axis_index("pw")
    own = jnp.stack((lax.axis_index("kpt"), device * (parts // 2))).astype(jnp.int32)
    former = chosen = None
    for band in range(band_count):
        forth = forth_y if band == band_count - 1 else None
        made_here = wave_band(
            kpts,
            tiles,
            pws * slots,
            scale,
            own,
            kpoint_counts,
            arrived[band],
            wave_y,
            wave_x,
            forth,
            former,
            chosen,
        )
        former = made_here[0]
        if band == 0:
            kernel, *chosen = made_here[kpts if forth is not None else 1 :][:3]
    half = exchange(made_here[-1].reshape(count, parts, planes, NX), everyone)
    blocks = [made_here[0]] + [
        lax.ppermute(made_here[s], "kpt", [(a, (a + s) % kpts) for a in range(kpts)])
        for s in range(1, kpts)
    ]
    back = poisson(pws, own, kernel, half, forth_z, back_z, both_x)
    back = exchange(back, everyone).reshape(count * parts * 8, LANES)
    return tuple(finish(NZ // pws, NX // kpts, own, back, back_y, blocks))


def fits_planes(kpts, pws):
    count = kpts * pws
    own = NZ // pws
    return (
        NZ % count == 0
        and NZ // count == 8
        and 2 * HALF % (2 * count) == 0
        and NX % kpts == 0
        and own % 8 == 0
        and own // 8 * (NX // kpts) == LANES
    )


def local(band_coeffs, miller_third, column_slot, column_map, kpoint_counts):
    slots = column_map.shape[0]
    plain = slots % LANES == 0 and LANES <= slots <= 8 * RANK_LOW
    plain = plain and column_slot.shape[1] == slots * LANES
    fits = plain and fits_planes(lax.axis_size("kpt"), lax.axis_size("pw"))
    chosen = local_planes if fits else local_general
    return chosen(band_coeffs, miller_third, column_slot, column_map, kpoint_counts)


def solution(mesh):
    return jax.shard_map(
        local,
        mesh=mesh,
        in_specs=(P("kpt", None, None, "pw"), P("kpt", "pw"), P("kpt", "pw"), P("pw"), P()),
        out_specs=(P("pw", "kpt", None), P("pw", "kpt", None)),
        check_vma=False,
    )
```

```python
import functools
import math

import jax
import jax.numpy as jnp
import numpy as np
from jax import lax
from jax.experimental import pallas as pl
from jax.experimental.pallas import tpu as pltpu
from jax.sharding import PartitionSpec as P

NX = 128
NY = 128
NZ = 256


SPACING = 0.25


def contract(pattern, former, latter):
    return jnp.einsum(
        pattern, former, latter, precision=lax.Precision.HIGHEST, preferred_element_type=jnp.float32
    )


def phase_tables(first_index, second_index, length):
    product = first_index[:, None] * second_index[None, :] % length
    angle = product.astype(jnp.float32) * (2.0 * math.pi / length)
    return (jnp.cos(angle), jnp.sin(angle))


def signed_freq(values, length):
    return jnp.where(values >= length // 2, values - length, values)


def coulomb(freq_z, freq_x, freq_y):
    wave_z = freq_z.astype(jnp.float32) / (NZ * SPACING)
    wave_x = freq_x.astype(jnp.float32) / (NX * SPACING)
    wave_y = freq_y.astype(jnp.float32) / (NY * SPACING)
    squared = (2.0 * math.pi) ** 2 * (wave_z * wave_z + wave_x * wave_x + wave_y * wave_y)
    anchor = (freq_z == 0) & (freq_x == 0) & (freq_y == 0)
    return jnp.where(anchor, 0.0, 4.0 * math.pi / jnp.where(anchor, 1.0, squared))


def poisson_columns(real_part, imag_part, freq_x, freq_y):
    length = real_part.shape[0]
    steps_z = jnp.arange(length, dtype=jnp.int32)
    cos_z, sin_z = phase_tables(steps_z, steps_z, length)
    spec_real = contract("zk,km->zm", cos_z, real_part) + contract("zk,km->zm", sin_z, imag_part)
    spec_imag = contract("zk,km->zm", cos_z, imag_part) - contract("zk,km->zm", sin_z, real_part)
    kernel = coulomb(signed_freq(steps_z, length)[:, None], freq_x[None, :], freq_y[None, :]) / (
        NX * NY * NZ
    )
    spec_real = spec_real * kernel
    spec_imag = spec_imag * kernel
    back_real = contract("zk,km->zm", cos_z, spec_real) - contract("zk,km->zm", sin_z, spec_imag)
    back_imag = contract("zk,km->zm", sin_z, spec_real) + contract("zk,km->zm", cos_z, spec_imag)
    return (back_real, back_imag)


def forward_planes(field):
    steps_x = jnp.arange(NX, dtype=jnp.int32)
    steps_y = jnp.arange(NY, dtype=jnp.int32)
    cos_y, sin_y = phase_tables(steps_y, steps_y, NY)
    cos_x, sin_x = phase_tables(steps_x, steps_x, NX)
    half_real = contract("pxy,ky->pxk", field, cos_y)
    half_imag = -contract("pxy,ky->pxk", field, sin_y)
    spec_real = contract("kx,pxy->pky", cos_x, half_real) + contract(
        "kx,pxy->pky", sin_x, half_imag
    )
    spec_imag = contract("kx,pxy->pky", cos_x, half_imag) - contract(
        "kx,pxy->pky", sin_x, half_real
    )
    return (spec_real, spec_imag)


def local_general(band_coeffs, miller_third, column_slot, column_map, kpoint_counts):
    pw_count = lax.axis_size("pw")
    kpt_count = lax.axis_size("kpt")
    pw_index = lax.axis_index("pw")
    kpt_index = lax.axis_index("kpt")
    col_dev = column_map.shape[0]
    ng_dev = column_slot.shape[1]
    band_count = band_coeffs.shape[1]
    z_width = ng_dev // col_dev
    planes = NZ // pw_count
    x_block = NX // kpt_count
    col_total = pw_count * col_dev
    steps_y = jnp.arange(NY, dtype=jnp.int32)
    steps_x = jnp.arange(NX, dtype=jnp.int32)
    cos_y, sin_y = phase_tables(steps_y, steps_y, NY)
    cos_x, sin_x = phase_tables(steps_x, steps_x, NX)
    all_columns = lax.all_gather(column_map, "pw", axis=0, tiled=True)
    position = (miller_third[0] + z_width // 2) * col_dev + column_slot[0]
    source_of = (
        jnp.zeros((ng_dev,), jnp.int32).at[position].set(jnp.arange(ng_dev, dtype=jnp.int32))
    )
    coeff_rows = band_coeffs[0].reshape(band_count * 2, ng_dev).T
    packed = jnp.take(coeff_rows, source_of, axis=0)
    packed = (
        packed.reshape(z_width, col_dev, band_count, 2)
        .transpose(0, 2, 3, 1)
        .reshape(z_width, band_count * 2 * col_dev)
    )
    cos_z, sin_z = phase_tables(
        jnp.arange(NZ, dtype=jnp.int32), jnp.arange(z_width, dtype=jnp.int32) - z_width // 2, NZ
    )
    by_cos = contract("zj,jc->zc", cos_z, packed).reshape(NZ, band_count, 2, col_dev)
    by_sin = contract("zj,jc->zc", sin_z, packed).reshape(NZ, band_count, 2, col_dev)
    pencil = jnp.stack(
        (by_cos[:, :, 0] - by_sin[:, :, 1], by_sin[:, :, 0] + by_cos[:, :, 1]), axis=2
    )
    pencil = pencil.reshape(NZ, band_count * 2 * col_dev)
    arrived = lax.all_to_all(pencil, "pw", split_axis=0, concat_axis=1, tiled=True)
    arrived = arrived.reshape(planes, pw_count, band_count, 2, col_dev).transpose(2, 1, 4, 3, 0)
    arrived = arrived.reshape(band_count, col_total, 2 * planes)
    arrived = jnp.concatenate(
        (arrived, jnp.zeros((band_count, 1, 2 * planes), jnp.float32)), axis=1
    )
    cell_source = (
        jnp.full((NX * NY,), col_total, jnp.int32)
        .at[all_columns]
        .set(jnp.arange(col_total, dtype=jnp.int32))
    )

    def add_band(band, running):
        one_band = lax.dynamic_index_in_dim(arrived, band, 0, keepdims=False)
        placed = jnp.take(one_band, cell_source, axis=0)
        placed = placed.reshape(NX, NY, 2, planes).transpose(2, 3, 0, 1)
        grid_real = placed[0]
        grid_imag = placed[1]
        mixed_real = contract("pxm,ym->pxy", grid_real, cos_y) - contract(
            "pxm,ym->pxy", grid_imag, sin_y
        )
        mixed_imag = contract("pxm,ym->pxy", grid_real, sin_y) + contract(
            "pxm,ym->pxy", grid_imag, cos_y
        )
        wave_real = contract("xm,pmy->pxy", cos_x, mixed_real) - contract(
            "xm,pmy->pxy", sin_x, mixed_imag
        )
        wave_imag = contract("xm,pmy->pxy", sin_x, mixed_real) + contract(
            "xm,pmy->pxy", cos_x, mixed_imag
        )
        return running + wave_real * wave_real + wave_imag * wave_imag

    squares_sum = lax.fori_loop(0, band_count, add_band, jnp.zeros((planes, NX, NY), jnp.float32))
    weight = (
        2.0
        * kpoint_counts[kpt_index].astype(jnp.float32)
        / jnp.sum(kpoint_counts).astype(jnp.float32)
    )
    weight = weight / (ng_dev * pw_count)
    partial_value = weight * squares_sum
    total_density = lax.psum(partial_value, "kpt")
    density = lax.dynamic_slice_in_dim(total_density, kpt_index * x_block, x_block, 1)
    spec_real, spec_imag = forward_planes(total_density)
    rows_pw = NX // pw_count
    pencil_real, pencil_imag = (
        lax.all_to_all(spec_real, "pw", split_axis=1, concat_axis=0, tiled=True),
        lax.all_to_all(spec_imag, "pw", split_axis=1, concat_axis=0, tiled=True),
    )
    local_x = pw_index * rows_pw + jnp.arange(rows_pw, dtype=jnp.int32)
    freq_x = jnp.repeat(signed_freq(local_x, NX), NY)
    freq_y = jnp.tile(signed_freq(steps_y, NY), rows_pw)
    back_real, back_imag = poisson_columns(
        pencil_real.reshape(NZ, rows_pw * NY), pencil_imag.reshape(NZ, rows_pw * NY), freq_x, freq_y
    )
    plane_real, plane_imag = (
        lax.all_to_all(
            back_real.reshape(NZ, rows_pw, NY), "pw", split_axis=0, concat_axis=1, tiled=True
        ),
        lax.all_to_all(
            back_imag.reshape(NZ, rows_pw, NY), "pw", split_axis=0, concat_axis=1, tiled=True
        ),
    )
    own_rows = kpt_index * x_block + jnp.arange(x_block, dtype=jnp.int32)
    cos_rows, sin_rows = phase_tables(own_rows, steps_x, NX)
    rows_real = contract("xk,pky->pxy", cos_rows, plane_real) - contract(
        "xk,pky->pxy", sin_rows, plane_imag
    )
    rows_imag = contract("xk,pky->pxy", sin_rows, plane_real) + contract(
        "xk,pky->pxy", cos_rows, plane_imag
    )
    hartree = contract("pxk,yk->pxy", rows_real, cos_y) - contract("pxk,yk->pxy", rows_imag, sin_y)
    return (density, hartree)


LANES = 128
HALF = 64
VMEM_LIMIT = 16 * 1024 * 1024
PACK_LIMIT = 56 * 1024 * 1024
NN = (((1,), (0,)), ((), ()))
NT = (((1,), (1,)), ((), ()))
TN = (((0,), (0,)), ((), ()))


def pieces(value):
    high = value.astype(jnp.bfloat16)
    low = (value - high.astype(jnp.float32)).astype(jnp.bfloat16)
    return high, low


def mul(former, latter, dims):
    return lax.dot_general(former, latter, dims, preferred_element_type=jnp.float32)


def mul3_left(former, latter, dims):
    high, low = pieces(latter)
    (unused,), (axis,) = dims[0]
    return mul(former, jnp.concatenate((high, high, low), axis=axis), dims)


def mul3_right(former, latter, dims):
    high, low = pieces(former)
    (axis,), (unused,) = dims[0]
    return mul(jnp.concatenate((high, high, low), axis=axis), latter, dims)


def stack_table(values, axis):
    high = values.astype(np.float32).astype(jnp.bfloat16)
    low = (values - high.astype(np.float64)).astype(np.float32).astype(jnp.bfloat16)
    return jnp.asarray(np.concatenate((high, low, high), axis=axis))


def angles(former, latter, length):
    return np.outer(former, latter) % length * (2.0 * np.pi / length)


def tables(kpts, pws, planes):
    count = kpts * pws
    low_freq = np.arange(HALF) - HALF // 2
    grid_x, grid_y, grid_z = np.arange(NX), np.arange(NY), np.arange(NZ)
    own_y = np.arange(HALF)

    device = np.arange(count)
    plane_of = (
        (device % pws)[:, None] * (NZ // pws)
        + (device // pws)[:, None] * planes
        + np.arange(planes)[None, :]
    )
    return_table = {}

    def pencil(z_width):
        angle = angles(plane_of.ravel(), np.arange(z_width) - z_width // 2, NZ)
        cos, sin = (
            part.reshape(count, 1, planes, z_width) for part in (np.cos(angle), np.sin(angle))
        )
        real = np.concatenate((cos, -sin), axis=3)
        imag = np.concatenate((sin, cos), axis=3)
        return np.concatenate((real, imag), axis=1).reshape(-1, 2 * z_width)

    return_table["pencil"] = pencil

    angle = angles(low_freq, grid_y, NY)
    cos, sin = np.cos(angle), np.sin(angle)
    return_table["wave_y"] = np.block([[cos, sin], [-sin, cos]])

    angle = angles(grid_x, low_freq, NX)
    cos, sin = np.cos(angle), np.sin(angle)
    return_table["wave_x"] = np.block([[cos, -sin], [sin, cos]])

    angle = angles(own_y, grid_y, NY)
    cos, sin = np.cos(angle), np.sin(angle)
    return_table["forth_y"] = np.stack((cos, -sin), axis=1).reshape(2 * HALF, NY).T
    twice = np.where(own_y == 0, 1.0, 2.0)[:, None]
    return_table["back_y"] = np.stack((twice * cos, -twice * sin), axis=1).reshape(2 * HALF, NY)

    angle = angles(grid_z, plane_of.ravel(), NZ)
    return_table["forth_z"] = np.concatenate((np.cos(angle), np.sin(angle)), axis=0)
    own = NZ // pws
    merged = own // 8
    order = (
        np.arange(pws)[None, :, None] * own
        + np.arange(8)[None, None, :] * merged
        + np.arange(merged)[:, None, None]
    )
    angle = angles(order.ravel(), grid_z, NZ)
    return_table["back_z"] = np.concatenate((np.cos(angle), np.sin(angle)), axis=0)

    angle = angles(grid_x, grid_x, NX)
    return_table["both_x"] = np.concatenate((np.cos(angle), np.sin(angle)), axis=1)
    return return_table


def ramp(shape, axis, first=0):
    steps = lax.broadcasted_iota(jnp.int32, shape, axis) + first
    return steps.astype(jnp.float32).astype(jnp.bfloat16)


def sixteen(row):
    return jnp.broadcast_to(row, (16, row.shape[1])).astype(jnp.bfloat16)


def one_hot_lanes(row, ramps):
    column = jnp.transpose(jnp.concatenate([sixteen(row)] * (LANES // 16), axis=0))
    one = jnp.ones(column.shape, jnp.bfloat16)
    zero = jnp.zeros(column.shape, jnp.bfloat16)
    return jnp.concatenate(
        [
            jnp.where(column == ramps[:, first : first + LANES], one, zero)
            for first in range(0, ramps.shape[1], LANES)
        ],
        axis=1,
    )


RANK_LOW = 64
WINDOW = 64


def exchange_rows(refs, low_bits, size_bits, descending):
    for outer in range(RANK_LOW):
        if any(outer >> bit & 1 for bit in low_bits[0]):
            continue
        touched = sorted(
            outer + sum(1 << bit for i, bit in enumerate(low_bits[0]) if pattern >> i & 1)
            for pattern in range(1 << len(low_bits[0]))
        )
        held = {v: [ref[v * 8 : v * 8 + 8, :] for ref in refs] for v in touched}
        for size, bits in zip(size_bits, low_bits[1:]):
            for bit in bits:
                for v in touched:
                    if v >> bit & 1:
                        continue
                    former, latter = held[v], held[v | 1 << bit]
                    if size < 6:
                        down = bool(v >> size & 1)
                        swap = former[0] < latter[0] if down else former[0] > latter[0]
                    else:
                        swap = former[0] > latter[0]
                        if descending is not None:
                            swap = jnp.logical_xor(swap, descending)
                    held[v] = [jnp.where(swap, y, x) for x, y in zip(former, latter)]
                    held[v | 1 << bit] = [jnp.where(swap, x, y) for x, y in zip(former, latter)]
        for v in touched:
            for ref, value in zip(refs, held[v]):
                ref[v * 8 : v * 8 + 8, :] = value


def exchange_sublanes(refs, stride, descending):
    sublane = lax.broadcasted_iota(jnp.int32, (8, LANES), 0)
    upper = sublane // stride % 2 == 1
    want_most = upper if descending is None else jnp.logical_xor(upper, descending)
    other = jnp.where(upper, sublane - stride, sublane + stride)

    for v in range(RANK_LOW):
        here = [ref[v * 8 : v * 8 + 8, :] for ref in refs]
        there = [jnp.take_along_axis(value, other, axis=0) for value in here]
        take = jnp.logical_xor(here[0] > there[0], want_most)
        for ref, x, y in zip(refs, here, there):
            ref[v * 8 : v * 8 + 8, :] = jnp.where(take, y, x)


def sort_columns(refs):
    sublane = lax.broadcasted_iota(jnp.int32, (8, LANES), 0)
    exchange_rows(refs, [(0, 1, 2), (0,), (1, 0), (2, 1, 0)], [1, 2, 3], None)
    exchange_rows(refs, [(3,), (3,)], [4], None)
    exchange_rows(refs, [(0, 1, 2), (2, 1, 0)], [4], None)
    exchange_rows(refs, [(3, 4), (4, 3)], [5], None)
    exchange_rows(refs, [(0, 1, 2), (2, 1, 0)], [5], None)
    for size in range(6, 10):
        descending = None if size == 9 else sublane // (1 << (size - 6)) % 2 == 1
        for bit in range(size - 1, 5, -1):
            exchange_sublanes(refs, 1 << (bit - 6), descending)
        exchange_rows(refs, [(3, 4, 5), (5, 4, 3)], [size], descending)
        exchange_rows(refs, [(0, 1, 2), (2, 1, 0)], [size], descending)


def pack_kernel(width, has_column, *refs):
    coeff_ref, miller_ref, slot_ref, pencil_ref = refs[:4]
    rest = list(refs[4:])
    column_ref = rest.pop(0) if has_column else None
    out_ref, total, key_ref, real_ref, imag_ref, lane_ref, real_low, imag_low, ramp_ref, step_ref, held, sem = rest
    fetch = pltpu.make_async_copy(pencil_ref, held, sem)
    fetch.start()
    half = total.shape[0] // 4
    slots = 2 * half
    count = out_ref.shape[0]
    rows = pencil_ref.shape[0] // count
    length = miller_ref.shape[0]
    ranks = key_ref.shape[0]

    slot = slot_ref[...]
    second = slot >= half
    lane = miller_ref[...] + width // 2
    key = jnp.where(second, slot - half, slot) * (2 * width) + jnp.where(second, lane + width, lane)
    key_ref[0:length] = key.astype(jnp.float32)
    real_ref[0:length] = coeff_ref[0, pl.ds(0, length, stride=2), :]
    imag_ref[0:length] = coeff_ref[0, pl.ds(1, length, stride=2), :]
    blank = jnp.zeros((ranks - length, LANES), jnp.float32)
    key_ref[length:] = blank + 2.0 * slots * width
    real_ref[length:] = blank
    imag_ref[length:] = blank
    sort_columns((key_ref, real_ref, imag_ref))

    def base_of(block):
        base = 8 * (block // 2) + 8 * (block % 2) - WINDOW // 2
        return jnp.minimum(jnp.maximum(base, 0), half - WINDOW)

    ramp_ref[...] = ramp(ramp_ref.shape, 1)
    step_ref[...] = ramp(step_ref.shape, 0)
    sublane = lax.broadcasted_iota(jnp.int32, (8, LANES), 0)
    astray = jnp.zeros((8, LANES), jnp.float32)
    for v in range(RANK_LOW):
        at = slice(v * 8, v * 8 + 8)
        keys = key_ref[at, :]
        high = jnp.floor(keys * (1.0 / (2 * width)))
        lane_ref[at, :] = keys - high * (2.0 * width)
        key_ref[at, :] = high
        for ref, low_ref in ((real_ref, real_low), (imag_ref, imag_low)):
            value = ref[at, :]
            rounded = value.astype(jnp.bfloat16).astype(jnp.float32)
            ref[at, :] = rounded
            low_ref[at, :] = value - rounded
        offset = high - base_of(sublane * (RANK_LOW // 8) + v // 8).astype(jnp.float32)
        outside = jnp.logical_or(offset < 0.0, offset >= 1.0 * WINDOW)
        astray = jnp.where(outside, 1.0, astray)
    astray = jnp.max(jnp.where(sublane * RANK_LOW < length, astray, 0.0))

    def add(block, base, window):
        first = block % (RANK_LOW // 8) * 64 + block // (RANK_LOW // 8)
        base_row = jnp.full((1, LANES), base, jnp.int32).astype(jnp.float32)
        zero = jnp.zeros((16, LANES), jnp.bfloat16)
        spread, chosen = [], []
        for t in range(8):
            row = pl.ds(first + 8 * t, 1)
            high = sixteen(key_ref[row, :] - base_row)
            masks = [high == step_ref[r : r + 16, :] for r in range(0, window, 16)]
            spread.append(
                jnp.concatenate(
                    [
                        jnp.where(mask, value, zero)
                        for value in [
                            sixteen(ref[row, :]) for ref in (real_ref, imag_ref, real_low, imag_low)
                        ]
                        for mask in masks
                    ],
                    axis=0,
                )
            )
            chosen.append(one_hot_lanes(lane_ref[row, :], ramp_ref[...]))
        found = mul(jnp.concatenate(spread, axis=1), jnp.concatenate(chosen, axis=0), NN)
        for i in range(4):
            if window == half:
                into = pl.ds(i * half, half)
            else:
                into = pl.ds(pl.multiple_of(i * half + base, 8), window)
            total[into, :] += found[i * window : (i + 1) * window]

    total[...] = jnp.zeros_like(total)
    blocks = length // 8
    together = 4 if blocks % 4 == 0 else 1

    @pl.when(astray == 0.0)
    def _():
        def some_blocks(i, unused):
            for s in range(together):
                block = together * i + s
                add(block, base_of(block), WINDOW)
            return unused

        lax.fori_loop(0, blocks // together, some_blocks, 0)

    @pl.when(astray > 0.0)
    def _():
        def one_block(block, unused):
            add(block, 0, half)
            return unused

        lax.fori_loop(0, blocks, one_block, 0)

    both = []
    for at in range(2):
        parts = [
            total[(2 * at + c) * half : (2 * at + c + 1) * half].astype(jnp.bfloat16)
            for c in range(2)
        ]
        both.append(
            jnp.concatenate(
                [
                    jnp.concatenate([part[:, h * width : (h + 1) * width] for part in parts], axis=1)
                    for h in range(2)
                ],
                axis=0,
            )
        )
    fetch.wait()
    pencils = mul(held[...], jnp.concatenate((both[0], both[0], both[1]), axis=1), NT)
    tiles = slots // LANES
    for t in range(tiles):
        tile = pencils[:, t * LANES : (t + 1) * LANES].reshape(count, rows, LANES)
        if not has_column:
            out_ref[:, t * rows : (t + 1) * rows] = tile
            continue
        for g in range(rows // 4):
            out_ref[:, t * (rows // 4) + g] = tile[:, 4 * g : 4 * g + 4]
    if has_column:
        column = [
            column_ref[t * LANES : (t + 1) * LANES].astype(jnp.float32).reshape(1, LANES)
            for t in range(tiles)
        ]
        column = jnp.concatenate(column + [jnp.zeros((4 - tiles, LANES), jnp.float32)], axis=0)
        out_ref[:, tiles * rows // 4] = jnp.broadcast_to(column[None], (count, 4, LANES))


def pack_band(band, count, coeffs, miller, slot, pencil, slots, column):
    length = miller.shape[0]
    width = pencil.shape[1] // 6
    rows = pencil.shape[0] // count * (slots // LANES)
    operands = [coeffs, miller, slot, pencil]
    out_shape = (count, rows, LANES)
    if column is not None:
        operands.append(column)
        out_shape = (count, rows // 4 + 1, 4, LANES)
    one_band = pl.BlockSpec((1, 2 * length, LANES), lambda i: (band, 0, 0))
    return pl.pallas_call(
        functools.partial(pack_kernel, width, column is not None),
        grid=(1,),
        in_specs=[one_band]
        + [
            pl.BlockSpec(memory_space=pl.ANY)
            if x is pencil
            else pl.BlockSpec(x.shape, lambda i, n=x.ndim: (0,) * n)
            for x in operands[1:]
        ],
        out_specs=pl.BlockSpec(out_shape, lambda i: (0,) * len(out_shape)),
        out_shape=jax.ShapeDtypeStruct(out_shape, jnp.float32),
        scratch_shapes=[pltpu.VMEM((2 * slots, 2 * width), jnp.float32)]
        + [pltpu.VMEM((8 * RANK_LOW, LANES), jnp.float32)] * 6
        + [
            pltpu.VMEM((LANES, 2 * width), jnp.bfloat16),
            pltpu.VMEM((slots // 2, LANES), jnp.bfloat16),
            pltpu.VMEM(pencil.shape, jnp.bfloat16),
            pltpu.SemaphoreType.DMA,
        ],
        compiler_params=pltpu.CompilerParams(vmem_limit_bytes=PACK_LIMIT),
        cost_estimate=pl.CostEstimate(
            flops=2 * length * LANES * slots * 4 * width,
            bytes_accessed=16 * length * LANES,
            transcendentals=0,
        ),
        name="pack_band",
    )(*operands)


def wave_kernel(kpts, tiles, scale, is_first, is_last, *refs):
    own_ref, count_ref, came_ref, wave_y_ref, wave_x_ref = refs[:5]
    rest = list(refs[5:])
    forth_ref = rest.pop(0) if is_last else None
    former_ref, cell_ref = (None, None) if is_first else (rest.pop(0), rest.pop(0))
    density_refs = [rest.pop(0) for _ in range(kpts if is_last else 1)]
    if is_first:
        coulomb_ref, cell_ref = rest.pop(0), rest.pop(0)
    send_ref = rest.pop(0) if is_last else None
    values, grid, whole, chosen_ref, high_ref = rest
    planes = density_refs[0].shape[0]
    block = NX // kpts
    part_rows = 2 * planes
    pws = came_ref.shape[0] // kpts
    rows = kpts * part_rows
    total = values.shape[1]

    for j in range(pws):
        for t in range(tiles):
            if is_first:
                groups = [
                    came_ref[k * pws + j, t * (part_rows // 4) + g]
                    for k in range(kpts)
                    for g in range(part_rows // 4)
                ]
            else:
                groups = [
                    came_ref[k * pws + j, t * part_rows : (t + 1) * part_rows] for k in range(kpts)
                ]
            taken = jnp.concatenate(groups, axis=0)
            high, low = pieces(taken)
            first = (j * tiles + t) * LANES
            values[0:rows, first : first + LANES] = high
            values[rows : 2 * rows, first : first + LANES] = low

    tile = 4 * HALF
    ramps = ramp((LANES, tile), 1)
    for j in range(pws):
        for t in range(tiles):
            first = (j * tiles + t) * LANES
            if is_first:
                column = came_ref[j, tiles * part_rows // 4, t : t + 1].astype(jnp.int32)
                cell = ((column // NY + NX // 2) % NX - HALF // 2) * HALF
                cell = cell + (column % NY + NY // 2) % NY - HALF // 2
                cell_ref[:, first : first + LANES] = cell
            else:
                cell = cell_ref[:, first : first + LANES]
            lane = (cell % tile).astype(jnp.float32)
            chosen_ref[first : first + LANES, :] = one_hot_lanes(lane, ramps)
            high_ref[:, first : first + LANES] = sixteen((cell // tile).astype(jnp.float32))
    if is_first:
        step_z = lax.broadcasted_iota(jnp.int32, (NZ, NX), 0)
        step_x = lax.broadcasted_iota(jnp.int32, (NZ, NX), 1)
        for q in range(coulomb_ref.shape[0]):
            freq_y = jnp.full((NZ, NX), own_ref[1] + q, jnp.int32)
            kernel = coulomb(signed_freq(step_z, NZ), signed_freq(step_x, NX), freq_y)
            coulomb_ref[q] = kernel * (1.0 / (NX * NY * NZ))
    left = lax.broadcasted_iota(jnp.int32, (planes, LANES), 1) < HALF
    together = 4

    def place(t, found):
        found = found[:rows] + found[rows:]
        for h in range(2):
            for k in range(kpts):
                real, imag = (
                    found[(2 * k + c) * planes : (2 * k + c + 1) * planes, h * LANES : (h + 1) * LANES]
                    for c in range(2)
                )
                first = (k * HALF + 4 * t + 2 * h) * planes
                grid[first : first + planes, :] = jnp.where(left, real, pltpu.roll(imag, HALF, 1))
                grid[first + planes : first + 2 * planes, :] = jnp.where(
                    left, pltpu.roll(real, HALF, 1), imag
                )

    high = high_ref[...]
    zero = jnp.zeros_like(high)
    for start in range(0, HALF // 4, together):
        kept = []
        for t in range(start, start + together):
            here = high == jnp.full_like(high, t)
            kept += [jnp.where(here, values[r : r + 16, :], zero) for r in range(0, 2 * rows, 16)]
        found = mul(jnp.concatenate(kept, axis=0), chosen_ref[...], NN)
        for s in range(together):
            place(start + s, found[2 * rows * s : 2 * rows * (s + 1)])

    sum_of = count_ref[0]
    for k in range(1, kpts):
        sum_of = sum_of + count_ref[k]

    def spread(number):
        return jnp.full((8, NY), number, jnp.int32).astype(jnp.float32)

    weights = [
        jnp.concatenate([spread(count_ref[k]) / spread(sum_of) * scale] * (NX // 8), axis=0)
        for k in range(kpts)
    ]
    lines = [grid[pl.ds(p, kpts * HALF, stride=planes), :] for p in range(planes)]
    lines = mul3_right(jnp.concatenate(lines, axis=0), wave_y_ref[...], NN)

    for p in range(planes):
        mixed = lines[p * kpts * HALF : (p + 1) * kpts * HALF]
        mixed = jnp.concatenate(
            [
                jnp.concatenate(
                    [mixed[k * HALF : (k + 1) * HALF, c * NY : (c + 1) * NY] for k in range(kpts)],
                    axis=1,
                )
                for c in range(2)
            ],
            axis=0,
        )
        wave = mul3_left(wave_x_ref[...], mixed, NN)
        square = wave[:NX] * wave[:NX] + wave[NX:] * wave[NX:]
        density = weights[0] * square[:, :NY]
        for k in range(1, kpts):
            density = density + weights[k] * square[:, k * NY : (k + 1) * NY]
        if former_ref is not None:
            density = density + former_ref[p]
        if is_last:
            whole[p] = density
        else:
            density_refs[0][p] = density

    if is_last:
        for s, density_ref in enumerate(density_refs):
            first = pl.multiple_of(lax.rem(own_ref[0] + s, kpts) * block, block)
            density_ref[...] = whole[:, pl.ds(first, block), :]
        level = jnp.mean(whole[0, :8, :], axis=(0, 1), keepdims=True)
        field = whole[...].reshape(planes * NX, NY) - level
        half = mul3_right(field, forth_ref[...], NN)
        first_row = lax.broadcasted_iota(jnp.int32, (2 * HALF, NX), 0) == 0
        for p in range(planes):
            turned = jnp.transpose(half[p * NX : (p + 1) * NX])
            turned = turned + jnp.where(first_row, level * NY, 0.0)
            send_ref[pl.ds(p, 2 * HALF, stride=planes), :] = turned


def wave_band(kpts, tiles, total, scale, own, counts, came, wave_y, wave_x, forth, former, cell):
    planes = NZ // came.shape[0]
    block = NX // kpts
    is_first, is_last = former is None, forth is not None
    vmem = pl.BlockSpec(memory_space=pltpu.VMEM)
    operands = [own, counts, came, wave_y, wave_x]
    if is_last:
        operands.append(forth)
    if not is_first:
        operands += [former, cell]
    if is_last:
        out_shape = [jax.ShapeDtypeStruct((planes, block, NY), jnp.float32)] * kpts
    else:
        out_shape = [jax.ShapeDtypeStruct((planes, NX, NY), jnp.float32)]
    if is_first:
        out_shape.append(jax.ShapeDtypeStruct((HALF // came.shape[0], NZ, NX), jnp.float32))
        out_shape.append(jax.ShapeDtypeStruct((1, total), jnp.int32))
    if is_last:
        out_shape.append(jax.ShapeDtypeStruct((2 * HALF * planes, NX), jnp.float32))
    rows = kpts * 2 * planes
    return pl.pallas_call(
        functools.partial(wave_kernel, kpts, tiles, scale, is_first, is_last),
        in_specs=[pl.BlockSpec(memory_space=pltpu.SMEM)] * 2 + [vmem] * (len(operands) - 2),
        out_specs=[vmem] * len(out_shape),
        out_shape=out_shape,
        scratch_shapes=[
            pltpu.VMEM((2 * rows, total), jnp.bfloat16),
            pltpu.VMEM((kpts * planes * HALF, LANES), jnp.float32),
            pltpu.VMEM((planes, NX, NY), jnp.float32),
            pltpu.VMEM((total, 4 * HALF), jnp.bfloat16),
            pltpu.VMEM((16, total), jnp.bfloat16),
        ],
        compiler_params=pltpu.CompilerParams(vmem_limit_bytes=VMEM_LIMIT),
        cost_estimate=pl.CostEstimate(
            flops=4 * rows * total * HALF * HALF, bytes_accessed=4 * came.size, transcendentals=0
        ),
        name="wave_band",
    )(*operands)


def poisson_kernel(pws, own_ref, kernel_ref, came_ref, forth_ref, back_ref, both_x_ref, send_ref):
    count, parts, planes, unused = came_ref.shape
    pairs = parts // 2
    fields = [came_ref[:, i].reshape(NZ, NX) for i in range(parts)]
    level = jnp.mean(fields[0], axis=(0, 1), keepdims=True)
    fields[0] = fields[0] - jnp.where(own_ref[1] == 0, level, 0.0)
    field = jnp.concatenate(fields, axis=1)
    turned = mul3_left(forth_ref[...], field, NN)

    def part(array, half, i):
        return array[half * NZ : (half + 1) * NZ, i * NX : (i + 1) * NX]

    lines = []
    for q in range(pairs):
        lines.append(part(turned, 0, 2 * q) + part(turned, 1, 2 * q + 1))
        lines.append(part(turned, 0, 2 * q + 1) - part(turned, 1, 2 * q))
    spectrum = mul3_right(jnp.concatenate(lines, axis=0), both_x_ref[...], NN)

    lines = []
    for q in range(pairs):
        real = spectrum[2 * q * NZ : (2 * q + 1) * NZ]
        imag = spectrum[(2 * q + 1) * NZ : (2 * q + 2) * NZ]
        kernel = kernel_ref[q]
        lines.append((real[:, :NX] + imag[:, NX:]) * kernel)
        lines.append((imag[:, :NX] - real[:, NX:]) * kernel)
    turned = mul3_right(jnp.concatenate(lines, axis=0), both_x_ref[...], NN)
    lines = []
    for q in range(pairs):
        real = turned[2 * q * NZ : (2 * q + 1) * NZ]
        imag = turned[(2 * q + 1) * NZ : (2 * q + 2) * NZ]
        lines.append(real[:, :NX] - imag[:, NX:])
        lines.append(real[:, NX:] + imag[:, :NX])
    turned = mul3_left(back_ref[...], jnp.concatenate(lines, axis=1), NN)

    kpts = count // pws
    merged = NZ // pws // 8
    block = NX // kpts
    rows = pws * 8
    lane = lax.broadcasted_iota(jnp.int32, (rows, LANES), 1) // block
    for q in range(pairs):
        real = part(turned, 0, 2 * q) - part(turned, 1, 2 * q + 1)
        imag = part(turned, 0, 2 * q + 1) + part(turned, 1, 2 * q)
        for c, value in enumerate((real, imag)):
            for a in range(kpts):
                packed = None
                for m in range(merged):
                    piece = value[m * rows : (m + 1) * rows]
                    shift = (m - a) * block % LANES
                    if shift:
                        piece = pltpu.roll(piece, shift, 1)
                    packed = piece if m == 0 else jnp.where(lane == m, piece, packed)
                send_ref[a * pws : (a + 1) * pws, 2 * q + c] = packed.reshape(pws, 8, LANES)


def poisson(pws, own, kernel, came, forth, back, both_x):
    vmem = pl.BlockSpec(memory_space=pltpu.VMEM)
    count, parts, unused, unused = came.shape
    return pl.pallas_call(
        functools.partial(poisson_kernel, pws),
        in_specs=[pl.BlockSpec(memory_space=pltpu.SMEM)] + [vmem] * 5,
        out_specs=vmem,
        out_shape=jax.ShapeDtypeStruct((count, parts, 8, LANES), jnp.float32),
        compiler_params=pltpu.CompilerParams(vmem_limit_bytes=VMEM_LIMIT),
        name="poisson",
    )(own, kernel, came, forth, back, both_x)


def finish_kernel(own_ref, came_ref, back_ref, *refs):
    block_refs, density_ref, out_ref = refs[:-2], refs[-2], refs[-1]
    kpts = len(block_refs)
    planes, block, unused = out_ref.shape
    merged = planes // 8
    for s, block_ref in enumerate(block_refs):
        sender = lax.rem(own_ref[0] + kpts - s, kpts)
        density_ref[pl.ds(sender * (planes // kpts), planes // kpts)] = block_ref[...]
    for h in range(8):
        lines = came_ref[pl.ds(h, 2 * HALF, stride=8), :]
        field = mul3_right(lines, back_ref[...], TN)
        out_ref[h * merged : (h + 1) * merged] = field.reshape(merged, block, NY)


def finish(planes, block, own, came, back_y, blocks):
    vmem = pl.BlockSpec(memory_space=pltpu.VMEM)
    return pl.pallas_call(
        finish_kernel,
        in_specs=[pl.BlockSpec(memory_space=pltpu.SMEM)] + [vmem] * (2 + len(blocks)),
        out_specs=[vmem] * 2,
        out_shape=[jax.ShapeDtypeStruct((planes, block, NY), jnp.float32)] * 2,
        compiler_params=pltpu.CompilerParams(vmem_limit_bytes=VMEM_LIMIT),
        name="finish",
    )(own, came, back_y, *blocks)


def exchange(array, axes):
    return lax.all_to_all(array, axes, split_axis=0, concat_axis=0, tiled=True)


def local_planes(band_coeffs, miller_third, column_slot, column_map, kpoint_counts):
    pws = lax.axis_size("pw")
    kpts = lax.axis_size("kpt")
    count = pws * kpts
    everyone = ("kpt", "pw")
    slots = column_map.shape[0]
    band_count = band_coeffs.shape[1]
    z_width = column_slot.shape[1] // slots
    planes = NZ // count
    parts = 2 * HALF // count
    made = tables(kpts, pws, planes)
    pencil = stack_table(made["pencil"](z_width), 1)
    wave_x, forth_z, back_z = (
        stack_table(made[name], 1) for name in ("wave_x", "forth_z", "back_z")
    )
    wave_y, forth_y, back_y, both_x = (
        stack_table(made[name], 0) for name in ("wave_y", "forth_y", "back_y", "both_x")
    )

    tiles = slots // LANES
    length = column_slot.shape[1] // LANES
    coeffs = band_coeffs.reshape(band_count, 2, length, LANES).transpose(0, 2, 1, 3)
    coeffs = coeffs.reshape(band_count, 2 * length, LANES)
    miller = miller_third.reshape(length, LANES)
    slot = column_slot.reshape(length, LANES)
    scale = 2.0 / (column_slot.shape[1] * pws)
    arrived = []
    for band in range(band_count):
        column = column_map if band == 0 else None
        packed = pack_band(
            band, count, coeffs, miller, slot, pencil, slots, column
        )
        arrived.append(exchange(packed, everyone))
    device = lax.axis_index("kpt") * pws + lax.axis_index("pw")
    own = jnp.stack((lax.axis_index("kpt"), device * (parts // 2))).astype(jnp.int32)
    former = cell = None
    for band in range(band_count):
        forth = forth_y if band == band_count - 1 else None
        made_here = wave_band(
            kpts,
            tiles,
            pws * slots,
            scale,
            own,
            kpoint_counts,
            arrived[band],
            wave_y,
            wave_x,
            forth,
            former,
            cell,
        )
        former = made_here[0]
        if band == 0:
            kernel, cell = made_here[kpts if forth is not None else 1 :][:2]
    half = exchange(made_here[-1].reshape(count, parts, planes, NX), everyone)
    blocks = [made_here[0]] + [
        lax.ppermute(made_here[s], "kpt", [(a, (a + s) % kpts) for a in range(kpts)])
        for s in range(1, kpts)
    ]
    back = poisson(pws, own, kernel, half, forth_z, back_z, both_x)
    back = exchange(back, everyone).reshape(count * parts * 8, LANES)
    return tuple(finish(NZ // pws, NX // kpts, own, back, back_y, blocks))


def fits_planes(kpts, pws):
    count = kpts * pws
    own = NZ // pws
    return (
        NZ % count == 0
        and NZ // count == 8
        and 2 * HALF % (2 * count) == 0
        and NX % kpts == 0
        and own % 8 == 0
        and own // 8 * (NX // kpts) == LANES
    )


def local(band_coeffs, miller_third, column_slot, column_map, kpoint_counts):
    slots = column_map.shape[0]
    plain = slots % LANES == 0 and LANES <= slots <= 8 * RANK_LOW
    plain = plain and column_slot.shape[1] == slots * LANES
    fits = plain and fits_planes(lax.axis_size("kpt"), lax.axis_size("pw"))
    chosen = local_planes if fits else local_general
    return chosen(band_coeffs, miller_third, column_slot, column_map, kpoint_counts)


def solution(mesh):
    return jax.shard_map(
        local,
        mesh=mesh,
        in_specs=(P("kpt", None, None, "pw"), P("kpt", "pw"), P("kpt", "pw"), P("pw"), P()),
        out_specs=(P("pw", "kpt", None), P("pw", "kpt", None)),
        check_vma=False,
    )
```

```python
import functools
import math

import jax
import jax.numpy as jnp
import numpy as np
from jax import lax
from jax.experimental import pallas as pl
from jax.experimental.pallas import tpu as pltpu
from jax.sharding import PartitionSpec as P

NX = 128
NY = 128
NZ = 256


SPACING = 0.25


def contract(pattern, former, latter):
    return jnp.einsum(
        pattern, former, latter, precision=lax.Precision.HIGHEST, preferred_element_type=jnp.float32
    )


def phase_tables(first_index, second_index, length):
    product = first_index[:, None] * second_index[None, :] % length
    angle = product.astype(jnp.float32) * (2.0 * math.pi / length)
    return (jnp.cos(angle), jnp.sin(angle))


def signed_freq(values, length):
    return jnp.where(values >= length // 2, values - length, values)


def coulomb(freq_z, freq_x, freq_y):
    wave_z = freq_z.astype(jnp.float32) / (NZ * SPACING)
    wave_x = freq_x.astype(jnp.float32) / (NX * SPACING)
    wave_y = freq_y.astype(jnp.float32) / (NY * SPACING)
    squared = (2.0 * math.pi) ** 2 * (wave_z * wave_z + wave_x * wave_x + wave_y * wave_y)
    anchor = (freq_z == 0) & (freq_x == 0) & (freq_y == 0)
    return jnp.where(anchor, 0.0, 4.0 * math.pi / jnp.where(anchor, 1.0, squared))


def poisson_columns(real_part, imag_part, freq_x, freq_y):
    length = real_part.shape[0]
    steps_z = jnp.arange(length, dtype=jnp.int32)
    cos_z, sin_z = phase_tables(steps_z, steps_z, length)
    spec_real = contract("zk,km->zm", cos_z, real_part) + contract("zk,km->zm", sin_z, imag_part)
    spec_imag = contract("zk,km->zm", cos_z, imag_part) - contract("zk,km->zm", sin_z, real_part)
    kernel = coulomb(signed_freq(steps_z, length)[:, None], freq_x[None, :], freq_y[None, :]) / (
        NX * NY * NZ
    )
    spec_real = spec_real * kernel
    spec_imag = spec_imag * kernel
    back_real = contract("zk,km->zm", cos_z, spec_real) - contract("zk,km->zm", sin_z, spec_imag)
    back_imag = contract("zk,km->zm", sin_z, spec_real) + contract("zk,km->zm", cos_z, spec_imag)
    return (back_real, back_imag)


def forward_planes(field):
    steps_x = jnp.arange(NX, dtype=jnp.int32)
    steps_y = jnp.arange(NY, dtype=jnp.int32)
    cos_y, sin_y = phase_tables(steps_y, steps_y, NY)
    cos_x, sin_x = phase_tables(steps_x, steps_x, NX)
    half_real = contract("pxy,ky->pxk", field, cos_y)
    half_imag = -contract("pxy,ky->pxk", field, sin_y)
    spec_real = contract("kx,pxy->pky", cos_x, half_real) + contract(
        "kx,pxy->pky", sin_x, half_imag
    )
    spec_imag = contract("kx,pxy->pky", cos_x, half_imag) - contract(
        "kx,pxy->pky", sin_x, half_real
    )
    return (spec_real, spec_imag)


def local_general(band_coeffs, miller_third, column_slot, column_map, kpoint_counts):
    pw_count = lax.axis_size("pw")
    kpt_count = lax.axis_size("kpt")
    pw_index = lax.axis_index("pw")
    kpt_index = lax.axis_index("kpt")
    col_dev = column_map.shape[0]
    ng_dev = column_slot.shape[1]
    band_count = band_coeffs.shape[1]
    z_width = ng_dev // col_dev
    planes = NZ // pw_count
    x_block = NX // kpt_count
    col_total = pw_count * col_dev
    steps_y = jnp.arange(NY, dtype=jnp.int32)
    steps_x = jnp.arange(NX, dtype=jnp.int32)
    cos_y, sin_y = phase_tables(steps_y, steps_y, NY)
    cos_x, sin_x = phase_tables(steps_x, steps_x, NX)
    all_columns = lax.all_gather(column_map, "pw", axis=0, tiled=True)
    position = (miller_third[0] + z_width // 2) * col_dev + column_slot[0]
    source_of = (
        jnp.zeros((ng_dev,), jnp.int32).at[position].set(jnp.arange(ng_dev, dtype=jnp.int32))
    )
    coeff_rows = band_coeffs[0].reshape(band_count * 2, ng_dev).T
    packed = jnp.take(coeff_rows, source_of, axis=0)
    packed = (
        packed.reshape(z_width, col_dev, band_count, 2)
        .transpose(0, 2, 3, 1)
        .reshape(z_width, band_count * 2 * col_dev)
    )
    cos_z, sin_z = phase_tables(
        jnp.arange(NZ, dtype=jnp.int32), jnp.arange(z_width, dtype=jnp.int32) - z_width // 2, NZ
    )
    by_cos = contract("zj,jc->zc", cos_z, packed).reshape(NZ, band_count, 2, col_dev)
    by_sin = contract("zj,jc->zc", sin_z, packed).reshape(NZ, band_count, 2, col_dev)
    pencil = jnp.stack(
        (by_cos[:, :, 0] - by_sin[:, :, 1], by_sin[:, :, 0] + by_cos[:, :, 1]), axis=2
    )
    pencil = pencil.reshape(NZ, band_count * 2 * col_dev)
    arrived = lax.all_to_all(pencil, "pw", split_axis=0, concat_axis=1, tiled=True)
    arrived = arrived.reshape(planes, pw_count, band_count, 2, col_dev).transpose(2, 1, 4, 3, 0)
    arrived = arrived.reshape(band_count, col_total, 2 * planes)
    arrived = jnp.concatenate(
        (arrived, jnp.zeros((band_count, 1, 2 * planes), jnp.float32)), axis=1
    )
    cell_source = (
        jnp.full((NX * NY,), col_total, jnp.int32)
        .at[all_columns]
        .set(jnp.arange(col_total, dtype=jnp.int32))
    )

    def add_band(band, running):
        one_band = lax.dynamic_index_in_dim(arrived, band, 0, keepdims=False)
        placed = jnp.take(one_band, cell_source, axis=0)
        placed = placed.reshape(NX, NY, 2, planes).transpose(2, 3, 0, 1)
        grid_real = placed[0]
        grid_imag = placed[1]
        mixed_real = contract("pxm,ym->pxy", grid_real, cos_y) - contract(
            "pxm,ym->pxy", grid_imag, sin_y
        )
        mixed_imag = contract("pxm,ym->pxy", grid_real, sin_y) + contract(
            "pxm,ym->pxy", grid_imag, cos_y
        )
        wave_real = contract("xm,pmy->pxy", cos_x, mixed_real) - contract(
            "xm,pmy->pxy", sin_x, mixed_imag
        )
        wave_imag = contract("xm,pmy->pxy", sin_x, mixed_real) + contract(
            "xm,pmy->pxy", cos_x, mixed_imag
        )
        return running + wave_real * wave_real + wave_imag * wave_imag

    squares_sum = lax.fori_loop(0, band_count, add_band, jnp.zeros((planes, NX, NY), jnp.float32))
    weight = (
        2.0
        * kpoint_counts[kpt_index].astype(jnp.float32)
        / jnp.sum(kpoint_counts).astype(jnp.float32)
    )
    weight = weight / (ng_dev * pw_count)
    partial_value = weight * squares_sum
    total_density = lax.psum(partial_value, "kpt")
    density = lax.dynamic_slice_in_dim(total_density, kpt_index * x_block, x_block, 1)
    spec_real, spec_imag = forward_planes(total_density)
    rows_pw = NX // pw_count
    pencil_real, pencil_imag = (
        lax.all_to_all(spec_real, "pw", split_axis=1, concat_axis=0, tiled=True),
        lax.all_to_all(spec_imag, "pw", split_axis=1, concat_axis=0, tiled=True),
    )
    local_x = pw_index * rows_pw + jnp.arange(rows_pw, dtype=jnp.int32)
    freq_x = jnp.repeat(signed_freq(local_x, NX), NY)
    freq_y = jnp.tile(signed_freq(steps_y, NY), rows_pw)
    back_real, back_imag = poisson_columns(
        pencil_real.reshape(NZ, rows_pw * NY), pencil_imag.reshape(NZ, rows_pw * NY), freq_x, freq_y
    )
    plane_real, plane_imag = (
        lax.all_to_all(
            back_real.reshape(NZ, rows_pw, NY), "pw", split_axis=0, concat_axis=1, tiled=True
        ),
        lax.all_to_all(
            back_imag.reshape(NZ, rows_pw, NY), "pw", split_axis=0, concat_axis=1, tiled=True
        ),
    )
    own_rows = kpt_index * x_block + jnp.arange(x_block, dtype=jnp.int32)
    cos_rows, sin_rows = phase_tables(own_rows, steps_x, NX)
    rows_real = contract("xk,pky->pxy", cos_rows, plane_real) - contract(
        "xk,pky->pxy", sin_rows, plane_imag
    )
    rows_imag = contract("xk,pky->pxy", sin_rows, plane_real) + contract(
        "xk,pky->pxy", cos_rows, plane_imag
    )
    hartree = contract("pxk,yk->pxy", rows_real, cos_y) - contract("pxk,yk->pxy", rows_imag, sin_y)
    return (density, hartree)


LANES = 128
HALF = 64
VMEM_LIMIT = 16 * 1024 * 1024
PACK_LIMIT = 56 * 1024 * 1024
NN = (((1,), (0,)), ((), ()))
NT = (((1,), (1,)), ((), ()))
TN = (((0,), (0,)), ((), ()))


def pieces(value):
    high = value.astype(jnp.bfloat16)
    low = (value - high.astype(jnp.float32)).astype(jnp.bfloat16)
    return high, low


def mul(former, latter, dims):
    return lax.dot_general(former, latter, dims, preferred_element_type=jnp.float32)


def mul3_left(former, latter, dims):
    high, low = pieces(latter)
    (unused,), (axis,) = dims[0]
    return mul(former, jnp.concatenate((high, high, low), axis=axis), dims)


def mul3_right(former, latter, dims):
    high, low = pieces(former)
    (axis,), (unused,) = dims[0]
    return mul(jnp.concatenate((high, high, low), axis=axis), latter, dims)


def stack_table(values, axis):
    high = values.astype(np.float32).astype(jnp.bfloat16)
    low = (values - high.astype(np.float64)).astype(np.float32).astype(jnp.bfloat16)
    return jnp.asarray(np.concatenate((high, low, high), axis=axis))


def angles(former, latter, length):
    return np.outer(former, latter) % length * (2.0 * np.pi / length)


def ring_order(length):
    return [0, *range(1, length, 2), *range(length - 2 + length % 2, 0, -2)] if length > 1 else [0]


def group_order(kpts, pws):
    cores = 2 if pws % 2 == 0 else 1
    return ring_order(kpts), [c * cores + i for c in ring_order(pws // cores) for i in range(cores)]


def tables(kpts, pws, planes):
    count = kpts * pws
    kpt_order, pw_order = (np.array(order) for order in group_order(kpts, pws))
    low_freq = np.arange(HALF) - HALF // 2
    grid_x, grid_y, grid_z = np.arange(NX), np.arange(NY), np.arange(NZ)
    own_y = np.arange(HALF)

    device = np.arange(count)
    plane_of = (
        pw_order[device % pws][:, None] * (NZ // pws)
        + kpt_order[device // pws][:, None] * planes
        + np.arange(planes)[None, :]
    )
    return_table = {}

    def pencil(z_width):
        angle = angles(plane_of.ravel(), np.arange(z_width) - z_width // 2, NZ)
        cos, sin = (
            part.reshape(count, 1, planes, z_width) for part in (np.cos(angle), np.sin(angle))
        )
        real = np.concatenate((cos, -sin), axis=3)
        imag = np.concatenate((sin, cos), axis=3)
        return np.concatenate((real, imag), axis=1).reshape(-1, 2 * z_width)

    return_table["pencil"] = pencil

    angle = angles(low_freq, grid_y, NY)
    cos, sin = np.cos(angle), np.sin(angle)
    return_table["wave_y"] = np.block([[cos, sin], [-sin, cos]])

    angle = angles(grid_x, low_freq, NX)
    cos, sin = np.cos(angle), np.sin(angle)
    return_table["wave_x"] = np.block([[cos, -sin], [sin, cos]])

    angle = angles(own_y, grid_y, NY)
    cos, sin = np.cos(angle), np.sin(angle)
    return_table["forth_y"] = np.stack((cos, -sin), axis=1).reshape(2 * HALF, NY).T
    twice = np.where(own_y == 0, 1.0, 2.0)[:, None]
    return_table["back_y"] = np.stack((twice * cos, -twice * sin), axis=1).reshape(2 * HALF, NY)

    angle = angles(grid_z, plane_of.ravel(), NZ)
    return_table["forth_z"] = np.concatenate((np.cos(angle), np.sin(angle)), axis=0)
    own = NZ // pws
    merged = own // 8
    order = (
        pw_order[None, :, None] * own
        + np.arange(8)[None, None, :] * merged
        + np.arange(merged)[:, None, None]
    )
    angle = angles(order.ravel(), grid_z, NZ)
    return_table["back_z"] = np.concatenate((np.cos(angle), np.sin(angle)), axis=0)

    angle = angles(grid_x, grid_x, NX)
    return_table["both_x"] = np.concatenate((np.cos(angle), np.sin(angle)), axis=1)
    return return_table


def ramp(shape, axis, first=0):
    steps = lax.broadcasted_iota(jnp.int32, shape, axis) + first
    return steps.astype(jnp.float32).astype(jnp.bfloat16)


def sixteen(row):
    return jnp.broadcast_to(row, (16, row.shape[1])).astype(jnp.bfloat16)


def one_hot_lanes(row, ramps):
    column = jnp.transpose(jnp.concatenate([sixteen(row)] * (LANES // 16), axis=0))
    one = jnp.ones(column.shape, jnp.bfloat16)
    zero = jnp.zeros(column.shape, jnp.bfloat16)
    return jnp.concatenate(
        [
            jnp.where(column == ramps[:, first : first + LANES], one, zero)
            for first in range(0, ramps.shape[1], LANES)
        ],
        axis=1,
    )


RANK_LOW = 64
WINDOW = 64


def exchange_rows(refs, low_bits, size_bits, descending):
    for outer in range(RANK_LOW):
        if any(outer >> bit & 1 for bit in low_bits[0]):
            continue
        touched = sorted(
            outer + sum(1 << bit for i, bit in enumerate(low_bits[0]) if pattern >> i & 1)
            for pattern in range(1 << len(low_bits[0]))
        )
        held = {v: [ref[v * 8 : v * 8 + 8, :] for ref in refs] for v in touched}
        for size, bits in zip(size_bits, low_bits[1:]):
            for bit in bits:
                for v in touched:
                    if v >> bit & 1:
                        continue
                    former, latter = held[v], held[v | 1 << bit]
                    if size < 6:
                        down = bool(v >> size & 1)
                        swap = former[0] < latter[0] if down else former[0] > latter[0]
                    else:
                        swap = former[0] > latter[0]
                        if descending is not None:
                            swap = jnp.logical_xor(swap, descending)
                    held[v] = [jnp.where(swap, y, x) for x, y in zip(former, latter)]
                    held[v | 1 << bit] = [jnp.where(swap, x, y) for x, y in zip(former, latter)]
        for v in touched:
            for ref, value in zip(refs, held[v]):
                ref[v * 8 : v * 8 + 8, :] = value


def exchange_sublanes(refs, stride, descending):
    sublane = lax.broadcasted_iota(jnp.int32, (8, LANES), 0)
    upper = sublane // stride % 2 == 1
    want_most = upper if descending is None else jnp.logical_xor(upper, descending)
    other = jnp.where(upper, sublane - stride, sublane + stride)

    for v in range(RANK_LOW):
        here = [ref[v * 8 : v * 8 + 8, :] for ref in refs]
        there = [jnp.take_along_axis(value, other, axis=0) for value in here]
        take = jnp.logical_xor(here[0] > there[0], want_most)
        for ref, x, y in zip(refs, here, there):
            ref[v * 8 : v * 8 + 8, :] = jnp.where(take, y, x)


def sort_columns(refs):
    sublane = lax.broadcasted_iota(jnp.int32, (8, LANES), 0)
    exchange_rows(refs, [(0, 1, 2), (0,), (1, 0), (2, 1, 0)], [1, 2, 3], None)
    exchange_rows(refs, [(3,), (3,)], [4], None)
    exchange_rows(refs, [(0, 1, 2), (2, 1, 0)], [4], None)
    exchange_rows(refs, [(3, 4), (4, 3)], [5], None)
    exchange_rows(refs, [(0, 1, 2), (2, 1, 0)], [5], None)
    for size in range(6, 10):
        descending = None if size == 9 else sublane // (1 << (size - 6)) % 2 == 1
        for bit in range(size - 1, 5, -1):
            exchange_sublanes(refs, 1 << (bit - 6), descending)
        exchange_rows(refs, [(3, 4, 5), (5, 4, 3)], [size], descending)
        exchange_rows(refs, [(0, 1, 2), (2, 1, 0)], [size], descending)


def pack_kernel(width, has_column, *refs):
    coeff_ref, miller_ref, slot_ref, pencil_ref = refs[:4]
    rest = list(refs[4:])
    column_ref = rest.pop(0) if has_column else None
    out_ref, total, key_ref, real_ref, imag_ref, lane_ref, real_low, imag_low, ramp_ref, step_ref, held, sem = rest
    fetch = pltpu.make_async_copy(pencil_ref, held, sem)
    fetch.start()
    half = total.shape[0] // 4
    slots = 2 * half
    count = out_ref.shape[0]
    rows = pencil_ref.shape[0] // count
    length = miller_ref.shape[0]
    ranks = key_ref.shape[0]

    slot = slot_ref[...]
    second = slot >= half
    lane = miller_ref[...] + width // 2
    key = jnp.where(second, slot - half, slot) * (2 * width) + jnp.where(second, lane + width, lane)
    key_ref[0:length] = key.astype(jnp.float32)
    real_ref[0:length] = coeff_ref[0, pl.ds(0, length, stride=2), :]
    imag_ref[0:length] = coeff_ref[0, pl.ds(1, length, stride=2), :]
    blank = jnp.zeros((ranks - length, LANES), jnp.float32)
    key_ref[length:] = blank + 2.0 * slots * width
    real_ref[length:] = blank
    imag_ref[length:] = blank
    sort_columns((key_ref, real_ref, imag_ref))

    def base_of(block):
        base = 8 * (block // 2) + 8 * (block % 2) - WINDOW // 2
        return jnp.minimum(jnp.maximum(base, 0), half - WINDOW)

    ramp_ref[...] = ramp(ramp_ref.shape, 1)
    step_ref[...] = ramp(step_ref.shape, 0)
    sublane = lax.broadcasted_iota(jnp.int32, (8, LANES), 0)
    astray = jnp.zeros((8, LANES), jnp.float32)
    for v in range(RANK_LOW):
        at = slice(v * 8, v * 8 + 8)
        keys = key_ref[at, :]
        high = jnp.floor(keys * (1.0 / (2 * width)))
        lane_ref[at, :] = keys - high * (2.0 * width)
        key_ref[at, :] = high
        for ref, low_ref in ((real_ref, real_low), (imag_ref, imag_low)):
            value = ref[at, :]
            rounded = value.astype(jnp.bfloat16).astype(jnp.float32)
            ref[at, :] = rounded
            low_ref[at, :] = value - rounded
        offset = high - base_of(sublane * (RANK_LOW // 8) + v // 8).astype(jnp.float32)
        outside = jnp.logical_or(offset < 0.0, offset >= 1.0 * WINDOW)
        astray = jnp.where(outside, 1.0, astray)
    astray = jnp.max(jnp.where(sublane * RANK_LOW < length, astray, 0.0))

    def add(block, base, window):
        first = block % (RANK_LOW // 8) * 64 + block // (RANK_LOW // 8)
        base_row = jnp.full((1, LANES), base, jnp.int32).astype(jnp.float32)
        zero = jnp.zeros((16, LANES), jnp.bfloat16)
        spread, chosen = [], []
        for t in range(8):
            row = pl.ds(first + 8 * t, 1)
            high = sixteen(key_ref[row, :] - base_row)
            masks = [high == step_ref[r : r + 16, :] for r in range(0, window, 16)]
            spread.append(
                jnp.concatenate(
                    [
                        jnp.where(mask, value, zero)
                        for value in [
                            sixteen(ref[row, :]) for ref in (real_ref, imag_ref, real_low, imag_low)
                        ]
                        for mask in masks
                    ],
                    axis=0,
                )
            )
            chosen.append(one_hot_lanes(lane_ref[row, :], ramp_ref[...]))
        found = mul(jnp.concatenate(spread, axis=1), jnp.concatenate(chosen, axis=0), NN)
        for i in range(4):
            if window == half:
                into = pl.ds(i * half, half)
            else:
                into = pl.ds(pl.multiple_of(i * half + base, 8), window)
            total[into, :] += found[i * window : (i + 1) * window]

    total[...] = jnp.zeros_like(total)
    blocks = length // 8
    together = 4 if blocks % 4 == 0 else 1

    @pl.when(astray == 0.0)
    def _():
        def some_blocks(i, unused):
            for s in range(together):
                block = together * i + s
                add(block, base_of(block), WINDOW)
            return unused

        lax.fori_loop(0, blocks // together, some_blocks, 0)

    @pl.when(astray > 0.0)
    def _():
        def one_block(block, unused):
            add(block, 0, half)
            return unused

        lax.fori_loop(0, blocks, one_block, 0)

    both = []
    for at in range(2):
        parts = [
            total[(2 * at + c) * half : (2 * at + c + 1) * half].astype(jnp.bfloat16)
            for c in range(2)
        ]
        both.append(
            jnp.concatenate(
                [
                    jnp.concatenate([part[:, h * width : (h + 1) * width] for part in parts], axis=1)
                    for h in range(2)
                ],
                axis=0,
            )
        )
    fetch.wait()
    pencils = mul(held[...], jnp.concatenate((both[0], both[0], both[1]), axis=1), NT)
    tiles = slots // LANES
    for t in range(tiles):
        tile = pencils[:, t * LANES : (t + 1) * LANES].reshape(count, rows, LANES)
        if not has_column:
            out_ref[:, t * rows : (t + 1) * rows] = tile
            continue
        for g in range(rows // 4):
            out_ref[:, t * (rows // 4) + g] = tile[:, 4 * g : 4 * g + 4]
    if has_column:
        column = [
            column_ref[t * LANES : (t + 1) * LANES].astype(jnp.float32).reshape(1, LANES)
            for t in range(tiles)
        ]
        column = jnp.concatenate(column + [jnp.zeros((4 - tiles, LANES), jnp.float32)], axis=0)
        out_ref[:, tiles * rows // 4] = jnp.broadcast_to(column[None], (count, 4, LANES))


def pack_band(band, count, coeffs, miller, slot, pencil, slots, column):
    length = miller.shape[0]
    width = pencil.shape[1] // 6
    rows = pencil.shape[0] // count * (slots // LANES)
    operands = [coeffs, miller, slot, pencil]
    out_shape = (count, rows, LANES)
    if column is not None:
        operands.append(column)
        out_shape = (count, rows // 4 + 1, 4, LANES)
    one_band = pl.BlockSpec((1, 2 * length, LANES), lambda i: (band, 0, 0))
    return pl.pallas_call(
        functools.partial(pack_kernel, width, column is not None),
        grid=(1,),
        in_specs=[one_band]
        + [
            pl.BlockSpec(memory_space=pl.ANY)
            if x is pencil
            else pl.BlockSpec(x.shape, lambda i, n=x.ndim: (0,) * n)
            for x in operands[1:]
        ],
        out_specs=pl.BlockSpec(out_shape, lambda i: (0,) * len(out_shape)),
        out_shape=jax.ShapeDtypeStruct(out_shape, jnp.float32),
        scratch_shapes=[pltpu.VMEM((2 * slots, 2 * width), jnp.float32)]
        + [pltpu.VMEM((8 * RANK_LOW, LANES), jnp.float32)] * 6
        + [
            pltpu.VMEM((LANES, 2 * width), jnp.bfloat16),
            pltpu.VMEM((slots // 2, LANES), jnp.bfloat16),
            pltpu.VMEM(pencil.shape, jnp.bfloat16),
            pltpu.SemaphoreType.DMA,
        ],
        compiler_params=pltpu.CompilerParams(vmem_limit_bytes=PACK_LIMIT),
        cost_estimate=pl.CostEstimate(
            flops=2 * length * LANES * slots * 4 * width,
            bytes_accessed=16 * length * LANES,
            transcendentals=0,
        ),
        name="pack_band",
    )(*operands)


def wave_kernel(kpts, tiles, scale, is_first, is_last, *refs):
    own_ref, count_ref, came_ref, wave_y_ref, wave_x_ref = refs[:5]
    rest = list(refs[5:])
    forth_ref = rest.pop(0) if is_last else None
    former_ref, cell_ref = (None, None) if is_first else (rest.pop(0), rest.pop(0))
    density_refs = [rest.pop(0) for _ in range(kpts if is_last else 1)]
    if is_first:
        coulomb_ref, cell_ref = rest.pop(0), rest.pop(0)
    send_ref = rest.pop(0) if is_last else None
    values, grid, whole, chosen_ref, high_ref = rest
    planes = density_refs[0].shape[0]
    block = NX // kpts
    part_rows = 2 * planes
    pws = came_ref.shape[0] // kpts
    rows = kpts * part_rows
    total = values.shape[1]

    for j in range(pws):
        for t in range(tiles):
            if is_first:
                groups = [
                    came_ref[k * pws + j, t * (part_rows // 4) + g]
                    for k in range(kpts)
                    for g in range(part_rows // 4)
                ]
            else:
                groups = [
                    came_ref[k * pws + j, t * part_rows : (t + 1) * part_rows] for k in range(kpts)
                ]
            taken = jnp.concatenate(groups, axis=0)
            high, low = pieces(taken)
            first = (j * tiles + t) * LANES
            values[0:rows, first : first + LANES] = high
            values[rows : 2 * rows, first : first + LANES] = low

    tile = 4 * HALF
    ramps = ramp((LANES, tile), 1)
    for j in range(pws):
        for t in range(tiles):
            first = (j * tiles + t) * LANES
            if is_first:
                column = came_ref[j, tiles * part_rows // 4, t : t + 1].astype(jnp.int32)
                cell = ((column // NY + NX // 2) % NX - HALF // 2) * HALF
                cell = cell + (column % NY + NY // 2) % NY - HALF // 2
                cell_ref[:, first : first + LANES] = cell
            else:
                cell = cell_ref[:, first : first + LANES]
            lane = (cell % tile).astype(jnp.float32)
            chosen_ref[first : first + LANES, :] = one_hot_lanes(lane, ramps)
            high_ref[:, first : first + LANES] = sixteen((cell // tile).astype(jnp.float32))
    if is_first:
        step_z = lax.broadcasted_iota(jnp.int32, (NZ, NX), 0)
        step_x = lax.broadcasted_iota(jnp.int32, (NZ, NX), 1)
        for q in range(coulomb_ref.shape[0]):
            freq_y = jnp.full((NZ, NX), own_ref[1] + q, jnp.int32)
            kernel = coulomb(signed_freq(step_z, NZ), signed_freq(step_x, NX), freq_y)
            coulomb_ref[q] = kernel * (1.0 / (NX * NY * NZ))
    left = lax.broadcasted_iota(jnp.int32, (planes, LANES), 1) < HALF
    together = 4

    def place(t, found):
        found = found[:rows] + found[rows:]
        for h in range(2):
            for k in range(kpts):
                real, imag = (
                    found[(2 * k + c) * planes : (2 * k + c + 1) * planes, h * LANES : (h + 1) * LANES]
                    for c in range(2)
                )
                first = (k * HALF + 4 * t + 2 * h) * planes
                grid[first : first + planes, :] = jnp.where(left, real, pltpu.roll(imag, HALF, 1))
                grid[first + planes : first + 2 * planes, :] = jnp.where(
                    left, pltpu.roll(real, HALF, 1), imag
                )

    high = high_ref[...]
    zero = jnp.zeros_like(high)
    for start in range(0, HALF // 4, together):
        kept = []
        for t in range(start, start + together):
            here = high == jnp.full_like(high, t)
            kept += [jnp.where(here, values[r : r + 16, :], zero) for r in range(0, 2 * rows, 16)]
        found = mul(jnp.concatenate(kept, axis=0), chosen_ref[...], NN)
        for s in range(together):
            place(start + s, found[2 * rows * s : 2 * rows * (s + 1)])

    sum_of = count_ref[0]
    for k in range(1, kpts):
        sum_of = sum_of + count_ref[k]

    def spread(number):
        return jnp.full((8, NY), number, jnp.int32).astype(jnp.float32)

    weights = [
        jnp.concatenate([spread(count_ref[k]) / spread(sum_of) * scale] * (NX // 8), axis=0)
        for k in ring_order(kpts)
    ]
    lines = [grid[pl.ds(p, kpts * HALF, stride=planes), :] for p in range(planes)]
    lines = mul3_right(jnp.concatenate(lines, axis=0), wave_y_ref[...], NN)

    for p in range(planes):
        mixed = lines[p * kpts * HALF : (p + 1) * kpts * HALF]
        mixed = jnp.concatenate(
            [
                jnp.concatenate(
                    [mixed[k * HALF : (k + 1) * HALF, c * NY : (c + 1) * NY] for k in range(kpts)],
                    axis=1,
                )
                for c in range(2)
            ],
            axis=0,
        )
        wave = mul3_left(wave_x_ref[...], mixed, NN)
        square = wave[:NX] * wave[:NX] + wave[NX:] * wave[NX:]
        density = weights[0] * square[:, :NY]
        for k in range(1, kpts):
            density = density + weights[k] * square[:, k * NY : (k + 1) * NY]
        if former_ref is not None:
            density = density + former_ref[p]
        if is_last:
            whole[p] = density
        else:
            density_refs[0][p] = density

    if is_last:
        for s, density_ref in enumerate(density_refs):
            first = pl.multiple_of(lax.rem(own_ref[0] + s, kpts) * block, block)
            density_ref[...] = whole[:, pl.ds(first, block), :]
        level = jnp.mean(whole[0, :8, :], axis=(0, 1), keepdims=True)
        field = whole[...].reshape(planes * NX, NY) - level
        half = mul3_right(field, forth_ref[...], NN)
        first_row = lax.broadcasted_iota(jnp.int32, (2 * HALF, NX), 0) == 0
        for p in range(planes):
            turned = jnp.transpose(half[p * NX : (p + 1) * NX])
            turned = turned + jnp.where(first_row, level * NY, 0.0)
            send_ref[pl.ds(p, 2 * HALF, stride=planes), :] = turned


def wave_band(kpts, tiles, total, scale, own, counts, came, wave_y, wave_x, forth, former, cell):
    planes = NZ // came.shape[0]
    block = NX // kpts
    is_first, is_last = former is None, forth is not None
    vmem = pl.BlockSpec(memory_space=pltpu.VMEM)
    operands = [own, counts, came, wave_y, wave_x]
    if is_last:
        operands.append(forth)
    if not is_first:
        operands += [former, cell]
    if is_last:
        out_shape = [jax.ShapeDtypeStruct((planes, block, NY), jnp.float32)] * kpts
    else:
        out_shape = [jax.ShapeDtypeStruct((planes, NX, NY), jnp.float32)]
    if is_first:
        out_shape.append(jax.ShapeDtypeStruct((HALF // came.shape[0], NZ, NX), jnp.float32))
        out_shape.append(jax.ShapeDtypeStruct((1, total), jnp.int32))
    if is_last:
        out_shape.append(jax.ShapeDtypeStruct((2 * HALF * planes, NX), jnp.float32))
    rows = kpts * 2 * planes
    return pl.pallas_call(
        functools.partial(wave_kernel, kpts, tiles, scale, is_first, is_last),
        in_specs=[pl.BlockSpec(memory_space=pltpu.SMEM)] * 2 + [vmem] * (len(operands) - 2),
        out_specs=[vmem] * len(out_shape),
        out_shape=out_shape,
        scratch_shapes=[
            pltpu.VMEM((2 * rows, total), jnp.bfloat16),
            pltpu.VMEM((kpts * planes * HALF, LANES), jnp.float32),
            pltpu.VMEM((planes, NX, NY), jnp.float32),
            pltpu.VMEM((total, 4 * HALF), jnp.bfloat16),
            pltpu.VMEM((16, total), jnp.bfloat16),
        ],
        compiler_params=pltpu.CompilerParams(vmem_limit_bytes=VMEM_LIMIT),
        cost_estimate=pl.CostEstimate(
            flops=4 * rows * total * HALF * HALF, bytes_accessed=4 * came.size, transcendentals=0
        ),
        name="wave_band",
    )(*operands)


def poisson_kernel(pws, own_ref, kernel_ref, came_ref, forth_ref, back_ref, both_x_ref, send_ref):
    count, parts, planes, unused = came_ref.shape
    pairs = parts // 2
    fields = [came_ref[:, i].reshape(NZ, NX) for i in range(parts)]
    level = jnp.mean(fields[0], axis=(0, 1), keepdims=True)
    fields[0] = fields[0] - jnp.where(own_ref[1] == 0, level, 0.0)
    field = jnp.concatenate(fields, axis=1)
    turned = mul3_left(forth_ref[...], field, NN)

    def part(array, half, i):
        return array[half * NZ : (half + 1) * NZ, i * NX : (i + 1) * NX]

    lines = []
    for q in range(pairs):
        lines.append(part(turned, 0, 2 * q) + part(turned, 1, 2 * q + 1))
        lines.append(part(turned, 0, 2 * q + 1) - part(turned, 1, 2 * q))
    spectrum = mul3_right(jnp.concatenate(lines, axis=0), both_x_ref[...], NN)

    lines = []
    for q in range(pairs):
        real = spectrum[2 * q * NZ : (2 * q + 1) * NZ]
        imag = spectrum[(2 * q + 1) * NZ : (2 * q + 2) * NZ]
        kernel = kernel_ref[q]
        lines.append((real[:, :NX] + imag[:, NX:]) * kernel)
        lines.append((imag[:, :NX] - real[:, NX:]) * kernel)
    turned = mul3_right(jnp.concatenate(lines, axis=0), both_x_ref[...], NN)
    lines = []
    for q in range(pairs):
        real = turned[2 * q * NZ : (2 * q + 1) * NZ]
        imag = turned[(2 * q + 1) * NZ : (2 * q + 2) * NZ]
        lines.append(real[:, :NX] - imag[:, NX:])
        lines.append(real[:, NX:] + imag[:, :NX])
    turned = mul3_left(back_ref[...], jnp.concatenate(lines, axis=1), NN)

    kpts = count // pws
    merged = NZ // pws // 8
    block = NX // kpts
    rows = pws * 8
    lane = lax.broadcasted_iota(jnp.int32, (rows, LANES), 1) // block
    for q in range(pairs):
        real = part(turned, 0, 2 * q) - part(turned, 1, 2 * q + 1)
        imag = part(turned, 0, 2 * q + 1) + part(turned, 1, 2 * q)
        for c, value in enumerate((real, imag)):
            for place, a in enumerate(ring_order(kpts)):
                packed = None
                for m in range(merged):
                    piece = value[m * rows : (m + 1) * rows]
                    shift = (m - a) * block % LANES
                    if shift:
                        piece = pltpu.roll(piece, shift, 1)
                    packed = piece if m == 0 else jnp.where(lane == m, piece, packed)
                send_ref[place * pws : (place + 1) * pws, 2 * q + c] = packed.reshape(pws, 8, LANES)


def poisson(pws, own, kernel, came, forth, back, both_x):
    vmem = pl.BlockSpec(memory_space=pltpu.VMEM)
    count, parts, unused, unused = came.shape
    return pl.pallas_call(
        functools.partial(poisson_kernel, pws),
        in_specs=[pl.BlockSpec(memory_space=pltpu.SMEM)] + [vmem] * 5,
        out_specs=vmem,
        out_shape=jax.ShapeDtypeStruct((count, parts, 8, LANES), jnp.float32),
        compiler_params=pltpu.CompilerParams(vmem_limit_bytes=VMEM_LIMIT),
        name="poisson",
    )(own, kernel, came, forth, back, both_x)


def finish_kernel(own_ref, came_ref, back_ref, *refs):
    block_refs, density_ref, out_ref = refs[:-2], refs[-2], refs[-1]
    kpts = len(block_refs)
    planes, block, unused = out_ref.shape
    merged = planes // 8
    for s, block_ref in enumerate(block_refs):
        sender = lax.rem(own_ref[0] + kpts - s, kpts)
        density_ref[pl.ds(sender * (planes // kpts), planes // kpts)] = block_ref[...]
    for h in range(8):
        lines = came_ref[pl.ds(h, 2 * HALF, stride=8), :]
        field = mul3_right(lines, back_ref[...], TN)
        out_ref[h * merged : (h + 1) * merged] = field.reshape(merged, block, NY)


def finish(planes, block, own, came, back_y, blocks):
    vmem = pl.BlockSpec(memory_space=pltpu.VMEM)
    return pl.pallas_call(
        finish_kernel,
        in_specs=[pl.BlockSpec(memory_space=pltpu.SMEM)] + [vmem] * (2 + len(blocks)),
        out_specs=[vmem] * 2,
        out_shape=[jax.ShapeDtypeStruct((planes, block, NY), jnp.float32)] * 2,
        compiler_params=pltpu.CompilerParams(vmem_limit_bytes=VMEM_LIMIT),
        name="finish",
    )(own, came, back_y, *blocks)


def exchange(array):
    kpts, pws = lax.axis_size("kpt"), lax.axis_size("pw")
    kpt_order, pw_order = group_order(kpts, pws)
    group = [k * pws + j for k in kpt_order for j in pw_order]
    return lax.all_to_all(
        array, ("kpt", "pw"), split_axis=0, concat_axis=0, tiled=True, axis_index_groups=[group]
    )


def place_in(order, axis):
    places = jnp.asarray(np.argsort(np.array(order)), jnp.int32)
    return lax.dynamic_index_in_dim(places, lax.axis_index(axis), 0, keepdims=False)


def local_planes(band_coeffs, miller_third, column_slot, column_map, kpoint_counts):
    pws = lax.axis_size("pw")
    kpts = lax.axis_size("kpt")
    count = pws * kpts
    slots = column_map.shape[0]
    band_count = band_coeffs.shape[1]
    z_width = column_slot.shape[1] // slots
    planes = NZ // count
    parts = 2 * HALF // count
    made = tables(kpts, pws, planes)
    pencil = stack_table(made["pencil"](z_width), 1)
    wave_x, forth_z, back_z = (
        stack_table(made[name], 1) for name in ("wave_x", "forth_z", "back_z")
    )
    wave_y, forth_y, back_y, both_x = (
        stack_table(made[name], 0) for name in ("wave_y", "forth_y", "back_y", "both_x")
    )

    tiles = slots // LANES
    length = column_slot.shape[1] // LANES
    coeffs = band_coeffs.reshape(band_count, 2, length, LANES).transpose(0, 2, 1, 3)
    coeffs = coeffs.reshape(band_count, 2 * length, LANES)
    miller = miller_third.reshape(length, LANES)
    slot = column_slot.reshape(length, LANES)
    scale = 2.0 / (column_slot.shape[1] * pws)
    arrived = []
    for band in range(band_count):
        column = column_map if band == 0 else None
        packed = pack_band(
            band, count, coeffs, miller, slot, pencil, slots, column
        )
        arrived.append(exchange(packed))
    kpt_order, pw_order = group_order(kpts, pws)
    device = place_in(kpt_order, "kpt") * pws + place_in(pw_order, "pw")
    own = jnp.stack((lax.axis_index("kpt"), device * (parts // 2))).astype(jnp.int32)
    former = cell = None
    for band in range(band_count):
        forth = forth_y if band == band_count - 1 else None
        made_here = wave_band(
            kpts,
            tiles,
            pws * slots,
            scale,
            own,
            kpoint_counts,
            arrived[band],
            wave_y,
            wave_x,
            forth,
            former,
            cell,
        )
        former = made_here[0]
        if band == 0:
            kernel, cell = made_here[kpts if forth is not None else 1 :][:2]
    half = exchange(made_here[-1].reshape(count, parts, planes, NX))
    blocks = [made_here[0]] + [
        lax.ppermute(made_here[s], "kpt", [(a, (a + s) % kpts) for a in range(kpts)])
        for s in range(1, kpts)
    ]
    back = poisson(pws, own, kernel, half, forth_z, back_z, both_x)
    back = exchange(back).reshape(count * parts * 8, LANES)
    return tuple(finish(NZ // pws, NX // kpts, own, back, back_y, blocks))


def fits_planes(kpts, pws):
    count = kpts * pws
    own = NZ // pws
    return (
        NZ % count == 0
        and NZ // count == 8
        and 2 * HALF % (2 * count) == 0
        and NX % kpts == 0
        and own % 8 == 0
        and own // 8 * (NX // kpts) == LANES
    )


def local(band_coeffs, miller_third, column_slot, column_map, kpoint_counts):
    slots = column_map.shape[0]
    plain = slots % LANES == 0 and LANES <= slots <= 8 * RANK_LOW
    plain = plain and column_slot.shape[1] == slots * LANES
    fits = plain and fits_planes(lax.axis_size("kpt"), lax.axis_size("pw"))
    chosen = local_planes if fits else local_general
    return chosen(band_coeffs, miller_third, column_slot, column_map, kpoint_counts)


def solution(mesh):
    return jax.shard_map(
        local,
        mesh=mesh,
        in_specs=(P("kpt", None, None, "pw"), P("kpt", "pw"), P("kpt", "pw"), P("pw"), P()),
        out_specs=(P("pw", "kpt", None), P("pw", "kpt", None)),
        check_vma=False,
    )
```

```python
import functools
import math

import jax
import jax.numpy as jnp
import numpy as np
from jax import lax
from jax.experimental import pallas as pl
from jax.experimental.pallas import tpu as pltpu
from jax.sharding import PartitionSpec as P

NX = 128
NY = 128
NZ = 256


SPACING = 0.25


def contract(pattern, former, latter):
    return jnp.einsum(
        pattern, former, latter, precision=lax.Precision.HIGHEST, preferred_element_type=jnp.float32
    )


def phase_tables(first_index, second_index, length):
    product = first_index[:, None] * second_index[None, :] % length
    angle = product.astype(jnp.float32) * (2.0 * math.pi / length)
    return (jnp.cos(angle), jnp.sin(angle))


def signed_freq(values, length):
    return jnp.where(values >= length // 2, values - length, values)


def coulomb(freq_z, freq_x, freq_y):
    wave_z = freq_z.astype(jnp.float32) / (NZ * SPACING)
    wave_x = freq_x.astype(jnp.float32) / (NX * SPACING)
    wave_y = freq_y.astype(jnp.float32) / (NY * SPACING)
    squared = (2.0 * math.pi) ** 2 * (wave_z * wave_z + wave_x * wave_x + wave_y * wave_y)
    anchor = (freq_z == 0) & (freq_x == 0) & (freq_y == 0)
    return jnp.where(anchor, 0.0, 4.0 * math.pi / jnp.where(anchor, 1.0, squared))


def poisson_columns(real_part, imag_part, freq_x, freq_y):
    length = real_part.shape[0]
    steps_z = jnp.arange(length, dtype=jnp.int32)
    cos_z, sin_z = phase_tables(steps_z, steps_z, length)
    spec_real = contract("zk,km->zm", cos_z, real_part) + contract("zk,km->zm", sin_z, imag_part)
    spec_imag = contract("zk,km->zm", cos_z, imag_part) - contract("zk,km->zm", sin_z, real_part)
    kernel = coulomb(signed_freq(steps_z, length)[:, None], freq_x[None, :], freq_y[None, :]) / (
        NX * NY * NZ
    )
    spec_real = spec_real * kernel
    spec_imag = spec_imag * kernel
    back_real = contract("zk,km->zm", cos_z, spec_real) - contract("zk,km->zm", sin_z, spec_imag)
    back_imag = contract("zk,km->zm", sin_z, spec_real) + contract("zk,km->zm", cos_z, spec_imag)
    return (back_real, back_imag)


def forward_planes(field):
    steps_x = jnp.arange(NX, dtype=jnp.int32)
    steps_y = jnp.arange(NY, dtype=jnp.int32)
    cos_y, sin_y = phase_tables(steps_y, steps_y, NY)
    cos_x, sin_x = phase_tables(steps_x, steps_x, NX)
    half_real = contract("pxy,ky->pxk", field, cos_y)
    half_imag = -contract("pxy,ky->pxk", field, sin_y)
    spec_real = contract("kx,pxy->pky", cos_x, half_real) + contract(
        "kx,pxy->pky", sin_x, half_imag
    )
    spec_imag = contract("kx,pxy->pky", cos_x, half_imag) - contract(
        "kx,pxy->pky", sin_x, half_real
    )
    return (spec_real, spec_imag)


def local_general(band_coeffs, miller_third, column_slot, column_map, kpoint_counts):
    pw_count = lax.axis_size("pw")
    kpt_count = lax.axis_size("kpt")
    pw_index = lax.axis_index("pw")
    kpt_index = lax.axis_index("kpt")
    col_dev = column_map.shape[0]
    ng_dev = column_slot.shape[1]
    band_count = band_coeffs.shape[1]
    z_width = ng_dev // col_dev
    planes = NZ // pw_count
    x_block = NX // kpt_count
    col_total = pw_count * col_dev
    steps_y = jnp.arange(NY, dtype=jnp.int32)
    steps_x = jnp.arange(NX, dtype=jnp.int32)
    cos_y, sin_y = phase_tables(steps_y, steps_y, NY)
    cos_x, sin_x = phase_tables(steps_x, steps_x, NX)
    all_columns = lax.all_gather(column_map, "pw", axis=0, tiled=True)
    position = (miller_third[0] + z_width // 2) * col_dev + column_slot[0]
    source_of = (
        jnp.zeros((ng_dev,), jnp.int32).at[position].set(jnp.arange(ng_dev, dtype=jnp.int32))
    )
    coeff_rows = band_coeffs[0].reshape(band_count * 2, ng_dev).T
    packed = jnp.take(coeff_rows, source_of, axis=0)
    packed = (
        packed.reshape(z_width, col_dev, band_count, 2)
        .transpose(0, 2, 3, 1)
        .reshape(z_width, band_count * 2 * col_dev)
    )
    cos_z, sin_z = phase_tables(
        jnp.arange(NZ, dtype=jnp.int32), jnp.arange(z_width, dtype=jnp.int32) - z_width // 2, NZ
    )
    by_cos = contract("zj,jc->zc", cos_z, packed).reshape(NZ, band_count, 2, col_dev)
    by_sin = contract("zj,jc->zc", sin_z, packed).reshape(NZ, band_count, 2, col_dev)
    pencil = jnp.stack(
        (by_cos[:, :, 0] - by_sin[:, :, 1], by_sin[:, :, 0] + by_cos[:, :, 1]), axis=2
    )
    pencil = pencil.reshape(NZ, band_count * 2 * col_dev)
    arrived = lax.all_to_all(pencil, "pw", split_axis=0, concat_axis=1, tiled=True)
    arrived = arrived.reshape(planes, pw_count, band_count, 2, col_dev).transpose(2, 1, 4, 3, 0)
    arrived = arrived.reshape(band_count, col_total, 2 * planes)
    arrived = jnp.concatenate(
        (arrived, jnp.zeros((band_count, 1, 2 * planes), jnp.float32)), axis=1
    )
    cell_source = (
        jnp.full((NX * NY,), col_total, jnp.int32)
        .at[all_columns]
        .set(jnp.arange(col_total, dtype=jnp.int32))
    )

    def add_band(band, running):
        one_band = lax.dynamic_index_in_dim(arrived, band, 0, keepdims=False)
        placed = jnp.take(one_band, cell_source, axis=0)
        placed = placed.reshape(NX, NY, 2, planes).transpose(2, 3, 0, 1)
        grid_real = placed[0]
        grid_imag = placed[1]
        mixed_real = contract("pxm,ym->pxy", grid_real, cos_y) - contract(
            "pxm,ym->pxy", grid_imag, sin_y
        )
        mixed_imag = contract("pxm,ym->pxy", grid_real, sin_y) + contract(
            "pxm,ym->pxy", grid_imag, cos_y
        )
        wave_real = contract("xm,pmy->pxy", cos_x, mixed_real) - contract(
            "xm,pmy->pxy", sin_x, mixed_imag
        )
        wave_imag = contract("xm,pmy->pxy", sin_x, mixed_real) + contract(
            "xm,pmy->pxy", cos_x, mixed_imag
        )
        return running + wave_real * wave_real + wave_imag * wave_imag

    squares_sum = lax.fori_loop(0, band_count, add_band, jnp.zeros((planes, NX, NY), jnp.float32))
    weight = (
        2.0
        * kpoint_counts[kpt_index].astype(jnp.float32)
        / jnp.sum(kpoint_counts).astype(jnp.float32)
    )
    weight = weight / (ng_dev * pw_count)
    partial_value = weight * squares_sum
    total_density = lax.psum(partial_value, "kpt")
    density = lax.dynamic_slice_in_dim(total_density, kpt_index * x_block, x_block, 1)
    spec_real, spec_imag = forward_planes(total_density)
    rows_pw = NX // pw_count
    pencil_real, pencil_imag = (
        lax.all_to_all(spec_real, "pw", split_axis=1, concat_axis=0, tiled=True),
        lax.all_to_all(spec_imag, "pw", split_axis=1, concat_axis=0, tiled=True),
    )
    local_x = pw_index * rows_pw + jnp.arange(rows_pw, dtype=jnp.int32)
    freq_x = jnp.repeat(signed_freq(local_x, NX), NY)
    freq_y = jnp.tile(signed_freq(steps_y, NY), rows_pw)
    back_real, back_imag = poisson_columns(
        pencil_real.reshape(NZ, rows_pw * NY), pencil_imag.reshape(NZ, rows_pw * NY), freq_x, freq_y
    )
    plane_real, plane_imag = (
        lax.all_to_all(
            back_real.reshape(NZ, rows_pw, NY), "pw", split_axis=0, concat_axis=1, tiled=True
        ),
        lax.all_to_all(
            back_imag.reshape(NZ, rows_pw, NY), "pw", split_axis=0, concat_axis=1, tiled=True
        ),
    )
    own_rows = kpt_index * x_block + jnp.arange(x_block, dtype=jnp.int32)
    cos_rows, sin_rows = phase_tables(own_rows, steps_x, NX)
    rows_real = contract("xk,pky->pxy", cos_rows, plane_real) - contract(
        "xk,pky->pxy", sin_rows, plane_imag
    )
    rows_imag = contract("xk,pky->pxy", sin_rows, plane_real) + contract(
        "xk,pky->pxy", cos_rows, plane_imag
    )
    hartree = contract("pxk,yk->pxy", rows_real, cos_y) - contract("pxk,yk->pxy", rows_imag, sin_y)
    return (density, hartree)


LANES = 128
HALF = 64
VMEM_LIMIT = 16 * 1024 * 1024
PACK_LIMIT = 56 * 1024 * 1024
NN = (((1,), (0,)), ((), ()))
NT = (((1,), (1,)), ((), ()))
TN = (((0,), (0,)), ((), ()))


def pieces(value):
    high = value.astype(jnp.bfloat16)
    low = (value - high.astype(jnp.float32)).astype(jnp.bfloat16)
    return high, low


def mul(former, latter, dims):
    return lax.dot_general(former, latter, dims, preferred_element_type=jnp.float32)


def mul3_left(former, latter, dims):
    high, low = pieces(latter)
    (unused,), (axis,) = dims[0]
    return mul(former, jnp.concatenate((high, high, low), axis=axis), dims)


def mul3_right(former, latter, dims):
    high, low = pieces(former)
    (axis,), (unused,) = dims[0]
    return mul(jnp.concatenate((high, high, low), axis=axis), latter, dims)


def stack_table(values, axis):
    high = values.astype(np.float32).astype(jnp.bfloat16)
    low = (values - high.astype(np.float64)).astype(np.float32).astype(jnp.bfloat16)
    return jnp.asarray(np.concatenate((high, low, high), axis=axis))


def angles(former, latter, length):
    return np.outer(former, latter) % length * (2.0 * np.pi / length)


def ring_order(length):
    return [0, *range(1, length, 2), *range(length - 2 + length % 2, 0, -2)] if length > 1 else [0]


def group_order(kpts, pws):
    cores = 2 if pws % 2 == 0 else 1
    return ring_order(kpts), [c * cores + i for i in range(cores) for c in ring_order(pws // cores)]


def tables(kpts, pws, planes):
    count = kpts * pws
    kpt_order, pw_order = (np.array(order) for order in group_order(kpts, pws))
    low_freq = np.arange(HALF) - HALF // 2
    grid_x, grid_y, grid_z = np.arange(NX), np.arange(NY), np.arange(NZ)
    own_y = np.arange(HALF)

    device = np.arange(count)
    plane_of = (
        pw_order[device % pws][:, None] * (NZ // pws)
        + kpt_order[device // pws][:, None] * planes
        + np.arange(planes)[None, :]
    )
    return_table = {}

    def pencil(z_width):
        angle = angles(plane_of.ravel(), np.arange(z_width) - z_width // 2, NZ)
        cos, sin = (
            part.reshape(count, 1, planes, z_width) for part in (np.cos(angle), np.sin(angle))
        )
        real = np.concatenate((cos, -sin), axis=3)
        imag = np.concatenate((sin, cos), axis=3)
        return np.concatenate((real, imag), axis=1).reshape(-1, 2 * z_width)

    return_table["pencil"] = pencil

    angle = angles(low_freq, grid_y, NY)
    cos, sin = np.cos(angle), np.sin(angle)
    return_table["wave_y"] = np.block([[cos, sin], [-sin, cos]])

    angle = angles(grid_x, low_freq, NX)
    cos, sin = np.cos(angle), np.sin(angle)
    return_table["wave_x"] = np.block([[cos, -sin], [sin, cos]])

    angle = angles(own_y, grid_y, NY)
    cos, sin = np.cos(angle), np.sin(angle)
    return_table["forth_y"] = np.stack((cos, -sin), axis=1).reshape(2 * HALF, NY).T
    twice = np.where(own_y == 0, 1.0, 2.0)[:, None]
    return_table["back_y"] = np.stack((twice * cos, -twice * sin), axis=1).reshape(2 * HALF, NY)

    angle = angles(grid_z, plane_of.ravel(), NZ)
    return_table["forth_z"] = np.concatenate((np.cos(angle), np.sin(angle)), axis=0)
    own = NZ // pws
    merged = own // 8
    order = (
        pw_order[None, :, None] * own
        + np.arange(8)[None, None, :] * merged
        + np.arange(merged)[:, None, None]
    )
    angle = angles(order.ravel(), grid_z, NZ)
    return_table["back_z"] = np.concatenate((np.cos(angle), np.sin(angle)), axis=0)

    angle = angles(grid_x, grid_x, NX)
    return_table["both_x"] = np.concatenate((np.cos(angle), np.sin(angle)), axis=1)
    return return_table


def ramp(shape, axis, first=0):
    steps = lax.broadcasted_iota(jnp.int32, shape, axis) + first
    return steps.astype(jnp.float32).astype(jnp.bfloat16)


def sixteen(row):
    return jnp.broadcast_to(row, (16, row.shape[1])).astype(jnp.bfloat16)


def one_hot_lanes(row, ramps):
    column = jnp.transpose(jnp.concatenate([sixteen(row)] * (LANES // 16), axis=0))
    one = jnp.ones(column.shape, jnp.bfloat16)
    zero = jnp.zeros(column.shape, jnp.bfloat16)
    return jnp.concatenate(
        [
            jnp.where(column == ramps[:, first : first + LANES], one, zero)
            for first in range(0, ramps.shape[1], LANES)
        ],
        axis=1,
    )


RANK_LOW = 64
WINDOW = 64


def exchange_rows(refs, low_bits, size_bits, descending):
    for outer in range(RANK_LOW):
        if any(outer >> bit & 1 for bit in low_bits[0]):
            continue
        touched = sorted(
            outer + sum(1 << bit for i, bit in enumerate(low_bits[0]) if pattern >> i & 1)
            for pattern in range(1 << len(low_bits[0]))
        )
        held = {v: [ref[v * 8 : v * 8 + 8, :] for ref in refs] for v in touched}
        for size, bits in zip(size_bits, low_bits[1:]):
            for bit in bits:
                for v in touched:
                    if v >> bit & 1:
                        continue
                    former, latter = held[v], held[v | 1 << bit]
                    if size < 6:
                        down = bool(v >> size & 1)
                        swap = former[0] < latter[0] if down else former[0] > latter[0]
                    else:
                        swap = former[0] > latter[0]
                        if descending is not None:
                            swap = jnp.logical_xor(swap, descending)
                    held[v] = [jnp.where(swap, y, x) for x, y in zip(former, latter)]
                    held[v | 1 << bit] = [jnp.where(swap, x, y) for x, y in zip(former, latter)]
        for v in touched:
            for ref, value in zip(refs, held[v]):
                ref[v * 8 : v * 8 + 8, :] = value


def exchange_sublanes(refs, stride, descending):
    sublane = lax.broadcasted_iota(jnp.int32, (8, LANES), 0)
    upper = sublane // stride % 2 == 1
    want_most = upper if descending is None else jnp.logical_xor(upper, descending)
    other = jnp.where(upper, sublane - stride, sublane + stride)

    for v in range(RANK_LOW):
        here = [ref[v * 8 : v * 8 + 8, :] for ref in refs]
        there = [jnp.take_along_axis(value, other, axis=0) for value in here]
        take = jnp.logical_xor(here[0] > there[0], want_most)
        for ref, x, y in zip(refs, here, there):
            ref[v * 8 : v * 8 + 8, :] = jnp.where(take, y, x)


def sort_columns(refs):
    sublane = lax.broadcasted_iota(jnp.int32, (8, LANES), 0)
    exchange_rows(refs, [(0, 1, 2), (0,), (1, 0), (2, 1, 0)], [1, 2, 3], None)
    exchange_rows(refs, [(3,), (3,)], [4], None)
    exchange_rows(refs, [(0, 1, 2), (2, 1, 0)], [4], None)
    exchange_rows(refs, [(3, 4), (4, 3)], [5], None)
    exchange_rows(refs, [(0, 1, 2), (2, 1, 0)], [5], None)
    for size in range(6, 10):
        descending = None if size == 9 else sublane // (1 << (size - 6)) % 2 == 1
        for bit in range(size - 1, 5, -1):
            exchange_sublanes(refs, 1 << (bit - 6), descending)
        exchange_rows(refs, [(3, 4, 5), (5, 4, 3)], [size], descending)
        if size < 9:
            exchange_rows(refs, [(0, 1, 2), (2, 1, 0)], [size], descending)


def pack_kernel(width, has_column, *refs):
    coeff_ref, miller_ref, slot_ref, pencil_ref = refs[:4]
    rest = list(refs[4:])
    column_ref = rest.pop(0) if has_column else None
    out_ref, total, key_ref, real_ref, imag_ref, lane_ref, real_low, imag_low, ramp_ref, step_ref, held, sem = rest
    fetch = pltpu.make_async_copy(pencil_ref, held, sem)
    fetch.start()
    half = total.shape[0] // 4
    slots = 2 * half
    count = out_ref.shape[0]
    rows = pencil_ref.shape[0] // count
    length = miller_ref.shape[0]
    ranks = key_ref.shape[0]

    slot = slot_ref[...]
    second = slot >= half
    lane = miller_ref[...] + width // 2
    key = jnp.where(second, slot - half, slot) * (2 * width) + jnp.where(second, lane + width, lane)
    key_ref[0:length] = key.astype(jnp.float32)
    real_ref[0:length] = coeff_ref[0, pl.ds(0, length, stride=2), :]
    imag_ref[0:length] = coeff_ref[0, pl.ds(1, length, stride=2), :]
    blank = jnp.zeros((ranks - length, LANES), jnp.float32)
    key_ref[length:] = blank + 2.0 * slots * width
    real_ref[length:] = blank
    imag_ref[length:] = blank
    sort_columns((key_ref, real_ref, imag_ref))

    def base_of(block):
        base = 8 * (block // 2) + 8 * (block % 2) - WINDOW // 2
        return jnp.minimum(jnp.maximum(base, 0), half - WINDOW)

    ramp_ref[...] = ramp(ramp_ref.shape, 1)
    step_ref[...] = ramp(step_ref.shape, 0)
    sublane = lax.broadcasted_iota(jnp.int32, (8, LANES), 0)
    astray = jnp.zeros((8, LANES), jnp.float32)
    for v in range(RANK_LOW):
        at = slice(v * 8, v * 8 + 8)
        keys = key_ref[at, :]
        high = jnp.floor(keys * (1.0 / (2 * width)))
        lane_ref[at, :] = keys - high * (2.0 * width)
        key_ref[at, :] = high
        for ref, low_ref in ((real_ref, real_low), (imag_ref, imag_low)):
            value = ref[at, :]
            rounded = value.astype(jnp.bfloat16).astype(jnp.float32)
            ref[at, :] = rounded
            low_ref[at, :] = value - rounded
        offset = high - base_of(sublane * (RANK_LOW // 8) + v // 8).astype(jnp.float32)
        outside = jnp.logical_or(offset < 0.0, offset >= 1.0 * WINDOW)
        astray = jnp.where(outside, 1.0, astray)
    astray = jnp.max(jnp.where(sublane * RANK_LOW < length, astray, 0.0))

    def add(block, base, window):
        first = block % (RANK_LOW // 8) * 64 + block // (RANK_LOW // 8)
        base_row = jnp.full((1, LANES), base, jnp.int32).astype(jnp.float32)
        zero = jnp.zeros((16, LANES), jnp.bfloat16)
        spread, chosen = [], []
        for t in range(8):
            row = pl.ds(first + 8 * t, 1)
            high = sixteen(key_ref[row, :] - base_row)
            masks = [high == step_ref[r : r + 16, :] for r in range(0, window, 16)]
            spread.append(
                jnp.concatenate(
                    [
                        jnp.where(mask, value, zero)
                        for value in [
                            sixteen(ref[row, :]) for ref in (real_ref, imag_ref, real_low, imag_low)
                        ]
                        for mask in masks
                    ],
                    axis=0,
                )
            )
            chosen.append(one_hot_lanes(lane_ref[row, :], ramp_ref[...]))
        found = mul(jnp.concatenate(spread, axis=1), jnp.concatenate(chosen, axis=0), NN)
        for i in range(4):
            if window == half:
                into = pl.ds(i * half, half)
            else:
                into = pl.ds(pl.multiple_of(i * half + base, 8), window)
            total[into, :] += found[i * window : (i + 1) * window]

    total[...] = jnp.zeros_like(total)
    blocks = length // 8
    together = 4 if blocks % 4 == 0 else 1

    @pl.when(astray == 0.0)
    def _():
        def some_blocks(i, unused):
            for s in range(together):
                block = together * i + s
                add(block, base_of(block), WINDOW)
            return unused

        lax.fori_loop(0, blocks // together, some_blocks, 0)

    @pl.when(astray > 0.0)
    def _():
        def one_block(block, unused):
            add(block, 0, half)
            return unused

        lax.fori_loop(0, blocks, one_block, 0)

    both = []
    for at in range(2):
        parts = [
            total[(2 * at + c) * half : (2 * at + c + 1) * half].astype(jnp.bfloat16)
            for c in range(2)
        ]
        both.append(
            jnp.concatenate(
                [
                    jnp.concatenate([part[:, h * width : (h + 1) * width] for part in parts], axis=1)
                    for h in range(2)
                ],
                axis=0,
            )
        )
    fetch.wait()
    pencils = mul(held[...], jnp.concatenate((both[0], both[0], both[1]), axis=1), NT)
    tiles = slots // LANES
    for t in range(tiles):
        tile = pencils[:, t * LANES : (t + 1) * LANES].reshape(count, rows, LANES)
        if not has_column:
            out_ref[:, t * rows : (t + 1) * rows] = tile
            continue
        for g in range(rows // 4):
            out_ref[:, t * (rows // 4) + g] = tile[:, 4 * g : 4 * g + 4]
    if has_column:
        column = [
            column_ref[t * LANES : (t + 1) * LANES].astype(jnp.float32).reshape(1, LANES)
            for t in range(tiles)
        ]
        column = jnp.concatenate(column + [jnp.zeros((4 - tiles, LANES), jnp.float32)], axis=0)
        out_ref[:, tiles * rows // 4] = jnp.broadcast_to(column[None], (count, 4, LANES))


def pack_band(band, count, coeffs, miller, slot, pencil, slots, column):
    length = miller.shape[0]
    width = pencil.shape[1] // 6
    rows = pencil.shape[0] // count * (slots // LANES)
    operands = [coeffs, miller, slot, pencil]
    out_shape = (count, rows, LANES)
    if column is not None:
        operands.append(column)
        out_shape = (count, rows // 4 + 1, 4, LANES)
    one_band = pl.BlockSpec((1, 2 * length, LANES), lambda i: (band, 0, 0))
    return pl.pallas_call(
        functools.partial(pack_kernel, width, column is not None),
        grid=(1,),
        in_specs=[one_band]
        + [
            pl.BlockSpec(memory_space=pl.ANY)
            if x is pencil
            else pl.BlockSpec(x.shape, lambda i, n=x.ndim: (0,) * n)
            for x in operands[1:]
        ],
        out_specs=pl.BlockSpec(out_shape, lambda i: (0,) * len(out_shape)),
        out_shape=jax.ShapeDtypeStruct(out_shape, jnp.float32),
        scratch_shapes=[pltpu.VMEM((2 * slots, 2 * width), jnp.float32)]
        + [pltpu.VMEM((8 * RANK_LOW, LANES), jnp.float32)] * 6
        + [
            pltpu.VMEM((LANES, 2 * width), jnp.bfloat16),
            pltpu.VMEM((slots // 2, LANES), jnp.bfloat16),
            pltpu.VMEM(pencil.shape, jnp.bfloat16),
            pltpu.SemaphoreType.DMA,
        ],
        compiler_params=pltpu.CompilerParams(vmem_limit_bytes=PACK_LIMIT),
        cost_estimate=pl.CostEstimate(
            flops=2 * length * LANES * slots * 4 * width,
            bytes_accessed=16 * length * LANES,
            transcendentals=0,
        ),
        name="pack_band",
    )(*operands)


def wave_kernel(kpts, tiles, scale, is_first, is_last, *refs):
    own_ref, count_ref, came_ref, wave_y_ref, wave_x_ref = refs[:5]
    rest = list(refs[5:])
    forth_ref = rest.pop(0) if is_last else None
    former_ref, cell_ref = (None, None) if is_first else (rest.pop(0), rest.pop(0))
    density_refs = [rest.pop(0) for _ in range(kpts if is_last else 1)]
    if is_first:
        coulomb_ref, cell_ref = rest.pop(0), rest.pop(0)
    send_ref = rest.pop(0) if is_last else None
    values, grid, whole, chosen_ref, high_ref = rest
    planes = density_refs[0].shape[0]
    block = NX // kpts
    part_rows = 2 * planes
    pws = came_ref.shape[0] // kpts
    rows = kpts * part_rows
    total = values.shape[1]

    for j in range(pws):
        for t in range(tiles):
            if is_first:
                groups = [
                    came_ref[k * pws + j, t * (part_rows // 4) + g]
                    for k in range(kpts)
                    for g in range(part_rows // 4)
                ]
            else:
                groups = [
                    came_ref[k * pws + j, t * part_rows : (t + 1) * part_rows] for k in range(kpts)
                ]
            taken = jnp.concatenate(groups, axis=0)
            high, low = pieces(taken)
            first = (j * tiles + t) * LANES
            values[0:rows, first : first + LANES] = high
            values[rows : 2 * rows, first : first + LANES] = low

    tile = 4 * HALF
    ramps = ramp((LANES, tile), 1)
    for j in range(pws):
        for t in range(tiles):
            first = (j * tiles + t) * LANES
            if is_first:
                column = came_ref[j, tiles * part_rows // 4, t : t + 1].astype(jnp.int32)
                cell = ((column // NY + NX // 2) % NX - HALF // 2) * HALF
                cell = cell + (column % NY + NY // 2) % NY - HALF // 2
                cell_ref[:, first : first + LANES] = cell
            else:
                cell = cell_ref[:, first : first + LANES]
            lane = (cell % tile).astype(jnp.float32)
            chosen_ref[first : first + LANES, :] = one_hot_lanes(lane, ramps)
            high_ref[:, first : first + LANES] = sixteen((cell // tile).astype(jnp.float32))
    if is_first:
        step_z = lax.broadcasted_iota(jnp.int32, (NZ, NX), 0)
        step_x = lax.broadcasted_iota(jnp.int32, (NZ, NX), 1)
        for q in range(coulomb_ref.shape[0]):
            freq_y = jnp.full((NZ, NX), own_ref[1] + q, jnp.int32)
            kernel = coulomb(signed_freq(step_z, NZ), signed_freq(step_x, NX), freq_y)
            coulomb_ref[q] = kernel * (1.0 / (NX * NY * NZ))
    left = lax.broadcasted_iota(jnp.int32, (planes, LANES), 1) < HALF
    together = 4

    def place(t, found):
        found = found[:rows] + found[rows:]
        for h in range(2):
            for k in range(kpts):
                real, imag = (
                    found[(2 * k + c) * planes : (2 * k + c + 1) * planes, h * LANES : (h + 1) * LANES]
                    for c in range(2)
                )
                first = (k * HALF + 4 * t + 2 * h) * planes
                grid[first : first + planes, :] = jnp.where(left, real, pltpu.roll(imag, HALF, 1))
                grid[first + planes : first + 2 * planes, :] = jnp.where(
                    left, pltpu.roll(real, HALF, 1), imag
                )

    high = high_ref[...]
    zero = jnp.zeros_like(high)
    for start in range(0, HALF // 4, together):
        kept = []
        for t in range(start, start + together):
            here = high == jnp.full_like(high, t)
            kept += [jnp.where(here, values[r : r + 16, :], zero) for r in range(0, 2 * rows, 16)]
        found = mul(jnp.concatenate(kept, axis=0), chosen_ref[...], NN)
        for s in range(together):
            place(start + s, found[2 * rows * s : 2 * rows * (s + 1)])

    sum_of = count_ref[0]
    for k in range(1, kpts):
        sum_of = sum_of + count_ref[k]

    def spread(number):
        return jnp.full((8, NY), number, jnp.int32).astype(jnp.float32)

    weights = [
        jnp.concatenate([spread(count_ref[k]) / spread(sum_of) * scale] * (NX // 8), axis=0)
        for k in ring_order(kpts)
    ]
    lines = [grid[pl.ds(p, kpts * HALF, stride=planes), :] for p in range(planes)]
    lines = mul3_right(jnp.concatenate(lines, axis=0), wave_y_ref[...], NN)

    for p in range(planes):
        mixed = lines[p * kpts * HALF : (p + 1) * kpts * HALF]
        mixed = jnp.concatenate(
            [
                jnp.concatenate(
                    [mixed[k * HALF : (k + 1) * HALF, c * NY : (c + 1) * NY] for k in range(kpts)],
                    axis=1,
                )
                for c in range(2)
            ],
            axis=0,
        )
        wave = mul3_left(wave_x_ref[...], mixed, NN)
        square = wave[:NX] * wave[:NX] + wave[NX:] * wave[NX:]
        density = weights[0] * square[:, :NY]
        for k in range(1, kpts):
            density = density + weights[k] * square[:, k * NY : (k + 1) * NY]
        if former_ref is not None:
            density = density + former_ref[p]
        if is_last:
            whole[p] = density
        else:
            density_refs[0][p] = density

    if is_last:
        for s, density_ref in enumerate(density_refs):
            first = pl.multiple_of(lax.rem(own_ref[0] + s, kpts) * block, block)
            density_ref[...] = whole[:, pl.ds(first, block), :]
        level = jnp.mean(whole[0, :8, :], axis=(0, 1), keepdims=True)
        field = whole[...].reshape(planes * NX, NY) - level
        half = mul3_right(field, forth_ref[...], NN)
        first_row = lax.broadcasted_iota(jnp.int32, (2 * HALF, NX), 0) == 0
        for p in range(planes):
            turned = jnp.transpose(half[p * NX : (p + 1) * NX])
            turned = turned + jnp.where(first_row, level * NY, 0.0)
            send_ref[pl.ds(p, 2 * HALF, stride=planes), :] = turned


def wave_band(kpts, tiles, total, scale, own, counts, came, wave_y, wave_x, forth, former, cell):
    planes = NZ // came.shape[0]
    block = NX // kpts
    is_first, is_last = former is None, forth is not None
    vmem = pl.BlockSpec(memory_space=pltpu.VMEM)
    operands = [own, counts, came, wave_y, wave_x]
    if is_last:
        operands.append(forth)
    if not is_first:
        operands += [former, cell]
    if is_last:
        out_shape = [jax.ShapeDtypeStruct((planes, block, NY), jnp.float32)] * kpts
    else:
        out_shape = [jax.ShapeDtypeStruct((planes, NX, NY), jnp.float32)]
    if is_first:
        out_shape.append(jax.ShapeDtypeStruct((HALF // came.shape[0], NZ, NX), jnp.float32))
        out_shape.append(jax.ShapeDtypeStruct((1, total), jnp.int32))
    if is_last:
        out_shape.append(jax.ShapeDtypeStruct((2 * HALF * planes, NX), jnp.float32))
    rows = kpts * 2 * planes
    return pl.pallas_call(
        functools.partial(wave_kernel, kpts, tiles, scale, is_first, is_last),
        in_specs=[pl.BlockSpec(memory_space=pltpu.SMEM)] * 2 + [vmem] * (len(operands) - 2),
        out_specs=[vmem] * len(out_shape),
        out_shape=out_shape,
        scratch_shapes=[
            pltpu.VMEM((2 * rows, total), jnp.bfloat16),
            pltpu.VMEM((kpts * planes * HALF, LANES), jnp.float32),
            pltpu.VMEM((planes, NX, NY), jnp.float32),
            pltpu.VMEM((total, 4 * HALF), jnp.bfloat16),
            pltpu.VMEM((16, total), jnp.bfloat16),
        ],
        compiler_params=pltpu.CompilerParams(vmem_limit_bytes=VMEM_LIMIT),
        cost_estimate=pl.CostEstimate(
            flops=4 * rows * total * HALF * HALF, bytes_accessed=4 * came.size, transcendentals=0
        ),
        name="wave_band",
    )(*operands)


def poisson_kernel(pws, own_ref, kernel_ref, came_ref, forth_ref, back_ref, both_x_ref, send_ref):
    count, parts, planes, unused = came_ref.shape
    pairs = parts // 2
    fields = [came_ref[:, i].reshape(NZ, NX) for i in range(parts)]
    level = jnp.mean(fields[0], axis=(0, 1), keepdims=True)
    fields[0] = fields[0] - jnp.where(own_ref[1] == 0, level, 0.0)
    field = jnp.concatenate(fields, axis=1)
    turned = mul3_left(forth_ref[...], field, NN)

    def part(array, half, i):
        return array[half * NZ : (half + 1) * NZ, i * NX : (i + 1) * NX]

    lines = []
    for q in range(pairs):
        lines.append(part(turned, 0, 2 * q) + part(turned, 1, 2 * q + 1))
        lines.append(part(turned, 0, 2 * q + 1) - part(turned, 1, 2 * q))
    spectrum = mul3_right(jnp.concatenate(lines, axis=0), both_x_ref[...], NN)

    lines = []
    for q in range(pairs):
        real = spectrum[2 * q * NZ : (2 * q + 1) * NZ]
        imag = spectrum[(2 * q + 1) * NZ : (2 * q + 2) * NZ]
        kernel = kernel_ref[q]
        lines.append((real[:, :NX] + imag[:, NX:]) * kernel)
        lines.append((imag[:, :NX] - real[:, NX:]) * kernel)
    turned = mul3_right(jnp.concatenate(lines, axis=0), both_x_ref[...], NN)
    lines = []
    for q in range(pairs):
        real = turned[2 * q * NZ : (2 * q + 1) * NZ]
        imag = turned[(2 * q + 1) * NZ : (2 * q + 2) * NZ]
        lines.append(real[:, :NX] - imag[:, NX:])
        lines.append(real[:, NX:] + imag[:, :NX])
    turned = mul3_left(back_ref[...], jnp.concatenate(lines, axis=1), NN)

    kpts = count // pws
    merged = NZ // pws // 8
    block = NX // kpts
    rows = pws * 8
    lane = lax.broadcasted_iota(jnp.int32, (rows, LANES), 1) // block
    for q in range(pairs):
        real = part(turned, 0, 2 * q) - part(turned, 1, 2 * q + 1)
        imag = part(turned, 0, 2 * q + 1) + part(turned, 1, 2 * q)
        for c, value in enumerate((real, imag)):
            for place, a in enumerate(ring_order(kpts)):
                packed = None
                for m in range(merged):
                    piece = value[m * rows : (m + 1) * rows]
                    shift = (m - a) * block % LANES
                    if shift:
                        piece = pltpu.roll(piece, shift, 1)
                    packed = piece if m == 0 else jnp.where(lane == m, piece, packed)
                send_ref[place * pws : (place + 1) * pws, 2 * q + c] = packed.reshape(pws, 8, LANES)


def poisson(pws, own, kernel, came, forth, back, both_x):
    vmem = pl.BlockSpec(memory_space=pltpu.VMEM)
    count, parts, unused, unused = came.shape
    return pl.pallas_call(
        functools.partial(poisson_kernel, pws),
        in_specs=[pl.BlockSpec(memory_space=pltpu.SMEM)] + [vmem] * 5,
        out_specs=vmem,
        out_shape=jax.ShapeDtypeStruct((count, parts, 8, LANES), jnp.float32),
        compiler_params=pltpu.CompilerParams(vmem_limit_bytes=VMEM_LIMIT),
        name="poisson",
    )(own, kernel, came, forth, back, both_x)


def finish_kernel(own_ref, came_ref, back_ref, *refs):
    block_refs, density_ref, out_ref = refs[:-2], refs[-2], refs[-1]
    kpts = len(block_refs)
    planes, block, unused = out_ref.shape
    merged = planes // 8
    for s, block_ref in enumerate(block_refs):
        sender = lax.rem(own_ref[0] + kpts - s, kpts)
        density_ref[pl.ds(sender * (planes // kpts), planes // kpts)] = block_ref[...]
    for h in range(8):
        lines = came_ref[pl.ds(h, 2 * HALF, stride=8), :]
        field = mul3_right(lines, back_ref[...], TN)
        out_ref[h * merged : (h + 1) * merged] = field.reshape(merged, block, NY)


def finish(planes, block, own, came, back_y, blocks):
    vmem = pl.BlockSpec(memory_space=pltpu.VMEM)
    return pl.pallas_call(
        finish_kernel,
        in_specs=[pl.BlockSpec(memory_space=pltpu.SMEM)] + [vmem] * (2 + len(blocks)),
        out_specs=[vmem] * 2,
        out_shape=[jax.ShapeDtypeStruct((planes, block, NY), jnp.float32)] * 2,
        compiler_params=pltpu.CompilerParams(vmem_limit_bytes=VMEM_LIMIT),
        name="finish",
    )(own, came, back_y, *blocks)


def exchange(array):
    kpts, pws = lax.axis_size("kpt"), lax.axis_size("pw")
    kpt_order, pw_order = group_order(kpts, pws)
    group = [k * pws + j for k in kpt_order for j in pw_order]
    return lax.all_to_all(
        array, ("kpt", "pw"), split_axis=0, concat_axis=0, tiled=True, axis_index_groups=[group]
    )


def place_in(order, axis):
    places = jnp.asarray(np.argsort(np.array(order)), jnp.int32)
    return lax.dynamic_index_in_dim(places, lax.axis_index(axis), 0, keepdims=False)


def local_planes(band_coeffs, miller_third, column_slot, column_map, kpoint_counts):
    pws = lax.axis_size("pw")
    kpts = lax.axis_size("kpt")
    count = pws * kpts
    slots = column_map.shape[0]
    band_count = band_coeffs.shape[1]
    z_width = column_slot.shape[1] // slots
    planes = NZ // count
    parts = 2 * HALF // count
    made = tables(kpts, pws, planes)
    pencil = stack_table(made["pencil"](z_width), 1)
    wave_x, forth_z, back_z = (
        stack_table(made[name], 1) for name in ("wave_x", "forth_z", "back_z")
    )
    wave_y, forth_y, back_y, both_x = (
        stack_table(made[name], 0) for name in ("wave_y", "forth_y", "back_y", "both_x")
    )

    tiles = slots // LANES
    length = column_slot.shape[1] // LANES
    coeffs = band_coeffs.reshape(band_count, 2, length, LANES).transpose(0, 2, 1, 3)
    coeffs = coeffs.reshape(band_count, 2 * length, LANES)
    miller = miller_third.reshape(length, LANES)
    slot = column_slot.reshape(length, LANES)
    scale = 2.0 / (column_slot.shape[1] * pws)
    arrived = []
    for band in range(band_count):
        column = column_map if band == 0 else None
        packed = pack_band(
            band, count, coeffs, miller, slot, pencil, slots, column
        )
        arrived.append(exchange(packed))
    kpt_order, pw_order = group_order(kpts, pws)
    device = place_in(kpt_order, "kpt") * pws + place_in(pw_order, "pw")
    own = jnp.stack((lax.axis_index("kpt"), device * (parts // 2))).astype(jnp.int32)
    former = cell = None
    for band in range(band_count):
        forth = forth_y if band == band_count - 1 else None
        made_here = wave_band(
            kpts,
            tiles,
            pws * slots,
            scale,
            own,
            kpoint_counts,
            arrived[band],
            wave_y,
            wave_x,
            forth,
            former,
            cell,
        )
        former = made_here[0]
        if band == 0:
            kernel, cell = made_here[kpts if forth is not None else 1 :][:2]
    half = exchange(made_here[-1].reshape(count, parts, planes, NX))
    blocks = [made_here[0]] + [
        lax.ppermute(made_here[s], "kpt", [(a, (a + s) % kpts) for a in range(kpts)])
        for s in range(1, kpts)
    ]
    back = poisson(pws, own, kernel, half, forth_z, back_z, both_x)
    back = exchange(back).reshape(count * parts * 8, LANES)
    return tuple(finish(NZ // pws, NX // kpts, own, back, back_y, blocks))


def fits_planes(kpts, pws):
    count = kpts * pws
    own = NZ // pws
    return (
        NZ % count == 0
        and NZ // count == 8
        and 2 * HALF % (2 * count) == 0
        and NX % kpts == 0
        and own % 8 == 0
        and own // 8 * (NX // kpts) == LANES
    )


def local(band_coeffs, miller_third, column_slot, column_map, kpoint_counts):
    slots = column_map.shape[0]
    plain = slots % LANES == 0 and LANES <= slots <= 8 * RANK_LOW
    plain = plain and column_slot.shape[1] == slots * LANES
    fits = plain and fits_planes(lax.axis_size("kpt"), lax.axis_size("pw"))
    chosen = local_planes if fits else local_general
    return chosen(band_coeffs, miller_third, column_slot, column_map, kpoint_counts)


def solution(mesh):
    return jax.shard_map(
        local,
        mesh=mesh,
        in_specs=(P("kpt", None, None, "pw"), P("kpt", "pw"), P("kpt", "pw"), P("pw"), P()),
        out_specs=(P("pw", "kpt", None), P("pw", "kpt", None)),
        check_vma=False,
    )
```

```python
import functools
import math

import jax
import jax.numpy as jnp
import numpy as np
from jax import lax
from jax.experimental import pallas as pl
from jax.experimental.pallas import tpu as pltpu
from jax.sharding import PartitionSpec as P

NX = 128
NY = 128
NZ = 256


SPACING = 0.25


def contract(pattern, former, latter):
    return jnp.einsum(
        pattern, former, latter, precision=lax.Precision.HIGHEST, preferred_element_type=jnp.float32
    )


def phase_tables(first_index, second_index, length):
    product = first_index[:, None] * second_index[None, :] % length
    angle = product.astype(jnp.float32) * (2.0 * math.pi / length)
    return (jnp.cos(angle), jnp.sin(angle))


def signed_freq(values, length):
    return jnp.where(values >= length // 2, values - length, values)


def coulomb(freq_z, freq_x, freq_y):
    wave_z = freq_z.astype(jnp.float32) / (NZ * SPACING)
    wave_x = freq_x.astype(jnp.float32) / (NX * SPACING)
    wave_y = freq_y.astype(jnp.float32) / (NY * SPACING)
    squared = (2.0 * math.pi) ** 2 * (wave_z * wave_z + wave_x * wave_x + wave_y * wave_y)
    anchor = (freq_z == 0) & (freq_x == 0) & (freq_y == 0)
    return jnp.where(anchor, 0.0, 4.0 * math.pi / jnp.where(anchor, 1.0, squared))


def poisson_columns(real_part, imag_part, freq_x, freq_y):
    length = real_part.shape[0]
    steps_z = jnp.arange(length, dtype=jnp.int32)
    cos_z, sin_z = phase_tables(steps_z, steps_z, length)
    spec_real = contract("zk,km->zm", cos_z, real_part) + contract("zk,km->zm", sin_z, imag_part)
    spec_imag = contract("zk,km->zm", cos_z, imag_part) - contract("zk,km->zm", sin_z, real_part)
    kernel = coulomb(signed_freq(steps_z, length)[:, None], freq_x[None, :], freq_y[None, :]) / (
        NX * NY * NZ
    )
    spec_real = spec_real * kernel
    spec_imag = spec_imag * kernel
    back_real = contract("zk,km->zm", cos_z, spec_real) - contract("zk,km->zm", sin_z, spec_imag)
    back_imag = contract("zk,km->zm", sin_z, spec_real) + contract("zk,km->zm", cos_z, spec_imag)
    return (back_real, back_imag)


def forward_planes(field):
    steps_x = jnp.arange(NX, dtype=jnp.int32)
    steps_y = jnp.arange(NY, dtype=jnp.int32)
    cos_y, sin_y = phase_tables(steps_y, steps_y, NY)
    cos_x, sin_x = phase_tables(steps_x, steps_x, NX)
    half_real = contract("pxy,ky->pxk", field, cos_y)
    half_imag = -contract("pxy,ky->pxk", field, sin_y)
    spec_real = contract("kx,pxy->pky", cos_x, half_real) + contract(
        "kx,pxy->pky", sin_x, half_imag
    )
    spec_imag = contract("kx,pxy->pky", cos_x, half_imag) - contract(
        "kx,pxy->pky", sin_x, half_real
    )
    return (spec_real, spec_imag)


def local_general(band_coeffs, miller_third, column_slot, column_map, kpoint_counts):
    pw_count = lax.axis_size("pw")
    kpt_count = lax.axis_size("kpt")
    pw_index = lax.axis_index("pw")
    kpt_index = lax.axis_index("kpt")
    col_dev = column_map.shape[0]
    ng_dev = column_slot.shape[1]
    band_count = band_coeffs.shape[1]
    z_width = ng_dev // col_dev
    planes = NZ // pw_count
    x_block = NX // kpt_count
    col_total = pw_count * col_dev
    steps_y = jnp.arange(NY, dtype=jnp.int32)
    steps_x = jnp.arange(NX, dtype=jnp.int32)
    cos_y, sin_y = phase_tables(steps_y, steps_y, NY)
    cos_x, sin_x = phase_tables(steps_x, steps_x, NX)
    all_columns = lax.all_gather(column_map, "pw", axis=0, tiled=True)
    position = (miller_third[0] + z_width // 2) * col_dev + column_slot[0]
    source_of = (
        jnp.zeros((ng_dev,), jnp.int32).at[position].set(jnp.arange(ng_dev, dtype=jnp.int32))
    )
    coeff_rows = band_coeffs[0].reshape(band_count * 2, ng_dev).T
    packed = jnp.take(coeff_rows, source_of, axis=0)
    packed = (
        packed.reshape(z_width, col_dev, band_count, 2)
        .transpose(0, 2, 3, 1)
        .reshape(z_width, band_count * 2 * col_dev)
    )
    cos_z, sin_z = phase_tables(
        jnp.arange(NZ, dtype=jnp.int32), jnp.arange(z_width, dtype=jnp.int32) - z_width // 2, NZ
    )
    by_cos = contract("zj,jc->zc", cos_z, packed).reshape(NZ, band_count, 2, col_dev)
    by_sin = contract("zj,jc->zc", sin_z, packed).reshape(NZ, band_count, 2, col_dev)
    pencil = jnp.stack(
        (by_cos[:, :, 0] - by_sin[:, :, 1], by_sin[:, :, 0] + by_cos[:, :, 1]), axis=2
    )
    pencil = pencil.reshape(NZ, band_count * 2 * col_dev)
    arrived = lax.all_to_all(pencil, "pw", split_axis=0, concat_axis=1, tiled=True)
    arrived = arrived.reshape(planes, pw_count, band_count, 2, col_dev).transpose(2, 1, 4, 3, 0)
    arrived = arrived.reshape(band_count, col_total, 2 * planes)
    arrived = jnp.concatenate(
        (arrived, jnp.zeros((band_count, 1, 2 * planes), jnp.float32)), axis=1
    )
    cell_source = (
        jnp.full((NX * NY,), col_total, jnp.int32)
        .at[all_columns]
        .set(jnp.arange(col_total, dtype=jnp.int32))
    )

    def add_band(band, running):
        one_band = lax.dynamic_index_in_dim(arrived, band, 0, keepdims=False)
        placed = jnp.take(one_band, cell_source, axis=0)
        placed = placed.reshape(NX, NY, 2, planes).transpose(2, 3, 0, 1)
        grid_real = placed[0]
        grid_imag = placed[1]
        mixed_real = contract("pxm,ym->pxy", grid_real, cos_y) - contract(
            "pxm,ym->pxy", grid_imag, sin_y
        )
        mixed_imag = contract("pxm,ym->pxy", grid_real, sin_y) + contract(
            "pxm,ym->pxy", grid_imag, cos_y
        )
        wave_real = contract("xm,pmy->pxy", cos_x, mixed_real) - contract(
            "xm,pmy->pxy", sin_x, mixed_imag
        )
        wave_imag = contract("xm,pmy->pxy", sin_x, mixed_real) + contract(
            "xm,pmy->pxy", cos_x, mixed_imag
        )
        return running + wave_real * wave_real + wave_imag * wave_imag

    squares_sum = lax.fori_loop(0, band_count, add_band, jnp.zeros((planes, NX, NY), jnp.float32))
    weight = (
        2.0
        * kpoint_counts[kpt_index].astype(jnp.float32)
        / jnp.sum(kpoint_counts).astype(jnp.float32)
    )
    weight = weight / (ng_dev * pw_count)
    partial_value = weight * squares_sum
    total_density = lax.psum(partial_value, "kpt")
    density = lax.dynamic_slice_in_dim(total_density, kpt_index * x_block, x_block, 1)
    spec_real, spec_imag = forward_planes(total_density)
    rows_pw = NX // pw_count
    pencil_real, pencil_imag = (
        lax.all_to_all(spec_real, "pw", split_axis=1, concat_axis=0, tiled=True),
        lax.all_to_all(spec_imag, "pw", split_axis=1, concat_axis=0, tiled=True),
    )
    local_x = pw_index * rows_pw + jnp.arange(rows_pw, dtype=jnp.int32)
    freq_x = jnp.repeat(signed_freq(local_x, NX), NY)
    freq_y = jnp.tile(signed_freq(steps_y, NY), rows_pw)
    back_real, back_imag = poisson_columns(
        pencil_real.reshape(NZ, rows_pw * NY), pencil_imag.reshape(NZ, rows_pw * NY), freq_x, freq_y
    )
    plane_real, plane_imag = (
        lax.all_to_all(
            back_real.reshape(NZ, rows_pw, NY), "pw", split_axis=0, concat_axis=1, tiled=True
        ),
        lax.all_to_all(
            back_imag.reshape(NZ, rows_pw, NY), "pw", split_axis=0, concat_axis=1, tiled=True
        ),
    )
    own_rows = kpt_index * x_block + jnp.arange(x_block, dtype=jnp.int32)
    cos_rows, sin_rows = phase_tables(own_rows, steps_x, NX)
    rows_real = contract("xk,pky->pxy", cos_rows, plane_real) - contract(
        "xk,pky->pxy", sin_rows, plane_imag
    )
    rows_imag = contract("xk,pky->pxy", sin_rows, plane_real) + contract(
        "xk,pky->pxy", cos_rows, plane_imag
    )
    hartree = contract("pxk,yk->pxy", rows_real, cos_y) - contract("pxk,yk->pxy", rows_imag, sin_y)
    return (density, hartree)


LANES = 128
HALF = 64
VMEM_LIMIT = 16 * 1024 * 1024
PACK_LIMIT = 56 * 1024 * 1024
NN = (((1,), (0,)), ((), ()))
NT = (((1,), (1,)), ((), ()))
TN = (((0,), (0,)), ((), ()))


def pieces(value):
    high = value.astype(jnp.bfloat16)
    low = (value - high.astype(jnp.float32)).astype(jnp.bfloat16)
    return high, low


def mul(former, latter, dims):
    return lax.dot_general(former, latter, dims, preferred_element_type=jnp.float32)


def mul3_left(former, latter, dims):
    high, low = pieces(latter)
    (unused,), (axis,) = dims[0]
    return mul(former, jnp.concatenate((high, high, low), axis=axis), dims)


def mul3_right(former, latter, dims):
    high, low = pieces(former)
    (axis,), (unused,) = dims[0]
    return mul(jnp.concatenate((high, high, low), axis=axis), latter, dims)


def stack_table(values, axis):
    high = values.astype(np.float32).astype(jnp.bfloat16)
    low = (values - high.astype(np.float64)).astype(np.float32).astype(jnp.bfloat16)
    return jnp.asarray(np.concatenate((high, low, high), axis=axis))


def angles(former, latter, length):
    return np.outer(former, latter) % length * (2.0 * np.pi / length)


def ring_order(length):
    return [0, *range(1, length, 2), *range(length - 2 + length % 2, 0, -2)] if length > 1 else [0]


def group_order(kpts, pws):
    cores = 2 if pws % 2 == 0 else 1
    return ring_order(kpts), [c * cores + i for c in ring_order(pws // cores) for i in range(cores)]


def tables(kpts, pws, planes):
    count = kpts * pws
    kpt_order, pw_order = (np.array(order) for order in group_order(kpts, pws))
    low_freq = np.arange(HALF) - HALF // 2
    grid_x, grid_y, grid_z = np.arange(NX), np.arange(NY), np.arange(NZ)
    own_y = np.arange(HALF)

    device = np.arange(count)
    plane_of = (
        pw_order[device % pws][:, None] * (NZ // pws)
        + kpt_order[device // pws][:, None] * planes
        + np.arange(planes)[None, :]
    )
    return_table = {}

    def pencil(z_width):
        angle = angles(plane_of.ravel(), np.arange(z_width) - z_width // 2, NZ)
        cos, sin = (
            part.reshape(count, 1, planes, z_width) for part in (np.cos(angle), np.sin(angle))
        )
        real = np.concatenate((cos, -sin), axis=3)
        imag = np.concatenate((sin, cos), axis=3)
        return np.concatenate((real, imag), axis=1).reshape(-1, 2 * z_width)

    return_table["pencil"] = pencil

    angle = angles(low_freq, grid_y, NY)
    cos, sin = np.cos(angle), np.sin(angle)
    return_table["wave_y"] = np.block([[cos, sin], [-sin, cos]])

    angle = angles(grid_x, low_freq, NX)
    cos, sin = np.cos(angle), np.sin(angle)
    return_table["wave_x"] = np.block([[cos, -sin], [sin, cos]])

    angle = angles(own_y, grid_y, NY)
    cos, sin = np.cos(angle), np.sin(angle)
    return_table["forth_y"] = np.stack((cos, -sin), axis=1).reshape(2 * HALF, NY).T
    twice = np.where(own_y == 0, 1.0, 2.0)[:, None]
    return_table["back_y"] = np.stack((twice * cos, -twice * sin), axis=1).reshape(2 * HALF, NY)

    angle = angles(grid_z, plane_of.ravel(), NZ)
    return_table["forth_z"] = np.concatenate((np.cos(angle), np.sin(angle)), axis=0)
    own = NZ // pws
    merged = own // 8
    order = (
        pw_order[None, :, None] * own
        + np.arange(8)[None, None, :] * merged
        + np.arange(merged)[:, None, None]
    )
    angle = angles(order.ravel(), grid_z, NZ)
    return_table["back_z"] = np.concatenate((np.cos(angle), np.sin(angle)), axis=0)

    angle = angles(grid_x, grid_x, NX)
    return_table["both_x"] = np.concatenate((np.cos(angle), np.sin(angle)), axis=1)
    return return_table


def ramp(shape, axis, first=0):
    steps = lax.broadcasted_iota(jnp.int32, shape, axis) + first
    return steps.astype(jnp.float32).astype(jnp.bfloat16)


def sixteen(row):
    return jnp.broadcast_to(row, (16, row.shape[1])).astype(jnp.bfloat16)


def one_hot_lanes(row, ramps):
    column = jnp.transpose(jnp.concatenate([sixteen(row)] * (LANES // 16), axis=0))
    one = jnp.ones(column.shape, jnp.bfloat16)
    zero = jnp.zeros(column.shape, jnp.bfloat16)
    return jnp.concatenate(
        [
            jnp.where(column == ramps[:, first : first + LANES], one, zero)
            for first in range(0, ramps.shape[1], LANES)
        ],
        axis=1,
    )


def turn(row):
    return jnp.transpose(jnp.broadcast_to(row, (LANES, LANES)))


def cell_of(column):
    cell = ((column // NY + NX // 2) % NX - HALF // 2) * HALF
    return cell + (column % NY + NY // 2) % NY - HALF // 2


def rank_rows(rows, turned):
    return [
        sum(jnp.sum(jnp.where(t < row, 1.0, 0.0), axis=0, keepdims=True) for t in turned)
        for row in rows
    ]


def sorted_rows(rows):
    turned = [turn(row) for row in rows]
    ranks = [turn(rank) for rank in rank_rows(rows, turned)]
    lane = lax.broadcasted_iota(jnp.int32, (LANES, LANES), 1).astype(jnp.float32)
    return [
        sum(
            jnp.sum(jnp.where(rank == lane + t * LANES, value, 0.0), axis=0, keepdims=True)
            for rank, value in zip(ranks, turned)
        )
        for t in range(len(rows))
    ]


def usual_tiles(total, tiles):
    signed = np.arange(NX) - NX // 2
    radius = (signed[:, None] * NY) ** 2 + ((np.arange(NY) - NY // 2)[None, :] * NX) ** 2
    kept = np.sort(np.argsort(radius.ravel(), kind="stable")[:total] // NY - NX // 2 + HALF // 2)
    slots = tiles * LANES
    ranges = []
    for t in range(tiles):
        ends = []
        for edge, sign in ((t / tiles, -1), ((t + 1) / tiles, 1)):
            edge += sign * 5 * math.sqrt(edge * (1 - edge) / slots)
            ends.append(int(kept[min(max(int(edge * total), 0), total - 1)]) // 16)
        ranges.append(ends)
    held = [[t for t in range(tiles) if ranges[t][0] <= g <= ranges[t][1]] for g in range(HALF // 16)]
    return [(ts[0], ts[-1] + 1) if ts else (0, tiles) for ts in held]


RANK_LOW = 64
WINDOW = 64


def exchange_rows(refs, low_bits, size_bits, descending):
    for outer in range(RANK_LOW):
        if any(outer >> bit & 1 for bit in low_bits[0]):
            continue
        touched = sorted(
            outer + sum(1 << bit for i, bit in enumerate(low_bits[0]) if pattern >> i & 1)
            for pattern in range(1 << len(low_bits[0]))
        )
        held = {v: [ref[v * 8 : v * 8 + 8, :] for ref in refs] for v in touched}
        for size, bits in zip(size_bits, low_bits[1:]):
            for bit in bits:
                for v in touched:
                    if v >> bit & 1:
                        continue
                    former, latter = held[v], held[v | 1 << bit]
                    if size < 6:
                        down = bool(v >> size & 1)
                        swap = former[0] < latter[0] if down else former[0] > latter[0]
                    else:
                        swap = former[0] > latter[0]
                        if descending is not None:
                            swap = jnp.logical_xor(swap, descending)
                    held[v] = [jnp.where(swap, y, x) for x, y in zip(former, latter)]
                    held[v | 1 << bit] = [jnp.where(swap, x, y) for x, y in zip(former, latter)]
        for v in touched:
            for ref, value in zip(refs, held[v]):
                ref[v * 8 : v * 8 + 8, :] = value


def exchange_sublanes(refs, stride, descending):
    sublane = lax.broadcasted_iota(jnp.int32, (8, LANES), 0)
    upper = sublane // stride % 2 == 1
    want_most = upper if descending is None else jnp.logical_xor(upper, descending)
    other = jnp.where(upper, sublane - stride, sublane + stride)

    for v in range(RANK_LOW):
        here = [ref[v * 8 : v * 8 + 8, :] for ref in refs]
        there = [jnp.take_along_axis(value, other, axis=0) for value in here]
        take = jnp.logical_xor(here[0] > there[0], want_most)
        for ref, x, y in zip(refs, here, there):
            ref[v * 8 : v * 8 + 8, :] = jnp.where(take, y, x)


def sort_columns(refs):
    sublane = lax.broadcasted_iota(jnp.int32, (8, LANES), 0)
    exchange_rows(refs, [(0, 1, 2), (0,), (1, 0), (2, 1, 0)], [1, 2, 3], None)
    exchange_rows(refs, [(3,), (3,)], [4], None)
    exchange_rows(refs, [(0, 1, 2), (2, 1, 0)], [4], None)
    exchange_rows(refs, [(3, 4), (4, 3)], [5], None)
    exchange_rows(refs, [(0, 1, 2), (2, 1, 0)], [5], None)
    for size in range(6, 10):
        descending = None if size == 9 else sublane // (1 << (size - 6)) % 2 == 1
        for bit in range(size - 1, 5, -1):
            exchange_sublanes(refs, 1 << (bit - 6), descending)
        exchange_rows(refs, [(3, 4, 5), (5, 4, 3)], [size], descending)
        if size < 9:
            exchange_rows(refs, [(0, 1, 2), (2, 1, 0)], [size], descending)


def pack_kernel(width, has_column, *refs):
    coeff_ref, miller_ref, slot_ref, pencil_ref, column_ref = refs[:5]
    rest = list(refs[5:])
    out_ref, total, key_ref, real_ref, imag_ref, lane_ref, real_low, imag_low, ramp_ref, step_ref, held, sem = rest
    fetch = pltpu.make_async_copy(pencil_ref, held, sem)
    fetch.start()
    half = total.shape[0] // 4
    slots = 2 * half
    count = out_ref.shape[0]
    rows = pencil_ref.shape[0] // count
    length = miller_ref.shape[0]
    ranks = key_ref.shape[0]

    slot = slot_ref[...]
    columns = [
        column_ref[t * LANES : (t + 1) * LANES].reshape(1, LANES) for t in range(slots // LANES)
    ]
    if not has_column:
        cells = [cell_of(column).astype(jnp.float32) for column in columns]
        near = slot % LANES
        rank = jnp.zeros(slot.shape, jnp.float32)
        for t, row in enumerate(rank_rows(cells, [turn(row) for row in cells])):
            found = jnp.take_along_axis(jnp.broadcast_to(row, slot.shape), near, axis=1)
            rank = jnp.where(slot // LANES == t, found, rank)
        slot = rank.astype(jnp.int32)
    second = slot >= half
    lane = miller_ref[...] + width // 2
    key = jnp.where(second, slot - half, slot) * (2 * width) + jnp.where(second, lane + width, lane)
    key_ref[0:length] = key.astype(jnp.float32)
    real_ref[0:length] = coeff_ref[0, pl.ds(0, length, stride=2), :]
    imag_ref[0:length] = coeff_ref[0, pl.ds(1, length, stride=2), :]
    blank = jnp.zeros((ranks - length, LANES), jnp.float32)
    key_ref[length:] = blank + 2.0 * slots * width
    real_ref[length:] = blank
    imag_ref[length:] = blank
    sort_columns((key_ref, real_ref, imag_ref))

    def base_of(block):
        base = 8 * (block // 2) + 8 * (block % 2) - WINDOW // 2
        return jnp.minimum(jnp.maximum(base, 0), half - WINDOW)

    ramp_ref[...] = ramp(ramp_ref.shape, 1)
    step_ref[...] = ramp(step_ref.shape, 0)
    sublane = lax.broadcasted_iota(jnp.int32, (8, LANES), 0)
    astray = jnp.zeros((8, LANES), jnp.float32)
    for v in range(RANK_LOW):
        at = slice(v * 8, v * 8 + 8)
        keys = key_ref[at, :]
        high = jnp.floor(keys * (1.0 / (2 * width)))
        lane_ref[at, :] = keys - high * (2.0 * width)
        key_ref[at, :] = high
        for ref, low_ref in ((real_ref, real_low), (imag_ref, imag_low)):
            value = ref[at, :]
            rounded = value.astype(jnp.bfloat16).astype(jnp.float32)
            ref[at, :] = rounded
            low_ref[at, :] = value - rounded
        offset = high - base_of(sublane * (RANK_LOW // 8) + v // 8).astype(jnp.float32)
        outside = jnp.logical_or(offset < 0.0, offset >= 1.0 * WINDOW)
        astray = jnp.where(outside, 1.0, astray)
    astray = jnp.max(jnp.where(sublane * RANK_LOW < length, astray, 0.0))

    def add(block, base, window):
        first = block % (RANK_LOW // 8) * 64 + block // (RANK_LOW // 8)
        base_row = jnp.full((1, LANES), base, jnp.int32).astype(jnp.float32)
        zero = jnp.zeros((16, LANES), jnp.bfloat16)
        spread, chosen = [], []
        for t in range(8):
            row = pl.ds(first + 8 * t, 1)
            high = sixteen(key_ref[row, :] - base_row)
            masks = [high == step_ref[r : r + 16, :] for r in range(0, window, 16)]
            spread.append(
                jnp.concatenate(
                    [
                        jnp.where(mask, value, zero)
                        for value in [
                            sixteen(ref[row, :]) for ref in (real_ref, imag_ref, real_low, imag_low)
                        ]
                        for mask in masks
                    ],
                    axis=0,
                )
            )
            chosen.append(one_hot_lanes(lane_ref[row, :], ramp_ref[...]))
        found = mul(jnp.concatenate(spread, axis=1), jnp.concatenate(chosen, axis=0), NN)
        for i in range(4):
            if window == half:
                into = pl.ds(i * half, half)
            else:
                into = pl.ds(pl.multiple_of(i * half + base, 8), window)
            total[into, :] += found[i * window : (i + 1) * window]

    total[...] = jnp.zeros_like(total)
    blocks = length // 8
    together = 4 if blocks % 4 == 0 else 1

    @pl.when(astray == 0.0)
    def _():
        def some_blocks(i, unused):
            for s in range(together):
                block = together * i + s
                add(block, base_of(block), WINDOW)
            return unused

        lax.fori_loop(0, blocks // together, some_blocks, 0)

    @pl.when(astray > 0.0)
    def _():
        def one_block(block, unused):
            add(block, 0, half)
            return unused

        lax.fori_loop(0, blocks, one_block, 0)

    both = []
    for at in range(2):
        parts = [
            total[(2 * at + c) * half : (2 * at + c + 1) * half].astype(jnp.bfloat16)
            for c in range(2)
        ]
        both.append(
            jnp.concatenate(
                [
                    jnp.concatenate([part[:, h * width : (h + 1) * width] for part in parts], axis=1)
                    for h in range(2)
                ],
                axis=0,
            )
        )
    fetch.wait()
    pencils = mul(held[...], jnp.concatenate((both[0], both[0], both[1]), axis=1), NT)
    tiles = slots // LANES
    for t in range(tiles):
        tile = pencils[:, t * LANES : (t + 1) * LANES].reshape(count, rows, LANES)
        if not has_column:
            out_ref[:, t * rows : (t + 1) * rows] = tile
            continue
        for g in range(rows // 4):
            out_ref[:, t * (rows // 4) + g] = tile[:, 4 * g : 4 * g + 4]
    if has_column:
        column = [column.astype(jnp.float32) for column in columns]
        column = jnp.concatenate(column + [jnp.zeros((4 - tiles, LANES), jnp.float32)], axis=0)
        out_ref[:, tiles * rows // 4] = jnp.broadcast_to(column[None], (count, 4, LANES))


def pack_band(band, count, coeffs, miller, slot, pencil, slots, column):
    has_column = band == 0
    length = miller.shape[0]
    width = pencil.shape[1] // 6
    rows = pencil.shape[0] // count * (slots // LANES)
    operands = [coeffs, miller, slot, pencil, column]
    out_shape = (count, rows, LANES)
    if has_column:
        out_shape = (count, rows // 4 + 1, 4, LANES)
    one_band = pl.BlockSpec((1, 2 * length, LANES), lambda i: (band, 0, 0))
    return pl.pallas_call(
        functools.partial(pack_kernel, width, has_column),
        grid=(1,),
        in_specs=[one_band]
        + [
            pl.BlockSpec(memory_space=pl.ANY)
            if x is pencil
            else pl.BlockSpec(x.shape, lambda i, n=x.ndim: (0,) * n)
            for x in operands[1:]
        ],
        out_specs=pl.BlockSpec(out_shape, lambda i: (0,) * len(out_shape)),
        out_shape=jax.ShapeDtypeStruct(out_shape, jnp.float32),
        scratch_shapes=[pltpu.VMEM((2 * slots, 2 * width), jnp.float32)]
        + [pltpu.VMEM((8 * RANK_LOW, LANES), jnp.float32)] * 6
        + [
            pltpu.VMEM((LANES, 2 * width), jnp.bfloat16),
            pltpu.VMEM((slots // 2, LANES), jnp.bfloat16),
            pltpu.VMEM(pencil.shape, jnp.bfloat16),
            pltpu.SemaphoreType.DMA,
        ],
        compiler_params=pltpu.CompilerParams(vmem_limit_bytes=PACK_LIMIT),
        cost_estimate=pl.CostEstimate(
            flops=2 * length * LANES * slots * 4 * width,
            bytes_accessed=16 * length * LANES,
            transcendentals=0,
        ),
        name="pack_band",
    )(*operands)


def wave_kernel(kpts, tiles, scale, is_first, is_last, *refs):
    own_ref, count_ref, came_ref, wave_y_ref, wave_x_ref = refs[:5]
    rest = list(refs[5:])
    forth_ref = rest.pop(0) if is_last else None
    former_ref, cell_ref = (None, None) if is_first else (rest.pop(0), rest.pop(0))
    density_refs = [rest.pop(0) for _ in range(kpts if is_last else 1)]
    if is_first:
        coulomb_ref, cell_ref = rest.pop(0), rest.pop(0)
    send_ref = rest.pop(0) if is_last else None
    values, grid, whole, chosen_ref, high_ref = rest
    planes = density_refs[0].shape[0]
    block = NX // kpts
    part_rows = 2 * planes
    pws = came_ref.shape[0] // kpts
    rows = kpts * part_rows
    total = values.shape[1]

    for j in range(pws):
        for t in range(tiles):
            if is_first:
                groups = [
                    came_ref[k * pws + j, t * (part_rows // 4) + g]
                    for k in range(kpts)
                    for g in range(part_rows // 4)
                ]
            else:
                groups = [
                    came_ref[k * pws + j, t * part_rows : (t + 1) * part_rows] for k in range(kpts)
                ]
            taken = jnp.concatenate(groups, axis=0)
            high, low = pieces(taken)
            first = (t * pws + j) * LANES
            values[0:rows, first : first + LANES] = high
            values[rows : 2 * rows, first : first + LANES] = low

    tile = 4 * HALF
    ramps = ramp((LANES, tile), 1)
    usual = usual_tiles(total, tiles)
    astray = jnp.zeros((1, LANES), jnp.float32)
    for j in range(pws):
        if is_first:
            columns = [came_ref[j, tiles * part_rows // 4, t : t + 1] for t in range(tiles)]
            cells = [cell_of(column.astype(jnp.int32)) for column in columns]
            ordered = sorted_rows([cell.astype(jnp.float32) for cell in cells])
        for t in range(tiles):
            first = (t * pws + j) * LANES
            if is_first:
                cell = cells[t]
                cell_ref[:, first : first + LANES] = ordered[t].astype(jnp.int32)
            else:
                cell = cell_ref[:, first : first + LANES]
                group = cell // (4 * tile)
                for g, (least, end) in enumerate(usual):
                    if not least <= t < end:
                        astray = jnp.where(group == g, 1.0, astray)
            lane = (cell % tile).astype(jnp.float32)
            chosen_ref[first : first + LANES, :] = one_hot_lanes(lane, ramps)
            high_ref[:, first : first + LANES] = sixteen((cell // tile).astype(jnp.float32))
    if is_first:
        step_z = lax.broadcasted_iota(jnp.int32, (NZ, NX), 0)
        step_x = lax.broadcasted_iota(jnp.int32, (NZ, NX), 1)
        for q in range(coulomb_ref.shape[0]):
            freq_y = jnp.full((NZ, NX), own_ref[1] + q, jnp.int32)
            kernel = coulomb(signed_freq(step_z, NZ), signed_freq(step_x, NX), freq_y)
            coulomb_ref[q] = kernel * (1.0 / (NX * NY * NZ))
    left = lax.broadcasted_iota(jnp.int32, (planes, LANES), 1) < HALF

    def place(t, found):
        found = found[:rows] + found[rows:]
        for h in range(2):
            for k in range(kpts):
                real, imag = (
                    found[(2 * k + c) * planes : (2 * k + c + 1) * planes, h * LANES : (h + 1) * LANES]
                    for c in range(2)
                )
                first = (k * HALF + 4 * t + 2 * h) * planes
                grid[first : first + planes, :] = jnp.where(left, real, pltpu.roll(imag, HALF, 1))
                grid[first + planes : first + 2 * planes, :] = jnp.where(
                    left, pltpu.roll(real, HALF, 1), imag
                )

    def place_all(ranges):
        for g, (least, end) in enumerate(ranges):
            held = slice(least * pws * LANES, end * pws * LANES)
            high = high_ref[:, held]
            zero = jnp.zeros_like(high)
            kept = []
            for t in range(4 * g, 4 * g + 4):
                here = high == jnp.full_like(high, t)
                kept += [
                    jnp.where(here, values[r : r + 16, held], zero) for r in range(0, 2 * rows, 16)
                ]
            found = mul(jnp.concatenate(kept, axis=0), chosen_ref[held, :], NN)
            for s in range(4):
                place(4 * g + s, found[2 * rows * s : 2 * rows * (s + 1)])

    whole_range = [(0, tiles)] * len(usual)
    if is_first:
        place_all(whole_range)
    else:
        astray = jnp.max(astray)

        @pl.when(astray == 0.0)
        def _():
            place_all(usual)

        @pl.when(astray > 0.0)
        def _():
            place_all(whole_range)

    sum_of = count_ref[0]
    for k in range(1, kpts):
        sum_of = sum_of + count_ref[k]

    def spread(number):
        return jnp.full((8, NY), number, jnp.int32).astype(jnp.float32)

    weights = [
        jnp.concatenate([spread(count_ref[k]) / spread(sum_of) * scale] * (NX // 8), axis=0)
        for k in ring_order(kpts)
    ]
    lines = [grid[pl.ds(p, kpts * HALF, stride=planes), :] for p in range(planes)]
    lines = mul3_right(jnp.concatenate(lines, axis=0), wave_y_ref[...], NN)

    for p in range(planes):
        mixed = lines[p * kpts * HALF : (p + 1) * kpts * HALF]
        mixed = jnp.concatenate(
            [
                jnp.concatenate(
                    [mixed[k * HALF : (k + 1) * HALF, c * NY : (c + 1) * NY] for k in range(kpts)],
                    axis=1,
                )
                for c in range(2)
            ],
            axis=0,
        )
        wave = mul3_left(wave_x_ref[...], mixed, NN)
        square = wave[:NX] * wave[:NX] + wave[NX:] * wave[NX:]
        density = weights[0] * square[:, :NY]
        for k in range(1, kpts):
            density = density + weights[k] * square[:, k * NY : (k + 1) * NY]
        if former_ref is not None:
            density = density + former_ref[p]
        if is_last:
            whole[p] = density
        else:
            density_refs[0][p] = density

    if is_last:
        for s, density_ref in enumerate(density_refs):
            first = pl.multiple_of(lax.rem(own_ref[0] + s, kpts) * block, block)
            density_ref[...] = whole[:, pl.ds(first, block), :]
        level = jnp.mean(whole[0, :8, :], axis=(0, 1), keepdims=True)
        field = whole[...].reshape(planes * NX, NY) - level
        half = mul3_right(field, forth_ref[...], NN)
        first_row = lax.broadcasted_iota(jnp.int32, (2 * HALF, NX), 0) == 0
        for p in range(planes):
            turned = jnp.transpose(half[p * NX : (p + 1) * NX])
            turned = turned + jnp.where(first_row, level * NY, 0.0)
            send_ref[pl.ds(p, 2 * HALF, stride=planes), :] = turned


def wave_band(kpts, tiles, total, scale, own, counts, came, wave_y, wave_x, forth, former, cell):
    planes = NZ // came.shape[0]
    block = NX // kpts
    is_first, is_last = former is None, forth is not None
    vmem = pl.BlockSpec(memory_space=pltpu.VMEM)
    operands = [own, counts, came, wave_y, wave_x]
    if is_last:
        operands.append(forth)
    if not is_first:
        operands += [former, cell]
    if is_last:
        out_shape = [jax.ShapeDtypeStruct((planes, block, NY), jnp.float32)] * kpts
    else:
        out_shape = [jax.ShapeDtypeStruct((planes, NX, NY), jnp.float32)]
    if is_first:
        out_shape.append(jax.ShapeDtypeStruct((HALF // came.shape[0], NZ, NX), jnp.float32))
        out_shape.append(jax.ShapeDtypeStruct((1, total), jnp.int32))
    if is_last:
        out_shape.append(jax.ShapeDtypeStruct((2 * HALF * planes, NX), jnp.float32))
    rows = kpts * 2 * planes
    return pl.pallas_call(
        functools.partial(wave_kernel, kpts, tiles, scale, is_first, is_last),
        in_specs=[pl.BlockSpec(memory_space=pltpu.SMEM)] * 2 + [vmem] * (len(operands) - 2),
        out_specs=[vmem] * len(out_shape),
        out_shape=out_shape,
        scratch_shapes=[
            pltpu.VMEM((2 * rows, total), jnp.bfloat16),
            pltpu.VMEM((kpts * planes * HALF, LANES), jnp.float32),
            pltpu.VMEM((planes, NX, NY), jnp.float32),
            pltpu.VMEM((total, 4 * HALF), jnp.bfloat16),
            pltpu.VMEM((16, total), jnp.bfloat16),
        ],
        compiler_params=pltpu.CompilerParams(vmem_limit_bytes=VMEM_LIMIT),
        cost_estimate=pl.CostEstimate(
            flops=4 * rows * total * HALF * HALF, bytes_accessed=4 * came.size, transcendentals=0
        ),
        name="wave_band",
    )(*operands)


def poisson_kernel(pws, own_ref, kernel_ref, came_ref, forth_ref, back_ref, both_x_ref, send_ref):
    count, parts, planes, unused = came_ref.shape
    pairs = parts // 2
    fields = [came_ref[:, i].reshape(NZ, NX) for i in range(parts)]
    level = jnp.mean(fields[0], axis=(0, 1), keepdims=True)
    fields[0] = fields[0] - jnp.where(own_ref[1] == 0, level, 0.0)
    field = jnp.concatenate(fields, axis=1)
    turned = mul3_left(forth_ref[...], field, NN)

    def part(array, half, i):
        return array[half * NZ : (half + 1) * NZ, i * NX : (i + 1) * NX]

    lines = []
    for q in range(pairs):
        lines.append(part(turned, 0, 2 * q) + part(turned, 1, 2 * q + 1))
        lines.append(part(turned, 0, 2 * q + 1) - part(turned, 1, 2 * q))
    spectrum = mul3_right(jnp.concatenate(lines, axis=0), both_x_ref[...], NN)

    lines = []
    for q in range(pairs):
        real = spectrum[2 * q * NZ : (2 * q + 1) * NZ]
        imag = spectrum[(2 * q + 1) * NZ : (2 * q + 2) * NZ]
        kernel = kernel_ref[q]
        lines.append((real[:, :NX] + imag[:, NX:]) * kernel)
        lines.append((imag[:, :NX] - real[:, NX:]) * kernel)
    turned = mul3_right(jnp.concatenate(lines, axis=0), both_x_ref[...], NN)
    lines = []
    for q in range(pairs):
        real = turned[2 * q * NZ : (2 * q + 1) * NZ]
        imag = turned[(2 * q + 1) * NZ : (2 * q + 2) * NZ]
        lines.append(real[:, :NX] - imag[:, NX:])
        lines.append(real[:, NX:] + imag[:, :NX])
    turned = mul3_left(back_ref[...], jnp.concatenate(lines, axis=1), NN)

    kpts = count // pws
    merged = NZ // pws // 8
    block = NX // kpts
    rows = pws * 8
    lane = lax.broadcasted_iota(jnp.int32, (rows, LANES), 1) // block
    for q in range(pairs):
        real = part(turned, 0, 2 * q) - part(turned, 1, 2 * q + 1)
        imag = part(turned, 0, 2 * q + 1) + part(turned, 1, 2 * q)
        for c, value in enumerate((real, imag)):
            for place, a in enumerate(ring_order(kpts)):
                packed = None
                for m in range(merged):
                    piece = value[m * rows : (m + 1) * rows]
                    shift = (m - a) * block % LANES
                    if shift:
                        piece = pltpu.roll(piece, shift, 1)
                    packed = piece if m == 0 else jnp.where(lane == m, piece, packed)
                send_ref[place * pws : (place + 1) * pws, 2 * q + c] = packed.reshape(pws, 8, LANES)


def poisson(pws, own, kernel, came, forth, back, both_x):
    vmem = pl.BlockSpec(memory_space=pltpu.VMEM)
    count, parts, unused, unused = came.shape
    return pl.pallas_call(
        functools.partial(poisson_kernel, pws),
        in_specs=[pl.BlockSpec(memory_space=pltpu.SMEM)] + [vmem] * 5,
        out_specs=vmem,
        out_shape=jax.ShapeDtypeStruct((count, parts, 8, LANES), jnp.float32),
        compiler_params=pltpu.CompilerParams(vmem_limit_bytes=VMEM_LIMIT),
        name="poisson",
    )(own, kernel, came, forth, back, both_x)


def finish_kernel(own_ref, came_ref, back_ref, *refs):
    block_refs, density_ref, out_ref = refs[:-2], refs[-2], refs[-1]
    kpts = len(block_refs)
    planes, block, unused = out_ref.shape
    merged = planes // 8
    for s, block_ref in enumerate(block_refs):
        sender = lax.rem(own_ref[0] + kpts - s, kpts)
        density_ref[pl.ds(sender * (planes // kpts), planes // kpts)] = block_ref[...]
    for h in range(8):
        lines = came_ref[pl.ds(h, 2 * HALF, stride=8), :]
        field = mul3_right(lines, back_ref[...], TN)
        out_ref[h * merged : (h + 1) * merged] = field.reshape(merged, block, NY)


def finish(planes, block, own, came, back_y, blocks):
    vmem = pl.BlockSpec(memory_space=pltpu.VMEM)
    return pl.pallas_call(
        finish_kernel,
        in_specs=[pl.BlockSpec(memory_space=pltpu.SMEM)] + [vmem] * (2 + len(blocks)),
        out_specs=[vmem] * 2,
        out_shape=[jax.ShapeDtypeStruct((planes, block, NY), jnp.float32)] * 2,
        compiler_params=pltpu.CompilerParams(vmem_limit_bytes=VMEM_LIMIT),
        name="finish",
    )(own, came, back_y, *blocks)


def exchange(array):
    kpts, pws = lax.axis_size("kpt"), lax.axis_size("pw")
    kpt_order, pw_order = group_order(kpts, pws)
    group = [k * pws + j for k in kpt_order for j in pw_order]
    return lax.all_to_all(
        array, ("kpt", "pw"), split_axis=0, concat_axis=0, tiled=True, axis_index_groups=[group]
    )


def place_in(order, axis):
    places = jnp.asarray(np.argsort(np.array(order)), jnp.int32)
    return lax.dynamic_index_in_dim(places, lax.axis_index(axis), 0, keepdims=False)


def local_planes(band_coeffs, miller_third, column_slot, column_map, kpoint_counts):
    pws = lax.axis_size("pw")
    kpts = lax.axis_size("kpt")
    count = pws * kpts
    slots = column_map.shape[0]
    band_count = band_coeffs.shape[1]
    z_width = column_slot.shape[1] // slots
    planes = NZ // count
    parts = 2 * HALF // count
    made = tables(kpts, pws, planes)
    pencil = stack_table(made["pencil"](z_width), 1)
    wave_x, forth_z, back_z = (
        stack_table(made[name], 1) for name in ("wave_x", "forth_z", "back_z")
    )
    wave_y, forth_y, back_y, both_x = (
        stack_table(made[name], 0) for name in ("wave_y", "forth_y", "back_y", "both_x")
    )

    tiles = slots // LANES
    length = column_slot.shape[1] // LANES
    coeffs = band_coeffs.reshape(band_count, 2, length, LANES).transpose(0, 2, 1, 3)
    coeffs = coeffs.reshape(band_count, 2 * length, LANES)
    miller = miller_third.reshape(length, LANES)
    slot = column_slot.reshape(length, LANES)
    scale = 2.0 / (column_slot.shape[1] * pws)
    arrived = []
    for band in range(band_count):
        packed = pack_band(
            band, count, coeffs, miller, slot, pencil, slots, column_map
        )
        arrived.append(exchange(packed))
    kpt_order, pw_order = group_order(kpts, pws)
    device = place_in(kpt_order, "kpt") * pws + place_in(pw_order, "pw")
    own = jnp.stack((lax.axis_index("kpt"), device * (parts // 2))).astype(jnp.int32)
    former = cell = None
    for band in range(band_count):
        forth = forth_y if band == band_count - 1 else None
        made_here = wave_band(
            kpts,
            tiles,
            pws * slots,
            scale,
            own,
            kpoint_counts,
            arrived[band],
            wave_y,
            wave_x,
            forth,
            former,
            cell,
        )
        former = made_here[0]
        if band == 0:
            kernel, cell = made_here[kpts if forth is not None else 1 :][:2]
    half = exchange(made_here[-1].reshape(count, parts, planes, NX))
    blocks = [made_here[0]] + [
        lax.ppermute(made_here[s], "kpt", [(a, (a + s) % kpts) for a in range(kpts)])
        for s in range(1, kpts)
    ]
    back = poisson(pws, own, kernel, half, forth_z, back_z, both_x)
    back = exchange(back).reshape(count * parts * 8, LANES)
    return tuple(finish(NZ // pws, NX // kpts, own, back, back_y, blocks))


def fits_planes(kpts, pws):
    count = kpts * pws
    own = NZ // pws
    return (
        NZ % count == 0
        and NZ // count == 8
        and 2 * HALF % (2 * count) == 0
        and NX % kpts == 0
        and own % 8 == 0
        and own // 8 * (NX // kpts) == LANES
    )


def local(band_coeffs, miller_third, column_slot, column_map, kpoint_counts):
    slots = column_map.shape[0]
    plain = slots % LANES == 0 and LANES <= slots <= 8 * RANK_LOW
    plain = plain and column_slot.shape[1] == slots * LANES
    fits = plain and fits_planes(lax.axis_size("kpt"), lax.axis_size("pw"))
    chosen = local_planes if fits else local_general
    return chosen(band_coeffs, miller_third, column_slot, column_map, kpoint_counts)


def solution(mesh):
    return jax.shard_map(
        local,
        mesh=mesh,
        in_specs=(P("kpt", None, None, "pw"), P("kpt", "pw"), P("kpt", "pw"), P("pw"), P()),
        out_specs=(P("pw", "kpt", None), P("pw", "kpt", None)),
        check_vma=False,
    )
```

```python
import functools
import math

import jax
import jax.numpy as jnp
import numpy as np
from jax import lax
from jax.experimental import pallas as pl
from jax.experimental.pallas import tpu as pltpu
from jax.sharding import PartitionSpec as P

NX = 128
NY = 128
NZ = 256


SPACING = 0.25


def contract(pattern, former, latter):
    return jnp.einsum(
        pattern, former, latter, precision=lax.Precision.HIGHEST, preferred_element_type=jnp.float32
    )


def phase_tables(first_index, second_index, length):
    product = first_index[:, None] * second_index[None, :] % length
    angle = product.astype(jnp.float32) * (2.0 * math.pi / length)
    return (jnp.cos(angle), jnp.sin(angle))


def signed_freq(values, length):
    return jnp.where(values >= length // 2, values - length, values)


def coulomb(freq_z, freq_x, freq_y):
    wave_z = freq_z.astype(jnp.float32) / (NZ * SPACING)
    wave_x = freq_x.astype(jnp.float32) / (NX * SPACING)
    wave_y = freq_y.astype(jnp.float32) / (NY * SPACING)
    squared = (2.0 * math.pi) ** 2 * (wave_z * wave_z + wave_x * wave_x + wave_y * wave_y)
    anchor = (freq_z == 0) & (freq_x == 0) & (freq_y == 0)
    return jnp.where(anchor, 0.0, 4.0 * math.pi / jnp.where(anchor, 1.0, squared))


def poisson_columns(real_part, imag_part, freq_x, freq_y):
    length = real_part.shape[0]
    steps_z = jnp.arange(length, dtype=jnp.int32)
    cos_z, sin_z = phase_tables(steps_z, steps_z, length)
    spec_real = contract("zk,km->zm", cos_z, real_part) + contract("zk,km->zm", sin_z, imag_part)
    spec_imag = contract("zk,km->zm", cos_z, imag_part) - contract("zk,km->zm", sin_z, real_part)
    kernel = coulomb(signed_freq(steps_z, length)[:, None], freq_x[None, :], freq_y[None, :]) / (
        NX * NY * NZ
    )
    spec_real = spec_real * kernel
    spec_imag = spec_imag * kernel
    back_real = contract("zk,km->zm", cos_z, spec_real) - contract("zk,km->zm", sin_z, spec_imag)
    back_imag = contract("zk,km->zm", sin_z, spec_real) + contract("zk,km->zm", cos_z, spec_imag)
    return (back_real, back_imag)


def forward_planes(field):
    steps_x = jnp.arange(NX, dtype=jnp.int32)
    steps_y = jnp.arange(NY, dtype=jnp.int32)
    cos_y, sin_y = phase_tables(steps_y, steps_y, NY)
    cos_x, sin_x = phase_tables(steps_x, steps_x, NX)
    half_real = contract("pxy,ky->pxk", field, cos_y)
    half_imag = -contract("pxy,ky->pxk", field, sin_y)
    spec_real = contract("kx,pxy->pky", cos_x, half_real) + contract(
        "kx,pxy->pky", sin_x, half_imag
    )
    spec_imag = contract("kx,pxy->pky", cos_x, half_imag) - contract(
        "kx,pxy->pky", sin_x, half_real
    )
    return (spec_real, spec_imag)


def local_general(band_coeffs, miller_third, column_slot, column_map, kpoint_counts):
    pw_count = lax.axis_size("pw")
    kpt_count = lax.axis_size("kpt")
    pw_index = lax.axis_index("pw")
    kpt_index = lax.axis_index("kpt")
    col_dev = column_map.shape[0]
    ng_dev = column_slot.shape[1]
    band_count = band_coeffs.shape[1]
    z_width = ng_dev // col_dev
    planes = NZ // pw_count
    x_block = NX // kpt_count
    col_total = pw_count * col_dev
    steps_y = jnp.arange(NY, dtype=jnp.int32)
    steps_x = jnp.arange(NX, dtype=jnp.int32)
    cos_y, sin_y = phase_tables(steps_y, steps_y, NY)
    cos_x, sin_x = phase_tables(steps_x, steps_x, NX)
    all_columns = lax.all_gather(column_map, "pw", axis=0, tiled=True)
    position = (miller_third[0] + z_width // 2) * col_dev + column_slot[0]
    source_of = (
        jnp.zeros((ng_dev,), jnp.int32).at[position].set(jnp.arange(ng_dev, dtype=jnp.int32))
    )
    coeff_rows = band_coeffs[0].reshape(band_count * 2, ng_dev).T
    packed = jnp.take(coeff_rows, source_of, axis=0)
    packed = (
        packed.reshape(z_width, col_dev, band_count, 2)
        .transpose(0, 2, 3, 1)
        .reshape(z_width, band_count * 2 * col_dev)
    )
    cos_z, sin_z = phase_tables(
        jnp.arange(NZ, dtype=jnp.int32), jnp.arange(z_width, dtype=jnp.int32) - z_width // 2, NZ
    )
    by_cos = contract("zj,jc->zc", cos_z, packed).reshape(NZ, band_count, 2, col_dev)
    by_sin = contract("zj,jc->zc", sin_z, packed).reshape(NZ, band_count, 2, col_dev)
    pencil = jnp.stack(
        (by_cos[:, :, 0] - by_sin[:, :, 1], by_sin[:, :, 0] + by_cos[:, :, 1]), axis=2
    )
    pencil = pencil.reshape(NZ, band_count * 2 * col_dev)
    arrived = lax.all_to_all(pencil, "pw", split_axis=0, concat_axis=1, tiled=True)
    arrived = arrived.reshape(planes, pw_count, band_count, 2, col_dev).transpose(2, 1, 4, 3, 0)
    arrived = arrived.reshape(band_count, col_total, 2 * planes)
    arrived = jnp.concatenate(
        (arrived, jnp.zeros((band_count, 1, 2 * planes), jnp.float32)), axis=1
    )
    cell_source = (
        jnp.full((NX * NY,), col_total, jnp.int32)
        .at[all_columns]
        .set(jnp.arange(col_total, dtype=jnp.int32))
    )

    def add_band(band, running):
        one_band = lax.dynamic_index_in_dim(arrived, band, 0, keepdims=False)
        placed = jnp.take(one_band, cell_source, axis=0)
        placed = placed.reshape(NX, NY, 2, planes).transpose(2, 3, 0, 1)
        grid_real = placed[0]
        grid_imag = placed[1]
        mixed_real = contract("pxm,ym->pxy", grid_real, cos_y) - contract(
            "pxm,ym->pxy", grid_imag, sin_y
        )
        mixed_imag = contract("pxm,ym->pxy", grid_real, sin_y) + contract(
            "pxm,ym->pxy", grid_imag, cos_y
        )
        wave_real = contract("xm,pmy->pxy", cos_x, mixed_real) - contract(
            "xm,pmy->pxy", sin_x, mixed_imag
        )
        wave_imag = contract("xm,pmy->pxy", sin_x, mixed_real) + contract(
            "xm,pmy->pxy", cos_x, mixed_imag
        )
        return running + wave_real * wave_real + wave_imag * wave_imag

    squares_sum = lax.fori_loop(0, band_count, add_band, jnp.zeros((planes, NX, NY), jnp.float32))
    weight = (
        2.0
        * kpoint_counts[kpt_index].astype(jnp.float32)
        / jnp.sum(kpoint_counts).astype(jnp.float32)
    )
    weight = weight / (ng_dev * pw_count)
    partial_value = weight * squares_sum
    total_density = lax.psum(partial_value, "kpt")
    density = lax.dynamic_slice_in_dim(total_density, kpt_index * x_block, x_block, 1)
    spec_real, spec_imag = forward_planes(total_density)
    rows_pw = NX // pw_count
    pencil_real, pencil_imag = (
        lax.all_to_all(spec_real, "pw", split_axis=1, concat_axis=0, tiled=True),
        lax.all_to_all(spec_imag, "pw", split_axis=1, concat_axis=0, tiled=True),
    )
    local_x = pw_index * rows_pw + jnp.arange(rows_pw, dtype=jnp.int32)
    freq_x = jnp.repeat(signed_freq(local_x, NX), NY)
    freq_y = jnp.tile(signed_freq(steps_y, NY), rows_pw)
    back_real, back_imag = poisson_columns(
        pencil_real.reshape(NZ, rows_pw * NY), pencil_imag.reshape(NZ, rows_pw * NY), freq_x, freq_y
    )
    plane_real, plane_imag = (
        lax.all_to_all(
            back_real.reshape(NZ, rows_pw, NY), "pw", split_axis=0, concat_axis=1, tiled=True
        ),
        lax.all_to_all(
            back_imag.reshape(NZ, rows_pw, NY), "pw", split_axis=0, concat_axis=1, tiled=True
        ),
    )
    own_rows = kpt_index * x_block + jnp.arange(x_block, dtype=jnp.int32)
    cos_rows, sin_rows = phase_tables(own_rows, steps_x, NX)
    rows_real = contract("xk,pky->pxy", cos_rows, plane_real) - contract(
        "xk,pky->pxy", sin_rows, plane_imag
    )
    rows_imag = contract("xk,pky->pxy", sin_rows, plane_real) + contract(
        "xk,pky->pxy", cos_rows, plane_imag
    )
    hartree = contract("pxk,yk->pxy", rows_real, cos_y) - contract("pxk,yk->pxy", rows_imag, sin_y)
    return (density, hartree)


LANES = 128
HALF = 64
VMEM_LIMIT = 16 * 1024 * 1024
PACK_LIMIT = 56 * 1024 * 1024
NN = (((1,), (0,)), ((), ()))
NT = (((1,), (1,)), ((), ()))
TN = (((0,), (0,)), ((), ()))


def pieces(value):
    high = value.astype(jnp.bfloat16)
    low = (value - high.astype(jnp.float32)).astype(jnp.bfloat16)
    return high, low


def mul(former, latter, dims):
    return lax.dot_general(former, latter, dims, preferred_element_type=jnp.float32)


def mul3_left(former, latter, dims):
    high, low = pieces(latter)
    (unused,), (axis,) = dims[0]
    return mul(former, jnp.concatenate((high, high, low), axis=axis), dims)


def mul3_right(former, latter, dims):
    high, low = pieces(former)
    (axis,), (unused,) = dims[0]
    return mul(jnp.concatenate((high, high, low), axis=axis), latter, dims)


def stack_table(values, axis):
    high = values.astype(np.float32).astype(jnp.bfloat16)
    low = (values - high.astype(np.float64)).astype(np.float32).astype(jnp.bfloat16)
    return jnp.asarray(np.concatenate((high, low, high), axis=axis))


def angles(former, latter, length):
    return np.outer(former, latter) % length * (2.0 * np.pi / length)


def ring_order(length):
    return [0, *range(1, length, 2), *range(length - 2 + length % 2, 0, -2)] if length > 1 else [0]


def group_order(kpts, pws):
    cores = 2 if pws % 2 == 0 else 1
    if pws == 8:
        return ring_order(kpts), [0, 1, 4, 2, 5, 3, 6, 7]
    return ring_order(kpts), [c * cores + i for c in ring_order(pws // cores) for i in range(cores)]


def tables(kpts, pws, planes):
    count = kpts * pws
    kpt_order, pw_order = (np.array(order) for order in group_order(kpts, pws))
    low_freq = np.arange(HALF) - HALF // 2
    grid_x, grid_y, grid_z = np.arange(NX), np.arange(NY), np.arange(NZ)
    own_y = np.arange(HALF)

    device = np.arange(count)
    plane_of = (
        pw_order[device % pws][:, None] * (NZ // pws)
        + kpt_order[device // pws][:, None] * planes
        + np.arange(planes)[None, :]
    )
    return_table = {}

    def pencil(z_width):
        angle = angles(plane_of.ravel(), np.arange(z_width) - z_width // 2, NZ)
        cos, sin = (
            part.reshape(count, 1, planes, z_width) for part in (np.cos(angle), np.sin(angle))
        )
        real = np.concatenate((cos, -sin), axis=3)
        imag = np.concatenate((sin, cos), axis=3)
        return np.concatenate((real, imag), axis=1).reshape(-1, 2 * z_width)

    return_table["pencil"] = pencil

    angle = angles(low_freq, grid_y, NY)
    cos, sin = np.cos(angle), np.sin(angle)
    return_table["wave_y"] = np.block([[cos, sin], [-sin, cos]])

    angle = angles(grid_x, low_freq, NX)
    cos, sin = np.cos(angle), np.sin(angle)
    return_table["wave_x"] = np.block([[cos, -sin], [sin, cos]])

    angle = angles(own_y, grid_y, NY)
    cos, sin = np.cos(angle), np.sin(angle)
    return_table["forth_y"] = np.stack((cos, -sin), axis=1).reshape(2 * HALF, NY).T
    twice = np.where(own_y == 0, 1.0, 2.0)[:, None]
    return_table["back_y"] = np.stack((twice * cos, -twice * sin), axis=1).reshape(2 * HALF, NY)

    angle = angles(grid_z, plane_of.ravel(), NZ)
    return_table["forth_z"] = np.concatenate((np.cos(angle), np.sin(angle)), axis=0)
    own = NZ // pws
    merged = own // 8
    order = (
        pw_order[None, :, None] * own
        + np.arange(8)[None, None, :] * merged
        + np.arange(merged)[:, None, None]
    )
    angle = angles(order.ravel(), grid_z, NZ)
    return_table["back_z"] = np.concatenate((np.cos(angle), np.sin(angle)), axis=0)

    angle = angles(grid_x, grid_x, NX)
    return_table["both_x"] = np.concatenate((np.cos(angle), np.sin(angle)), axis=1)
    return return_table


def ramp(shape, axis, first=0):
    steps = lax.broadcasted_iota(jnp.int32, shape, axis) + first
    return steps.astype(jnp.float32).astype(jnp.bfloat16)


def sixteen(row):
    return jnp.broadcast_to(row, (16, row.shape[1])).astype(jnp.bfloat16)


def one_hot_lanes(row, ramps):
    column = jnp.transpose(jnp.concatenate([sixteen(row)] * (LANES // 16), axis=0))
    one = jnp.ones(column.shape, jnp.bfloat16)
    zero = jnp.zeros(column.shape, jnp.bfloat16)
    return jnp.concatenate(
        [
            jnp.where(column == ramps[:, first : first + LANES], one, zero)
            for first in range(0, ramps.shape[1], LANES)
        ],
        axis=1,
    )


def turn(row):
    return jnp.transpose(jnp.broadcast_to(row, (LANES, LANES)))


def cell_of(column):
    cell = ((column // NY + NX // 2) % NX - HALF // 2) * HALF
    return cell + (column % NY + NY // 2) % NY - HALF // 2


def rank_rows(rows, turned):
    return [
        sum(jnp.sum(jnp.where(t < row, 1.0, 0.0), axis=0, keepdims=True) for t in turned)
        for row in rows
    ]


def sorted_rows(rows):
    turned = [turn(row) for row in rows]
    ranks = [turn(rank) for rank in rank_rows(rows, turned)]
    lane = lax.broadcasted_iota(jnp.int32, (LANES, LANES), 1).astype(jnp.float32)
    return [
        sum(
            jnp.sum(jnp.where(rank == lane + t * LANES, value, 0.0), axis=0, keepdims=True)
            for rank, value in zip(ranks, turned)
        )
        for t in range(len(rows))
    ]


def usual_tiles(total, tiles):
    signed = np.arange(NX) - NX // 2
    radius = (signed[:, None] * NY) ** 2 + ((np.arange(NY) - NY // 2)[None, :] * NX) ** 2
    kept = np.sort(np.argsort(radius.ravel(), kind="stable")[:total] // NY - NX // 2 + HALF // 2)
    slots = tiles * LANES
    ranges = []
    for t in range(tiles):
        ends = []
        for edge, sign in ((t / tiles, -1), ((t + 1) / tiles, 1)):
            edge += sign * 5 * math.sqrt(edge * (1 - edge) / slots)
            ends.append(int(kept[min(max(int(edge * total), 0), total - 1)]) // 16)
        ranges.append(ends)
    held = [[t for t in range(tiles) if ranges[t][0] <= g <= ranges[t][1]] for g in range(HALF // 16)]
    return [(ts[0], ts[-1] + 1) if ts else (0, tiles) for ts in held]


RANK_LOW = 64
WINDOW = 64
END_WINDOW = 48


def exchange_rows(refs, low_bits, size_bits, descending):
    for outer in range(RANK_LOW):
        if any(outer >> bit & 1 for bit in low_bits[0]):
            continue
        touched = sorted(
            outer + sum(1 << bit for i, bit in enumerate(low_bits[0]) if pattern >> i & 1)
            for pattern in range(1 << len(low_bits[0]))
        )
        held = {v: [ref[v * 8 : v * 8 + 8, :] for ref in refs] for v in touched}
        for size, bits in zip(size_bits, low_bits[1:]):
            for bit in bits:
                for v in touched:
                    if v >> bit & 1:
                        continue
                    former, latter = held[v], held[v | 1 << bit]
                    if size < 6:
                        down = bool(v >> size & 1)
                        swap = former[0] < latter[0] if down else former[0] > latter[0]
                    else:
                        swap = former[0] > latter[0]
                        if descending is not None:
                            swap = jnp.logical_xor(swap, descending)
                    held[v] = [jnp.where(swap, y, x) for x, y in zip(former, latter)]
                    held[v | 1 << bit] = [jnp.where(swap, x, y) for x, y in zip(former, latter)]
        for v in touched:
            for ref, value in zip(refs, held[v]):
                ref[v * 8 : v * 8 + 8, :] = value


def exchange_sublanes(refs, stride, descending):
    sublane = lax.broadcasted_iota(jnp.int32, (8, LANES), 0)
    upper = sublane // stride % 2 == 1
    want_most = upper if descending is None else jnp.logical_xor(upper, descending)
    other = jnp.where(upper, sublane - stride, sublane + stride)

    for v in range(RANK_LOW):
        here = [ref[v * 8 : v * 8 + 8, :] for ref in refs]
        there = [jnp.take_along_axis(value, other, axis=0) for value in here]
        take = jnp.logical_xor(here[0] > there[0], want_most)
        for ref, x, y in zip(refs, here, there):
            ref[v * 8 : v * 8 + 8, :] = jnp.where(take, y, x)


def sort_columns(refs):
    sublane = lax.broadcasted_iota(jnp.int32, (8, LANES), 0)
    exchange_rows(refs, [(0, 1, 2), (0,), (1, 0), (2, 1, 0)], [1, 2, 3], None)
    exchange_rows(refs, [(3,), (3,)], [4], None)
    exchange_rows(refs, [(0, 1, 2), (2, 1, 0)], [4], None)
    exchange_rows(refs, [(3, 4), (4, 3)], [5], None)
    exchange_rows(refs, [(0, 1, 2), (2, 1, 0)], [5], None)
    for size in range(6, 10):
        descending = None if size == 9 else sublane // (1 << (size - 6)) % 2 == 1
        for bit in range(size - 1, 5, -1):
            exchange_sublanes(refs, 1 << (bit - 6), descending)
        exchange_rows(refs, [(3, 4, 5), (5, 4, 3)], [size], descending)
        if size < 9:
            exchange_rows(refs, [(0, 1, 2), (2, 1, 0)], [size], descending)


def pack_kernel(width, has_column, *refs):
    coeff_ref, miller_ref, slot_ref, pencil_ref, column_ref = refs[:5]
    rest = list(refs[5:])
    out_ref, total, key_ref, real_ref, imag_ref, lane_ref, real_low, imag_low, ramp_ref, step_ref, held, sem = rest
    fetch = pltpu.make_async_copy(pencil_ref, held, sem)
    fetch.start()
    half = total.shape[0] // 4
    slots = 2 * half
    count = out_ref.shape[0]
    rows = pencil_ref.shape[0] // count
    length = miller_ref.shape[0]
    ranks = key_ref.shape[0]

    slot = slot_ref[...]
    columns = [
        column_ref[t * LANES : (t + 1) * LANES].reshape(1, LANES) for t in range(slots // LANES)
    ]
    if not has_column:
        cells = [cell_of(column).astype(jnp.float32) for column in columns]
        near = slot % LANES
        rank = jnp.zeros(slot.shape, jnp.float32)
        for t, row in enumerate(rank_rows(cells, [turn(row) for row in cells])):
            found = jnp.take_along_axis(jnp.broadcast_to(row, slot.shape), near, axis=1)
            rank = jnp.where(slot // LANES == t, found, rank)
        slot = rank.astype(jnp.int32)
    second = slot >= half
    lane = miller_ref[...] + width // 2
    key = jnp.where(second, slot - half, slot) * (2 * width) + jnp.where(second, lane + width, lane)
    key_ref[0:length] = key.astype(jnp.float32)
    real_ref[0:length] = coeff_ref[0, pl.ds(0, length, stride=2), :]
    imag_ref[0:length] = coeff_ref[0, pl.ds(1, length, stride=2), :]
    blank = jnp.zeros((ranks - length, LANES), jnp.float32)
    key_ref[length:] = blank + 2.0 * slots * width
    real_ref[length:] = blank
    imag_ref[length:] = blank
    sort_columns((key_ref, real_ref, imag_ref))

    blocks = length // 8
    ends = blocks // 6

    def base_of(block, window):
        base = 8 * (block // 2) + 8 * (block % 2) - window // 2
        return jnp.minimum(jnp.maximum(base, 0), half - window)

    ramp_ref[...] = ramp(ramp_ref.shape, 1)
    step_ref[...] = ramp(step_ref.shape, 0)
    sublane = lax.broadcasted_iota(jnp.int32, (8, LANES), 0)
    astray = jnp.zeros((8, LANES), jnp.float32)
    for v in range(RANK_LOW):
        at = slice(v * 8, v * 8 + 8)
        keys = key_ref[at, :]
        high = jnp.floor(keys * (1.0 / (2 * width)))
        lane_ref[at, :] = keys - high * (2.0 * width)
        key_ref[at, :] = high
        for ref, low_ref in ((real_ref, real_low), (imag_ref, imag_low)):
            value = ref[at, :]
            rounded = value.astype(jnp.bfloat16).astype(jnp.float32)
            ref[at, :] = rounded
            low_ref[at, :] = value - rounded
        block = sublane * (RANK_LOW // 8) + v // 8
        at_end = jnp.logical_or(block < ends, block >= blocks - ends)
        base = jnp.where(at_end, base_of(block, END_WINDOW), base_of(block, WINDOW))
        offset = high - base.astype(jnp.float32)
        outside = jnp.logical_or(offset < 0.0, offset >= jnp.where(at_end, 1.0 * END_WINDOW, 1.0 * WINDOW))
        astray = jnp.where(outside, 1.0, astray)
    astray = jnp.max(jnp.where(sublane * RANK_LOW < length, astray, 0.0))

    def add(block, base, window):
        first = block % (RANK_LOW // 8) * 64 + block // (RANK_LOW // 8)
        base_row = jnp.full((1, LANES), base, jnp.int32).astype(jnp.float32)
        zero = jnp.zeros((16, LANES), jnp.bfloat16)
        spread, chosen = [], []
        for t in range(8):
            row = pl.ds(first + 8 * t, 1)
            high = sixteen(key_ref[row, :] - base_row)
            masks = [high == step_ref[r : r + 16, :] for r in range(0, window, 16)]
            spread.append(
                jnp.concatenate(
                    [
                        jnp.where(mask, value, zero)
                        for value in [
                            sixteen(ref[row, :]) for ref in (real_ref, imag_ref, real_low, imag_low)
                        ]
                        for mask in masks
                    ],
                    axis=0,
                )
            )
            chosen.append(one_hot_lanes(lane_ref[row, :], ramp_ref[...]))
        found = mul(jnp.concatenate(spread, axis=1), jnp.concatenate(chosen, axis=0), NN)
        for i in range(4):
            if window == half:
                into = pl.ds(i * half, half)
            else:
                into = pl.ds(pl.multiple_of(i * half + base, 8), window)
            total[into, :] += found[i * window : (i + 1) * window]

    total[...] = jnp.zeros_like(total)
    together = 4 if ends % 4 == 0 and blocks % 4 == 0 else 1

    def add_blocks(first, end, window):
        def some_blocks(i, unused):
            for s in range(together):
                block = first + together * i + s
                add(block, base_of(block, window), window)
            return unused

        lax.fori_loop(0, (end - first) // together, some_blocks, 0)

    add_blocks(0, ends, END_WINDOW)
    add_blocks(ends, blocks - ends, WINDOW)
    add_blocks(blocks - ends, blocks, END_WINDOW)

    @pl.when(astray > 0.0)
    def _():
        total[...] = jnp.zeros_like(total)

        def one_block(block, unused):
            add(block, 0, half)
            return unused

        lax.fori_loop(0, blocks, one_block, 0)

    both = []
    for at in range(2):
        parts = [
            total[(2 * at + c) * half : (2 * at + c + 1) * half].astype(jnp.bfloat16)
            for c in range(2)
        ]
        both.append(
            jnp.concatenate(
                [
                    jnp.concatenate([part[:, h * width : (h + 1) * width] for part in parts], axis=1)
                    for h in range(2)
                ],
                axis=0,
            )
        )
    fetch.wait()
    pencils = mul(held[...], jnp.concatenate((both[0], both[0], both[1]), axis=1), NT)
    tiles = slots // LANES
    for t in range(tiles):
        tile = pencils[:, t * LANES : (t + 1) * LANES].reshape(count, rows, LANES)
        if not has_column:
            out_ref[:, t * rows : (t + 1) * rows] = tile
            continue
        for g in range(rows // 4):
            out_ref[:, t * (rows // 4) + g] = tile[:, 4 * g : 4 * g + 4]
    if has_column:
        column = [column.astype(jnp.float32) for column in columns]
        column = jnp.concatenate(column + [jnp.zeros((4 - tiles, LANES), jnp.float32)], axis=0)
        out_ref[:, tiles * rows // 4] = jnp.broadcast_to(column[None], (count, 4, LANES))


def pack_band(band, count, coeffs, miller, slot, pencil, slots, column):
    has_column = band == 0
    length = miller.shape[0]
    width = pencil.shape[1] // 6
    rows = pencil.shape[0] // count * (slots // LANES)
    operands = [coeffs, miller, slot, pencil, column]
    out_shape = (count, rows, LANES)
    if has_column:
        out_shape = (count, rows // 4 + 1, 4, LANES)
    one_band = pl.BlockSpec((1, 2 * length, LANES), lambda i: (band, 0, 0))
    return pl.pallas_call(
        functools.partial(pack_kernel, width, has_column),
        grid=(1,),
        in_specs=[one_band]
        + [
            pl.BlockSpec(memory_space=pl.ANY)
            if x is pencil
            else pl.BlockSpec(x.shape, lambda i, n=x.ndim: (0,) * n)
            for x in operands[1:]
        ],
        out_specs=pl.BlockSpec(out_shape, lambda i: (0,) * len(out_shape)),
        out_shape=jax.ShapeDtypeStruct(out_shape, jnp.float32),
        scratch_shapes=[pltpu.VMEM((2 * slots, 2 * width), jnp.float32)]
        + [pltpu.VMEM((8 * RANK_LOW, LANES), jnp.float32)] * 6
        + [
            pltpu.VMEM((LANES, 2 * width), jnp.bfloat16),
            pltpu.VMEM((slots // 2, LANES), jnp.bfloat16),
            pltpu.VMEM(pencil.shape, jnp.bfloat16),
            pltpu.SemaphoreType.DMA,
        ],
        compiler_params=pltpu.CompilerParams(vmem_limit_bytes=PACK_LIMIT),
        cost_estimate=pl.CostEstimate(
            flops=2 * length * LANES * slots * 4 * width,
            bytes_accessed=16 * length * LANES,
            transcendentals=0,
        ),
        name="pack_band",
    )(*operands)


def wave_kernel(kpts, tiles, scale, is_first, is_last, *refs):
    own_ref, count_ref, came_ref, wave_y_ref, wave_x_ref = refs[:5]
    rest = list(refs[5:])
    forth_ref = rest.pop(0) if is_last else None
    former_ref, cell_ref = (None, None) if is_first else (rest.pop(0), rest.pop(0))
    density_refs = [rest.pop(0) for _ in range(kpts if is_last else 1)]
    if is_first:
        coulomb_ref, cell_ref = rest.pop(0), rest.pop(0)
    send_ref = rest.pop(0) if is_last else None
    values, grid, whole, chosen_ref, high_ref = rest
    planes = density_refs[0].shape[0]
    block = NX // kpts
    part_rows = 2 * planes
    pws = came_ref.shape[0] // kpts
    rows = kpts * part_rows
    total = values.shape[1]

    for j in range(pws):
        for t in range(tiles):
            if is_first:
                groups = [
                    came_ref[k * pws + j, t * (part_rows // 4) + g]
                    for k in range(kpts)
                    for g in range(part_rows // 4)
                ]
            else:
                groups = [
                    came_ref[k * pws + j, t * part_rows : (t + 1) * part_rows] for k in range(kpts)
                ]
            taken = jnp.concatenate(groups, axis=0)
            high, low = pieces(taken)
            first = (t * pws + j) * LANES
            values[0:rows, first : first + LANES] = high
            values[rows : 2 * rows, first : first + LANES] = low

    tile = 4 * HALF
    ramps = ramp((LANES, tile), 1)
    usual = usual_tiles(total, tiles)
    astray = jnp.zeros((1, LANES), jnp.float32)
    for j in range(pws):
        if is_first:
            columns = [came_ref[j, tiles * part_rows // 4, t : t + 1] for t in range(tiles)]
            cells = [cell_of(column.astype(jnp.int32)) for column in columns]
            ordered = sorted_rows([cell.astype(jnp.float32) for cell in cells])
        for t in range(tiles):
            first = (t * pws + j) * LANES
            if is_first:
                cell = cells[t]
                cell_ref[:, first : first + LANES] = ordered[t].astype(jnp.int32)
            else:
                cell = cell_ref[:, first : first + LANES]
                group = cell // (4 * tile)
                for g, (least, end) in enumerate(usual):
                    if not least <= t < end:
                        astray = jnp.where(group == g, 1.0, astray)
            lane = (cell % tile).astype(jnp.float32)
            chosen_ref[first : first + LANES, :] = one_hot_lanes(lane, ramps)
            high_ref[:, first : first + LANES] = sixteen((cell // tile).astype(jnp.float32))
    if is_first:
        step_z = lax.broadcasted_iota(jnp.int32, (NZ, NX), 0)
        step_x = lax.broadcasted_iota(jnp.int32, (NZ, NX), 1)
        for q in range(coulomb_ref.shape[0]):
            freq_y = jnp.full((NZ, NX), own_ref[1] + q, jnp.int32)
            kernel = coulomb(signed_freq(step_z, NZ), signed_freq(step_x, NX), freq_y)
            coulomb_ref[q] = kernel * (1.0 / (NX * NY * NZ))
    left = lax.broadcasted_iota(jnp.int32, (planes, LANES), 1) < HALF

    def place(t, found):
        found = found[:rows] + found[rows:]
        for h in range(2):
            for k in range(kpts):
                real, imag = (
                    found[(2 * k + c) * planes : (2 * k + c + 1) * planes, h * LANES : (h + 1) * LANES]
                    for c in range(2)
                )
                first = (k * HALF + 4 * t + 2 * h) * planes
                grid[first : first + planes, :] = jnp.where(left, real, pltpu.roll(imag, HALF, 1))
                grid[first + planes : first + 2 * planes, :] = jnp.where(
                    left, pltpu.roll(real, HALF, 1), imag
                )

    def place_all(ranges):
        for g, (least, end) in enumerate(ranges):
            held = slice(least * pws * LANES, end * pws * LANES)
            high = high_ref[:, held]
            zero = jnp.zeros_like(high)
            kept = []
            for t in range(4 * g, 4 * g + 4):
                here = high == jnp.full_like(high, t)
                kept += [
                    jnp.where(here, values[r : r + 16, held], zero) for r in range(0, 2 * rows, 16)
                ]
            found = mul(jnp.concatenate(kept, axis=0), chosen_ref[held, :], NN)
            for s in range(4):
                place(4 * g + s, found[2 * rows * s : 2 * rows * (s + 1)])

    whole_range = [(0, tiles)] * len(usual)
    if is_first:
        place_all(whole_range)
    else:
        astray = jnp.max(astray)

        place_all(usual)

        @pl.when(astray > 0.0)
        def _():
            place_all(whole_range)

    sum_of = count_ref[0]
    for k in range(1, kpts):
        sum_of = sum_of + count_ref[k]

    def spread(number):
        return jnp.full((8, NY), number, jnp.int32).astype(jnp.float32)

    weights = [
        jnp.concatenate([spread(count_ref[k]) / spread(sum_of) * scale] * (NX // 8), axis=0)
        for k in ring_order(kpts)
    ]
    lines = [grid[pl.ds(p, kpts * HALF, stride=planes), :] for p in range(planes)]
    lines = mul3_right(jnp.concatenate(lines, axis=0), wave_y_ref[...], NN)

    for p in range(planes):
        mixed = lines[p * kpts * HALF : (p + 1) * kpts * HALF]
        mixed = jnp.concatenate(
            [
                jnp.concatenate(
                    [mixed[k * HALF : (k + 1) * HALF, c * NY : (c + 1) * NY] for k in range(kpts)],
                    axis=1,
                )
                for c in range(2)
            ],
            axis=0,
        )
        wave = mul3_left(wave_x_ref[...], mixed, NN)
        square = wave[:NX] * wave[:NX] + wave[NX:] * wave[NX:]
        density = weights[0] * square[:, :NY]
        for k in range(1, kpts):
            density = density + weights[k] * square[:, k * NY : (k + 1) * NY]
        if former_ref is not None:
            density = density + former_ref[p]
        if is_last:
            whole[p] = density
        else:
            density_refs[0][p] = density

    if is_last:
        for s, density_ref in enumerate(density_refs):
            first = pl.multiple_of(lax.rem(own_ref[0] + s, kpts) * block, block)
            density_ref[...] = whole[:, pl.ds(first, block), :]
        level = jnp.mean(whole[0, :8, :], axis=(0, 1), keepdims=True)
        field = whole[...].reshape(planes * NX, NY) - level
        half = mul3_right(field, forth_ref[...], NN)
        first_row = lax.broadcasted_iota(jnp.int32, (2 * HALF, NX), 0) == 0
        for p in range(planes):
            turned = jnp.transpose(half[p * NX : (p + 1) * NX])
            turned = turned + jnp.where(first_row, level * NY, 0.0)
            send_ref[pl.ds(p, 2 * HALF, stride=planes), :] = turned


def wave_band(kpts, tiles, total, scale, own, counts, came, wave_y, wave_x, forth, former, cell):
    planes = NZ // came.shape[0]
    block = NX // kpts
    is_first, is_last = former is None, forth is not None
    vmem = pl.BlockSpec(memory_space=pltpu.VMEM)
    operands = [own, counts, came, wave_y, wave_x]
    if is_last:
        operands.append(forth)
    if not is_first:
        operands += [former, cell]
    if is_last:
        out_shape = [jax.ShapeDtypeStruct((planes, block, NY), jnp.float32)] * kpts
    else:
        out_shape = [jax.ShapeDtypeStruct((planes, NX, NY), jnp.float32)]
    if is_first:
        out_shape.append(jax.ShapeDtypeStruct((HALF // came.shape[0], NZ, NX), jnp.float32))
        out_shape.append(jax.ShapeDtypeStruct((1, total), jnp.int32))
    if is_last:
        out_shape.append(jax.ShapeDtypeStruct((2 * HALF * planes, NX), jnp.float32))
    rows = kpts * 2 * planes
    return pl.pallas_call(
        functools.partial(wave_kernel, kpts, tiles, scale, is_first, is_last),
        in_specs=[pl.BlockSpec(memory_space=pltpu.SMEM)] * 2 + [vmem] * (len(operands) - 2),
        out_specs=[vmem] * len(out_shape),
        out_shape=out_shape,
        scratch_shapes=[
            pltpu.VMEM((2 * rows, total), jnp.bfloat16),
            pltpu.VMEM((kpts * planes * HALF, LANES), jnp.float32),
            pltpu.VMEM((planes, NX, NY), jnp.float32),
            pltpu.VMEM((total, 4 * HALF), jnp.bfloat16),
            pltpu.VMEM((16, total), jnp.bfloat16),
        ],
        compiler_params=pltpu.CompilerParams(vmem_limit_bytes=VMEM_LIMIT),
        cost_estimate=pl.CostEstimate(
            flops=4 * rows * total * HALF * HALF, bytes_accessed=4 * came.size, transcendentals=0
        ),
        name="wave_band",
    )(*operands)


def poisson_kernel(pws, own_ref, kernel_ref, came_ref, forth_ref, back_ref, both_x_ref, send_ref):
    count, parts, planes, unused = came_ref.shape
    pairs = parts // 2
    fields = [came_ref[:, i].reshape(NZ, NX) for i in range(parts)]
    level = jnp.mean(fields[0], axis=(0, 1), keepdims=True)
    fields[0] = fields[0] - jnp.where(own_ref[1] == 0, level, 0.0)
    field = jnp.concatenate(fields, axis=1)
    turned = mul3_left(forth_ref[...], field, NN)

    def part(array, half, i):
        return array[half * NZ : (half + 1) * NZ, i * NX : (i + 1) * NX]

    lines = []
    for q in range(pairs):
        lines.append(part(turned, 0, 2 * q) + part(turned, 1, 2 * q + 1))
        lines.append(part(turned, 0, 2 * q + 1) - part(turned, 1, 2 * q))
    spectrum = mul3_right(jnp.concatenate(lines, axis=0), both_x_ref[...], NN)

    lines = []
    for q in range(pairs):
        real = spectrum[2 * q * NZ : (2 * q + 1) * NZ]
        imag = spectrum[(2 * q + 1) * NZ : (2 * q + 2) * NZ]
        kernel = kernel_ref[q]
        lines.append((real[:, :NX] + imag[:, NX:]) * kernel)
        lines.append((imag[:, :NX] - real[:, NX:]) * kernel)
    turned = mul3_right(jnp.concatenate(lines, axis=0), both_x_ref[...], NN)
    lines = []
    for q in range(pairs):
        real = turned[2 * q * NZ : (2 * q + 1) * NZ]
        imag = turned[(2 * q + 1) * NZ : (2 * q + 2) * NZ]
        lines.append(real[:, :NX] - imag[:, NX:])
        lines.append(real[:, NX:] + imag[:, :NX])
    turned = mul3_left(back_ref[...], jnp.concatenate(lines, axis=1), NN)

    kpts = count // pws
    merged = NZ // pws // 8
    block = NX // kpts
    rows = pws * 8
    lane = lax.broadcasted_iota(jnp.int32, (rows, LANES), 1) // block
    for q in range(pairs):
        real = part(turned, 0, 2 * q) - part(turned, 1, 2 * q + 1)
        imag = part(turned, 0, 2 * q + 1) + part(turned, 1, 2 * q)
        for c, value in enumerate((real, imag)):
            for place, a in enumerate(ring_order(kpts)):
                packed = None
                for m in range(merged):
                    piece = value[m * rows : (m + 1) * rows]
                    shift = (m - a) * block % LANES
                    if shift:
                        piece = pltpu.roll(piece, shift, 1)
                    packed = piece if m == 0 else jnp.where(lane == m, piece, packed)
                send_ref[place * pws : (place + 1) * pws, 2 * q + c] = packed.reshape(pws, 8, LANES)


def poisson(pws, own, kernel, came, forth, back, both_x):
    vmem = pl.BlockSpec(memory_space=pltpu.VMEM)
    count, parts, unused, unused = came.shape
    return pl.pallas_call(
        functools.partial(poisson_kernel, pws),
        in_specs=[pl.BlockSpec(memory_space=pltpu.SMEM)] + [vmem] * 5,
        out_specs=vmem,
        out_shape=jax.ShapeDtypeStruct((count, parts, 8, LANES), jnp.float32),
        compiler_params=pltpu.CompilerParams(vmem_limit_bytes=VMEM_LIMIT),
        name="poisson",
    )(own, kernel, came, forth, back, both_x)


def finish_kernel(own_ref, came_ref, back_ref, *refs):
    block_refs, density_ref, out_ref = refs[:-2], refs[-2], refs[-1]
    kpts = len(block_refs)
    planes, block, unused = out_ref.shape
    merged = planes // 8
    for s, block_ref in enumerate(block_refs):
        sender = lax.rem(own_ref[0] + kpts - s, kpts)
        density_ref[pl.ds(sender * (planes // kpts), planes // kpts)] = block_ref[...]
    for h in range(8):
        lines = came_ref[pl.ds(h, 2 * HALF, stride=8), :]
        field = mul3_right(lines, back_ref[...], TN)
        out_ref[h * merged : (h + 1) * merged] = field.reshape(merged, block, NY)


def finish(planes, block, own, came, back_y, blocks):
    vmem = pl.BlockSpec(memory_space=pltpu.VMEM)
    return pl.pallas_call(
        finish_kernel,
        in_specs=[pl.BlockSpec(memory_space=pltpu.SMEM)] + [vmem] * (2 + len(blocks)),
        out_specs=[vmem] * 2,
        out_shape=[jax.ShapeDtypeStruct((planes, block, NY), jnp.float32)] * 2,
        compiler_params=pltpu.CompilerParams(vmem_limit_bytes=VMEM_LIMIT),
        name="finish",
    )(own, came, back_y, *blocks)


def exchange(array):
    kpts, pws = lax.axis_size("kpt"), lax.axis_size("pw")
    kpt_order, pw_order = group_order(kpts, pws)
    group = [k * pws + j for k in kpt_order for j in pw_order]
    return lax.all_to_all(
        array, ("kpt", "pw"), split_axis=0, concat_axis=0, tiled=True, axis_index_groups=[group]
    )


def place_in(order, axis):
    places = jnp.asarray(np.argsort(np.array(order)), jnp.int32)
    return lax.dynamic_index_in_dim(places, lax.axis_index(axis), 0, keepdims=False)


def local_planes(band_coeffs, miller_third, column_slot, column_map, kpoint_counts):
    pws = lax.axis_size("pw")
    kpts = lax.axis_size("kpt")
    count = pws * kpts
    slots = column_map.shape[0]
    band_count = band_coeffs.shape[1]
    z_width = column_slot.shape[1] // slots
    planes = NZ // count
    parts = 2 * HALF // count
    made = tables(kpts, pws, planes)
    pencil = stack_table(made["pencil"](z_width), 1)
    wave_x, forth_z, back_z = (
        stack_table(made[name], 1) for name in ("wave_x", "forth_z", "back_z")
    )
    wave_y, forth_y, back_y, both_x = (
        stack_table(made[name], 0) for name in ("wave_y", "forth_y", "back_y", "both_x")
    )

    tiles = slots // LANES
    length = column_slot.shape[1] // LANES
    coeffs = band_coeffs.reshape(band_count, 2, length, LANES).transpose(0, 2, 1, 3)
    coeffs = coeffs.reshape(band_count, 2 * length, LANES)
    miller = miller_third.reshape(length, LANES)
    slot = column_slot.reshape(length, LANES)
    scale = 2.0 / (column_slot.shape[1] * pws)
    arrived = []
    for band in range(band_count):
        packed = pack_band(
            band, count, coeffs, miller, slot, pencil, slots, column_map
        )
        arrived.append(exchange(packed))
    kpt_order, pw_order = group_order(kpts, pws)
    device = place_in(kpt_order, "kpt") * pws + place_in(pw_order, "pw")
    own = jnp.stack((lax.axis_index("kpt"), device * (parts // 2))).astype(jnp.int32)
    former = cell = None
    for band in range(band_count):
        forth = forth_y if band == band_count - 1 else None
        made_here = wave_band(
            kpts,
            tiles,
            pws * slots,
            scale,
            own,
            kpoint_counts,
            arrived[band],
            wave_y,
            wave_x,
            forth,
            former,
            cell,
        )
        former = made_here[0]
        if band == 0:
            kernel, cell = made_here[kpts if forth is not None else 1 :][:2]
    half = exchange(made_here[-1].reshape(count, parts, planes, NX))
    blocks = [made_here[0]] + [
        lax.ppermute(made_here[s], "kpt", [(a, (a + s) % kpts) for a in range(kpts)])
        for s in range(1, kpts)
    ]
    back = poisson(pws, own, kernel, half, forth_z, back_z, both_x)
    back = exchange(back).reshape(count * parts * 8, LANES)
    return tuple(finish(NZ // pws, NX // kpts, own, back, back_y, blocks))


def fits_planes(kpts, pws):
    count = kpts * pws
    own = NZ // pws
    return (
        NZ % count == 0
        and NZ // count == 8
        and 2 * HALF % (2 * count) == 0
        and NX % kpts == 0
        and own % 8 == 0
        and own // 8 * (NX // kpts) == LANES
    )


def local(band_coeffs, miller_third, column_slot, column_map, kpoint_counts):
    slots = column_map.shape[0]
    plain = slots % LANES == 0 and LANES <= slots <= 8 * RANK_LOW
    plain = plain and column_slot.shape[1] == slots * LANES
    fits = plain and fits_planes(lax.axis_size("kpt"), lax.axis_size("pw"))
    chosen = local_planes if fits else local_general
    return chosen(band_coeffs, miller_third, column_slot, column_map, kpoint_counts)


def solution(mesh):
    return jax.shard_map(
        local,
        mesh=mesh,
        in_specs=(P("kpt", None, None, "pw"), P("kpt", "pw"), P("kpt", "pw"), P("pw"), P()),
        out_specs=(P("pw", "kpt", None), P("pw", "kpt", None)),
        check_vma=False,
    )
```

```python
import functools
import math

import jax
import jax.numpy as jnp
import numpy as np
from jax import lax
from jax.experimental import pallas as pl
from jax.experimental.pallas import tpu as pltpu
from jax.sharding import PartitionSpec as P

NX = 128
NY = 128
NZ = 256


SPACING = 0.25


def contract(pattern, former, latter):
    return jnp.einsum(
        pattern, former, latter, precision=lax.Precision.HIGHEST, preferred_element_type=jnp.float32
    )


def phase_tables(first_index, second_index, length):
    product = first_index[:, None] * second_index[None, :] % length
    angle = product.astype(jnp.float32) * (2.0 * math.pi / length)
    return (jnp.cos(angle), jnp.sin(angle))


def signed_freq(values, length):
    return jnp.where(values >= length // 2, values - length, values)


def coulomb(freq_z, freq_x, freq_y):
    wave_z = freq_z.astype(jnp.float32) / (NZ * SPACING)
    wave_x = freq_x.astype(jnp.float32) / (NX * SPACING)
    wave_y = freq_y.astype(jnp.float32) / (NY * SPACING)
    squared = (2.0 * math.pi) ** 2 * (wave_z * wave_z + wave_x * wave_x + wave_y * wave_y)
    anchor = (freq_z == 0) & (freq_x == 0) & (freq_y == 0)
    return jnp.where(anchor, 0.0, 4.0 * math.pi / jnp.where(anchor, 1.0, squared))


def poisson_columns(real_part, imag_part, freq_x, freq_y):
    length = real_part.shape[0]
    steps_z = jnp.arange(length, dtype=jnp.int32)
    cos_z, sin_z = phase_tables(steps_z, steps_z, length)
    spec_real = contract("zk,km->zm", cos_z, real_part) + contract("zk,km->zm", sin_z, imag_part)
    spec_imag = contract("zk,km->zm", cos_z, imag_part) - contract("zk,km->zm", sin_z, real_part)
    kernel = coulomb(signed_freq(steps_z, length)[:, None], freq_x[None, :], freq_y[None, :]) / (
        NX * NY * NZ
    )
    spec_real = spec_real * kernel
    spec_imag = spec_imag * kernel
    back_real = contract("zk,km->zm", cos_z, spec_real) - contract("zk,km->zm", sin_z, spec_imag)
    back_imag = contract("zk,km->zm", sin_z, spec_real) + contract("zk,km->zm", cos_z, spec_imag)
    return (back_real, back_imag)


def forward_planes(field):
    steps_x = jnp.arange(NX, dtype=jnp.int32)
    steps_y = jnp.arange(NY, dtype=jnp.int32)
    cos_y, sin_y = phase_tables(steps_y, steps_y, NY)
    cos_x, sin_x = phase_tables(steps_x, steps_x, NX)
    half_real = contract("pxy,ky->pxk", field, cos_y)
    half_imag = -contract("pxy,ky->pxk", field, sin_y)
    spec_real = contract("kx,pxy->pky", cos_x, half_real) + contract(
        "kx,pxy->pky", sin_x, half_imag
    )
    spec_imag = contract("kx,pxy->pky", cos_x, half_imag) - contract(
        "kx,pxy->pky", sin_x, half_real
    )
    return (spec_real, spec_imag)


def local_general(band_coeffs, miller_third, column_slot, column_map, kpoint_counts):
    pw_count = lax.axis_size("pw")
    kpt_count = lax.axis_size("kpt")
    pw_index = lax.axis_index("pw")
    kpt_index = lax.axis_index("kpt")
    col_dev = column_map.shape[0]
    ng_dev = column_slot.shape[1]
    band_count = band_coeffs.shape[1]
    z_width = ng_dev // col_dev
    planes = NZ // pw_count
    x_block = NX // kpt_count
    col_total = pw_count * col_dev
    steps_y = jnp.arange(NY, dtype=jnp.int32)
    steps_x = jnp.arange(NX, dtype=jnp.int32)
    cos_y, sin_y = phase_tables(steps_y, steps_y, NY)
    cos_x, sin_x = phase_tables(steps_x, steps_x, NX)
    all_columns = lax.all_gather(column_map, "pw", axis=0, tiled=True)
    position = (miller_third[0] + z_width // 2) * col_dev + column_slot[0]
    source_of = (
        jnp.zeros((ng_dev,), jnp.int32).at[position].set(jnp.arange(ng_dev, dtype=jnp.int32))
    )
    coeff_rows = band_coeffs[0].reshape(band_count * 2, ng_dev).T
    packed = jnp.take(coeff_rows, source_of, axis=0)
    packed = (
        packed.reshape(z_width, col_dev, band_count, 2)
        .transpose(0, 2, 3, 1)
        .reshape(z_width, band_count * 2 * col_dev)
    )
    cos_z, sin_z = phase_tables(
        jnp.arange(NZ, dtype=jnp.int32), jnp.arange(z_width, dtype=jnp.int32) - z_width // 2, NZ
    )
    by_cos = contract("zj,jc->zc", cos_z, packed).reshape(NZ, band_count, 2, col_dev)
    by_sin = contract("zj,jc->zc", sin_z, packed).reshape(NZ, band_count, 2, col_dev)
    pencil = jnp.stack(
        (by_cos[:, :, 0] - by_sin[:, :, 1], by_sin[:, :, 0] + by_cos[:, :, 1]), axis=2
    )
    pencil = pencil.reshape(NZ, band_count * 2 * col_dev)
    arrived = lax.all_to_all(pencil, "pw", split_axis=0, concat_axis=1, tiled=True)
    arrived = arrived.reshape(planes, pw_count, band_count, 2, col_dev).transpose(2, 1, 4, 3, 0)
    arrived = arrived.reshape(band_count, col_total, 2 * planes)
    arrived = jnp.concatenate(
        (arrived, jnp.zeros((band_count, 1, 2 * planes), jnp.float32)), axis=1
    )
    cell_source = (
        jnp.full((NX * NY,), col_total, jnp.int32)
        .at[all_columns]
        .set(jnp.arange(col_total, dtype=jnp.int32))
    )

    def add_band(band, running):
        one_band = lax.dynamic_index_in_dim(arrived, band, 0, keepdims=False)
        placed = jnp.take(one_band, cell_source, axis=0)
        placed = placed.reshape(NX, NY, 2, planes).transpose(2, 3, 0, 1)
        grid_real = placed[0]
        grid_imag = placed[1]
        mixed_real = contract("pxm,ym->pxy", grid_real, cos_y) - contract(
            "pxm,ym->pxy", grid_imag, sin_y
        )
        mixed_imag = contract("pxm,ym->pxy", grid_real, sin_y) + contract(
            "pxm,ym->pxy", grid_imag, cos_y
        )
        wave_real = contract("xm,pmy->pxy", cos_x, mixed_real) - contract(
            "xm,pmy->pxy", sin_x, mixed_imag
        )
        wave_imag = contract("xm,pmy->pxy", sin_x, mixed_real) + contract(
            "xm,pmy->pxy", cos_x, mixed_imag
        )
        return running + wave_real * wave_real + wave_imag * wave_imag

    squares_sum = lax.fori_loop(0, band_count, add_band, jnp.zeros((planes, NX, NY), jnp.float32))
    weight = (
        2.0
        * kpoint_counts[kpt_index].astype(jnp.float32)
        / jnp.sum(kpoint_counts).astype(jnp.float32)
    )
    weight = weight / (ng_dev * pw_count)
    partial_value = weight * squares_sum
    total_density = lax.psum(partial_value, "kpt")
    density = lax.dynamic_slice_in_dim(total_density, kpt_index * x_block, x_block, 1)
    spec_real, spec_imag = forward_planes(total_density)
    rows_pw = NX // pw_count
    pencil_real, pencil_imag = (
        lax.all_to_all(spec_real, "pw", split_axis=1, concat_axis=0, tiled=True),
        lax.all_to_all(spec_imag, "pw", split_axis=1, concat_axis=0, tiled=True),
    )
    local_x = pw_index * rows_pw + jnp.arange(rows_pw, dtype=jnp.int32)
    freq_x = jnp.repeat(signed_freq(local_x, NX), NY)
    freq_y = jnp.tile(signed_freq(steps_y, NY), rows_pw)
    back_real, back_imag = poisson_columns(
        pencil_real.reshape(NZ, rows_pw * NY), pencil_imag.reshape(NZ, rows_pw * NY), freq_x, freq_y
    )
    plane_real, plane_imag = (
        lax.all_to_all(
            back_real.reshape(NZ, rows_pw, NY), "pw", split_axis=0, concat_axis=1, tiled=True
        ),
        lax.all_to_all(
            back_imag.reshape(NZ, rows_pw, NY), "pw", split_axis=0, concat_axis=1, tiled=True
        ),
    )
    own_rows = kpt_index * x_block + jnp.arange(x_block, dtype=jnp.int32)
    cos_rows, sin_rows = phase_tables(own_rows, steps_x, NX)
    rows_real = contract("xk,pky->pxy", cos_rows, plane_real) - contract(
        "xk,pky->pxy", sin_rows, plane_imag
    )
    rows_imag = contract("xk,pky->pxy", sin_rows, plane_real) + contract(
        "xk,pky->pxy", cos_rows, plane_imag
    )
    hartree = contract("pxk,yk->pxy", rows_real, cos_y) - contract("pxk,yk->pxy", rows_imag, sin_y)
    return (density, hartree)


LANES = 128
HALF = 64
VMEM_LIMIT = 16 * 1024 * 1024
PACK_LIMIT = 56 * 1024 * 1024
NN = (((1,), (0,)), ((), ()))
NT = (((1,), (1,)), ((), ()))
TN = (((0,), (0,)), ((), ()))


def pieces(value):
    high = value.astype(jnp.bfloat16)
    low = (value - high.astype(jnp.float32)).astype(jnp.bfloat16)
    return high, low


def mul(former, latter, dims):
    return lax.dot_general(former, latter, dims, preferred_element_type=jnp.float32)


def mul3_left(former, latter, dims):
    high, low = pieces(latter)
    (unused,), (axis,) = dims[0]
    return mul(former, jnp.concatenate((high, high, low), axis=axis), dims)


def mul3_right(former, latter, dims):
    high, low = pieces(former)
    (axis,), (unused,) = dims[0]
    return mul(jnp.concatenate((high, high, low), axis=axis), latter, dims)


def stack_table(values, axis):
    high = values.astype(np.float32).astype(jnp.bfloat16)
    low = (values - high.astype(np.float64)).astype(np.float32).astype(jnp.bfloat16)
    return jnp.asarray(np.concatenate((high, low, high), axis=axis))


def angles(former, latter, length):
    return np.outer(former, latter) % length * (2.0 * np.pi / length)


def ring_order(length):
    return [0, *range(1, length, 2), *range(length - 2 + length % 2, 0, -2)] if length > 1 else [0]


def group_order(kpts, pws):
    cores = 2 if pws % 2 == 0 else 1
    return ring_order(kpts), [c * cores + i for c in ring_order(pws // cores) for i in range(cores)]


def tables(kpts, pws, planes):
    count = kpts * pws
    kpt_order, pw_order = (np.array(order) for order in group_order(kpts, pws))
    low_freq = np.arange(HALF) - HALF // 2
    grid_x, grid_y, grid_z = np.arange(NX), np.arange(NY), np.arange(NZ)
    own_y = np.arange(HALF)

    device = np.arange(count)
    plane_of = (
        pw_order[device % pws][:, None] * (NZ // pws)
        + kpt_order[device // pws][:, None] * planes
        + np.arange(planes)[None, :]
    )
    return_table = {}

    def pencil(z_width):
        angle = angles(plane_of.ravel(), np.arange(z_width) - z_width // 2, NZ)
        cos, sin = (
            part.reshape(count, 1, planes, z_width) for part in (np.cos(angle), np.sin(angle))
        )
        real = np.concatenate((cos, -sin), axis=3)
        imag = np.concatenate((sin, cos), axis=3)
        return np.concatenate((real, imag), axis=1).reshape(-1, 2 * z_width)

    return_table["pencil"] = pencil

    angle = angles(low_freq, grid_y, NY)
    cos, sin = np.cos(angle), np.sin(angle)
    return_table["wave_y"] = np.block([[cos, sin], [-sin, cos]])

    angle = angles(grid_x, low_freq, NX)
    cos, sin = np.cos(angle), np.sin(angle)
    return_table["wave_x"] = np.block([[cos, -sin], [sin, cos]])

    angle = angles(own_y, grid_y, NY)
    cos, sin = np.cos(angle), np.sin(angle)
    return_table["forth_y"] = np.stack((cos, -sin), axis=1).reshape(2 * HALF, NY).T
    twice = np.where(own_y == 0, 1.0, 2.0)[:, None]
    return_table["back_y"] = np.stack((twice * cos, -twice * sin), axis=1).reshape(2 * HALF, NY)

    angle = angles(grid_z, plane_of.ravel(), NZ)
    return_table["forth_z"] = np.concatenate((np.cos(angle), np.sin(angle)), axis=0)
    own = NZ // pws
    merged = own // 8
    order = (
        pw_order[None, :, None] * own
        + np.arange(8)[None, None, :] * merged
        + np.arange(merged)[:, None, None]
    )
    angle = angles(order.ravel(), grid_z, NZ)
    return_table["back_z"] = np.concatenate((np.cos(angle), np.sin(angle)), axis=0)

    angle = angles(grid_x, grid_x, NX)
    return_table["both_x"] = np.concatenate((np.cos(angle), np.sin(angle)), axis=1)
    return return_table


def ramp(shape, axis, first=0):
    steps = lax.broadcasted_iota(jnp.int32, shape, axis) + first
    return steps.astype(jnp.float32).astype(jnp.bfloat16)


def sixteen(row):
    return jnp.broadcast_to(row, (16, row.shape[1])).astype(jnp.bfloat16)


def one_hot_lanes(row, ramps):
    column = jnp.transpose(jnp.concatenate([sixteen(row)] * (LANES // 16), axis=0))
    one = jnp.ones(column.shape, jnp.bfloat16)
    zero = jnp.zeros(column.shape, jnp.bfloat16)
    return jnp.concatenate(
        [
            jnp.where(column == ramps[:, first : first + LANES], one, zero)
            for first in range(0, ramps.shape[1], LANES)
        ],
        axis=1,
    )


def turn(row):
    return jnp.transpose(jnp.broadcast_to(row, (LANES, LANES)))


def cell_of(column):
    cell = ((column // NY + NX // 2) % NX - HALF // 2) * HALF
    return cell + (column % NY + NY // 2) % NY - HALF // 2


def rank_rows(rows, turned):
    return [
        sum(jnp.sum(jnp.where(t < row, 1.0, 0.0), axis=0, keepdims=True) for t in turned)
        for row in rows
    ]


def sorted_rows(rows):
    turned = [turn(row) for row in rows]
    ranks = [turn(rank) for rank in rank_rows(rows, turned)]
    lane = lax.broadcasted_iota(jnp.int32, (LANES, LANES), 1).astype(jnp.float32)
    return [
        sum(
            jnp.sum(jnp.where(rank == lane + t * LANES, value, 0.0), axis=0, keepdims=True)
            for rank, value in zip(ranks, turned)
        )
        for t in range(len(rows))
    ]


def usual_tiles(total, tiles):
    signed = np.arange(NX) - NX // 2
    radius = (signed[:, None] * NY) ** 2 + ((np.arange(NY) - NY // 2)[None, :] * NX) ** 2
    kept = np.sort(np.argsort(radius.ravel(), kind="stable")[:total] // NY - NX // 2 + HALF // 2)
    slots = tiles * LANES
    ranges = []
    for t in range(tiles):
        ends = []
        for edge, sign in ((t / tiles, -1), ((t + 1) / tiles, 1)):
            edge += sign * 5 * math.sqrt(edge * (1 - edge) / slots)
            ends.append(int(kept[min(max(int(edge * total), 0), total - 1)]) // 16)
        ranges.append(ends)
    held = [[t for t in range(tiles) if ranges[t][0] <= g <= ranges[t][1]] for g in range(HALF // 16)]
    return [(ts[0], ts[-1] + 1) if ts else (0, tiles) for ts in held]


RANK_LOW = 64
WINDOW = 64
END_WINDOW = 48


def exchange_rows(refs, low_bits, size_bits, descending):
    for outer in range(RANK_LOW):
        if any(outer >> bit & 1 for bit in low_bits[0]):
            continue
        touched = sorted(
            outer + sum(1 << bit for i, bit in enumerate(low_bits[0]) if pattern >> i & 1)
            for pattern in range(1 << len(low_bits[0]))
        )
        held = {v: [ref[v * 8 : v * 8 + 8, :] for ref in refs] for v in touched}
        for size, bits in zip(size_bits, low_bits[1:]):
            for bit in bits:
                for v in touched:
                    if v >> bit & 1:
                        continue
                    former, latter = held[v], held[v | 1 << bit]
                    if size < 6:
                        down = bool(v >> size & 1)
                        swap = former[0] < latter[0] if down else former[0] > latter[0]
                    else:
                        swap = former[0] > latter[0]
                        if descending is not None:
                            swap = jnp.logical_xor(swap, descending)
                    held[v] = [jnp.where(swap, y, x) for x, y in zip(former, latter)]
                    held[v | 1 << bit] = [jnp.where(swap, x, y) for x, y in zip(former, latter)]
        for v in touched:
            for ref, value in zip(refs, held[v]):
                ref[v * 8 : v * 8 + 8, :] = value


def exchange_sublanes(refs, stride, descending):
    sublane = lax.broadcasted_iota(jnp.int32, (8, LANES), 0)
    upper = sublane // stride % 2 == 1
    want_most = upper if descending is None else jnp.logical_xor(upper, descending)
    other = jnp.where(upper, sublane - stride, sublane + stride)

    for v in range(RANK_LOW):
        here = [ref[v * 8 : v * 8 + 8, :] for ref in refs]
        there = [jnp.take_along_axis(value, other, axis=0) for value in here]
        take = jnp.logical_xor(here[0] > there[0], want_most)
        for ref, x, y in zip(refs, here, there):
            ref[v * 8 : v * 8 + 8, :] = jnp.where(take, y, x)


def sort_columns(refs):
    sublane = lax.broadcasted_iota(jnp.int32, (8, LANES), 0)
    exchange_rows(refs, [(0, 1, 2), (0,), (1, 0), (2, 1, 0)], [1, 2, 3], None)
    exchange_rows(refs, [(3,), (3,)], [4], None)
    exchange_rows(refs, [(0, 1, 2), (2, 1, 0)], [4], None)
    exchange_rows(refs, [(3, 4), (4, 3)], [5], None)
    exchange_rows(refs, [(0, 1, 2), (2, 1, 0)], [5], None)
    for size in range(6, 10):
        descending = None if size == 9 else sublane // (1 << (size - 6)) % 2 == 1
        for bit in range(size - 1, 5, -1):
            exchange_sublanes(refs, 1 << (bit - 6), descending)
        exchange_rows(refs, [(3, 4, 5), (5, 4, 3)], [size], descending)
        if size < 9:
            exchange_rows(refs, [(0, 1, 2), (2, 1, 0)], [size], descending)


def pack_kernel(width, has_column, *refs):
    coeff_ref, miller_ref, slot_ref, pencil_ref, column_ref = refs[:5]
    rest = list(refs[5:])
    out_ref, total, key_ref, real_ref, imag_ref, lane_ref, real_low, imag_low, ramp_ref, step_ref, held, sem = rest
    fetch = pltpu.make_async_copy(pencil_ref, held, sem)
    fetch.start()
    half = total.shape[0] // 4
    slots = 2 * half
    count = out_ref.shape[0]
    rows = pencil_ref.shape[0] // count
    length = miller_ref.shape[0]
    ranks = key_ref.shape[0]

    slot = slot_ref[...]
    columns = [
        column_ref[t * LANES : (t + 1) * LANES].reshape(1, LANES) for t in range(slots // LANES)
    ]
    if not has_column:
        cells = [cell_of(column).astype(jnp.float32) for column in columns]
        near = slot % LANES
        rank = jnp.zeros(slot.shape, jnp.float32)
        for t, row in enumerate(rank_rows(cells, [turn(row) for row in cells])):
            found = jnp.take_along_axis(jnp.broadcast_to(row, slot.shape), near, axis=1)
            rank = jnp.where(slot // LANES == t, found, rank)
        slot = rank.astype(jnp.int32)
    second = slot >= half
    lane = miller_ref[...] + width // 2
    key = jnp.where(second, slot - half, slot) * (2 * width) + jnp.where(second, lane + width, lane)
    key_ref[0:length] = key.astype(jnp.float32)
    real_ref[0:length] = coeff_ref[0, pl.ds(0, length, stride=2), :]
    imag_ref[0:length] = coeff_ref[0, pl.ds(1, length, stride=2), :]
    blank = jnp.zeros((ranks - length, LANES), jnp.float32)
    key_ref[length:] = blank + 2.0 * slots * width
    real_ref[length:] = blank
    imag_ref[length:] = blank
    sort_columns((key_ref, real_ref, imag_ref))

    blocks = length // 8
    ends = blocks // 6

    def base_of(block, window):
        base = 8 * (block // 2) + 8 * (block % 2) - window // 2
        return jnp.minimum(jnp.maximum(base, 0), half - window)

    ramp_ref[...] = ramp(ramp_ref.shape, 1)
    step_ref[...] = ramp(step_ref.shape, 0)
    sublane = lax.broadcasted_iota(jnp.int32, (8, LANES), 0)
    astray = jnp.zeros((8, LANES), jnp.float32)
    for v in range(RANK_LOW):
        at = slice(v * 8, v * 8 + 8)
        keys = key_ref[at, :]
        high = jnp.floor(keys * (1.0 / (2 * width)))
        lane_ref[at, :] = keys - high * (2.0 * width)
        key_ref[at, :] = high
        for ref, low_ref in ((real_ref, real_low), (imag_ref, imag_low)):
            value = ref[at, :]
            rounded = value.astype(jnp.bfloat16).astype(jnp.float32)
            ref[at, :] = rounded
            low_ref[at, :] = value - rounded
        block = sublane * (RANK_LOW // 8) + v // 8
        at_end = jnp.logical_or(block < ends, block >= blocks - ends)
        base = jnp.where(at_end, base_of(block, END_WINDOW), base_of(block, WINDOW))
        offset = high - base.astype(jnp.float32)
        outside = jnp.logical_or(offset < 0.0, offset >= jnp.where(at_end, 1.0 * END_WINDOW, 1.0 * WINDOW))
        astray = jnp.where(outside, 1.0, astray)
    astray = jnp.max(jnp.where(sublane * RANK_LOW < length, astray, 0.0))

    def add(block, base, window):
        first = block % (RANK_LOW // 8) * 64 + block // (RANK_LOW // 8)
        base_row = jnp.full((1, LANES), base, jnp.int32).astype(jnp.float32)
        zero = jnp.zeros((16, LANES), jnp.bfloat16)
        spread, chosen = [], []
        for t in range(8):
            row = pl.ds(first + 8 * t, 1)
            high = sixteen(key_ref[row, :] - base_row)
            masks = [high == step_ref[r : r + 16, :] for r in range(0, window, 16)]
            spread.append(
                jnp.concatenate(
                    [
                        jnp.where(mask, value, zero)
                        for value in [
                            sixteen(ref[row, :]) for ref in (real_ref, imag_ref, real_low, imag_low)
                        ]
                        for mask in masks
                    ],
                    axis=0,
                )
            )
            chosen.append(one_hot_lanes(lane_ref[row, :], ramp_ref[...]))
        found = mul(jnp.concatenate(spread, axis=1), jnp.concatenate(chosen, axis=0), NN)
        for i in range(4):
            if window == half:
                into = pl.ds(i * half, half)
            else:
                into = pl.ds(pl.multiple_of(i * half + base, 8), window)
            total[into, :] += found[i * window : (i + 1) * window]

    total[...] = jnp.zeros_like(total)
    together = 4 if ends % 4 == 0 and blocks % 4 == 0 else 1

    def add_blocks(first, end, window):
        def some_blocks(i, unused):
            for s in range(together):
                block = first + together * i + s
                add(block, base_of(block, window), window)
            return unused

        lax.fori_loop(0, (end - first) // together, some_blocks, 0)

    add_blocks(0, ends, END_WINDOW)
    add_blocks(ends, blocks - ends, WINDOW)
    add_blocks(blocks - ends, blocks, END_WINDOW)

    @pl.when(astray > 0.0)
    def _():
        total[...] = jnp.zeros_like(total)

        def one_block(block, unused):
            add(block, 0, half)
            return unused

        lax.fori_loop(0, blocks, one_block, 0)

    both = []
    for at in range(2):
        parts = [
            total[(2 * at + c) * half : (2 * at + c + 1) * half].astype(jnp.bfloat16)
            for c in range(2)
        ]
        both.append(
            jnp.concatenate(
                [
                    jnp.concatenate([part[:, h * width : (h + 1) * width] for part in parts], axis=1)
                    for h in range(2)
                ],
                axis=0,
            )
        )
    fetch.wait()
    pencils = mul(held[...], jnp.concatenate((both[0], both[0], both[1]), axis=1), NT)
    tiles = slots // LANES
    for t in range(tiles):
        tile = pencils[:, t * LANES : (t + 1) * LANES].reshape(count, rows, LANES)
        if not has_column:
            out_ref[:, t * rows : (t + 1) * rows] = tile
            continue
        for g in range(rows // 4):
            out_ref[:, t * (rows // 4) + g] = tile[:, 4 * g : 4 * g + 4]
    if has_column:
        column = [column.astype(jnp.float32) for column in columns]
        column = jnp.concatenate(column + [jnp.zeros((4 - tiles, LANES), jnp.float32)], axis=0)
        out_ref[:, tiles * rows // 4] = jnp.broadcast_to(column[None], (count, 4, LANES))


def pack_band(band, count, coeffs, miller, slot, pencil, slots, column):
    has_column = band == 0
    length = miller.shape[0]
    width = pencil.shape[1] // 6
    rows = pencil.shape[0] // count * (slots // LANES)
    operands = [coeffs, miller, slot, pencil, column]
    out_shape = (count, rows, LANES)
    if has_column:
        out_shape = (count, rows // 4 + 1, 4, LANES)
    one_band = pl.BlockSpec((1, 2 * length, LANES), lambda i: (band, 0, 0))
    return pl.pallas_call(
        functools.partial(pack_kernel, width, has_column),
        grid=(1,),
        in_specs=[one_band]
        + [
            pl.BlockSpec(memory_space=pl.ANY)
            if x is pencil
            else pl.BlockSpec(x.shape, lambda i, n=x.ndim: (0,) * n)
            for x in operands[1:]
        ],
        out_specs=pl.BlockSpec(out_shape, lambda i: (0,) * len(out_shape)),
        out_shape=jax.ShapeDtypeStruct(out_shape, jnp.float32),
        scratch_shapes=[pltpu.VMEM((2 * slots, 2 * width), jnp.float32)]
        + [pltpu.VMEM((8 * RANK_LOW, LANES), jnp.float32)] * 6
        + [
            pltpu.VMEM((LANES, 2 * width), jnp.bfloat16),
            pltpu.VMEM((slots // 2, LANES), jnp.bfloat16),
            pltpu.VMEM(pencil.shape, jnp.bfloat16),
            pltpu.SemaphoreType.DMA,
        ],
        compiler_params=pltpu.CompilerParams(vmem_limit_bytes=PACK_LIMIT),
        cost_estimate=pl.CostEstimate(
            flops=2 * length * LANES * slots * 4 * width,
            bytes_accessed=16 * length * LANES,
            transcendentals=0,
        ),
        name="pack_band",
    )(*operands)


def wave_kernel(kpts, tiles, scale, is_first, is_last, *refs):
    own_ref, count_ref, came_ref, wave_y_ref, wave_x_ref = refs[:5]
    rest = list(refs[5:])
    forth_ref = rest.pop(0) if is_last else None
    former_ref, cell_ref = (None, None) if is_first else (rest.pop(0), rest.pop(0))
    density_refs = [rest.pop(0) for _ in range(kpts if is_last else 1)]
    if is_first:
        coulomb_ref, cell_ref = rest.pop(0), rest.pop(0)
    send_ref = rest.pop(0) if is_last else None
    values, grid, whole, chosen_ref, high_ref = rest
    planes = density_refs[0].shape[0]
    block = NX // kpts
    part_rows = 2 * planes
    pws = came_ref.shape[0] // kpts
    rows = kpts * part_rows
    total = values.shape[1]

    for j in range(pws):
        for t in range(tiles):
            if is_first:
                groups = [
                    came_ref[k * pws + j, t * (part_rows // 4) + g]
                    for k in range(kpts)
                    for g in range(part_rows // 4)
                ]
            else:
                groups = [
                    came_ref[k * pws + j, t * part_rows : (t + 1) * part_rows] for k in range(kpts)
                ]
            taken = jnp.concatenate(groups, axis=0)
            high, low = pieces(taken)
            first = (t * pws + j) * LANES
            values[0:rows, first : first + LANES] = high
            values[rows : 2 * rows, first : first + LANES] = low

    tile = 4 * HALF
    ramps = ramp((LANES, tile), 1)
    usual = usual_tiles(total, tiles)
    astray = jnp.zeros((1, LANES), jnp.float32)
    for j in range(pws):
        if is_first:
            columns = [came_ref[j, tiles * part_rows // 4, t : t + 1] for t in range(tiles)]
            cells = [cell_of(column.astype(jnp.int32)) for column in columns]
            ordered = sorted_rows([cell.astype(jnp.float32) for cell in cells])
        for t in range(tiles):
            first = (t * pws + j) * LANES
            if is_first:
                cell = cells[t]
                cell_ref[:, first : first + LANES] = ordered[t].astype(jnp.int32)
            else:
                cell = cell_ref[:, first : first + LANES]
                group = cell // (4 * tile)
                for g, (least, end) in enumerate(usual):
                    if not least <= t < end:
                        astray = jnp.where(group == g, 1.0, astray)
            lane = (cell % tile).astype(jnp.float32)
            chosen_ref[first : first + LANES, :] = one_hot_lanes(lane, ramps)
            high_ref[:, first : first + LANES] = sixteen((cell // tile).astype(jnp.float32))
    if is_first:
        step_z = lax.broadcasted_iota(jnp.int32, (NZ, NX), 0)
        step_x = lax.broadcasted_iota(jnp.int32, (NZ, NX), 1)
        for q in range(coulomb_ref.shape[0]):
            freq_y = jnp.full((NZ, NX), own_ref[1] + q, jnp.int32)
            kernel = coulomb(signed_freq(step_z, NZ), signed_freq(step_x, NX), freq_y)
            coulomb_ref[q] = kernel * (1.0 / (NX * NY * NZ))
    left = lax.broadcasted_iota(jnp.int32, (planes, LANES), 1) < HALF

    def place(t, found):
        found = found[:rows] + found[rows:]
        for h in range(2):
            for k in range(kpts):
                real, imag = (
                    found[(2 * k + c) * planes : (2 * k + c + 1) * planes, h * LANES : (h + 1) * LANES]
                    for c in range(2)
                )
                first = (k * HALF + 4 * t + 2 * h) * planes
                grid[first : first + planes, :] = jnp.where(left, real, pltpu.roll(imag, HALF, 1))
                grid[first + planes : first + 2 * planes, :] = jnp.where(
                    left, pltpu.roll(real, HALF, 1), imag
                )

    def place_all(ranges):
        for g, (least, end) in enumerate(ranges):
            held = slice(least * pws * LANES, end * pws * LANES)
            high = high_ref[:, held]
            zero = jnp.zeros_like(high)
            kept = []
            for t in range(4 * g, 4 * g + 4):
                here = high == jnp.full_like(high, t)
                kept += [
                    jnp.where(here, values[r : r + 16, held], zero) for r in range(0, 2 * rows, 16)
                ]
            found = mul(jnp.concatenate(kept, axis=0), chosen_ref[held, :], NN)
            for s in range(4):
                place(4 * g + s, found[2 * rows * s : 2 * rows * (s + 1)])

    whole_range = [(0, tiles)] * len(usual)
    if is_first:
        place_all(whole_range)
    else:
        astray = jnp.max(astray)

        place_all(usual)

        @pl.when(astray > 0.0)
        def _():
            place_all(whole_range)

    sum_of = count_ref[0]
    for k in range(1, kpts):
        sum_of = sum_of + count_ref[k]

    def spread(number):
        return jnp.full((8, NY), number, jnp.int32).astype(jnp.float32)

    weights = [
        jnp.concatenate([spread(count_ref[k]) / spread(sum_of) * scale] * (NX // 8), axis=0)
        for k in ring_order(kpts)
    ]
    lines = [grid[pl.ds(p, kpts * HALF, stride=planes), :] for p in range(planes)]
    lines = mul3_right(jnp.concatenate(lines, axis=0), wave_y_ref[...], NN)

    for p in range(planes):
        mixed = lines[p * kpts * HALF : (p + 1) * kpts * HALF]
        mixed = jnp.concatenate(
            [
                jnp.concatenate(
                    [mixed[k * HALF : (k + 1) * HALF, c * NY : (c + 1) * NY] for k in range(kpts)],
                    axis=1,
                )
                for c in range(2)
            ],
            axis=0,
        )
        wave = mul3_left(wave_x_ref[...], mixed, NN)
        square = wave[:NX] * wave[:NX] + wave[NX:] * wave[NX:]
        density = weights[0] * square[:, :NY]
        for k in range(1, kpts):
            density = density + weights[k] * square[:, k * NY : (k + 1) * NY]
        if former_ref is not None:
            density = density + former_ref[p]
        if is_last:
            whole[p] = density
        else:
            density_refs[0][p] = density

    if is_last:
        for s, density_ref in enumerate(density_refs):
            first = pl.multiple_of(lax.rem(own_ref[0] + s, kpts) * block, block)
            density_ref[...] = whole[:, pl.ds(first, block), :]
        level = jnp.mean(whole[0, :8, :], axis=(0, 1), keepdims=True)
        field = whole[...].reshape(planes * NX, NY) - level
        half = mul3_right(field, forth_ref[...], NN)
        first_row = lax.broadcasted_iota(jnp.int32, (2 * HALF, NX), 0) == 0
        for p in range(planes):
            turned = jnp.transpose(half[p * NX : (p + 1) * NX])
            turned = turned + jnp.where(first_row, level * NY, 0.0)
            send_ref[pl.ds(p, 2 * HALF, stride=planes), :] = turned


def wave_band(kpts, tiles, total, scale, own, counts, came, wave_y, wave_x, forth, former, cell):
    planes = NZ // came.shape[0]
    block = NX // kpts
    is_first, is_last = former is None, forth is not None
    vmem = pl.BlockSpec(memory_space=pltpu.VMEM)
    operands = [own, counts, came, wave_y, wave_x]
    if is_last:
        operands.append(forth)
    if not is_first:
        operands += [former, cell]
    if is_last:
        out_shape = [jax.ShapeDtypeStruct((planes, block, NY), jnp.float32)] * kpts
    else:
        out_shape = [jax.ShapeDtypeStruct((planes, NX, NY), jnp.float32)]
    if is_first:
        out_shape.append(jax.ShapeDtypeStruct((HALF // came.shape[0], NZ, NX), jnp.float32))
        out_shape.append(jax.ShapeDtypeStruct((1, total), jnp.int32))
    if is_last:
        out_shape.append(jax.ShapeDtypeStruct((2 * HALF * planes, NX), jnp.float32))
    rows = kpts * 2 * planes
    return pl.pallas_call(
        functools.partial(wave_kernel, kpts, tiles, scale, is_first, is_last),
        in_specs=[pl.BlockSpec(memory_space=pltpu.SMEM)] * 2 + [vmem] * (len(operands) - 2),
        out_specs=[vmem] * len(out_shape),
        out_shape=out_shape,
        scratch_shapes=[
            pltpu.VMEM((2 * rows, total), jnp.bfloat16),
            pltpu.VMEM((kpts * planes * HALF, LANES), jnp.float32),
            pltpu.VMEM((planes, NX, NY), jnp.float32),
            pltpu.VMEM((total, 4 * HALF), jnp.bfloat16),
            pltpu.VMEM((16, total), jnp.bfloat16),
        ],
        compiler_params=pltpu.CompilerParams(vmem_limit_bytes=VMEM_LIMIT),
        cost_estimate=pl.CostEstimate(
            flops=4 * rows * total * HALF * HALF, bytes_accessed=4 * came.size, transcendentals=0
        ),
        name="wave_band",
    )(*operands)


def poisson_kernel(pws, own_ref, kernel_ref, came_ref, forth_ref, back_ref, both_x_ref, send_ref):
    count, parts, planes, unused = came_ref.shape
    pairs = parts // 2
    fields = [came_ref[:, i].reshape(NZ, NX) for i in range(parts)]
    level = jnp.mean(fields[0], axis=(0, 1), keepdims=True)
    fields[0] = fields[0] - jnp.where(own_ref[1] == 0, level, 0.0)
    field = jnp.concatenate(fields, axis=1)
    turned = mul3_left(forth_ref[...], field, NN)

    def part(array, half, i):
        return array[half * NZ : (half + 1) * NZ, i * NX : (i + 1) * NX]

    lines = []
    for q in range(pairs):
        lines.append(part(turned, 0, 2 * q) + part(turned, 1, 2 * q + 1))
        lines.append(part(turned, 0, 2 * q + 1) - part(turned, 1, 2 * q))
    spectrum = mul3_right(jnp.concatenate(lines, axis=0), both_x_ref[...], NN)

    lines = []
    for q in range(pairs):
        real = spectrum[2 * q * NZ : (2 * q + 1) * NZ]
        imag = spectrum[(2 * q + 1) * NZ : (2 * q + 2) * NZ]
        kernel = kernel_ref[q]
        lines.append((real[:, :NX] + imag[:, NX:]) * kernel)
        lines.append((imag[:, :NX] - real[:, NX:]) * kernel)
    turned = mul3_right(jnp.concatenate(lines, axis=0), both_x_ref[...], NN)
    lines = []
    for q in range(pairs):
        real = turned[2 * q * NZ : (2 * q + 1) * NZ]
        imag = turned[(2 * q + 1) * NZ : (2 * q + 2) * NZ]
        lines.append(real[:, :NX] - imag[:, NX:])
        lines.append(real[:, NX:] + imag[:, :NX])
    turned = mul3_left(back_ref[...], jnp.concatenate(lines, axis=1), NN)

    kpts = count // pws
    merged = NZ // pws // 8
    block = NX // kpts
    rows = pws * 8
    lane = lax.broadcasted_iota(jnp.int32, (rows, LANES), 1) // block
    for q in range(pairs):
        real = part(turned, 0, 2 * q) - part(turned, 1, 2 * q + 1)
        imag = part(turned, 0, 2 * q + 1) + part(turned, 1, 2 * q)
        for c, value in enumerate((real, imag)):
            for place, a in enumerate(ring_order(kpts)):
                packed = None
                for m in range(merged):
                    piece = value[m * rows : (m + 1) * rows]
                    shift = (m - a) * block % LANES
                    if shift:
                        piece = pltpu.roll(piece, shift, 1)
                    packed = piece if m == 0 else jnp.where(lane == m, piece, packed)
                send_ref[place * pws : (place + 1) * pws, 2 * q + c] = packed.reshape(pws, 8, LANES)


def poisson(pws, own, kernel, came, forth, back, both_x):
    vmem = pl.BlockSpec(memory_space=pltpu.VMEM)
    count, parts, unused, unused = came.shape
    return pl.pallas_call(
        functools.partial(poisson_kernel, pws),
        in_specs=[pl.BlockSpec(memory_space=pltpu.SMEM)] + [vmem] * 5,
        out_specs=vmem,
        out_shape=jax.ShapeDtypeStruct((count, parts, 8, LANES), jnp.float32),
        compiler_params=pltpu.CompilerParams(vmem_limit_bytes=VMEM_LIMIT),
        name="poisson",
    )(own, kernel, came, forth, back, both_x)


def finish_kernel(own_ref, came_ref, back_ref, *refs):
    block_refs, density_ref, out_ref = refs[:-2], refs[-2], refs[-1]
    kpts = len(block_refs)
    planes, block, unused = out_ref.shape
    merged = planes // 8
    for s, block_ref in enumerate(block_refs):
        sender = lax.rem(own_ref[0] + kpts - s, kpts)
        density_ref[pl.ds(sender * (planes // kpts), planes // kpts)] = block_ref[...]
    for h in range(8):
        lines = came_ref[pl.ds(h, 2 * HALF, stride=8), :]
        field = mul3_right(lines, back_ref[...], TN)
        out_ref[h * merged : (h + 1) * merged] = field.reshape(merged, block, NY)


def finish(planes, block, own, came, back_y, blocks):
    vmem = pl.BlockSpec(memory_space=pltpu.VMEM)
    return pl.pallas_call(
        finish_kernel,
        in_specs=[pl.BlockSpec(memory_space=pltpu.SMEM)] + [vmem] * (2 + len(blocks)),
        out_specs=[vmem] * 2,
        out_shape=[jax.ShapeDtypeStruct((planes, block, NY), jnp.float32)] * 2,
        compiler_params=pltpu.CompilerParams(vmem_limit_bytes=VMEM_LIMIT),
        name="finish",
    )(own, came, back_y, *blocks)


def exchange(array):
    kpts, pws = lax.axis_size("kpt"), lax.axis_size("pw")
    kpt_order, pw_order = group_order(kpts, pws)
    group = [k * pws + j for k in kpt_order for j in pw_order]
    return lax.all_to_all(
        array, ("kpt", "pw"), split_axis=0, concat_axis=0, tiled=True, axis_index_groups=[group]
    )


def place_in(order, axis):
    places = jnp.asarray(np.argsort(np.array(order)), jnp.int32)
    return lax.dynamic_index_in_dim(places, lax.axis_index(axis), 0, keepdims=False)


def local_planes(band_coeffs, miller_third, column_slot, column_map, kpoint_counts):
    pws = lax.axis_size("pw")
    kpts = lax.axis_size("kpt")
    count = pws * kpts
    slots = column_map.shape[0]
    band_count = band_coeffs.shape[1]
    z_width = column_slot.shape[1] // slots
    planes = NZ // count
    parts = 2 * HALF // count
    made = tables(kpts, pws, planes)
    pencil = stack_table(made["pencil"](z_width), 1)
    wave_x, forth_z, back_z = (
        stack_table(made[name], 1) for name in ("wave_x", "forth_z", "back_z")
    )
    wave_y, forth_y, back_y, both_x = (
        stack_table(made[name], 0) for name in ("wave_y", "forth_y", "back_y", "both_x")
    )

    tiles = slots // LANES
    length = column_slot.shape[1] // LANES
    coeffs = band_coeffs.reshape(band_count, 2, length, LANES).transpose(0, 2, 1, 3)
    coeffs = coeffs.reshape(band_count, 2 * length, LANES)
    miller = miller_third.reshape(length, LANES)
    slot = column_slot.reshape(length, LANES)
    scale = 2.0 / (column_slot.shape[1] * pws)
    arrived = []
    for band in range(band_count):
        packed = pack_band(
            band, count, coeffs, miller, slot, pencil, slots, column_map
        )
        arrived.append(exchange(packed))
    kpt_order, pw_order = group_order(kpts, pws)
    device = place_in(kpt_order, "kpt") * pws + place_in(pw_order, "pw")
    own = jnp.stack((lax.axis_index("kpt"), device * (parts // 2))).astype(jnp.int32)
    former = cell = None
    for band in range(band_count):
        forth = forth_y if band == band_count - 1 else None
        made_here = wave_band(
            kpts,
            tiles,
            pws * slots,
            scale,
            own,
            kpoint_counts,
            arrived[band],
            wave_y,
            wave_x,
            forth,
            former,
            cell,
        )
        former = made_here[0]
        if band == 0:
            kernel, cell = made_here[kpts if forth is not None else 1 :][:2]
    half = exchange(made_here[-1].reshape(count, parts, planes, NX))
    blocks = [made_here[0]] + [
        lax.ppermute(made_here[s], "kpt", [(a, (a + s) % kpts) for a in range(kpts)])
        for s in range(1, kpts)
    ]
    back = poisson(pws, own, kernel, half, forth_z, back_z, both_x)
    back = exchange(back).reshape(count * parts * 8, LANES)
    return tuple(finish(NZ // pws, NX // kpts, own, back, back_y, blocks))


def fits_planes(kpts, pws):
    count = kpts * pws
    own = NZ // pws
    return (
        NZ % count == 0
        and NZ // count == 8
        and 2 * HALF % (2 * count) == 0
        and NX % kpts == 0
        and own % 8 == 0
        and own // 8 * (NX // kpts) == LANES
    )


def local(band_coeffs, miller_third, column_slot, column_map, kpoint_counts):
    slots = column_map.shape[0]
    plain = slots % LANES == 0 and LANES <= slots <= 8 * RANK_LOW
    plain = plain and column_slot.shape[1] == slots * LANES
    fits = plain and fits_planes(lax.axis_size("kpt"), lax.axis_size("pw"))
    chosen = local_planes if fits else local_general
    return chosen(band_coeffs, miller_third, column_slot, column_map, kpoint_counts)


def solution(mesh):
    return jax.shard_map(
        local,
        mesh=mesh,
        in_specs=(P("kpt", None, None, "pw"), P("kpt", "pw"), P("kpt", "pw"), P("pw"), P()),
        out_specs=(P("pw", "kpt", None), P("pw", "kpt", None)),
        check_vma=False,
    )
```

```python
import functools
import math

import jax
import jax.numpy as jnp
import numpy as np
from jax import lax
from jax.experimental import pallas as pl
from jax.experimental.pallas import tpu as pltpu
from jax.sharding import PartitionSpec as P

NX = 128
NY = 128
NZ = 256


SPACING = 0.25


def contract(pattern, former, latter):
    return jnp.einsum(
        pattern, former, latter, precision=lax.Precision.HIGHEST, preferred_element_type=jnp.float32
    )


def phase_tables(first_index, second_index, length):
    product = first_index[:, None] * second_index[None, :] % length
    angle = product.astype(jnp.float32) * (2.0 * math.pi / length)
    return (jnp.cos(angle), jnp.sin(angle))


def signed_freq(values, length):
    return jnp.where(values >= length // 2, values - length, values)


def coulomb(freq_z, freq_x, freq_y):
    wave_z = freq_z.astype(jnp.float32) / (NZ * SPACING)
    wave_x = freq_x.astype(jnp.float32) / (NX * SPACING)
    wave_y = freq_y.astype(jnp.float32) / (NY * SPACING)
    squared = (2.0 * math.pi) ** 2 * (wave_z * wave_z + wave_x * wave_x + wave_y * wave_y)
    anchor = (freq_z == 0) & (freq_x == 0) & (freq_y == 0)
    return jnp.where(anchor, 0.0, 4.0 * math.pi / jnp.where(anchor, 1.0, squared))


def poisson_columns(real_part, imag_part, freq_x, freq_y):
    length = real_part.shape[0]
    steps_z = jnp.arange(length, dtype=jnp.int32)
    cos_z, sin_z = phase_tables(steps_z, steps_z, length)
    spec_real = contract("zk,km->zm", cos_z, real_part) + contract("zk,km->zm", sin_z, imag_part)
    spec_imag = contract("zk,km->zm", cos_z, imag_part) - contract("zk,km->zm", sin_z, real_part)
    kernel = coulomb(signed_freq(steps_z, length)[:, None], freq_x[None, :], freq_y[None, :]) / (
        NX * NY * NZ
    )
    spec_real = spec_real * kernel
    spec_imag = spec_imag * kernel
    back_real = contract("zk,km->zm", cos_z, spec_real) - contract("zk,km->zm", sin_z, spec_imag)
    back_imag = contract("zk,km->zm", sin_z, spec_real) + contract("zk,km->zm", cos_z, spec_imag)
    return (back_real, back_imag)


def forward_planes(field):
    steps_x = jnp.arange(NX, dtype=jnp.int32)
    steps_y = jnp.arange(NY, dtype=jnp.int32)
    cos_y, sin_y = phase_tables(steps_y, steps_y, NY)
    cos_x, sin_x = phase_tables(steps_x, steps_x, NX)
    half_real = contract("pxy,ky->pxk", field, cos_y)
    half_imag = -contract("pxy,ky->pxk", field, sin_y)
    spec_real = contract("kx,pxy->pky", cos_x, half_real) + contract(
        "kx,pxy->pky", sin_x, half_imag
    )
    spec_imag = contract("kx,pxy->pky", cos_x, half_imag) - contract(
        "kx,pxy->pky", sin_x, half_real
    )
    return (spec_real, spec_imag)


def local_general(band_coeffs, miller_third, column_slot, column_map, kpoint_counts):
    pw_count = lax.axis_size("pw")
    kpt_count = lax.axis_size("kpt")
    pw_index = lax.axis_index("pw")
    kpt_index = lax.axis_index("kpt")
    col_dev = column_map.shape[0]
    ng_dev = column_slot.shape[1]
    band_count = band_coeffs.shape[1]
    z_width = ng_dev // col_dev
    planes = NZ // pw_count
    x_block = NX // kpt_count
    col_total = pw_count * col_dev
    steps_y = jnp.arange(NY, dtype=jnp.int32)
    steps_x = jnp.arange(NX, dtype=jnp.int32)
    cos_y, sin_y = phase_tables(steps_y, steps_y, NY)
    cos_x, sin_x = phase_tables(steps_x, steps_x, NX)
    all_columns = lax.all_gather(column_map, "pw", axis=0, tiled=True)
    position = (miller_third[0] + z_width // 2) * col_dev + column_slot[0]
    source_of = (
        jnp.zeros((ng_dev,), jnp.int32).at[position].set(jnp.arange(ng_dev, dtype=jnp.int32))
    )
    coeff_rows = band_coeffs[0].reshape(band_count * 2, ng_dev).T
    packed = jnp.take(coeff_rows, source_of, axis=0)
    packed = (
        packed.reshape(z_width, col_dev, band_count, 2)
        .transpose(0, 2, 3, 1)
        .reshape(z_width, band_count * 2 * col_dev)
    )
    cos_z, sin_z = phase_tables(
        jnp.arange(NZ, dtype=jnp.int32), jnp.arange(z_width, dtype=jnp.int32) - z_width // 2, NZ
    )
    by_cos = contract("zj,jc->zc", cos_z, packed).reshape(NZ, band_count, 2, col_dev)
    by_sin = contract("zj,jc->zc", sin_z, packed).reshape(NZ, band_count, 2, col_dev)
    pencil = jnp.stack(
        (by_cos[:, :, 0] - by_sin[:, :, 1], by_sin[:, :, 0] + by_cos[:, :, 1]), axis=2
    )
    pencil = pencil.reshape(NZ, band_count * 2 * col_dev)
    arrived = lax.all_to_all(pencil, "pw", split_axis=0, concat_axis=1, tiled=True)
    arrived = arrived.reshape(planes, pw_count, band_count, 2, col_dev).transpose(2, 1, 4, 3, 0)
    arrived = arrived.reshape(band_count, col_total, 2 * planes)
    arrived = jnp.concatenate(
        (arrived, jnp.zeros((band_count, 1, 2 * planes), jnp.float32)), axis=1
    )
    cell_source = (
        jnp.full((NX * NY,), col_total, jnp.int32)
        .at[all_columns]
        .set(jnp.arange(col_total, dtype=jnp.int32))
    )

    def add_band(band, running):
        one_band = lax.dynamic_index_in_dim(arrived, band, 0, keepdims=False)
        placed = jnp.take(one_band, cell_source, axis=0)
        placed = placed.reshape(NX, NY, 2, planes).transpose(2, 3, 0, 1)
        grid_real = placed[0]
        grid_imag = placed[1]
        mixed_real = contract("pxm,ym->pxy", grid_real, cos_y) - contract(
            "pxm,ym->pxy", grid_imag, sin_y
        )
        mixed_imag = contract("pxm,ym->pxy", grid_real, sin_y) + contract(
            "pxm,ym->pxy", grid_imag, cos_y
        )
        wave_real = contract("xm,pmy->pxy", cos_x, mixed_real) - contract(
            "xm,pmy->pxy", sin_x, mixed_imag
        )
        wave_imag = contract("xm,pmy->pxy", sin_x, mixed_real) + contract(
            "xm,pmy->pxy", cos_x, mixed_imag
        )
        return running + wave_real * wave_real + wave_imag * wave_imag

    squares_sum = lax.fori_loop(0, band_count, add_band, jnp.zeros((planes, NX, NY), jnp.float32))
    weight = (
        2.0
        * kpoint_counts[kpt_index].astype(jnp.float32)
        / jnp.sum(kpoint_counts).astype(jnp.float32)
    )
    weight = weight / (ng_dev * pw_count)
    partial_value = weight * squares_sum
    total_density = lax.psum(partial_value, "kpt")
    density = lax.dynamic_slice_in_dim(total_density, kpt_index * x_block, x_block, 1)
    spec_real, spec_imag = forward_planes(total_density)
    rows_pw = NX // pw_count
    pencil_real, pencil_imag = (
        lax.all_to_all(spec_real, "pw", split_axis=1, concat_axis=0, tiled=True),
        lax.all_to_all(spec_imag, "pw", split_axis=1, concat_axis=0, tiled=True),
    )
    local_x = pw_index * rows_pw + jnp.arange(rows_pw, dtype=jnp.int32)
    freq_x = jnp.repeat(signed_freq(local_x, NX), NY)
    freq_y = jnp.tile(signed_freq(steps_y, NY), rows_pw)
    back_real, back_imag = poisson_columns(
        pencil_real.reshape(NZ, rows_pw * NY), pencil_imag.reshape(NZ, rows_pw * NY), freq_x, freq_y
    )
    plane_real, plane_imag = (
        lax.all_to_all(
            back_real.reshape(NZ, rows_pw, NY), "pw", split_axis=0, concat_axis=1, tiled=True
        ),
        lax.all_to_all(
            back_imag.reshape(NZ, rows_pw, NY), "pw", split_axis=0, concat_axis=1, tiled=True
        ),
    )
    own_rows = kpt_index * x_block + jnp.arange(x_block, dtype=jnp.int32)
    cos_rows, sin_rows = phase_tables(own_rows, steps_x, NX)
    rows_real = contract("xk,pky->pxy", cos_rows, plane_real) - contract(
        "xk,pky->pxy", sin_rows, plane_imag
    )
    rows_imag = contract("xk,pky->pxy", sin_rows, plane_real) + contract(
        "xk,pky->pxy", cos_rows, plane_imag
    )
    hartree = contract("pxk,yk->pxy", rows_real, cos_y) - contract("pxk,yk->pxy", rows_imag, sin_y)
    return (density, hartree)


LANES = 128
HALF = 64
VMEM_LIMIT = 16 * 1024 * 1024
PACK_LIMIT = 56 * 1024 * 1024
NN = (((1,), (0,)), ((), ()))
NT = (((1,), (1,)), ((), ()))
TN = (((0,), (0,)), ((), ()))


def pieces(value):
    high = value.astype(jnp.bfloat16)
    low = (value - high.astype(jnp.float32)).astype(jnp.bfloat16)
    return high, low


def mul(former, latter, dims):
    return lax.dot_general(former, latter, dims, preferred_element_type=jnp.float32)


def mul3_left(former, latter, dims):
    high, low = pieces(latter)
    (unused,), (axis,) = dims[0]
    return mul(former, jnp.concatenate((high, high, low), axis=axis), dims)


def mul3_right(former, latter, dims):
    high, low = pieces(former)
    (axis,), (unused,) = dims[0]
    return mul(jnp.concatenate((high, high, low), axis=axis), latter, dims)


def stack_table(values, axis):
    high = values.astype(np.float32).astype(jnp.bfloat16)
    low = (values - high.astype(np.float64)).astype(np.float32).astype(jnp.bfloat16)
    return jnp.asarray(np.concatenate((high, low, high), axis=axis))


def angles(former, latter, length):
    return np.outer(former, latter) % length * (2.0 * np.pi / length)


def ring_order(length):
    return [0, *range(1, length, 2), *range(length - 2 + length % 2, 0, -2)] if length > 1 else [0]


def group_order(kpts, pws):
    cores = 2 if pws % 2 == 0 else 1
    return ring_order(kpts), [c * cores + i for c in ring_order(pws // cores) for i in range(cores)]


def tables(kpts, pws, planes):
    count = kpts * pws
    kpt_order, pw_order = (np.array(order) for order in group_order(kpts, pws))
    low_freq = np.arange(HALF) - HALF // 2
    grid_x, grid_y, grid_z = np.arange(NX), np.arange(NY), np.arange(NZ)
    own_y = np.arange(HALF)

    device = np.arange(count)
    plane_of = (
        pw_order[device % pws][:, None] * (NZ // pws)
        + kpt_order[device // pws][:, None] * planes
        + np.arange(planes)[None, :]
    )
    return_table = {}

    def pencil(z_width):
        angle = angles(plane_of.ravel(), np.arange(z_width) - z_width // 2, NZ)
        cos, sin = (
            part.reshape(count, 1, planes, z_width) for part in (np.cos(angle), np.sin(angle))
        )
        real = np.concatenate((cos, -sin), axis=3)
        imag = np.concatenate((sin, cos), axis=3)
        return np.concatenate((real, imag), axis=1).reshape(-1, 2 * z_width)

    return_table["pencil"] = pencil

    angle = angles(low_freq, grid_y, NY)
    cos, sin = np.cos(angle), np.sin(angle)
    return_table["wave_y"] = np.block([[cos, sin], [-sin, cos]])

    angle = angles(grid_x, low_freq, NX)
    cos, sin = np.cos(angle), np.sin(angle)
    return_table["wave_x"] = np.block([[cos, -sin], [sin, cos]])

    angle = angles(own_y, grid_y, NY)
    cos, sin = np.cos(angle), np.sin(angle)
    return_table["forth_y"] = np.stack((cos, -sin), axis=1).reshape(2 * HALF, NY).T
    twice = np.where(own_y == 0, 1.0, 2.0)[:, None]
    return_table["back_y"] = np.stack((twice * cos, -twice * sin), axis=1).reshape(2 * HALF, NY)

    angle = angles(grid_z, plane_of.ravel(), NZ)
    return_table["forth_z"] = np.concatenate((np.cos(angle), np.sin(angle)), axis=0)
    own = NZ // pws
    merged = own // 8
    order = (
        pw_order[None, :, None] * own
        + np.arange(8)[None, None, :] * merged
        + np.arange(merged)[:, None, None]
    )
    angle = angles(order.ravel(), grid_z, NZ)
    return_table["back_z"] = np.concatenate((np.cos(angle), np.sin(angle)), axis=0)

    angle = angles(grid_x, grid_x, NX)
    return_table["both_x"] = np.concatenate((np.cos(angle), np.sin(angle)), axis=1)
    return return_table


def ramp(shape, axis, first=0):
    steps = lax.broadcasted_iota(jnp.int32, shape, axis) + first
    return steps.astype(jnp.float32).astype(jnp.bfloat16)


def sixteen(row):
    return jnp.broadcast_to(row, (16, row.shape[1])).astype(jnp.bfloat16)


def one_hot_lanes(row, ramps):
    column = jnp.transpose(jnp.concatenate([sixteen(row)] * (LANES // 16), axis=0))
    one = jnp.ones(column.shape, jnp.bfloat16)
    zero = jnp.zeros(column.shape, jnp.bfloat16)
    return jnp.concatenate(
        [
            jnp.where(column == ramps[:, first : first + LANES], one, zero)
            for first in range(0, ramps.shape[1], LANES)
        ],
        axis=1,
    )


def turn(row):
    return jnp.transpose(jnp.broadcast_to(row, (LANES, LANES)))


def cell_of(column):
    cell = ((column // NY + NX // 2) % NX - HALF // 2) * HALF
    return cell + (column % NY + NY // 2) % NY - HALF // 2


def rank_rows(rows, turned):
    return [
        sum(jnp.sum(jnp.where(t < row, 1.0, 0.0), axis=0, keepdims=True) for t in turned)
        for row in rows
    ]


def sorted_rows(rows):
    turned = [turn(row) for row in rows]
    ranks = [turn(rank) for rank in rank_rows(rows, turned)]
    lane = lax.broadcasted_iota(jnp.int32, (LANES, LANES), 1).astype(jnp.float32)
    return [
        sum(
            jnp.sum(jnp.where(rank == lane + t * LANES, value, 0.0), axis=0, keepdims=True)
            for rank, value in zip(ranks, turned)
        )
        for t in range(len(rows))
    ]


def usual_tiles(total, tiles):
    signed = np.arange(NX) - NX // 2
    radius = (signed[:, None] * NY) ** 2 + ((np.arange(NY) - NY // 2)[None, :] * NX) ** 2
    kept = np.sort(np.argsort(radius.ravel(), kind="stable")[:total] // NY - NX // 2 + HALF // 2)
    slots = tiles * LANES
    ranges = []
    for t in range(tiles):
        ends = []
        for edge, sign in ((t / tiles, -1), ((t + 1) / tiles, 1)):
            edge += sign * 5 * math.sqrt(edge * (1 - edge) / slots)
            ends.append(int(kept[min(max(int(edge * total), 0), total - 1)]) // 16)
        ranges.append(ends)
    held = [[t for t in range(tiles) if ranges[t][0] <= g <= ranges[t][1]] for g in range(HALF // 16)]
    return [(ts[0], ts[-1] + 1) if ts else (0, tiles) for ts in held]


RANK_LOW = 64
WINDOW = 64
END_WINDOW = 48


def exchange_rows(refs, low_bits, size_bits, descending):
    for outer in range(RANK_LOW):
        if any(outer >> bit & 1 for bit in low_bits[0]):
            continue
        touched = sorted(
            outer + sum(1 << bit for i, bit in enumerate(low_bits[0]) if pattern >> i & 1)
            for pattern in range(1 << len(low_bits[0]))
        )
        held = {v: [ref[v * 8 : v * 8 + 8, :] for ref in refs] for v in touched}
        for size, bits in zip(size_bits, low_bits[1:]):
            for bit in bits:
                for v in touched:
                    if v >> bit & 1:
                        continue
                    former, latter = held[v], held[v | 1 << bit]
                    if size < 6:
                        down = bool(v >> size & 1)
                        swap = former[0] < latter[0] if down else former[0] > latter[0]
                    else:
                        swap = former[0] > latter[0]
                        if descending is not None:
                            swap = jnp.logical_xor(swap, descending)
                    held[v] = [jnp.where(swap, y, x) for x, y in zip(former, latter)]
                    held[v | 1 << bit] = [jnp.where(swap, x, y) for x, y in zip(former, latter)]
        for v in touched:
            for ref, value in zip(refs, held[v]):
                ref[v * 8 : v * 8 + 8, :] = value


def exchange_sublanes(refs, stride, descending):
    sublane = lax.broadcasted_iota(jnp.int32, (8, LANES), 0)
    upper = sublane // stride % 2 == 1
    want_most = upper if descending is None else jnp.logical_xor(upper, descending)
    other = jnp.where(upper, sublane - stride, sublane + stride)

    for v in range(RANK_LOW):
        here = [ref[v * 8 : v * 8 + 8, :] for ref in refs]
        there = [jnp.take_along_axis(value, other, axis=0) for value in here]
        take = jnp.logical_xor(here[0] > there[0], want_most)
        for ref, x, y in zip(refs, here, there):
            ref[v * 8 : v * 8 + 8, :] = jnp.where(take, y, x)


def sort_columns(refs):
    sublane = lax.broadcasted_iota(jnp.int32, (8, LANES), 0)
    exchange_rows(refs, [(0, 1, 2), (0,), (1, 0), (2, 1, 0)], [1, 2, 3], None)
    exchange_rows(refs, [(3,), (3,)], [4], None)
    exchange_rows(refs, [(0, 1, 2), (2, 1, 0)], [4], None)
    exchange_rows(refs, [(3, 4), (4, 3)], [5], None)
    exchange_rows(refs, [(0, 1, 2), (2, 1, 0)], [5], None)
    for size in range(6, 10):
        descending = None if size == 9 else sublane // (1 << (size - 6)) % 2 == 1
        for bit in range(size - 1, 5, -1):
            exchange_sublanes(refs, 1 << (bit - 6), descending)
        exchange_rows(refs, [(3, 4, 5), (5, 4, 3)], [size], descending)
        if size < 9:
            exchange_rows(refs, [(0, 1, 2), (2, 1, 0)], [size], descending)


def pack_kernel(width, has_column, *refs):
    coeff_ref, miller_ref, slot_ref, pencil_ref, column_ref = refs[:5]
    rest = list(refs[5:])
    out_ref, total, key_ref, real_ref, imag_ref, lane_ref, real_low, imag_low, ramp_ref, step_ref, pairs, held, sem = rest
    fetch = pltpu.make_async_copy(pencil_ref, held, sem)
    fetch.start()
    half = total.shape[0] // 4
    slots = 2 * half
    count = out_ref.shape[0]
    rows = pencil_ref.shape[0] // count
    length = miller_ref.shape[0]
    ranks = key_ref.shape[0]

    slot = slot_ref[...]
    columns = [
        column_ref[t * LANES : (t + 1) * LANES].reshape(1, LANES) for t in range(slots // LANES)
    ]
    if not has_column:
        cells = [cell_of(column).astype(jnp.float32) for column in columns]
        near = slot % LANES
        rank = jnp.zeros(slot.shape, jnp.float32)
        for t, row in enumerate(rank_rows(cells, [turn(row) for row in cells])):
            found = jnp.take_along_axis(jnp.broadcast_to(row, slot.shape), near, axis=1)
            rank = jnp.where(slot // LANES == t, found, rank)
        slot = rank.astype(jnp.int32)
    second = slot >= half
    lane = miller_ref[...] + width // 2
    key = jnp.where(second, slot - half, slot) * (2 * width) + jnp.where(second, lane + width, lane)
    key_ref[0:length] = key.astype(jnp.float32)
    pairs[0 : 2 * length, :] = coeff_ref[0]
    real_ref[0:length] = pairs[pl.ds(0, length, stride=2), :]
    imag_ref[0:length] = pairs[pl.ds(1, length, stride=2), :]
    blank = jnp.zeros((ranks - length, LANES), jnp.float32)
    key_ref[length:] = blank + 2.0 * slots * width
    real_ref[length:] = blank
    imag_ref[length:] = blank
    sort_columns((key_ref, real_ref, imag_ref))

    blocks = length // 8
    ends = blocks // 6

    def base_of(block, window):
        base = 8 * (block // 2) + 8 * (block % 2) - window // 2
        return jnp.minimum(jnp.maximum(base, 0), half - window)

    ramp_ref[...] = ramp(ramp_ref.shape, 1)
    step_ref[...] = ramp(step_ref.shape, 0)
    sublane = lax.broadcasted_iota(jnp.int32, (8, LANES), 0)
    astray = jnp.zeros((8, LANES), jnp.float32)
    for v in range(RANK_LOW):
        at = slice(v * 8, v * 8 + 8)
        keys = key_ref[at, :]
        high = jnp.floor(keys * (1.0 / (2 * width)))
        lane_ref[at, :] = keys - high * (2.0 * width)
        key_ref[at, :] = high
        for ref, low_ref in ((real_ref, real_low), (imag_ref, imag_low)):
            value = ref[at, :]
            rounded = value.astype(jnp.bfloat16).astype(jnp.float32)
            ref[at, :] = rounded
            low_ref[at, :] = value - rounded
        block = sublane * (RANK_LOW // 8) + v // 8
        at_end = jnp.logical_or(block < ends, block >= blocks - ends)
        base = jnp.where(at_end, base_of(block, END_WINDOW), base_of(block, WINDOW))
        offset = high - base.astype(jnp.float32)
        outside = jnp.logical_or(offset < 0.0, offset >= jnp.where(at_end, 1.0 * END_WINDOW, 1.0 * WINDOW))
        astray = jnp.where(outside, 1.0, astray)
    astray = jnp.max(jnp.where(sublane * RANK_LOW < length, astray, 0.0))

    def add(block, base, window):
        first = block % (RANK_LOW // 8) * 64 + block // (RANK_LOW // 8)
        base_row = jnp.full((1, LANES), base, jnp.int32).astype(jnp.float32)
        zero = jnp.zeros((16, LANES), jnp.bfloat16)
        spread, chosen = [], []
        for t in range(8):
            row = pl.ds(first + 8 * t, 1)
            high = sixteen(key_ref[row, :] - base_row)
            masks = [high == step_ref[r : r + 16, :] for r in range(0, window, 16)]
            spread.append(
                jnp.concatenate(
                    [
                        jnp.where(mask, value, zero)
                        for value in [
                            sixteen(ref[row, :]) for ref in (real_ref, imag_ref, real_low, imag_low)
                        ]
                        for mask in masks
                    ],
                    axis=0,
                )
            )
            chosen.append(one_hot_lanes(lane_ref[row, :], ramp_ref[...]))
        found = mul(jnp.concatenate(spread, axis=1), jnp.concatenate(chosen, axis=0), NN)
        for i in range(4):
            if window == half:
                into = pl.ds(i * half, half)
            else:
                into = pl.ds(pl.multiple_of(i * half + base, 8), window)
            total[into, :] += found[i * window : (i + 1) * window]

    total[...] = jnp.zeros_like(total)
    together = 4 if ends % 4 == 0 and blocks % 4 == 0 else 1

    def add_blocks(first, end, window):
        def some_blocks(i, unused):
            for s in range(together):
                block = first + together * i + s
                add(block, base_of(block, window), window)
            return unused

        lax.fori_loop(0, (end - first) // together, some_blocks, 0)

    add_blocks(0, ends, END_WINDOW)
    add_blocks(ends, blocks - ends, WINDOW)
    add_blocks(blocks - ends, blocks, END_WINDOW)

    @pl.when(astray > 0.0)
    def _():
        total[...] = jnp.zeros_like(total)

        def one_block(block, unused):
            add(block, 0, half)
            return unused

        lax.fori_loop(0, blocks, one_block, 0)

    both = []
    for at in range(2):
        parts = [
            total[(2 * at + c) * half : (2 * at + c + 1) * half].astype(jnp.bfloat16)
            for c in range(2)
        ]
        both.append(
            jnp.concatenate(
                [
                    jnp.concatenate([part[:, h * width : (h + 1) * width] for part in parts], axis=1)
                    for h in range(2)
                ],
                axis=0,
            )
        )
    fetch.wait()
    pencils = mul(held[...], jnp.concatenate((both[0], both[0], both[1]), axis=1), NT)
    tiles = slots // LANES
    for t in range(tiles):
        tile = pencils[:, t * LANES : (t + 1) * LANES].reshape(count, rows, LANES)
        if not has_column:
            out_ref[:, t * rows : (t + 1) * rows] = tile
            continue
        for g in range(rows // 4):
            out_ref[:, t * (rows // 4) + g] = tile[:, 4 * g : 4 * g + 4]
    if has_column:
        column = [column.astype(jnp.float32) for column in columns]
        column = jnp.concatenate(column + [jnp.zeros((4 - tiles, LANES), jnp.float32)], axis=0)
        out_ref[:, tiles * rows // 4] = jnp.broadcast_to(column[None], (count, 4, LANES))


def pack_band(band, count, coeffs, miller, slot, pencil, slots, column):
    has_column = band == 0
    length = miller.shape[0]
    width = pencil.shape[1] // 6
    rows = pencil.shape[0] // count * (slots // LANES)
    operands = [coeffs, miller, slot, pencil, column]
    out_shape = (count, rows, LANES)
    if has_column:
        out_shape = (count, rows // 4 + 1, 4, LANES)
    one_band = pl.BlockSpec((1, 2 * length, LANES), lambda i: (band, 0, 0))
    return pl.pallas_call(
        functools.partial(pack_kernel, width, has_column),
        grid=(1,),
        in_specs=[one_band]
        + [
            pl.BlockSpec(memory_space=pl.ANY)
            if x is pencil
            else pl.BlockSpec(x.shape, lambda i, n=x.ndim: (0,) * n)
            for x in operands[1:]
        ],
        out_specs=pl.BlockSpec(out_shape, lambda i: (0,) * len(out_shape)),
        out_shape=jax.ShapeDtypeStruct(out_shape, jnp.float32),
        scratch_shapes=[pltpu.VMEM((2 * slots, 2 * width), jnp.float32)]
        + [pltpu.VMEM((8 * RANK_LOW, LANES), jnp.float32)] * 6
        + [
            pltpu.VMEM((LANES, 2 * width), jnp.bfloat16),
            pltpu.VMEM((slots // 2, LANES), jnp.bfloat16),
            pltpu.VMEM((2 * length + 8, LANES), jnp.float32),
            pltpu.VMEM(pencil.shape, jnp.bfloat16),
            pltpu.SemaphoreType.DMA,
        ],
        compiler_params=pltpu.CompilerParams(vmem_limit_bytes=PACK_LIMIT),
        cost_estimate=pl.CostEstimate(
            flops=2 * length * LANES * slots * 4 * width,
            bytes_accessed=16 * length * LANES,
            transcendentals=0,
        ),
        name="pack_band",
    )(*operands)


def wave_kernel(kpts, tiles, scale, is_first, is_last, *refs):
    own_ref, count_ref, came_ref, wave_y_ref, wave_x_ref = refs[:5]
    rest = list(refs[5:])
    forth_ref = rest.pop(0) if is_last else None
    former_ref, cell_ref = (None, None) if is_first else (rest.pop(0), rest.pop(0))
    density_refs = [rest.pop(0) for _ in range(kpts if is_last else 1)]
    if is_first:
        coulomb_ref, cell_ref = rest.pop(0), rest.pop(0)
    send_ref = rest.pop(0) if is_last else None
    values, grid, whole, chosen_ref, high_ref, sent = rest
    planes = density_refs[0].shape[0]
    block = NX // kpts
    part_rows = 2 * planes
    pws = came_ref.shape[0] // kpts
    rows = kpts * part_rows
    total = values.shape[1]

    for j in range(pws):
        for t in range(tiles):
            if is_first:
                groups = [
                    came_ref[k * pws + j, t * (part_rows // 4) + g]
                    for k in range(kpts)
                    for g in range(part_rows // 4)
                ]
            else:
                groups = [
                    came_ref[k * pws + j, t * part_rows : (t + 1) * part_rows] for k in range(kpts)
                ]
            taken = jnp.concatenate(groups, axis=0)
            high, low = pieces(taken)
            first = (t * pws + j) * LANES
            values[0:rows, first : first + LANES] = high
            values[rows : 2 * rows, first : first + LANES] = low

    tile = 4 * HALF
    ramps = ramp((LANES, tile), 1)
    usual = usual_tiles(total, tiles)
    astray = jnp.zeros((1, LANES), jnp.float32)
    for j in range(pws):
        if is_first:
            columns = [came_ref[j, tiles * part_rows // 4, t : t + 1] for t in range(tiles)]
            cells = [cell_of(column.astype(jnp.int32)) for column in columns]
            ordered = sorted_rows([cell.astype(jnp.float32) for cell in cells])
        for t in range(tiles):
            first = (t * pws + j) * LANES
            if is_first:
                cell = cells[t]
                cell_ref[:, first : first + LANES] = ordered[t].astype(jnp.int32)
            else:
                cell = cell_ref[:, first : first + LANES]
                group = cell // (4 * tile)
                for g, (least, end) in enumerate(usual):
                    if not least <= t < end:
                        astray = jnp.where(group == g, 1.0, astray)
            lane = (cell % tile).astype(jnp.float32)
            chosen_ref[first : first + LANES, :] = one_hot_lanes(lane, ramps)
            high_ref[:, first : first + LANES] = sixteen((cell // tile).astype(jnp.float32))
    if is_first:
        step_z = lax.broadcasted_iota(jnp.int32, (NZ, NX), 0)
        step_x = lax.broadcasted_iota(jnp.int32, (NZ, NX), 1)
        for q in range(coulomb_ref.shape[0]):
            freq_y = jnp.full((NZ, NX), own_ref[1] + q, jnp.int32)
            kernel = coulomb(signed_freq(step_z, NZ), signed_freq(step_x, NX), freq_y)
            coulomb_ref[q] = kernel * (1.0 / (NX * NY * NZ))
    left = lax.broadcasted_iota(jnp.int32, (planes, LANES), 1) < HALF

    def place(t, found):
        found = found[:rows] + found[rows:]
        for h in range(2):
            for k in range(kpts):
                real, imag = (
                    found[(2 * k + c) * planes : (2 * k + c + 1) * planes, h * LANES : (h + 1) * LANES]
                    for c in range(2)
                )
                first = (k * HALF + 4 * t + 2 * h) * planes
                grid[first : first + planes, :] = jnp.where(left, real, pltpu.roll(imag, HALF, 1))
                grid[first + planes : first + 2 * planes, :] = jnp.where(
                    left, pltpu.roll(real, HALF, 1), imag
                )

    def place_all(ranges):
        for g, (least, end) in enumerate(ranges):
            held = slice(least * pws * LANES, end * pws * LANES)
            high = high_ref[:, held]
            zero = jnp.zeros_like(high)
            kept = []
            for t in range(4 * g, 4 * g + 4):
                here = high == jnp.full_like(high, t)
                kept += [
                    jnp.where(here, values[r : r + 16, held], zero) for r in range(0, 2 * rows, 16)
                ]
            found = mul(jnp.concatenate(kept, axis=0), chosen_ref[held, :], NN)
            for s in range(4):
                place(4 * g + s, found[2 * rows * s : 2 * rows * (s + 1)])

    whole_range = [(0, tiles)] * len(usual)
    if is_first:
        place_all(whole_range)
    else:
        astray = jnp.max(astray)

        place_all(usual)

        @pl.when(astray > 0.0)
        def _():
            place_all(whole_range)

    sum_of = count_ref[0]
    for k in range(1, kpts):
        sum_of = sum_of + count_ref[k]

    def spread(number):
        return jnp.full((8, NY), number, jnp.int32).astype(jnp.float32)

    weights = [
        jnp.concatenate([spread(count_ref[k]) / spread(sum_of) * scale] * (NX // 8), axis=0)
        for k in ring_order(kpts)
    ]
    lines = [grid[pl.ds(p, kpts * HALF, stride=planes), :] for p in range(planes)]
    lines = mul3_right(jnp.concatenate(lines, axis=0), wave_y_ref[...], NN)

    for p in range(planes):
        mixed = lines[p * kpts * HALF : (p + 1) * kpts * HALF]
        mixed = jnp.concatenate(
            [
                jnp.concatenate(
                    [mixed[k * HALF : (k + 1) * HALF, c * NY : (c + 1) * NY] for k in range(kpts)],
                    axis=1,
                )
                for c in range(2)
            ],
            axis=0,
        )
        wave = mul3_left(wave_x_ref[...], mixed, NN)
        square = wave[:NX] * wave[:NX] + wave[NX:] * wave[NX:]
        density = weights[0] * square[:, :NY]
        for k in range(1, kpts):
            density = density + weights[k] * square[:, k * NY : (k + 1) * NY]
        if former_ref is not None:
            density = density + former_ref[p]
        if is_last:
            whole[p] = density
        else:
            density_refs[0][p] = density

    if is_last:
        for s, density_ref in enumerate(density_refs):
            first = pl.multiple_of(lax.rem(own_ref[0] + s, kpts) * block, block)
            density_ref[...] = whole[:, pl.ds(first, block), :]
        level = jnp.mean(whole[0, :8, :], axis=(0, 1), keepdims=True)
        field = whole[...].reshape(planes * NX, NY) - level
        half = mul3_right(field, forth_ref[...], NN)
        first_row = lax.broadcasted_iota(jnp.int32, (2 * HALF, NX), 0) == 0
        for p in range(planes):
            turned = jnp.transpose(half[p * NX : (p + 1) * NX])
            turned = turned + jnp.where(first_row, level * NY, 0.0)
            sent[pl.ds(p, 2 * HALF, stride=planes), :] = turned
        send_ref[...] = sent[0 : 2 * HALF * planes, :]


def wave_band(kpts, tiles, total, scale, own, counts, came, wave_y, wave_x, forth, former, cell):
    planes = NZ // came.shape[0]
    block = NX // kpts
    is_first, is_last = former is None, forth is not None
    vmem = pl.BlockSpec(memory_space=pltpu.VMEM)
    operands = [own, counts, came, wave_y, wave_x]
    if is_last:
        operands.append(forth)
    if not is_first:
        operands += [former, cell]
    if is_last:
        out_shape = [jax.ShapeDtypeStruct((planes, block, NY), jnp.float32)] * kpts
    else:
        out_shape = [jax.ShapeDtypeStruct((planes, NX, NY), jnp.float32)]
    if is_first:
        out_shape.append(jax.ShapeDtypeStruct((HALF // came.shape[0], NZ, NX), jnp.float32))
        out_shape.append(jax.ShapeDtypeStruct((1, total), jnp.int32))
    if is_last:
        out_shape.append(jax.ShapeDtypeStruct((2 * HALF * planes, NX), jnp.float32))
    rows = kpts * 2 * planes
    return pl.pallas_call(
        functools.partial(wave_kernel, kpts, tiles, scale, is_first, is_last),
        in_specs=[pl.BlockSpec(memory_space=pltpu.SMEM)] * 2 + [vmem] * (len(operands) - 2),
        out_specs=[vmem] * len(out_shape),
        out_shape=out_shape,
        scratch_shapes=[
            pltpu.VMEM((2 * rows, total), jnp.bfloat16),
            pltpu.VMEM((kpts * planes * HALF + planes, LANES), jnp.float32),
            pltpu.VMEM((planes, NX, NY), jnp.float32),
            pltpu.VMEM((total, 4 * HALF), jnp.bfloat16),
            pltpu.VMEM((16, total), jnp.bfloat16),
            pltpu.VMEM(((2 * HALF + 1) * planes, NX), jnp.float32),
        ],
        compiler_params=pltpu.CompilerParams(vmem_limit_bytes=VMEM_LIMIT),
        cost_estimate=pl.CostEstimate(
            flops=4 * rows * total * HALF * HALF, bytes_accessed=4 * came.size, transcendentals=0
        ),
        name="wave_band",
    )(*operands)


def poisson_kernel(pws, own_ref, kernel_ref, came_ref, forth_ref, back_ref, both_x_ref, send_ref):
    count, parts, planes, unused = came_ref.shape
    pairs = parts // 2
    fields = [came_ref[:, i].reshape(NZ, NX) for i in range(parts)]
    level = jnp.mean(fields[0], axis=(0, 1), keepdims=True)
    fields[0] = fields[0] - jnp.where(own_ref[1] == 0, level, 0.0)
    field = jnp.concatenate(fields, axis=1)
    turned = mul3_left(forth_ref[...], field, NN)

    def part(array, half, i):
        return array[half * NZ : (half + 1) * NZ, i * NX : (i + 1) * NX]

    lines = []
    for q in range(pairs):
        lines.append(part(turned, 0, 2 * q) + part(turned, 1, 2 * q + 1))
        lines.append(part(turned, 0, 2 * q + 1) - part(turned, 1, 2 * q))
    spectrum = mul3_right(jnp.concatenate(lines, axis=0), both_x_ref[...], NN)

    lines = []
    for q in range(pairs):
        real = spectrum[2 * q * NZ : (2 * q + 1) * NZ]
        imag = spectrum[(2 * q + 1) * NZ : (2 * q + 2) * NZ]
        kernel = kernel_ref[q]
        lines.append((real[:, :NX] + imag[:, NX:]) * kernel)
        lines.append((imag[:, :NX] - real[:, NX:]) * kernel)
    turned = mul3_right(jnp.concatenate(lines, axis=0), both_x_ref[...], NN)
    lines = []
    for q in range(pairs):
        real = turned[2 * q * NZ : (2 * q + 1) * NZ]
        imag = turned[(2 * q + 1) * NZ : (2 * q + 2) * NZ]
        lines.append(real[:, :NX] - imag[:, NX:])
        lines.append(real[:, NX:] + imag[:, :NX])
    turned = mul3_left(back_ref[...], jnp.concatenate(lines, axis=1), NN)

    kpts = count // pws
    merged = NZ // pws // 8
    block = NX // kpts
    rows = pws * 8
    lane = lax.broadcasted_iota(jnp.int32, (rows, LANES), 1) // block
    for q in range(pairs):
        real = part(turned, 0, 2 * q) - part(turned, 1, 2 * q + 1)
        imag = part(turned, 0, 2 * q + 1) + part(turned, 1, 2 * q)
        for c, value in enumerate((real, imag)):
            for place, a in enumerate(ring_order(kpts)):
                packed = None
                for m in range(merged):
                    piece = value[m * rows : (m + 1) * rows]
                    shift = (m - a) * block % LANES
                    if shift:
                        piece = pltpu.roll(piece, shift, 1)
                    packed = piece if m == 0 else jnp.where(lane == m, piece, packed)
                send_ref[place * pws : (place + 1) * pws, 2 * q + c] = packed.reshape(pws, 8, LANES)


def poisson(pws, own, kernel, came, forth, back, both_x):
    vmem = pl.BlockSpec(memory_space=pltpu.VMEM)
    count, parts, unused, unused = came.shape
    return pl.pallas_call(
        functools.partial(poisson_kernel, pws),
        in_specs=[pl.BlockSpec(memory_space=pltpu.SMEM)] + [vmem] * 5,
        out_specs=vmem,
        out_shape=jax.ShapeDtypeStruct((count, parts, 8, LANES), jnp.float32),
        compiler_params=pltpu.CompilerParams(vmem_limit_bytes=VMEM_LIMIT),
        name="poisson",
    )(own, kernel, came, forth, back, both_x)


def finish_kernel(own_ref, came_ref, back_ref, *refs):
    *block_refs, density_ref, out_ref, held = refs
    kpts = len(block_refs)
    planes, block, unused = out_ref.shape
    merged = planes // 8
    for s, block_ref in enumerate(block_refs):
        sender = lax.rem(own_ref[0] + kpts - s, kpts)
        density_ref[pl.ds(sender * (planes // kpts), planes // kpts)] = block_ref[...]
    held[0 : 16 * HALF, :] = came_ref[...]
    for h in range(8):
        lines = held[pl.ds(h, 2 * HALF, stride=8), :]
        field = mul3_right(lines, back_ref[...], TN)
        out_ref[h * merged : (h + 1) * merged] = field.reshape(merged, block, NY)


def finish(planes, block, own, came, back_y, blocks):
    vmem = pl.BlockSpec(memory_space=pltpu.VMEM)
    return pl.pallas_call(
        finish_kernel,
        in_specs=[pl.BlockSpec(memory_space=pltpu.SMEM)] + [vmem] * (2 + len(blocks)),
        out_specs=[vmem] * 2,
        out_shape=[jax.ShapeDtypeStruct((planes, block, NY), jnp.float32)] * 2,
        scratch_shapes=[pltpu.VMEM((16 * HALF + 8, LANES), jnp.float32)],
        compiler_params=pltpu.CompilerParams(vmem_limit_bytes=VMEM_LIMIT),
        name="finish",
    )(own, came, back_y, *blocks)


def exchange(array):
    kpts, pws = lax.axis_size("kpt"), lax.axis_size("pw")
    kpt_order, pw_order = group_order(kpts, pws)
    group = [k * pws + j for k in kpt_order for j in pw_order]
    return lax.all_to_all(
        array, ("kpt", "pw"), split_axis=0, concat_axis=0, tiled=True, axis_index_groups=[group]
    )


def place_in(order, axis):
    places = jnp.asarray(np.argsort(np.array(order)), jnp.int32)
    return lax.dynamic_index_in_dim(places, lax.axis_index(axis), 0, keepdims=False)


def local_planes(band_coeffs, miller_third, column_slot, column_map, kpoint_counts):
    pws = lax.axis_size("pw")
    kpts = lax.axis_size("kpt")
    count = pws * kpts
    slots = column_map.shape[0]
    band_count = band_coeffs.shape[1]
    z_width = column_slot.shape[1] // slots
    planes = NZ // count
    parts = 2 * HALF // count
    made = tables(kpts, pws, planes)
    pencil = stack_table(made["pencil"](z_width), 1)
    wave_x, forth_z, back_z = (
        stack_table(made[name], 1) for name in ("wave_x", "forth_z", "back_z")
    )
    wave_y, forth_y, back_y, both_x = (
        stack_table(made[name], 0) for name in ("wave_y", "forth_y", "back_y", "both_x")
    )

    tiles = slots // LANES
    length = column_slot.shape[1] // LANES
    coeffs = band_coeffs.reshape(band_count, 2, length, LANES).transpose(0, 2, 1, 3)
    coeffs = coeffs.reshape(band_count, 2 * length, LANES)
    miller = miller_third.reshape(length, LANES)
    slot = column_slot.reshape(length, LANES)
    scale = 2.0 / (column_slot.shape[1] * pws)
    arrived = []
    for band in range(band_count):
        packed = pack_band(
            band, count, coeffs, miller, slot, pencil, slots, column_map
        )
        arrived.append(exchange(packed))
    kpt_order, pw_order = group_order(kpts, pws)
    device = place_in(kpt_order, "kpt") * pws + place_in(pw_order, "pw")
    own = jnp.stack((lax.axis_index("kpt"), device * (parts // 2))).astype(jnp.int32)
    former = cell = None
    for band in range(band_count):
        forth = forth_y if band == band_count - 1 else None
        made_here = wave_band(
            kpts,
            tiles,
            pws * slots,
            scale,
            own,
            kpoint_counts,
            arrived[band],
            wave_y,
            wave_x,
            forth,
            former,
            cell,
        )
        former = made_here[0]
        if band == 0:
            kernel, cell = made_here[kpts if forth is not None else 1 :][:2]
    half = exchange(made_here[-1].reshape(count, parts, planes, NX))
    blocks = [made_here[0]] + [
        lax.ppermute(made_here[s], "kpt", [(a, (a + s) % kpts) for a in range(kpts)])
        for s in range(1, kpts)
    ]
    back = poisson(pws, own, kernel, half, forth_z, back_z, both_x)
    back = exchange(back).reshape(count * parts * 8, LANES)
    return tuple(finish(NZ // pws, NX // kpts, own, back, back_y, blocks))


def fits_planes(kpts, pws):
    count = kpts * pws
    own = NZ // pws
    return (
        NZ % count == 0
        and NZ // count == 8
        and 2 * HALF % (2 * count) == 0
        and NX % kpts == 0
        and own % 8 == 0
        and own // 8 * (NX // kpts) == LANES
    )


def local(band_coeffs, miller_third, column_slot, column_map, kpoint_counts):
    slots = column_map.shape[0]
    plain = slots % LANES == 0 and LANES <= slots <= 8 * RANK_LOW
    plain = plain and column_slot.shape[1] == slots * LANES
    fits = plain and fits_planes(lax.axis_size("kpt"), lax.axis_size("pw"))
    chosen = local_planes if fits else local_general
    return chosen(band_coeffs, miller_third, column_slot, column_map, kpoint_counts)


def solution(mesh):
    return jax.shard_map(
        local,
        mesh=mesh,
        in_specs=(P("kpt", None, None, "pw"), P("kpt", "pw"), P("kpt", "pw"), P("pw"), P()),
        out_specs=(P("pw", "kpt", None), P("pw", "kpt", None)),
        check_vma=False,
    )
```
